32 devices in a mesh: section: 2 (over core), dp: 4 (over y, x), tensor: 4 (over z).
Axes of the slice: x: 2, y: 2, z: 4, core: 2. Of those that a mesh axis runs over, the one named last changes fastest.
Arguments:
- images: bfloat16 [4, 3152, 768], P(None, ('dp', 'tensor')), may hold values from -6 to 6
- cotangent: bfloat16 [4, 3152, 768], P(None, ('dp', 'tensor')), may hold values from -6 to 6
- counts: int32 [4, 4], P(None, 'dp'), may hold values from 1 to 4, as said below
- ln1_gain: bfloat16 [2, 768], P('section', 'dp'), may hold values from 0.099609375 to 1.8984375
- ln1_bias: bfloat16 [2, 768], P('section', 'dp'), may hold values from -2 to 2
- q_bias: bfloat16 [2, 12, 64], P('section', 'tensor', 'dp'), may hold values from -3 to 3
- v_bias: bfloat16 [2, 12, 64], P('section', 'tensor', 'dp'), may hold values from -3 to 3
- qkv_weight: bfloat16 [2, 768, 3, 768], P('section', 'dp', None, 'tensor'), may hold values from -0.21875 to 0.21875
- out_weight: bfloat16 [2, 768, 768], P('section', 'tensor', 'dp'), may hold values from -0.875 to 0.875
- out_bias: bfloat16 [2, 768], P('section', 'dp'), may hold values from -2 to 2
- ln2_gain: bfloat16 [2, 768], P('section', 'dp'), may hold values from 0.099609375 to 1.8984375
- ln2_bias: bfloat16 [2, 768], P('section', 'dp'), may hold values from -2 to 2
- up_weight: bfloat16 [2, 768, 3072], P('section', 'dp', 'tensor'), may hold values from -0.21875 to 0.21875
- up_bias: bfloat16 [2, 48, 64], P('section', 'tensor', 'dp'), may hold values from -3 to 3
- down_weight: bfloat16 [2, 3072, 768], P('section', 'tensor', 'dp'), may hold values from -0.109375 to 0.109375
- down_bias: bfloat16 [2, 768], P('section', 'dp'), may hold values from -2 to 2
Outputs:
- section_out: bfloat16 [2, 4, 3152, 768], P('section', None, ('dp', 'tensor'))
- input_grad: bfloat16 [2, 4, 3152, 768], P('section', None, ('dp', 'tensor'))
- qkv_grad: float32 [2, 768, 3, 768], P('section', 'dp', None, 'tensor')
- out_weight_grad: float32 [2, 768, 768], P('section', 'tensor', 'dp')
- up_weight_grad: float32 [2, 768, 3072], P('section', 'dp', 'tensor')
- down_weight_grad: float32 [2, 3072, 768], P('section', 'tensor', 'dp')
- q_bias_grad: float32 [2, 12, 64], P('section', 'tensor', 'dp')
- v_bias_grad: float32 [2, 12, 64], P('section', 'tensor', 'dp')
- up_bias_grad: float32 [2, 48, 64], P('section', 'tensor', 'dp')
- vector_grad: float32 [2, 6, 768], P('section', None, ('dp', 'tensor'))
The draws below stay inside these ranges and needn't reach their ends.
Inputs may be any that keep to these rules, and one draw needn't show every extreme that they name: counts[m, i] live image slots of dp index i in micro-batch m are its first ones; in every micro-batch some index has all 4 live.
All inputs are finite; a program needn't handle non-finite values.
Results may differ from the reference program's by a relative error of at most 0.017.
Values may be sent and summed in bfloat16 or wider, within the bound.
A program may use at most 256 MiB of HBM per device.

```python
import jax
import jax.numpy as jnp
from jax import lax

D = 768
H = 12
DH = 64
FF = 3072
SEQ = 197
SLOTS = 4
MB = 4
ROWS = 3152
N_SECTION = 2
N_DP = 4


def draw_counts(key, part):
    key = jax.random.fold_in(key, 7)
    first_key, second_key = jax.random.split(key)
    base_counts = jax.random.randint(first_key, (MB, N_DP), 1, SLOTS + 1)
    full_index = jax.random.randint(second_key, (MB, 1), 0, N_DP)
    columns = jnp.arange(N_DP)[None, :]
    return jnp.where(columns == full_index, SLOTS, base_counts).astype(jnp.int32)


def level_of(own_key, dims, cuts, smallest, largest):
    loudness = 1.0
    for position, blocks in cuts:
        heights = jax.random.uniform(jax.random.fold_in(jax.random.fold_in(own_key, 6), position), (blocks,), jnp.float32, smallest / len(cuts), largest / len(cuts))
        loudness = loudness * jnp.repeat(jnp.exp(heights), dims[position] // blocks).reshape((-1,) + (1,) * (len(dims) - 1 - position))
    return loudness


def noise(stream_key, shape, scale, limit, pieces=(), kind=jnp.bfloat16):
    factor_of = level_of(stream_key, shape, pieces, -0.22, 0.18) if pieces else 1.0
    array = jax.random.normal(stream_key, shape, jnp.float32) * scale * factor_of
    return jnp.minimum(jnp.maximum(array, -limit), limit).astype(kind)


def setup_inputs(seed: int = 0) -> dict:
    seeds = jax.random.split(jax.random.key(seed), 17)
    images = noise(seeds[0], (MB, ROWS, D), 1.0, 6.0, ((1, 16),))
    cotangent = noise(seeds[1], (MB, ROWS, D), 1.0, 6.0, ((1, 16),))
    counts = draw_counts(jax.random.fold_in(seeds[16], 71), 0)
    ln1_gain = jnp.clip(1.0 + 0.18 * jax.random.normal(seeds[3], (N_SECTION, D), jnp.float32), 0.099609375, 1.8984375).astype(jnp.bfloat16)
    ln1_bias = noise(seeds[4], (N_SECTION, D), 0.3, 2.0, ((0, 2), (1, 4)))
    q_bias = noise(seeds[5], (N_SECTION, H, DH), 0.5, 3.0, ((0, 2), (1, 4), (2, 4)))
    v_bias = noise(seeds[6], (N_SECTION, H, DH), 0.5, 3.0, ((0, 2), (1, 4), (2, 4)))
    qkv_weight = noise(seeds[7], (N_SECTION, D, 3, D), D ** -0.5, 0.21875, ((0, 2), (1, 4), (3, 4)))
    out_weight = noise(seeds[8], (N_SECTION, D, D), (D // 16) ** -0.5, 0.875, ((0, 2), (1, 4), (2, 4)))
    out_bias = noise(seeds[9], (N_SECTION, D), 0.3, 2.0, ((0, 2), (1, 4)))
    ln2_gain = jnp.clip(1.0 + 0.18 * jax.random.normal(seeds[10], (N_SECTION, D), jnp.float32), 0.099609375, 1.8984375).astype(jnp.bfloat16)
    ln2_bias = noise(seeds[11], (N_SECTION, D), 0.3, 2.0, ((0, 2), (1, 4)))
    up_weight = noise(seeds[12], (N_SECTION, D, FF), D ** -0.5, 0.21875, ((0, 2), (1, 4), (2, 4)))
    up_bias = noise(seeds[13], (N_SECTION, FF // DH, DH), 0.5, 3.0, ((0, 2), (1, 4), (2, 4)))
    down_weight = noise(seeds[14], (N_SECTION, FF, D), FF ** -0.5, 0.109375, ((0, 2), (1, 4), (2, 4)))
    down_bias = noise(seeds[15], (N_SECTION, D), 0.3, 2.0, ((0, 2), (1, 4)))
    return {"images": images, "cotangent": cotangent, "counts": counts, "ln1_gain": ln1_gain, "ln1_bias": ln1_bias, "q_bias": q_bias, "v_bias": v_bias, "qkv_weight": qkv_weight, "out_weight": out_weight, "out_bias": out_bias, "ln2_gain": ln2_gain, "ln2_bias": ln2_bias, "up_weight": up_weight, "up_bias": up_bias, "down_weight": down_weight, "down_bias": down_bias}


@jax.custom_vjp
def low(v):
    return lax.optimization_barrier(v.astype(jnp.bfloat16)).astype(jnp.float32)

@jax.custom_vjp
def low_back(v):
    return v

def low_keep(v):
    return (low(v), None)

def low_pass(kept, grad):
    return (grad,)

def back_keep(v):
    return (v, None)

def back_low(kept, grad):
    return (low(grad),)
low.defvjp(low_keep, low_pass)
low_back.defvjp(back_keep, back_low)
precise = lax.Precision.HIGHEST

def norm_rows(values, row_gain, row_shift):
    average = lax.optimization_barrier(jnp.mean(values, axis=-1, keepdims=True))
    centered = values - average
    spread = lax.optimization_barrier(jnp.mean(centered * centered, axis=-1, keepdims=True))
    return centered * lax.rsqrt(spread + 1e-06) * row_gain + row_shift

def attend(triple):
    queries, key_rows, val_rows = triple
    scores = low_back(jnp.einsum('ishd,ithd->ihst', queries, key_rows, precision=precise) * DH ** (-0.5))
    weights = low(jax.nn.softmax(scores, axis=-1))
    return jnp.einsum('ihst,ithd->ishd', weights, val_rows, precision=precise)

def encoder(rows_in, params, live_rows):
    gain_one, shift_one, bias_q, bias_v, w_qkv, w_out, bias_out, gain_two, shift_two, w_up, bias_up, w_down, bias_down = params
    normed = low(norm_rows(rows_in, gain_one, shift_one))
    zeros_row = jnp.zeros((D,), jnp.float32)
    bias_all = jnp.stack([bias_q.reshape(D), zeros_row, bias_v.reshape(D)])
    mixed = jnp.einsum('rd,dce->rce', normed, w_qkv, precision=precise) + bias_all
    mixed = low_back(low(mixed))
    shaped = mixed.reshape(N_DP, SLOTS, SEQ, 3, H, DH)
    heads_out = lax.map(jax.checkpoint(attend), (shaped[:, :, :, 0], shaped[:, :, :, 1], shaped[:, :, :, 2]))
    heads_out = low_back(low(heads_out.reshape(ROWS, D)))
    middle = rows_in + low_back(jnp.dot(heads_out, w_out, precision=precise)) + bias_out
    normed_two = low(norm_rows(middle, gain_two, shift_two))
    hidden = low_back(jnp.dot(normed_two, w_up, precision=precise) + bias_up.reshape(FF))
    active = low(jax.nn.gelu(hidden, approximate=False))
    result = middle + low_back(jnp.dot(active, w_down, precision=precise)) + bias_down
    return result * live_rows[:, None]

def reference(images, cotangent, counts, ln1_gain, ln1_bias, q_bias, v_bias, qkv_weight, out_weight, out_bias, ln2_gain, ln2_bias, up_weight, up_bias, down_weight, down_bias):
    params = tuple((weight_arg.astype(jnp.float32) for weight_arg in (ln1_gain, ln1_bias, q_bias, v_bias, qkv_weight, out_weight, out_bias, ln2_gain, ln2_bias, up_weight, up_bias, down_weight, down_bias)))
    inputs = images.astype(jnp.float32)
    upstream = cotangent.astype(jnp.float32)
    rows_index = jnp.arange(ROWS)
    slot_of_row = rows_index % (SLOTS * SEQ) // SEQ
    group_of_row = rows_index // (SLOTS * SEQ)

    def forward(inputs, params, extra_grad):
        section_one = [weight_arg[0] for weight_arg in params]
        section_two = [weight_arg[1] for weight_arg in params]

        def one_batch(batch_item):
            block_rows, added_grad, count_row = batch_item
            live_rows = (slot_of_row < count_row[group_of_row]).astype(jnp.float32)
            sent_rows = low(encoder(block_rows, section_one, live_rows))
            final_rows = encoder(low_back(sent_rows + added_grad), section_two, live_rows)
            return (sent_rows, final_rows)
        return lax.map(jax.checkpoint(one_batch), (inputs, extra_grad, counts))
    extra_grad = jnp.zeros_like(inputs)
    (sent_rows, final_rows), pullback = jax.vjp(forward, inputs, params, extra_grad)
    grad_in, grad_params, grad_extra = pullback((jnp.zeros_like(sent_rows), upstream))
    section_out = jnp.stack([sent_rows, final_rows]).astype(jnp.bfloat16)
    input_grad = jnp.stack([grad_in, grad_extra]).astype(jnp.bfloat16)
    vectors = jnp.stack([grad_params[0], grad_params[1], grad_params[6], grad_params[7], grad_params[8], grad_params[12]], axis=1)
    return (section_out, input_grad, grad_params[4], grad_params[5], grad_params[9], grad_params[11], grad_params[2], grad_params[3], grad_params[10], vectors)
```

```python
import jax
import jax.numpy as jnp
from jax import lax
from jax.sharding import PartitionSpec as P

DH = 64
SEQ = 197
EPS = 1e-06

rows_by_rows = (((0,), (0,)), ((), ()))
cols_by_cols = (((1,), (1,)), ((), ()))
AXES = ("section", "tensor", "dp")


def norm_rows(values, row_gain, row_shift):
    average = jnp.mean(values, axis=-1, keepdims=True)
    centered = values - average
    spread = jnp.mean(centered * centered, axis=-1, keepdims=True)
    return centered * lax.rsqrt(spread + EPS) * row_gain + row_shift


def gelu_exact(values):
    return jax.nn.gelu(values, approximate=False)


def split_heads(mixed):
    blocks = mixed.reshape(-1, SEQ, 3, mixed.shape[1] // (3 * DH), DH)
    return (blocks[:, :, 0], blocks[:, :, 1], blocks[:, :, 2])


def attend_rows(mixed):
    queries, key_rows, val_rows = split_heads(mixed)
    scores = jnp.einsum(
        "sqhd,skhd->shqk", queries, key_rows, preferred_element_type=jnp.float32
    ) * DH ** (-0.5)
    row_top = jnp.max(scores, axis=-1, keepdims=True)
    log_total = row_top + jnp.log(jnp.sum(jnp.exp(scores - row_top), axis=-1, keepdims=True))
    weights = jnp.exp(scores - log_total).astype(jnp.bfloat16)
    output = jnp.einsum("shqk,skhd->sqhd", weights, val_rows, preferred_element_type=jnp.float32)
    return (output.reshape(mixed.shape[0], -1).astype(jnp.bfloat16), log_total)


def attend_back(mixed, log_total, grad_heads):
    queries, key_rows, val_rows = split_heads(mixed)
    scaling = DH ** (-0.5)
    scores = (
        jnp.einsum("sqhd,skhd->shqk", queries, key_rows, preferred_element_type=jnp.float32)
        * scaling
    )
    chances = jnp.exp(scores - log_total)
    grad_out = grad_heads.reshape(queries.shape)
    grad_chances = jnp.einsum(
        "sqhd,skhd->shqk", grad_out, val_rows, preferred_element_type=jnp.float32
    )
    grad_scores = (
        chances * (grad_chances - jnp.sum(chances * grad_chances, axis=-1, keepdims=True))
    ).astype(jnp.bfloat16)
    grad_q = (
        jnp.einsum("shqk,skhd->sqhd", grad_scores, key_rows, preferred_element_type=jnp.float32)
        * scaling
    )
    grad_k = (
        jnp.einsum("shqk,sqhd->skhd", grad_scores, queries, preferred_element_type=jnp.float32)
        * scaling
    )
    grad_v = jnp.einsum(
        "shqk,sqhd->skhd",
        chances.astype(jnp.bfloat16),
        grad_out,
        preferred_element_type=jnp.float32,
    )
    stacked = jnp.stack([grad_q, grad_k, grad_v], axis=2)
    return stacked.reshape(mixed.shape[0], -1).astype(jnp.bfloat16)


def full_weights(blocks):
    n_tensor, width, span = blocks.shape[1:]
    part = span // 4
    w_qkv = blocks[0, :, :, : 3 * part].reshape(n_tensor, width, 3, part)
    w_qkv = w_qkv.transpose(1, 2, 0, 3).reshape(width, -1)
    w_out = blocks[0, :, :, 3 * part :].transpose(0, 2, 1).reshape(-1, width)
    w_up = blocks[1].transpose(1, 0, 2).reshape(width, -1)
    w_down = blocks[2].transpose(0, 2, 1).reshape(-1, width)
    return (w_qkv, w_out, w_up, w_down)


def grad_blocks(n_tensor, w_qkv, w_out, w_up, w_down):
    width = w_up.shape[0]
    part = width // n_tensor
    qkv = w_qkv.reshape(width, 3, n_tensor, part).transpose(2, 0, 1, 3).reshape(n_tensor, width, -1)
    out = w_out.reshape(n_tensor, part, width).transpose(0, 2, 1)
    up = w_up.reshape(width, n_tensor, -1).transpose(1, 0, 2)
    down = w_down.reshape(n_tensor, -1, width).transpose(0, 2, 1)
    return jnp.stack([jnp.concatenate([qkv, out], axis=2), up, down])


def forward_rows(rows_in, params, live_rows):
    vectors, bias_all, bias_up, w_qkv, w_out, w_up, w_down = params
    normed = norm_rows(rows_in, vectors[0], vectors[1]).astype(jnp.bfloat16)
    mixed = (jnp.dot(normed, w_qkv, preferred_element_type=jnp.float32) + bias_all).astype(
        jnp.bfloat16
    )
    heads_out, log_total = attend_rows(mixed)
    middle = rows_in + jnp.dot(heads_out, w_out, preferred_element_type=jnp.float32) + vectors[2]
    normed_two = norm_rows(middle, vectors[3], vectors[4]).astype(jnp.bfloat16)
    hidden = jnp.dot(normed_two, w_up, preferred_element_type=jnp.float32) + bias_up
    active = gelu_exact(hidden).astype(jnp.bfloat16)
    ffn_term = jnp.dot(active, w_down, preferred_element_type=jnp.float32)
    result = (middle + ffn_term + vectors[5]) * live_rows
    return result, (rows_in, normed, mixed, log_total, heads_out, middle, normed_two, hidden, active)


def backward_rows(grad_result, saved, params, live_rows):
    vectors, bias_all, bias_up, w_qkv, w_out, w_up, w_down = params
    rows_in, normed, mixed, log_total, heads_out, middle, normed_two, hidden, active = saved
    grad_res = grad_result * live_rows
    grad_low = grad_res.astype(jnp.bfloat16)
    w_down_grad = lax.dot_general(
        active, grad_low, rows_by_rows, preferred_element_type=jnp.float32
    )
    grad_active = lax.dot_general(grad_low, w_down, cols_by_cols, preferred_element_type=jnp.float32)
    _, gelu_pull = jax.vjp(gelu_exact, hidden)
    grad_hidden = gelu_pull(grad_active)[0].astype(jnp.bfloat16)
    up_bias_grad = jnp.sum(grad_hidden, axis=0, dtype=jnp.float32)
    w_up_grad = lax.dot_general(
        normed_two, grad_hidden, rows_by_rows, preferred_element_type=jnp.float32
    )
    grad_norm_two = lax.dot_general(
        grad_hidden, w_up, cols_by_cols, preferred_element_type=jnp.float32
    )
    _, norm_pull_two = jax.vjp(norm_rows, middle, vectors[3], vectors[4])
    grad_middle, gain_two_grad, shift_two_grad = norm_pull_two(grad_norm_two)
    grad_middle = grad_res + grad_middle
    middle_low = grad_middle.astype(jnp.bfloat16)
    w_out_grad = lax.dot_general(
        heads_out, middle_low, rows_by_rows, preferred_element_type=jnp.float32
    )
    grad_heads = lax.dot_general(
        middle_low, w_out, cols_by_cols, preferred_element_type=jnp.float32
    ).astype(jnp.bfloat16)
    grad_mixed = attend_back(mixed, log_total, grad_heads)
    bias_sums = jnp.sum(grad_mixed, axis=0, dtype=jnp.float32).reshape(3, -1)
    w_qkv_grad = lax.dot_general(
        normed, grad_mixed, rows_by_rows, preferred_element_type=jnp.float32
    )
    grad_norm_one = lax.dot_general(
        grad_mixed, w_qkv, cols_by_cols, preferred_element_type=jnp.float32
    )
    _, norm_pull_one = jax.vjp(norm_rows, rows_in, vectors[0], vectors[1])
    grad_rows, gain_one_grad, shift_one_grad = norm_pull_one(grad_norm_one)
    grad_rows = grad_middle + grad_rows
    vector_grads = jnp.stack(
        [
            gain_one_grad,
            shift_one_grad,
            jnp.sum(grad_middle, axis=0),
            gain_two_grad,
            shift_two_grad,
            jnp.sum(grad_res, axis=0),
        ]
    )
    return (
        grad_rows,
        tuple(g.astype(jnp.bfloat16) for g in (w_qkv_grad, w_out_grad, w_up_grad, w_down_grad)),
        (vector_grads, bias_sums[0], bias_sums[2], up_bias_grad),
    )


def shards(
    images,
    cotangent,
    counts,
    ln1_gain,
    ln1_bias,
    q_bias,
    v_bias,
    qkv_weight,
    out_weight,
    out_bias,
    ln2_gain,
    ln2_bias,
    up_weight,
    up_bias,
    down_weight,
    down_bias,
):
    n_section, n_dp, n_tensor = (lax.axis_size(a) for a in ("section", "dp", "tensor"))
    section_idx = lax.axis_index("section")
    micro_count, share_rows, width = images.shape
    own_count = micro_count // n_section
    depth = qkv_weight.shape[1]
    part = qkv_weight.shape[3]

    own = section_idx * own_count
    own_images = lax.dynamic_slice_in_dim(images, own, own_count, 0).reshape(-1, width)
    own_grads = lax.dynamic_slice_in_dim(cotangent, own, own_count, 0).reshape(-1, width)
    row_place = lax.axis_index("tensor") * share_rows + jnp.arange(share_rows)
    own_counts = lax.dynamic_slice_in_dim(counts, own, own_count, 0)
    live_rows = (row_place // SEQ < own_counts).astype(jnp.float32).reshape(-1, 1)

    shard = jnp.stack(
        [
            jnp.concatenate([qkv_weight[0].reshape(depth, -1), out_weight[0].T], axis=1),
            up_weight[0],
            down_weight[0].T,
        ]
    )
    gathered = lax.all_gather(shard, AXES, axis=0)
    gathered = gathered.reshape(n_section, n_tensor, n_dp, 3, depth, -1).transpose(0, 3, 1, 2, 4, 5)
    gathered = gathered.reshape(n_section, 3, n_tensor, width, -1)

    small = [ln1_gain, ln1_bias, out_bias, ln2_gain, ln2_bias, down_bias, q_bias, v_bias, up_bias]
    sizes = [piece.size for piece in small]
    all_small = lax.all_gather(jnp.concatenate([s.reshape(-1) for s in small]), AXES, axis=0)
    all_small = all_small.reshape(n_section, n_tensor, n_dp, -1).astype(jnp.float32)

    def params_of(sec):
        pieces, start = [], 0
        for size in sizes:
            pieces.append(all_small[sec, :, :, start : start + size])
            start += size
        vectors = [p[0].reshape(-1) for p in pieces[:6]]
        heads = [
            p.reshape(n_tensor, n_dp, -1, DH // n_dp).transpose(0, 2, 1, 3).reshape(-1)
            for p in pieces[6:]
        ]
        bias_all = jnp.concatenate([heads[0], jnp.zeros_like(heads[0]), heads[1]])
        return (vectors, bias_all, heads[2], *full_weights(gathered[sec]))

    params = [params_of(sec) for sec in range(n_section)]

    first_out, first_saved = forward_rows(own_images.astype(jnp.float32), params[0], live_rows)
    first_low = first_out.astype(jnp.bfloat16)
    second_out, second_saved = forward_rows(first_low.astype(jnp.float32), params[1], live_rows)
    second_low = second_out.astype(jnp.bfloat16)
    second_grad, second_w, second_v = backward_rows(
        own_grads.astype(jnp.float32), second_saved, params[1], live_rows
    )
    second_grad = second_grad.astype(jnp.bfloat16)
    first_grad, first_w, first_v = backward_rows(
        second_grad.astype(jnp.float32), first_saved, params[0], live_rows
    )
    first_grad = first_grad.astype(jnp.bfloat16)

    def placed_rows(first, second):
        is_first = section_idx == 0
        away = jnp.where(is_first, second, first)
        came = lax.ppermute(away, "section", [(0, 1), (1, 0)])
        home = jnp.where(is_first, first, second)
        shape = (own_count, share_rows, width)
        home, came = home.reshape(shape), came.reshape(shape)
        low = jnp.where(is_first, home, came)
        high = jnp.where(is_first, came, home)
        return jnp.concatenate([low, high], axis=0)[None]

    section_out = placed_rows(first_low, second_low)
    input_grad = placed_rows(first_grad, second_grad)

    weight_parts = jnp.stack([grad_blocks(n_tensor, *first_w), grad_blocks(n_tensor, *second_w)])
    weight_parts = weight_parts.reshape(n_section, 3, n_tensor, n_dp, depth, -1)
    weight_parts = weight_parts.transpose(0, 2, 3, 1, 4, 5).reshape(
        n_section * n_tensor * n_dp, 3, depth, -1
    )
    weight_sum = lax.psum_scatter(weight_parts, AXES, scatter_dimension=0)
    weight_sum = weight_sum.astype(jnp.float32)

    def small_parts(vector_grads, q_sum, v_sum, up_sum):
        vec = vector_grads.reshape(6, n_dp, n_tensor, -1).transpose(2, 1, 0, 3)
        heads = [
            h.reshape(n_tensor, -1, n_dp, DH // n_dp).transpose(0, 2, 1, 3)
            for h in (q_sum, v_sum, up_sum)
        ]
        return jnp.concatenate([p.reshape(n_tensor, n_dp, -1) for p in (vec, *heads)], axis=2)

    small_all = jnp.stack([small_parts(*first_v), small_parts(*second_v)])
    small_sum = lax.psum_scatter(
        small_all.reshape(n_section * n_tensor * n_dp, -1), AXES, scatter_dimension=0
    )
    vec_size = 6 * width // (n_dp * n_tensor)
    head_size = q_bias.size
    vec = small_sum[:vec_size].reshape(1, 6, -1)
    q_sum = small_sum[vec_size : vec_size + head_size].reshape(q_bias.shape)
    v_sum = small_sum[vec_size + head_size : vec_size + 2 * head_size].reshape(v_bias.shape)
    up_sum = small_sum[vec_size + 2 * head_size :].reshape(up_bias.shape)

    return (
        section_out,
        input_grad,
        weight_sum[0, :, : 3 * part].reshape(qkv_weight.shape),
        weight_sum[0, :, 3 * part :].T[None],
        weight_sum[1][None],
        weight_sum[2].T[None],
        q_sum,
        v_sum,
        up_sum,
        vec,
    )


def solution(mesh):
    placed = (
        P(None, ("dp", "tensor"), None),
        P(None, ("dp", "tensor"), None),
        P(None, "dp"),
        P("section", "dp"),
        P("section", "dp"),
        P("section", "tensor", "dp"),
        P("section", "tensor", "dp"),
        P("section", "dp", None, "tensor"),
        P("section", "tensor", "dp"),
        P("section", "dp"),
        P("section", "dp"),
        P("section", "dp"),
        P("section", "dp", "tensor"),
        P("section", "tensor", "dp"),
        P("section", "tensor", "dp"),
        P("section", "dp"),
    )
    return jax.shard_map(
        shards,
        mesh=mesh,
        in_specs=placed,
        out_specs=(
            P("section", None, ("dp", "tensor"), None),
            P("section", None, ("dp", "tensor"), None),
            P("section", "dp", None, "tensor"),
            P("section", "tensor", "dp"),
            P("section", "dp", "tensor"),
            P("section", "tensor", "dp"),
            P("section", "tensor", "dp"),
            P("section", "tensor", "dp"),
            P("section", "tensor", "dp"),
            P("section", None, ("dp", "tensor")),
        ),
        check_vma=False,
    )
```

```python
import functools
import jax
import jax.numpy as jnp
from jax import lax
from jax.experimental import pallas as pl
from jax.experimental.pallas import tpu as pltpu
from jax.sharding import PartitionSpec as P

CHUNK_ROWS = 48
MESH_ID = pl.DeviceIdType.MESH


def slot_sizes(n_dp, n_tensor):
    bits = [b for b in range(n_dp.bit_length()) if (1 << b) < n_dp]
    mid = n_tensor // 2
    weights = [bin(e).count("1") for e in range(n_dp)]

    def plane(weight):
        total = 0
        for j in range(mid):
            for e in range(n_dp):
                if weights[e] == weight:
                    for b in bits:
                        if not e >> b & 1:
                            chosen = [c for c in bits if (e | 1 << b) >> c & 1]
                            total += chosen[j % len(chosen)] == b
                    total += 2 * (weight >= 2) + 1
        return total

    first = [2 + len(bits)]
    columns = [2 * (2 + len(bits))] * (n_tensor - 1)
    planes = [plane(w) for w in range(1, len(bits) + 1)]
    crossed = [3 * mid * sum(w >= 2 for w in weights)]
    rest = [mid * sum(w == 1 for w in weights)]
    return first + [columns[0], planes[0], columns[1]] + planes[1:] + columns[2:] + crossed + rest


class Place:
    def __init__(self, n_dp, n_tensor):
        self.n_dp, self.n_tensor = n_dp, n_tensor
        self.mid = n_tensor // 2
        self.bits = [b for b in range(n_dp.bit_length()) if (1 << b) < n_dp]
        self.s = lax.axis_index("section")
        self.d = lax.axis_index("dp")
        self.t = lax.axis_index("tensor")
        self.upper = lax.div(self.t, self.mid)
        self.has_next = self.t < n_tensor - 1
        self.has_prev = self.t > 0

    def away(self, e):
        other = self.d
        for b in self.bits:
            if e >> b & 1:
                other = other + (1 << b) * (1 - 2 * lax.rem(lax.div(self.d, 1 << b), 2))
        return other

    def last_bit(self, e, j):
        chosen = [b for b in self.bits if e >> b & 1]
        return chosen[j % len(chosen)]

    def own_side(self, j):
        return self.upper * self.mid + j

    def other_side(self, j):
        return (1 - self.upper) * self.mid + j

    def sibling(self):
        return (1 - self.s, self.d, self.t)

    def along(self, step):
        return (self.s, self.d, self.t + step)

    def hop(self, b):
        return (self.s, self.away(1 << b), self.t)

    def meet(self):
        barrier = pltpu.get_barrier_semaphore()

        def greet(device):
            pl.semaphore_signal(barrier, inc=1, device_id=device, device_id_type=MESH_ID)

        greet(self.sibling())
        for b in self.bits:
            greet(self.hop(b))

        @pl.when(self.has_next)
        def _():
            greet(self.along(1))

        @pl.when(self.has_prev)
        def _():
            greet(self.along(-1))

        ends = jnp.where(self.has_next, 1, 0) + jnp.where(self.has_prev, 1, 0)
        pl.semaphore_wait(barrier, 1 + len(self.bits) + ends)

    def by_weight(self, weight):
        return [e for e in range(self.n_dp) if bin(e).count("1") == weight]


def gather_kernel(n_dp, n_tensor, shard, out, own_sem, sib_sem, recv_sem, send_sem, part_sem):
    at = Place(n_dp, n_tensor)
    n_blk, depth, span = shard.shape
    half = span // 2
    n_all = out.shape[0] * n_blk
    at.meet()

    def rows(e):
        return pl.ds(pl.multiple_of(at.away(e) * depth, 16), depth)

    lanes = pl.ds(pl.multiple_of(at.s * half, 128), half)

    def piece(i, e, tt):
        return out.at[lax.div(i, n_blk), lax.rem(i, n_blk), tt, rows(e), lanes]

    def whole(sec, b):
        return out.at[sec, b, at.t, rows(0), :]

    def share(b):
        return pltpu.make_async_remote_copy(
            src_ref=shard.at[b],
            dst_ref=whole(at.s, b),
            send_sem=own_sem.at[1, b],
            recv_sem=own_sem.at[2, b],
            device_id=at.sibling(),
            device_id_type=MESH_ID,
        )

    def keep(b):
        return pltpu.make_async_copy(shard.at[b], whole(at.s, b), own_sem.at[0, b])

    for b in range(n_blk):
        keep(b).start()
        share(b).start()

    def push(i, e, tt, device, e_there, slot, start):
        copy = pltpu.make_async_remote_copy(
            src_ref=piece(i, e, tt),
            dst_ref=piece(i, e, tt),
            send_sem=send_sem.at[i, slot],
            recv_sem=recv_sem.at[i, e_there * n_tensor + tt],
            device_id=device,
            device_id_type=MESH_ID,
        )
        if start:
            copy.start()
        else:
            copy.wait_send()

    def push_sib(i, e, tt, slot, start):
        copy = pltpu.make_async_remote_copy(
            src_ref=piece(i, e, tt),
            dst_ref=piece(i, e, tt),
            send_sem=send_sem.at[i, slot],
            recv_sem=part_sem.at[i, 0 if e == 0 else 1],
            device_id=at.sibling(),
            device_id_type=MESH_ID,
        )
        if start:
            copy.start()
        else:
            copy.wait_send()

    def await_piece(i, e, tt):
        pltpu.make_async_remote_copy(
            src_ref=piece(i, e, tt),
            dst_ref=piece(i, e, tt),
            send_sem=send_sem.at[i, 0],
            recv_sem=recv_sem.at[i, e * n_tensor + tt],
            device_id=at.sibling(),
            device_id_type=MESH_ID,
        ).wait_recv()

    def steps(i, start):
        slots = iter(range(10_000))

        def maybe(cond, action):
            if cond is None:
                action()
            else:
                pl.when(cond)(action)

        def ready(e, tt, cond=None):
            if start:
                maybe(cond, lambda: await_piece(i, e, tt))

        def go(e, tt, device, e_there, cond=None):
            slot = next(slots)
            maybe(cond, lambda: push(i, e, tt, device, e_there, slot, start))

        def go_sib(e, tt, cond=None):
            slot = next(slots)
            maybe(cond, lambda: push_sib(i, e, tt, slot, start))

        def first():
            sec, b = lax.div(i, n_blk), lax.rem(i, n_blk)
            if start:

                @pl.when(sec == at.s)
                def _():
                    pltpu.make_async_copy(shard.at[b], whole(at.s, b), own_sem.at[0, b]).wait()

                @pl.when(sec != at.s)
                def _():
                    pltpu.make_async_remote_copy(
                        src_ref=shard.at[b],
                        dst_ref=whole(1 - at.s, b),
                        send_sem=own_sem.at[1, b],
                        recv_sem=own_sem.at[2, b],
                        device_id=at.sibling(),
                        device_id_type=MESH_ID,
                    ).wait_recv()

            go(0, at.t, at.along(1), 0, at.has_next)
            go(0, at.t, at.along(-1), 0, at.has_prev)
            for b in at.bits:
                go(0, at.t, at.hop(b), 1 << b)

        def column(k):
            low, high = at.t >= k, at.t + k < n_tensor
            for tt, cond, dev, more in (
                (at.t - k, low, at.along(1), jnp.logical_and(low, at.has_next)),
                (at.t + k, high, at.along(-1), jnp.logical_and(high, at.has_prev)),
            ):
                ready(0, tt, cond)
                go(0, tt, dev, 0, more)
                for b in at.bits:
                    go(0, tt, at.hop(b), 1 << b, cond)
                go_sib(0, tt, cond)

        def plane(weight):
            for j in range(at.mid):
                for e in at.by_weight(weight):
                    tt = at.own_side(j)
                    ready(e, tt)
                    for b in at.bits:
                        if not e >> b & 1 and at.last_bit(e | 1 << b, j) == b:
                            go(e, tt, at.hop(b), e | 1 << b)
                    if weight >= 2:
                        go(e, tt, at.along(1), e, at.t == at.mid - 1)
                        go(e, tt, at.along(-1), e, at.t == at.mid)
                    go_sib(e, tt)

        def crossed():
            for weight in range(2, len(at.bits) + 1):
                for e in at.by_weight(weight):
                    for j in range(at.mid):
                        tt = at.other_side(j)
                        ready(e, tt)
                        up = jnp.logical_and(at.t >= at.mid, at.has_next)
                        down = jnp.logical_and(at.t < at.mid, at.has_prev)
                        go(e, tt, at.along(1), e, up)
                        go(e, tt, at.along(-1), e, down)
                        go_sib(e, tt)

        def rest():
            for e in at.by_weight(1):
                for j in range(at.mid):
                    tt = at.other_side(j)
                    ready(e, tt)
                    go_sib(e, tt)

        groups = [first]
        for k in range(1, n_tensor):
            groups.append(functools.partial(column, k))
        planes = [functools.partial(plane, w) for w in range(1, len(at.bits) + 1)]
        merged = [groups[0]]
        order = [groups[1], planes[0], groups[2]] + planes[1:] + groups[3:] + [crossed, rest]
        return merged + order, slots

    lags = [g - (g >= 3) - (g >= 5) for g in range(len(slot_sizes(n_dp, n_tensor)))]
    tail = max(lags)

    def body(it, carry):
        for g, lag in sorted(enumerate(lags), key=lambda item: item[1]):
            i = it - lag

            @pl.when(jnp.logical_and(i >= 0, i < n_all))
            def _():
                run_group(i, g)

        return carry

    def run_group(i, g):
        groups, slots = steps(i, True)
        sizes = slot_sizes(n_dp, n_tensor)
        for _ in range(sum(sizes[:g])):
            next(slots)
        groups[g]()

    def all_of(i, start):
        groups, _ = steps(i, start)
        for g in groups:
            g()

    lax.fori_loop(0, n_all + tail, body, 0)

    def finish(i, carry):
        all_of(i, False)
        sec, b = lax.div(i, n_blk), lax.rem(i, n_blk)
        for k, ref in (
            (0, out.at[sec, b, pl.ds(0, n_tensor - 1), pl.ds(0, depth), pl.ds(0, half)]),
            (1, out.at[sec, b, :, pl.ds(0, (n_dp - 1) * depth), pl.ds(0, half)]),
        ):
            pltpu.make_async_copy(ref, ref, part_sem.at[i, k]).wait()
        return carry

    lax.fori_loop(0, n_all, finish, 0)
    for b in range(n_blk):
        share(b).wait_send()


def gather_weights(shard, n_section, n_dp, n_tensor):
    n_blk, depth, span = shard.shape
    n_all = n_section * n_blk
    n_bits = n_dp.bit_length() - 1
    n_sends = (2 + n_bits) + (n_tensor - 1) * 2 * (2 + n_bits) + 6 * n_dp * n_tensor
    return pl.pallas_call(
        functools.partial(gather_kernel, n_dp, n_tensor),
        out_shape=jax.ShapeDtypeStruct((n_section, n_blk, n_tensor, n_dp * depth, span), shard.dtype),
        in_specs=[pl.BlockSpec(memory_space=pl.ANY)],
        out_specs=pl.BlockSpec(memory_space=pl.ANY),
        scratch_shapes=[
            pltpu.SemaphoreType.DMA((3, n_blk)),
            pltpu.SemaphoreType.DMA((1,)),
            pltpu.SemaphoreType.DMA((n_all, n_dp * n_tensor)),
            pltpu.SemaphoreType.DMA((n_all, n_sends)),
            pltpu.SemaphoreType.DMA((n_all, 2)),
        ],
        compiler_params=pltpu.CompilerParams(collective_id=0, has_side_effects=True),
    )(shard)


class Slots:
    def __init__(self, n_dp, n_tensor):
        self.n_tensor = n_tensor
        bits = [b for b in range(n_dp.bit_length()) if (1 << b) < n_dp]
        mid = n_tensor // 2
        count = len(bits) * n_tensor
        self.line = count
        count += 2 * n_tensor
        self.hops = {}
        self.cross = {}
        for e in range(1, n_dp):
            if bin(e).count("1") >= 2:
                self.cross[e] = count
                count += n_tensor
            for j in range(mid):
                for b in bits:
                    if not e >> b & 1:
                        chosen = [c for c in bits if (e | 1 << b) >> c & 1]
                        if chosen[j % len(chosen)] == b:
                            self.hops[e, j, b] = count
                            count += 1
        self.count = count


def reduce_kernel(n_dp, n_tensor, parts, out, own, sib, came, final, load_sem, share_sem, recv_sem, send_sem, out_sem):
    at = Place(n_dp, n_tensor)
    slots = Slots(n_dp, n_tensor)
    n_section, n_blk = parts.shape[:2]
    n_all = n_section * n_blk
    depth, half = final.shape[1:]
    lanes = pl.ds(pl.multiple_of(at.s * half, 128), half)
    other_lanes = pl.ds(pl.multiple_of((1 - at.s) * half, 128), half)
    at.meet()

    def place(i):
        return n_section - 1 - lax.div(i, n_blk), n_blk - 1 - lax.rem(i, n_blk)

    def load(i):
        sec, b = place(i)
        return pltpu.make_async_copy(parts.at[sec, b, :, :, lanes], own.at[i], load_sem.at[i])

    def share(i):
        sec, b = place(i)
        return pltpu.make_async_remote_copy(
            src_ref=parts.at[sec, b, :, :, other_lanes],
            dst_ref=sib.at[i],
            send_sem=share_sem.at[0, i],
            recv_sem=share_sem.at[1, i],
            device_id=at.sibling(),
            device_id_type=MESH_ID,
        )

    def begin(i, carry):
        load(i).start()
        share(i).start()
        return carry

    lax.fori_loop(0, n_all, begin, 0)

    def steps(i, start):
        counter = iter(range(10_000))

        def rows(e):
            return pl.multiple_of(at.away(e) * depth, 16)

        def piece(e, tt):
            return own.at[i, tt, pl.ds(rows(e), depth), :]

        def maybe(cond, action):
            if cond is None:
                action()
            else:
                pl.when(cond)(action)

        def remote(e, tt, device, slot):
            k = next(counter)
            return pltpu.make_async_remote_copy(
                src_ref=piece(e, tt),
                dst_ref=came.at[i, slot],
                send_sem=send_sem.at[i, k],
                recv_sem=recv_sem.at[i, slot],
                device_id=device,
                device_id_type=MESH_ID,
            )

        def send(e, tt, device, slot, cond=None):
            copy = remote(e, tt, device, slot)
            maybe(cond, copy.start if start else copy.wait_send)

        def arrive(slot, cond=None):
            if start:
                copy = pltpu.make_async_copy(came.at[i, slot], came.at[i, slot], recv_sem.at[i, slot])
                maybe(cond, copy.wait)

        def total(e, tt, arrived, target=None):
            if not start:
                return
            base = rows(e)

            def chunk(c, carry):
                here = pl.ds(pl.multiple_of(base + c * CHUNK_ROWS, 16), CHUNK_ROWS)
                local = pl.ds(pl.multiple_of(c * CHUNK_ROWS, 16), CHUNK_ROWS)
                acc = own[i, tt, here, :].astype(jnp.float32) + sib[i, tt, here, :].astype(jnp.float32)
                for slot in arrived:
                    acc = acc + came[i, slot, local, :].astype(jnp.float32)
                if target is None:
                    own[i, tt, here, :] = acc.astype(own.dtype)
                else:
                    target[i, local, :] = acc
                return carry

            lax.fori_loop(0, depth // CHUNK_ROWS, chunk, 0)

        def more(e, tt, slot, target=None):
            base = rows(e)

            def chunk(c, carry):
                here = pl.ds(pl.multiple_of(base + c * CHUNK_ROWS, 16), CHUNK_ROWS)
                local = pl.ds(pl.multiple_of(c * CHUNK_ROWS, 16), CHUNK_ROWS)
                acc = came[i, slot, local, :].astype(jnp.float32)
                if target is None:
                    own[i, tt, here, :] = (own[i, tt, here, :].astype(jnp.float32) + acc).astype(own.dtype)
                else:
                    target[i, local, :] = target[i, local, :] + acc
                return carry

            lax.fori_loop(0, depth // CHUNK_ROWS, chunk, 0)

        def also(e, tt, slot, cond, target=None):
            if start:

                def add():
                    arrive(slot)
                    more(e, tt, slot, target)

                pl.when(cond)(add)

        def line_slot(tt, from_next):
            return slots.line + (0 if from_next else n_tensor) + tt

        def crossing():
            if start:
                load(i).wait()
                share(i).wait_recv()
            for e in range(1, n_dp):
                if bin(e).count("1") >= 2:
                    for j in range(at.mid):
                        tt = at.other_side(j)
                        slot = slots.cross[e] + tt
                        total(e, tt, [])
                        is_upper = at.t >= at.mid
                        also(e, tt, slot, jnp.logical_and(is_upper, at.has_next))
                        also(e, tt, slot, jnp.logical_and(jnp.logical_not(is_upper), at.has_prev))
                        send(e, tt, at.along(-1), slot, is_upper)
                        send(e, tt, at.along(1), slot, jnp.logical_not(is_upper))

        def leaves():
            for j in range(at.mid):
                for e in at.by_weight(1):
                    tt = at.other_side(j)
                    b = at.last_bit(e, j)
                    total(e, tt, [])
                    send(e, tt, at.hop(b), b * n_tensor + tt)

        def plane(weight):
            for e in at.by_weight(weight):
                for j in range(at.mid):
                    tt = at.own_side(j)
                    b = at.last_bit(e, j)
                    arrived = [slots.hops[e, j, c] for c in at.bits if (e, j, c) in slots.hops]
                    for slot in arrived:
                        arrive(slot)
                    total(e, tt, arrived)
                    if weight >= 2:
                        slot = slots.cross[e] + tt
                        also(e, tt, slot, at.t == at.mid - 1)
                        also(e, tt, slot, at.t == at.mid)
                    rest = e & ~(1 << b)
                    there = b * n_tensor + tt if rest == 0 else slots.hops[rest, j, b]
                    send(e, tt, at.hop(b), there)

        def column(k):
            low, high = at.t >= k, at.t + k < n_tensor
            for tt, cond, step, chain, from_next in (
                (at.t - k, low, -1, jnp.logical_and(low, at.has_next), True),
                (at.t + k, high, 1, jnp.logical_and(high, at.has_prev), False),
            ):
                arrived = [b * n_tensor + tt for b in at.bits]

                def sums(tt=tt, arrived=arrived):
                    for slot in arrived:
                        arrive(slot)
                    total(0, tt, arrived)

                if start:
                    pl.when(cond)(sums)
                slot = line_slot(tt, from_next)
                also(0, tt, slot, chain)
                send(0, tt, at.along(step), slot, cond)

        def last():
            arrived = [b * n_tensor + at.t for b in at.bits]
            for slot in arrived:
                arrive(slot)
            total(0, at.t, arrived, final)
            also(0, at.t, line_slot(at.t, True), at.has_next, final)
            also(0, at.t, line_slot(at.t, False), at.has_prev, final)
            sec, b = place(i)
            stay = pltpu.make_async_copy(final.at[i], out.at[b, :, lanes], out_sem.at[0, i])
            go = pltpu.make_async_remote_copy(
                src_ref=final.at[i],
                dst_ref=out.at[b, :, lanes],
                send_sem=out_sem.at[1, i],
                recv_sem=out_sem.at[2, i],
                device_id=at.sibling(),
                device_id_type=MESH_ID,
            )

            @pl.when(sec == at.s)
            def _():
                if start:
                    stay.start()
                else:
                    stay.wait()

            @pl.when(sec != at.s)
            def _():
                if start:
                    go.start()
                else:
                    go.wait_send()

        groups = [crossing, leaves]
        groups += [functools.partial(plane, w) for w in range(len(at.bits), 0, -1)]
        groups += [functools.partial(column, k) for k in range(n_tensor - 1, 0, -1)] + [last]
        return groups, counter

    sizes = send_sizes(n_dp, n_tensor)
    lags = [g - (g >= 1) - (g >= 6) for g in range(len(sizes))]

    def run_group(i, g):
        groups, counter = steps(i, True)
        for _ in range(sum(sizes[:g])):
            next(counter)
        groups[g]()

    def body(it, carry):
        for g, lag in sorted(enumerate(lags), key=lambda item: item[1]):
            i = it - lag

            @pl.when(jnp.logical_and(i >= 0, i < n_all))
            def _():
                run_group(i, g)

        return carry

    lax.fori_loop(0, n_all + max(lags), body, 0)

    def finish(i, carry):
        groups, _ = steps(i, False)
        for g in groups:
            g()
        share(i).wait_send()
        sec, b = place(i)

        @pl.when(sec == at.s)
        def _():
            pltpu.make_async_copy(final.at[i], final.at[i], out_sem.at[2, i]).wait()

        return carry

    lax.fori_loop(0, n_all, finish, 0)


def send_sizes(n_dp, n_tensor):
    bits = n_dp.bit_length() - 1
    mid = n_tensor // 2
    weights = [bin(e).count("1") for e in range(n_dp)]
    sizes = [2 * mid * sum(w >= 2 for w in weights), mid * bits]
    sizes += [mid * sum(w == k for w in weights) for k in range(bits, 0, -1)]
    return sizes + [2] * (n_tensor - 1) + [0]


def reduce_weights(parts, n_dp, n_tensor):
    n_section, n_blk, _, width, span = parts.shape
    n_all = n_section * n_blk
    depth, half = width // n_dp, span // 2
    slots = Slots(n_dp, n_tensor)
    n_sends = sum(send_sizes(n_dp, n_tensor))
    return pl.pallas_call(
        functools.partial(reduce_kernel, n_dp, n_tensor),
        out_shape=jax.ShapeDtypeStruct((n_blk, depth, span), jnp.float32),
        in_specs=[pl.BlockSpec(memory_space=pl.ANY)],
        out_specs=pl.BlockSpec(memory_space=pl.ANY),
        scratch_shapes=[
            pltpu.VMEM((n_all, n_tensor, width, half), parts.dtype),
            pltpu.VMEM((n_all, n_tensor, width, half), parts.dtype),
            pltpu.VMEM((n_all, slots.count, depth, half), parts.dtype),
            pltpu.VMEM((n_all, depth, half), jnp.float32),
            pltpu.SemaphoreType.DMA((n_all,)),
            pltpu.SemaphoreType.DMA((2, n_all)),
            pltpu.SemaphoreType.DMA((n_all, slots.count)),
            pltpu.SemaphoreType.DMA((n_all, n_sends)),
            pltpu.SemaphoreType.DMA((3, n_all)),
        ],
        compiler_params=pltpu.CompilerParams(
            collective_id=1, has_side_effects=True, vmem_limit_bytes=60 * 1024 * 1024
        ),
    )(parts)


DH = 64
SEQ = 197
EPS = 1e-06

rows_by_rows = (((0,), (0,)), ((), ()))
cols_by_cols = (((1,), (1,)), ((), ()))
AXES = ("section", "tensor", "dp")


def norm_rows(values, row_gain, row_shift):
    average = jnp.mean(values, axis=-1, keepdims=True)
    centered = values - average
    spread = jnp.mean(centered * centered, axis=-1, keepdims=True)
    return centered * lax.rsqrt(spread + EPS) * row_gain + row_shift


def gelu_exact(values):
    return jax.nn.gelu(values, approximate=False)


def split_heads(mixed):
    blocks = mixed.reshape(-1, SEQ, 3, mixed.shape[1] // (3 * DH), DH)
    return (blocks[:, :, 0], blocks[:, :, 1], blocks[:, :, 2])


def attend_rows(mixed):
    queries, key_rows, val_rows = split_heads(mixed)
    scores = jnp.einsum(
        "sqhd,skhd->shqk", queries, key_rows, preferred_element_type=jnp.float32
    ) * DH ** (-0.5)
    row_top = jnp.max(scores, axis=-1, keepdims=True)
    log_total = row_top + jnp.log(jnp.sum(jnp.exp(scores - row_top), axis=-1, keepdims=True))
    weights = jnp.exp(scores - log_total).astype(jnp.bfloat16)
    output = jnp.einsum("shqk,skhd->sqhd", weights, val_rows, preferred_element_type=jnp.float32)
    return (output.reshape(mixed.shape[0], -1).astype(jnp.bfloat16), log_total)


def attend_back(mixed, log_total, grad_heads):
    queries, key_rows, val_rows = split_heads(mixed)
    scaling = DH ** (-0.5)
    scores = (
        jnp.einsum("sqhd,skhd->shqk", queries, key_rows, preferred_element_type=jnp.float32)
        * scaling
    )
    chances = jnp.exp(scores - log_total)
    grad_out = grad_heads.reshape(queries.shape)
    grad_chances = jnp.einsum(
        "sqhd,skhd->shqk", grad_out, val_rows, preferred_element_type=jnp.float32
    )
    grad_scores = (
        chances * (grad_chances - jnp.sum(chances * grad_chances, axis=-1, keepdims=True))
    ).astype(jnp.bfloat16)
    grad_q = (
        jnp.einsum("shqk,skhd->sqhd", grad_scores, key_rows, preferred_element_type=jnp.float32)
        * scaling
    )
    grad_k = (
        jnp.einsum("shqk,sqhd->skhd", grad_scores, queries, preferred_element_type=jnp.float32)
        * scaling
    )
    grad_v = jnp.einsum(
        "shqk,sqhd->skhd",
        chances.astype(jnp.bfloat16),
        grad_out,
        preferred_element_type=jnp.float32,
    )
    stacked = jnp.stack([grad_q, grad_k, grad_v], axis=2)
    return stacked.reshape(mixed.shape[0], -1).astype(jnp.bfloat16)


def full_weights(blocks):
    n_tensor, width, span = blocks.shape[1:]
    part = span // 4
    w_qkv = blocks[0, :, :, : 3 * part].reshape(n_tensor, width, 3, part)
    w_qkv = w_qkv.transpose(1, 2, 0, 3).reshape(width, -1)
    w_out = blocks[0, :, :, 3 * part :].transpose(0, 2, 1).reshape(-1, width)
    w_up = blocks[1].transpose(1, 0, 2).reshape(width, -1)
    w_down = blocks[2].transpose(0, 2, 1).reshape(-1, width)
    return (w_qkv, w_out, w_up, w_down)


def grad_blocks(n_tensor, w_qkv, w_out, w_up, w_down):
    width = w_up.shape[0]
    part = width // n_tensor
    qkv = w_qkv.reshape(width, 3, n_tensor, part).transpose(2, 0, 1, 3).reshape(n_tensor, width, -1)
    out = w_out.reshape(n_tensor, part, width).transpose(0, 2, 1)
    up = w_up.reshape(width, n_tensor, -1).transpose(1, 0, 2)
    down = w_down.reshape(n_tensor, -1, width).transpose(0, 2, 1)
    return jnp.stack([jnp.concatenate([qkv, out], axis=2), up, down])


def forward_rows(rows_in, params, live_rows):
    vectors, bias_all, bias_up, w_qkv, w_out, w_up, w_down = params
    normed = norm_rows(rows_in, vectors[0], vectors[1]).astype(jnp.bfloat16)
    mixed = (jnp.dot(normed, w_qkv, preferred_element_type=jnp.float32) + bias_all).astype(
        jnp.bfloat16
    )
    heads_out, log_total = attend_rows(mixed)
    middle = rows_in + jnp.dot(heads_out, w_out, preferred_element_type=jnp.float32) + vectors[2]
    normed_two = norm_rows(middle, vectors[3], vectors[4]).astype(jnp.bfloat16)
    hidden = jnp.dot(normed_two, w_up, preferred_element_type=jnp.float32) + bias_up
    active = gelu_exact(hidden).astype(jnp.bfloat16)
    ffn_term = jnp.dot(active, w_down, preferred_element_type=jnp.float32)
    result = (middle + ffn_term + vectors[5]) * live_rows
    return result, (rows_in, normed, mixed, log_total, heads_out, middle, normed_two, hidden, active)


def backward_rows(grad_result, saved, params, live_rows):
    vectors, bias_all, bias_up, w_qkv, w_out, w_up, w_down = params
    rows_in, normed, mixed, log_total, heads_out, middle, normed_two, hidden, active = saved
    grad_res = grad_result * live_rows
    grad_low = grad_res.astype(jnp.bfloat16)
    w_down_grad = lax.dot_general(
        active, grad_low, rows_by_rows, preferred_element_type=jnp.float32
    )
    grad_active = lax.dot_general(grad_low, w_down, cols_by_cols, preferred_element_type=jnp.float32)
    _, gelu_pull = jax.vjp(gelu_exact, hidden)
    grad_hidden = gelu_pull(grad_active)[0].astype(jnp.bfloat16)
    up_bias_grad = jnp.sum(grad_hidden, axis=0, dtype=jnp.float32)
    w_up_grad = lax.dot_general(
        normed_two, grad_hidden, rows_by_rows, preferred_element_type=jnp.float32
    )
    grad_norm_two = lax.dot_general(
        grad_hidden, w_up, cols_by_cols, preferred_element_type=jnp.float32
    )
    _, norm_pull_two = jax.vjp(norm_rows, middle, vectors[3], vectors[4])
    grad_middle, gain_two_grad, shift_two_grad = norm_pull_two(grad_norm_two)
    grad_middle = grad_res + grad_middle
    middle_low = grad_middle.astype(jnp.bfloat16)
    w_out_grad = lax.dot_general(
        heads_out, middle_low, rows_by_rows, preferred_element_type=jnp.float32
    )
    grad_heads = lax.dot_general(
        middle_low, w_out, cols_by_cols, preferred_element_type=jnp.float32
    ).astype(jnp.bfloat16)
    grad_mixed = attend_back(mixed, log_total, grad_heads)
    bias_sums = jnp.sum(grad_mixed, axis=0, dtype=jnp.float32).reshape(3, -1)
    w_qkv_grad = lax.dot_general(
        normed, grad_mixed, rows_by_rows, preferred_element_type=jnp.float32
    )
    grad_norm_one = lax.dot_general(
        grad_mixed, w_qkv, cols_by_cols, preferred_element_type=jnp.float32
    )
    _, norm_pull_one = jax.vjp(norm_rows, rows_in, vectors[0], vectors[1])
    grad_rows, gain_one_grad, shift_one_grad = norm_pull_one(grad_norm_one)
    grad_rows = grad_middle + grad_rows
    vector_grads = jnp.stack(
        [
            gain_one_grad,
            shift_one_grad,
            jnp.sum(grad_middle, axis=0),
            gain_two_grad,
            shift_two_grad,
            jnp.sum(grad_res, axis=0),
        ]
    )
    return (
        grad_rows,
        tuple(g.astype(jnp.bfloat16) for g in (w_qkv_grad, w_out_grad, w_up_grad, w_down_grad)),
        (vector_grads, bias_sums[0], bias_sums[2], up_bias_grad),
    )


def shards(
    images,
    cotangent,
    counts,
    ln1_gain,
    ln1_bias,
    q_bias,
    v_bias,
    qkv_weight,
    out_weight,
    out_bias,
    ln2_gain,
    ln2_bias,
    up_weight,
    up_bias,
    down_weight,
    down_bias,
):
    n_section, n_dp, n_tensor = (lax.axis_size(a) for a in ("section", "dp", "tensor"))
    section_idx = lax.axis_index("section")
    micro_count, share_rows, width = images.shape
    own_count = micro_count // n_section
    depth = qkv_weight.shape[1]
    part = qkv_weight.shape[3]

    own = section_idx * own_count
    own_images = lax.dynamic_slice_in_dim(images, own, own_count, 0).reshape(-1, width)
    own_grads = lax.dynamic_slice_in_dim(cotangent, own, own_count, 0).reshape(-1, width)
    row_place = lax.axis_index("tensor") * share_rows + jnp.arange(share_rows)
    own_counts = lax.dynamic_slice_in_dim(counts, own, own_count, 0)
    live_rows = (row_place // SEQ < own_counts).astype(jnp.float32).reshape(-1, 1)

    shard = jnp.stack(
        [
            jnp.concatenate([qkv_weight[0].reshape(depth, -1), out_weight[0].T], axis=1),
            up_weight[0],
            down_weight[0].T,
        ]
    )
    gathered = gather_weights(shard, n_section, n_dp, n_tensor)

    small = [ln1_gain, ln1_bias, out_bias, ln2_gain, ln2_bias, down_bias, q_bias, v_bias, up_bias]
    sizes = [piece.size for piece in small]
    all_small = lax.all_gather(jnp.concatenate([s.reshape(-1) for s in small]), AXES, axis=0)
    all_small = all_small.reshape(n_section, n_tensor, n_dp, -1).astype(jnp.float32)

    def params_of(sec):
        pieces, start = [], 0
        for size in sizes:
            pieces.append(all_small[sec, :, :, start : start + size])
            start += size
        vectors = [p[0].reshape(-1) for p in pieces[:6]]
        heads = [
            p.reshape(n_tensor, n_dp, -1, DH // n_dp).transpose(0, 2, 1, 3).reshape(-1)
            for p in pieces[6:]
        ]
        bias_all = jnp.concatenate([heads[0], jnp.zeros_like(heads[0]), heads[1]])
        return (vectors, bias_all, heads[2], *full_weights(gathered[sec]))

    params = [params_of(sec) for sec in range(n_section)]

    first_out, first_saved = forward_rows(own_images.astype(jnp.float32), params[0], live_rows)
    first_low = first_out.astype(jnp.bfloat16)
    second_out, second_saved = forward_rows(first_low.astype(jnp.float32), params[1], live_rows)
    second_low = second_out.astype(jnp.bfloat16)
    second_grad, second_w, second_v = backward_rows(
        own_grads.astype(jnp.float32), second_saved, params[1], live_rows
    )
    second_grad = second_grad.astype(jnp.bfloat16)
    first_grad, first_w, first_v = backward_rows(
        second_grad.astype(jnp.float32), first_saved, params[0], live_rows
    )
    first_grad = first_grad.astype(jnp.bfloat16)

    def placed_rows(first, second):
        is_first = section_idx == 0
        away = jnp.where(is_first, second, first)
        came = lax.ppermute(away, "section", [(0, 1), (1, 0)])
        home = jnp.where(is_first, first, second)
        shape = (own_count, share_rows, width)
        home, came = home.reshape(shape), came.reshape(shape)
        low = jnp.where(is_first, home, came)
        high = jnp.where(is_first, came, home)
        return jnp.concatenate([low, high], axis=0)[None]

    section_out = placed_rows(first_low, second_low)
    input_grad = placed_rows(first_grad, second_grad)

    weight_parts = jnp.stack([grad_blocks(n_tensor, *first_w), grad_blocks(n_tensor, *second_w)])
    weight_sum = reduce_weights(weight_parts, n_dp, n_tensor)

    def small_parts(vector_grads, q_sum, v_sum, up_sum):
        vec = vector_grads.reshape(6, n_dp, n_tensor, -1).transpose(2, 1, 0, 3)
        heads = [
            h.reshape(n_tensor, -1, n_dp, DH // n_dp).transpose(0, 2, 1, 3)
            for h in (q_sum, v_sum, up_sum)
        ]
        return jnp.concatenate([p.reshape(n_tensor, n_dp, -1) for p in (vec, *heads)], axis=2)

    small_all = jnp.stack([small_parts(*first_v), small_parts(*second_v)])
    small_sum = lax.psum_scatter(
        small_all.reshape(n_section * n_tensor * n_dp, -1), AXES, scatter_dimension=0
    )
    vec_size = 6 * width // (n_dp * n_tensor)
    head_size = q_bias.size
    vec = small_sum[:vec_size].reshape(1, 6, -1)
    q_sum = small_sum[vec_size : vec_size + head_size].reshape(q_bias.shape)
    v_sum = small_sum[vec_size + head_size : vec_size + 2 * head_size].reshape(v_bias.shape)
    up_sum = small_sum[vec_size + 2 * head_size :].reshape(up_bias.shape)

    return (
        section_out,
        input_grad,
        weight_sum[0, :, : 3 * part].reshape(qkv_weight.shape),
        weight_sum[0, :, 3 * part :].T[None],
        weight_sum[1][None],
        weight_sum[2].T[None],
        q_sum,
        v_sum,
        up_sum,
        vec,
    )


def solution(mesh):
    placed = (
        P(None, ("dp", "tensor"), None),
        P(None, ("dp", "tensor"), None),
        P(None, "dp"),
        P("section", "dp"),
        P("section", "dp"),
        P("section", "tensor", "dp"),
        P("section", "tensor", "dp"),
        P("section", "dp", None, "tensor"),
        P("section", "tensor", "dp"),
        P("section", "dp"),
        P("section", "dp"),
        P("section", "dp"),
        P("section", "dp", "tensor"),
        P("section", "tensor", "dp"),
        P("section", "tensor", "dp"),
        P("section", "dp"),
    )
    return jax.shard_map(
        shards,
        mesh=mesh,
        in_specs=placed,
        out_specs=(
            P("section", None, ("dp", "tensor"), None),
            P("section", None, ("dp", "tensor"), None),
            P("section", "dp", None, "tensor"),
            P("section", "tensor", "dp"),
            P("section", "dp", "tensor"),
            P("section", "tensor", "dp"),
            P("section", "tensor", "dp"),
            P("section", "tensor", "dp"),
            P("section", "tensor", "dp"),
            P("section", None, ("dp", "tensor")),
        ),
        check_vma=False,
    )
```

```python
import functools
import jax
import jax.numpy as jnp
from jax import lax
from jax.experimental import pallas as pl
from jax.experimental.pallas import tpu as pltpu
from jax.sharding import PartitionSpec as P

CHUNK_ROWS = 48
MESH_ID = pl.DeviceIdType.MESH


def slot_sizes(n_dp, n_tensor):
    bits = [b for b in range(n_dp.bit_length()) if (1 << b) < n_dp]
    mid = n_tensor // 2
    weights = [bin(e).count("1") for e in range(n_dp)]

    def plane(weight):
        total = 0
        for j in range(mid):
            for e in range(n_dp):
                if weights[e] == weight:
                    for b in bits:
                        if not e >> b & 1:
                            chosen = [c for c in bits if (e | 1 << b) >> c & 1]
                            total += chosen[j % len(chosen)] == b
                    total += 2 * (weight >= 2) + 1
        return total

    first = [2 + len(bits)]
    columns = [2 * (2 + len(bits))] * (n_tensor - 1)
    planes = [plane(w) for w in range(1, len(bits) + 1)]
    crossed = [3 * mid * sum(w >= 2 for w in weights)]
    rest = [mid * sum(w == 1 for w in weights)]
    return first + [columns[0], planes[0], columns[1]] + planes[1:] + columns[2:] + crossed + rest


class Place:
    def __init__(self, n_dp, n_tensor):
        self.n_dp, self.n_tensor = n_dp, n_tensor
        self.mid = n_tensor // 2
        self.bits = [b for b in range(n_dp.bit_length()) if (1 << b) < n_dp]
        self.s = lax.axis_index("section")
        self.d = lax.axis_index("dp")
        self.t = lax.axis_index("tensor")
        self.upper = lax.div(self.t, self.mid)
        self.has_next = self.t < n_tensor - 1
        self.has_prev = self.t > 0

    def away(self, e):
        other = self.d
        for b in self.bits:
            if e >> b & 1:
                other = other + (1 << b) * (1 - 2 * lax.rem(lax.div(self.d, 1 << b), 2))
        return other

    def last_bit(self, e, j):
        chosen = [b for b in self.bits if e >> b & 1]
        return chosen[j % len(chosen)]

    def own_side(self, j):
        return self.upper * self.mid + j

    def other_side(self, j):
        return (1 - self.upper) * self.mid + j

    def sibling(self):
        return (1 - self.s, self.d, self.t)

    def along(self, step):
        return (self.s, self.d, self.t + step)

    def hop(self, b):
        return (self.s, self.away(1 << b), self.t)

    def meet(self):
        barrier = pltpu.get_barrier_semaphore()

        def greet(device):
            pl.semaphore_signal(barrier, inc=1, device_id=device, device_id_type=MESH_ID)

        greet(self.sibling())
        for b in self.bits:
            greet(self.hop(b))

        @pl.when(self.has_next)
        def _():
            greet(self.along(1))

        @pl.when(self.has_prev)
        def _():
            greet(self.along(-1))

        ends = jnp.where(self.has_next, 1, 0) + jnp.where(self.has_prev, 1, 0)
        pl.semaphore_wait(barrier, 1 + len(self.bits) + ends)

    def by_weight(self, weight):
        return [e for e in range(self.n_dp) if bin(e).count("1") == weight]


def gather_kernel(n_dp, n_tensor, shard, out, own_sem, sib_sem, recv_sem, send_sem, part_sem):
    at = Place(n_dp, n_tensor)
    n_blk, depth, span = shard.shape
    half = span // 2
    n_all = out.shape[0] * n_blk
    at.meet()

    def rows(e):
        return pl.ds(pl.multiple_of(at.away(e) * depth, 16), depth)

    lanes = pl.ds(pl.multiple_of(at.s * half, 128), half)

    def piece(i, e, tt):
        return out.at[lax.div(i, n_blk), lax.rem(i, n_blk), tt, rows(e), lanes]

    def whole(sec, b):
        return out.at[sec, b, at.t, rows(0), :]

    def share(b):
        return pltpu.make_async_remote_copy(
            src_ref=shard.at[b],
            dst_ref=whole(at.s, b),
            send_sem=own_sem.at[1, b],
            recv_sem=own_sem.at[2, b],
            device_id=at.sibling(),
            device_id_type=MESH_ID,
        )

    def keep(b):
        return pltpu.make_async_copy(shard.at[b], whole(at.s, b), own_sem.at[0, b])

    for b in range(n_blk):
        keep(b).start()
        share(b).start()

    def push(i, e, tt, device, e_there, slot, start):
        copy = pltpu.make_async_remote_copy(
            src_ref=piece(i, e, tt),
            dst_ref=piece(i, e, tt),
            send_sem=send_sem.at[i, slot],
            recv_sem=recv_sem.at[i, e_there * n_tensor + tt],
            device_id=device,
            device_id_type=MESH_ID,
        )
        if start:
            copy.start()
        else:
            copy.wait_send()

    def push_sib(i, e, tt, slot, start):
        copy = pltpu.make_async_remote_copy(
            src_ref=piece(i, e, tt),
            dst_ref=piece(i, e, tt),
            send_sem=send_sem.at[i, slot],
            recv_sem=part_sem.at[i, 0 if e == 0 else 1],
            device_id=at.sibling(),
            device_id_type=MESH_ID,
        )
        if start:
            copy.start()
        else:
            copy.wait_send()

    def await_piece(i, e, tt):
        pltpu.make_async_remote_copy(
            src_ref=piece(i, e, tt),
            dst_ref=piece(i, e, tt),
            send_sem=send_sem.at[i, 0],
            recv_sem=recv_sem.at[i, e * n_tensor + tt],
            device_id=at.sibling(),
            device_id_type=MESH_ID,
        ).wait_recv()

    def steps(i, start):
        slots = iter(range(10_000))

        def maybe(cond, action):
            if cond is None:
                action()
            else:
                pl.when(cond)(action)

        def ready(e, tt, cond=None):
            if start:
                maybe(cond, lambda: await_piece(i, e, tt))

        def go(e, tt, device, e_there, cond=None):
            slot = next(slots)
            maybe(cond, lambda: push(i, e, tt, device, e_there, slot, start))

        def go_sib(e, tt, cond=None):
            slot = next(slots)
            maybe(cond, lambda: push_sib(i, e, tt, slot, start))

        def first():
            sec, b = lax.div(i, n_blk), lax.rem(i, n_blk)
            if start:

                @pl.when(sec == at.s)
                def _():
                    pltpu.make_async_copy(shard.at[b], whole(at.s, b), own_sem.at[0, b]).wait()

                @pl.when(sec != at.s)
                def _():
                    pltpu.make_async_remote_copy(
                        src_ref=shard.at[b],
                        dst_ref=whole(1 - at.s, b),
                        send_sem=own_sem.at[1, b],
                        recv_sem=own_sem.at[2, b],
                        device_id=at.sibling(),
                        device_id_type=MESH_ID,
                    ).wait_recv()

            go(0, at.t, at.along(1), 0, at.has_next)
            go(0, at.t, at.along(-1), 0, at.has_prev)
            for b in at.bits:
                go(0, at.t, at.hop(b), 1 << b)

        def column(k):
            low, high = at.t >= k, at.t + k < n_tensor
            for tt, cond, dev, more in (
                (at.t - k, low, at.along(1), jnp.logical_and(low, at.has_next)),
                (at.t + k, high, at.along(-1), jnp.logical_and(high, at.has_prev)),
            ):
                ready(0, tt, cond)
                go(0, tt, dev, 0, more)
                for b in at.bits:
                    go(0, tt, at.hop(b), 1 << b, cond)
                go_sib(0, tt, cond)

        def plane(weight):
            for j in range(at.mid):
                for e in at.by_weight(weight):
                    tt = at.own_side(j)
                    ready(e, tt)
                    for b in at.bits:
                        if not e >> b & 1 and at.last_bit(e | 1 << b, j) == b:
                            go(e, tt, at.hop(b), e | 1 << b)
                    if weight >= 2:
                        go(e, tt, at.along(1), e, at.t == at.mid - 1)
                        go(e, tt, at.along(-1), e, at.t == at.mid)
                    go_sib(e, tt)

        def crossed():
            for weight in range(2, len(at.bits) + 1):
                for e in at.by_weight(weight):
                    for j in range(at.mid):
                        tt = at.other_side(j)
                        ready(e, tt)
                        up = jnp.logical_and(at.t >= at.mid, at.has_next)
                        down = jnp.logical_and(at.t < at.mid, at.has_prev)
                        go(e, tt, at.along(1), e, up)
                        go(e, tt, at.along(-1), e, down)
                        go_sib(e, tt)

        def rest():
            for e in at.by_weight(1):
                for j in range(at.mid):
                    tt = at.other_side(j)
                    ready(e, tt)
                    go_sib(e, tt)

        groups = [first]
        for k in range(1, n_tensor):
            groups.append(functools.partial(column, k))
        planes = [functools.partial(plane, w) for w in range(1, len(at.bits) + 1)]
        merged = [groups[0]]
        order = [groups[1], planes[0], groups[2]] + planes[1:] + groups[3:] + [crossed, rest]
        return merged + order, slots

    lags = [g - (g >= 3) - (g >= 5) for g in range(len(slot_sizes(n_dp, n_tensor)))]
    tail = max(lags)

    def body(it, carry):
        for g, lag in sorted(enumerate(lags), key=lambda item: item[1]):
            i = it - lag

            @pl.when(jnp.logical_and(i >= 0, i < n_all))
            def _():
                run_group(i, g)

        return carry

    def run_group(i, g):
        groups, slots = steps(i, True)
        sizes = slot_sizes(n_dp, n_tensor)
        for _ in range(sum(sizes[:g])):
            next(slots)
        groups[g]()

    def all_of(i, start):
        groups, _ = steps(i, start)
        for g in groups:
            g()

    lax.fori_loop(0, n_all + tail, body, 0)

    def finish(i, carry):
        all_of(i, False)
        sec, b = lax.div(i, n_blk), lax.rem(i, n_blk)
        for k, ref in (
            (0, out.at[sec, b, pl.ds(0, n_tensor - 1), pl.ds(0, depth), pl.ds(0, half)]),
            (1, out.at[sec, b, :, pl.ds(0, (n_dp - 1) * depth), pl.ds(0, half)]),
        ):
            pltpu.make_async_copy(ref, ref, part_sem.at[i, k]).wait()
        return carry

    lax.fori_loop(0, n_all, finish, 0)
    for b in range(n_blk):
        share(b).wait_send()


def gather_weights(shard, n_section, n_dp, n_tensor):
    n_blk, depth, span = shard.shape
    n_all = n_section * n_blk
    n_bits = n_dp.bit_length() - 1
    n_sends = (2 + n_bits) + (n_tensor - 1) * 2 * (2 + n_bits) + 6 * n_dp * n_tensor
    return pl.pallas_call(
        functools.partial(gather_kernel, n_dp, n_tensor),
        out_shape=jax.ShapeDtypeStruct((n_section, n_blk, n_tensor, n_dp * depth, span), shard.dtype),
        in_specs=[pl.BlockSpec(memory_space=pl.ANY)],
        out_specs=pl.BlockSpec(memory_space=pl.ANY),
        scratch_shapes=[
            pltpu.SemaphoreType.DMA((3, n_blk)),
            pltpu.SemaphoreType.DMA((1,)),
            pltpu.SemaphoreType.DMA((n_all, n_dp * n_tensor)),
            pltpu.SemaphoreType.DMA((n_all, n_sends)),
            pltpu.SemaphoreType.DMA((n_all, 2)),
        ],
        compiler_params=pltpu.CompilerParams(collective_id=0, has_side_effects=True),
    )(shard)


class Slots:
    def __init__(self, n_dp, n_tensor):
        self.n_tensor = n_tensor
        bits = [b for b in range(n_dp.bit_length()) if (1 << b) < n_dp]
        mid = n_tensor // 2
        count = len(bits) * n_tensor
        self.line = count
        count += 2 * n_tensor
        self.hops = {}
        self.cross = {}
        for e in range(1, n_dp):
            if bin(e).count("1") >= 2:
                self.cross[e] = count
                count += n_tensor
            for j in range(mid):
                for b in bits:
                    if not e >> b & 1:
                        chosen = [c for c in bits if (e | 1 << b) >> c & 1]
                        if chosen[j % len(chosen)] == b:
                            self.hops[e, j, b] = count
                            count += 1
        self.count = count


def reduce_kernel(n_dp, n_tensor, n_blk, *refs):
    *parts, out, own, sib, came, final, load_sem, share_sem, recv_sem, send_sem, out_sem = refs
    at = Place(n_dp, n_tensor)
    slots = Slots(n_dp, n_tensor)
    n_all = len(parts)
    n_section = n_all // n_blk
    depth, half = final.shape[1:]
    lanes = pl.ds(pl.multiple_of(at.s * half, 128), half)
    other_lanes = pl.ds(pl.multiple_of((1 - at.s) * half, 128), half)
    at.meet()

    def place(i):
        return n_section - 1 - lax.div(i, n_blk), n_blk - 1 - lax.rem(i, n_blk)

    for i in range(n_all):
        part = parts[n_all - 1 - i]
        pltpu.make_async_copy(part.at[:, :, lanes], own.at[i], load_sem.at[i]).start()
        pltpu.make_async_remote_copy(
            src_ref=part.at[:, :, other_lanes],
            dst_ref=sib.at[i],
            send_sem=share_sem.at[0, i],
            recv_sem=share_sem.at[1, i],
            device_id=at.sibling(),
            device_id_type=MESH_ID,
        ).start()

    def steps(i, start):
        counter = iter(range(10_000))

        def rows(e):
            return pl.multiple_of(at.away(e) * depth, 16)

        def piece(e, tt):
            return own.at[i, tt, pl.ds(rows(e), depth), :]

        def maybe(cond, action):
            if cond is None:
                action()
            else:
                pl.when(cond)(action)

        def remote(e, tt, device, slot):
            k = next(counter)
            return pltpu.make_async_remote_copy(
                src_ref=piece(e, tt),
                dst_ref=came.at[i, slot],
                send_sem=send_sem.at[i, k],
                recv_sem=recv_sem.at[i, slot],
                device_id=device,
                device_id_type=MESH_ID,
            )

        def send(e, tt, device, slot, cond=None):
            copy = remote(e, tt, device, slot)
            maybe(cond, copy.start if start else copy.wait_send)

        def arrive(slot, cond=None):
            if start:
                copy = pltpu.make_async_copy(came.at[i, slot], came.at[i, slot], recv_sem.at[i, slot])
                maybe(cond, copy.wait)

        def total(e, tt, arrived, target=None):
            if not start:
                return
            base = rows(e)

            def chunk(c, carry):
                here = pl.ds(pl.multiple_of(base + c * CHUNK_ROWS, 16), CHUNK_ROWS)
                local = pl.ds(pl.multiple_of(c * CHUNK_ROWS, 16), CHUNK_ROWS)
                acc = own[i, tt, here, :].astype(jnp.float32) + sib[i, tt, here, :].astype(jnp.float32)
                for slot in arrived:
                    acc = acc + came[i, slot, local, :].astype(jnp.float32)
                if target is None:
                    own[i, tt, here, :] = acc.astype(own.dtype)
                else:
                    target[i, local, :] = acc
                return carry

            lax.fori_loop(0, depth // CHUNK_ROWS, chunk, 0)

        def more(e, tt, slot, target=None):
            base = rows(e)

            def chunk(c, carry):
                here = pl.ds(pl.multiple_of(base + c * CHUNK_ROWS, 16), CHUNK_ROWS)
                local = pl.ds(pl.multiple_of(c * CHUNK_ROWS, 16), CHUNK_ROWS)
                acc = came[i, slot, local, :].astype(jnp.float32)
                if target is None:
                    own[i, tt, here, :] = (own[i, tt, here, :].astype(jnp.float32) + acc).astype(own.dtype)
                else:
                    target[i, local, :] = target[i, local, :] + acc
                return carry

            lax.fori_loop(0, depth // CHUNK_ROWS, chunk, 0)

        def also(e, tt, slot, cond, target=None):
            if start:

                def add():
                    arrive(slot)
                    more(e, tt, slot, target)

                pl.when(cond)(add)

        def line_slot(tt, from_next):
            return slots.line + (0 if from_next else n_tensor) + tt

        def crossing():
            if start:
                pltpu.make_async_copy(own.at[i], own.at[i], load_sem.at[i]).wait()
                pltpu.make_async_copy(sib.at[i], sib.at[i], share_sem.at[1, i]).wait()
            for e in range(1, n_dp):
                if bin(e).count("1") >= 2:
                    for j in range(at.mid):
                        tt = at.other_side(j)
                        slot = slots.cross[e] + tt
                        total(e, tt, [])
                        is_upper = at.t >= at.mid
                        also(e, tt, slot, jnp.logical_and(is_upper, at.has_next))
                        also(e, tt, slot, jnp.logical_and(jnp.logical_not(is_upper), at.has_prev))
                        send(e, tt, at.along(-1), slot, is_upper)
                        send(e, tt, at.along(1), slot, jnp.logical_not(is_upper))

        def leaves():
            for j in range(at.mid):
                for e in at.by_weight(1):
                    tt = at.other_side(j)
                    b = at.last_bit(e, j)
                    total(e, tt, [])
                    send(e, tt, at.hop(b), b * n_tensor + tt)

        def plane(weight):
            for e in at.by_weight(weight):
                for j in range(at.mid):
                    tt = at.own_side(j)
                    b = at.last_bit(e, j)
                    arrived = [slots.hops[e, j, c] for c in at.bits if (e, j, c) in slots.hops]
                    for slot in arrived:
                        arrive(slot)
                    total(e, tt, arrived)
                    if weight >= 2:
                        slot = slots.cross[e] + tt
                        also(e, tt, slot, at.t == at.mid - 1)
                        also(e, tt, slot, at.t == at.mid)
                    rest = e & ~(1 << b)
                    there = b * n_tensor + tt if rest == 0 else slots.hops[rest, j, b]
                    send(e, tt, at.hop(b), there)

        def column(k):
            low, high = at.t >= k, at.t + k < n_tensor
            for tt, cond, step, chain, from_next in (
                (at.t - k, low, -1, jnp.logical_and(low, at.has_next), True),
                (at.t + k, high, 1, jnp.logical_and(high, at.has_prev), False),
            ):
                arrived = [b * n_tensor + tt for b in at.bits]

                def sums(tt=tt, arrived=arrived):
                    for slot in arrived:
                        arrive(slot)
                    total(0, tt, arrived)

                if start:
                    pl.when(cond)(sums)
                slot = line_slot(tt, from_next)
                also(0, tt, slot, chain)
                send(0, tt, at.along(step), slot, cond)

        def last():
            arrived = [b * n_tensor + at.t for b in at.bits]
            for slot in arrived:
                arrive(slot)
            total(0, at.t, arrived, final)
            also(0, at.t, line_slot(at.t, True), at.has_next, final)
            also(0, at.t, line_slot(at.t, False), at.has_prev, final)
            sec, b = place(i)
            stay = pltpu.make_async_copy(final.at[i], out.at[b, :, lanes], out_sem.at[0, i])
            go = pltpu.make_async_remote_copy(
                src_ref=final.at[i],
                dst_ref=out.at[b, :, lanes],
                send_sem=out_sem.at[1, i],
                recv_sem=out_sem.at[2, i],
                device_id=at.sibling(),
                device_id_type=MESH_ID,
            )

            @pl.when(sec == at.s)
            def _():
                if start:
                    stay.start()
                else:
                    stay.wait()

            @pl.when(sec != at.s)
            def _():
                if start:
                    go.start()
                else:
                    go.wait_send()

        groups = [crossing, leaves]
        groups += [functools.partial(plane, w) for w in range(len(at.bits), 0, -1)]
        groups += [functools.partial(column, k) for k in range(n_tensor - 1, 0, -1)] + [last]
        return groups, counter

    sizes = send_sizes(n_dp, n_tensor)
    lags = [g - (g >= 1) - (g >= 6) for g in range(len(sizes))]

    def run_group(i, g):
        groups, counter = steps(i, True)
        for _ in range(sum(sizes[:g])):
            next(counter)
        groups[g]()

    def body(it, carry):
        for g, lag in sorted(enumerate(lags), key=lambda item: item[1]):
            i = it - lag

            @pl.when(jnp.logical_and(i >= 0, i < n_all))
            def _():
                run_group(i, g)

        return carry

    lax.fori_loop(0, n_all + max(lags), body, 0)

    def finish(i, carry):
        groups, _ = steps(i, False)
        for g in groups:
            g()
        pltpu.make_async_copy(sib.at[i], sib.at[i], share_sem.at[0, i]).wait()
        sec, b = place(i)

        @pl.when(sec == at.s)
        def _():
            pltpu.make_async_copy(final.at[i], final.at[i], out_sem.at[2, i]).wait()

        return carry

    lax.fori_loop(0, n_all, finish, 0)


def send_sizes(n_dp, n_tensor):
    bits = n_dp.bit_length() - 1
    mid = n_tensor // 2
    weights = [bin(e).count("1") for e in range(n_dp)]
    sizes = [2 * mid * sum(w >= 2 for w in weights), mid * bits]
    sizes += [mid * sum(w == k for w in weights) for k in range(bits, 0, -1)]
    return sizes + [2] * (n_tensor - 1) + [0]


def reduce_weights(parts, n_dp, n_tensor, n_blk):
    _, width, span = parts[0].shape
    n_all = len(parts)
    kind = parts[0].dtype
    depth, half = width // n_dp, span // 2
    slots = Slots(n_dp, n_tensor)
    n_sends = sum(send_sizes(n_dp, n_tensor))
    return pl.pallas_call(
        functools.partial(reduce_kernel, n_dp, n_tensor, n_blk),
        out_shape=jax.ShapeDtypeStruct((n_blk, depth, span), jnp.float32),
        in_specs=[pl.BlockSpec(memory_space=pl.ANY)] * n_all,
        out_specs=pl.BlockSpec(memory_space=pl.ANY),
        scratch_shapes=[
            pltpu.VMEM((n_all, n_tensor, width, half), kind),
            pltpu.VMEM((n_all, n_tensor, width, half), kind),
            pltpu.VMEM((n_all, slots.count, depth, half), kind),
            pltpu.VMEM((n_all, depth, half), jnp.float32),
            pltpu.SemaphoreType.DMA((n_all,)),
            pltpu.SemaphoreType.DMA((2, n_all)),
            pltpu.SemaphoreType.DMA((n_all, slots.count)),
            pltpu.SemaphoreType.DMA((n_all, n_sends)),
            pltpu.SemaphoreType.DMA((3, n_all)),
        ],
        compiler_params=pltpu.CompilerParams(
            collective_id=1, has_side_effects=True, vmem_limit_bytes=60 * 1024 * 1024
        ),
    )(*parts)


DH = 64
SEQ = 197
EPS = 1e-06
F32 = jnp.float32
BF16 = jnp.bfloat16
ROWS = 208


def dot(left, right):
    return jnp.dot(left, right, preferred_element_type=F32)


def dot_cols(left, right):
    return lax.dot_general(left, right, (((1,), (1,)), ((), ())), preferred_element_type=F32)


def unit_rows(values):
    average = jnp.mean(values, axis=-1, keepdims=True)
    centered = values - average
    scale = lax.rsqrt(jnp.mean(centered * centered, axis=-1, keepdims=True) + EPS)
    return centered * scale, scale


def unit_rows_back(grad_unit, unit, scale):
    along = jnp.mean(grad_unit * unit, axis=-1, keepdims=True)
    return scale * (grad_unit - jnp.mean(grad_unit, axis=-1, keepdims=True) - unit * along)


def gelu_parts(hidden):
    below = 0.5 * (1.0 + lax.erf(hidden * (0.5**0.5)))
    density = jnp.exp(-0.5 * hidden * hidden) * 0.3989422804014327
    return hidden * below, below + hidden * density


def forward_kernel(
    n_tensor, images, rows, live, vec, qkv_bias, up_bias, w_attn, w_up, w_down,
    out, qkv_out, p_out, heads_out, middle_out, hidden_out, normed, acc,
):
    j = pl.program_id(0)
    part = vec.shape[1] // n_tensor
    n_heads = part // DH

    @pl.when(j == 0)
    def _():
        values = rows[...].astype(F32)
        unit, _ = unit_rows(values)
        normed[...] = (unit * vec[0:1] + vec[1:2]).astype(BF16)
        acc[...] = values + vec[2:3]

    @pl.when(j < n_tensor)
    def _():
        mixed = (dot(normed[...], w_attn[:, : 3 * part]) + qkv_bias[...]).astype(BF16)
        qkv_out[...] = mixed
        keep = lax.broadcasted_iota(jnp.int32, (ROWS, ROWS), 1) < SEQ
        per_image = []
        for image in range(images):
            here = mixed[image * ROWS : (image + 1) * ROWS]
            per_head = []
            for head in range(n_heads):
                q, k, v = (
                    here[:, c * part + head * DH : c * part + (head + 1) * DH] for c in range(3)
                )
                scores = jnp.where(keep, dot_cols(q, k) * DH**-0.5, -1e30)
                scores = jnp.exp(scores - jnp.max(scores, axis=-1, keepdims=True))
                total = jnp.sum(scores, axis=-1, keepdims=True)
                weights = (scores * (1.0 / total)).astype(BF16)
                p_out[image, head] = weights
                per_head.append(dot(weights, v).astype(BF16))
            per_image.append(jnp.concatenate(per_head, axis=1))
        heads = jnp.concatenate(per_image, axis=0)
        heads_out[...] = heads
        acc[...] += dot_cols(heads, w_attn[:, 3 * part :])

    @pl.when(j == n_tensor)
    def _():
        middle = acc[...]
        middle_out[...] = middle
        unit, _ = unit_rows(middle)
        normed[...] = (unit * vec[3:4] + vec[4:5]).astype(BF16)
        acc[...] = middle + vec[5:6]

    @pl.when(j >= n_tensor)
    def _():
        hidden = dot(normed[...], w_up[...]) + up_bias[...]
        hidden_out[...] = hidden
        active = hidden * (0.5 * (1.0 + lax.erf(hidden * (0.5**0.5))))
        acc[...] += dot_cols(active.astype(BF16), w_down[...])

    @pl.when(j == 2 * n_tensor - 1)
    def _():
        out[...] = (acc[...] * live[...]).astype(BF16)


def backward_kernel(
    n_tensor, images, grad, rows, live, vec, w_attn, w_up, w_down, qkv, p, heads_in, middle, hidden,
    grad_rows, d_attn, d_up, d_down, d_vec, d_qkv_bias, d_up_bias,
    grad_low, left_t, right_t, acc, grad_mid, rest,
):
    j = pl.program_id(0)
    part = vec.shape[1] // n_tensor
    n_heads = part // DH

    def column_sum(values):
        return jnp.sum(values, axis=0, keepdims=True)

    @pl.when(j == 0)
    def _():
        low = (grad[...].astype(F32) * live[...]).astype(BF16)
        grad_low[...] = low
        left_t[...] = low.T
        unit, _ = unit_rows(middle[...])
        right_t[...] = (unit * vec[3:4] + vec[4:5]).astype(BF16).T
        acc[...] = jnp.zeros_like(acc)

    @pl.when(j < n_tensor)
    def _():
        active, slope = gelu_parts(hidden[...])
        d_down[...] = dot(left_t[...], active.astype(BF16)).astype(BF16)
        grad_hidden = (dot(grad_low[...], w_down[...]) * slope).astype(BF16)
        d_up_bias[...] = column_sum(grad_hidden.astype(F32))
        d_up[...] = dot(right_t[...], grad_hidden).astype(BF16)
        acc[...] += dot_cols(grad_hidden, w_up[...])

    @pl.when(j == n_tensor)
    def _():
        unit, scale = unit_rows(middle[...])
        grad_norm = acc[...]
        low = grad_low[...].astype(F32)
        mid = low + unit_rows_back(grad_norm * vec[3:4], unit, scale)
        grad_mid[...] = mid
        d_vec[2:3] = column_sum(mid)
        d_vec[3:4] = column_sum(grad_norm * unit)
        d_vec[4:5] = column_sum(grad_norm)
        d_vec[5:6] = column_sum(low)
        mid = mid.astype(BF16)
        grad_low[...] = mid
        left_t[...] = mid.T
        unit, _ = unit_rows(rows[...].astype(F32))
        right_t[...] = (unit * vec[0:1] + vec[1:2]).astype(BF16).T
        acc[...] = jnp.zeros_like(acc)

    @pl.when(j >= n_tensor)
    def _():
        d_out = dot(left_t[...], heads_in[...]).astype(BF16)
        grad_heads = dot(grad_low[...], w_attn[:, 3 * part :]).astype(BF16)
        per_image = []
        for image in range(images):
            span = slice(image * ROWS, (image + 1) * ROWS)
            per_head = [[], [], []]
            for head in range(n_heads):
                q, k, v = (
                    qkv[span, c * part + head * DH : c * part + (head + 1) * DH] for c in range(3)
                )
                grad_out = grad_heads[span, head * DH : (head + 1) * DH]
                weights = p[image, head]
                chances = weights.astype(F32)
                grad_chances = dot_cols(grad_out, v)
                row = jnp.sum(chances * grad_chances, axis=-1, keepdims=True)
                grad_scores = (chances * (grad_chances - row)).astype(BF16)
                per_head[0].append((dot(grad_scores, k) * DH**-0.5).astype(BF16))
                per_head[1].append((dot(grad_scores.T, q) * DH**-0.5).astype(BF16))
                per_head[2].append(dot(weights.T, grad_out).astype(BF16))
            per_image.append(jnp.concatenate(per_head[0] + per_head[1] + per_head[2], axis=1))
        grad_mixed = jnp.concatenate(per_image, axis=0)
        d_qkv_bias[...] = column_sum(grad_mixed.astype(F32))
        d_qkv = dot(right_t[...], grad_mixed).astype(BF16)
        d_attn[...] = jnp.concatenate([d_qkv, d_out], axis=1)
        acc[...] += dot_cols(grad_mixed, w_attn[:, : 3 * part])

    @pl.when(j == 2 * n_tensor - 1)
    def _():
        unit, scale = unit_rows(rows[...].astype(F32))
        grad_norm = acc[...]
        d_vec[0:1] = column_sum(grad_norm * unit)
        d_vec[1:2] = column_sum(grad_norm)
        total = grad_mid[...] + unit_rows_back(grad_norm * vec[0:1], unit, scale)
        grad_rows[...] = total.astype(BF16)


def whole(*shape):
    return pl.BlockSpec(shape, lambda j: (0,) * len(shape))


def layer_specs(n_tensor, n_rows, width, images, span, section, first):
    part = width // n_tensor

    def attn(j):
        return jnp.clip(j - first * n_tensor, 0, n_tensor - 1)

    def ffn(j):
        return jnp.clip(j - (1 - first) * n_tensor, 0, n_tensor - 1)

    block = (None, None, None, width, span)
    return {
        "w_attn": pl.BlockSpec(block, lambda j: (section, 0, attn(j), 0, 0)),
        "w_up": pl.BlockSpec(block, lambda j: (section, 1, ffn(j), 0, 0)),
        "w_down": pl.BlockSpec(block, lambda j: (section, 2, ffn(j), 0, 0)),
        "qkv": pl.BlockSpec((None, n_rows, 3 * part), lambda j: (attn(j), 0, 0)),
        "p": pl.BlockSpec((None, images, part // DH, ROWS, ROWS), lambda j: (attn(j), 0, 0, 0, 0)),
        "heads": pl.BlockSpec((None, n_rows, part), lambda j: (attn(j), 0, 0)),
        "hidden": pl.BlockSpec((None, n_rows, span), lambda j: (ffn(j), 0, 0)),
        "qkv_bias": pl.BlockSpec((None, 1, 3 * part), lambda j: (attn(j), 0, 0)),
        "up_bias": pl.BlockSpec((None, 1, span), lambda j: (ffn(j), 0, 0)),
        "d_attn": pl.BlockSpec((None, width, span), lambda j: (attn(j), 0, 0)),
        "d_ffn": pl.BlockSpec((None, width, span), lambda j: (ffn(j), 0, 0)),
        "rows": whole(n_rows, width),
        "live": whole(n_rows, 1),
        "vec": whole(6, width),
    }


def forward_layer(section, weights, rows, live, vec, qkv_bias, up_bias):
    _, _, n_tensor, width, span = weights.shape
    n_rows = rows.shape[0]
    images = n_rows // ROWS
    part = width // n_tensor
    spec = layer_specs(n_tensor, n_rows, width, images, span, section, 0)
    shape = jax.ShapeDtypeStruct
    names = ["rows", "live", "vec", "qkv_bias", "up_bias", "w_attn", "w_up", "w_down"]
    out_names = ["rows", "qkv", "p", "heads", "rows", "hidden"]
    return pl.pallas_call(
        functools.partial(forward_kernel, n_tensor, images),
        grid=(2 * n_tensor,),
        in_specs=[spec[n] for n in names],
        out_specs=[spec[n] for n in out_names],
        out_shape=[
            shape((n_rows, width), BF16),
            shape((n_tensor, n_rows, 3 * part), BF16),
            shape((n_tensor, images, part // DH, ROWS, ROWS), BF16),
            shape((n_tensor, n_rows, part), BF16),
            shape((n_rows, width), F32),
            shape((n_tensor, n_rows, span), F32),
        ],
        scratch_shapes=[pltpu.VMEM((n_rows, width), BF16), pltpu.VMEM((n_rows, width), F32)],
        compiler_params=pltpu.CompilerParams(
            dimension_semantics=("arbitrary",), vmem_limit_bytes=48 * 1024 * 1024
        ),
    )(rows, live, vec, qkv_bias, up_bias, weights, weights, weights)


def backward_layer(section, weights, grad, rows, live, vec, saved):
    _, _, n_tensor, width, span = weights.shape
    n_rows = rows.shape[0]
    images = n_rows // ROWS
    part = width // n_tensor
    spec = layer_specs(n_tensor, n_rows, width, images, span, section, 1)
    shape = jax.ShapeDtypeStruct
    names = ["rows", "rows", "live", "vec", "w_attn", "w_up", "w_down"]
    names += ["qkv", "p", "heads", "rows", "hidden"]
    out_names = ["rows", "d_attn", "d_ffn", "d_ffn", "vec", "qkv_bias", "up_bias"]
    return pl.pallas_call(
        functools.partial(backward_kernel, n_tensor, images),
        grid=(2 * n_tensor,),
        in_specs=[spec[n] for n in names],
        out_specs=[spec[n] for n in out_names],
        out_shape=[
            shape((n_rows, width), BF16),
            shape((n_tensor, width, span), BF16),
            shape((n_tensor, width, span), BF16),
            shape((n_tensor, width, span), BF16),
            shape((6, width), F32),
            shape((n_tensor, 1, 3 * part), F32),
            shape((n_tensor, 1, span), F32),
        ],
        scratch_shapes=[
            pltpu.VMEM((n_rows, width), BF16),
            pltpu.VMEM((width, n_rows), BF16),
            pltpu.VMEM((width, n_rows), BF16),
            pltpu.VMEM((n_rows, width), F32),
            pltpu.VMEM((n_rows, width), F32),
            pltpu.VMEM((8, 128), F32),
        ],
        compiler_params=pltpu.CompilerParams(
            dimension_semantics=("arbitrary",), vmem_limit_bytes=48 * 1024 * 1024
        ),
    )(grad, rows, live, vec, weights, weights, weights, *saved)


AXES = ("section", "tensor", "dp")


def shards(
    images,
    cotangent,
    counts,
    ln1_gain,
    ln1_bias,
    q_bias,
    v_bias,
    qkv_weight,
    out_weight,
    out_bias,
    ln2_gain,
    ln2_bias,
    up_weight,
    up_bias,
    down_weight,
    down_bias,
):
    n_section, n_dp, n_tensor = (lax.axis_size(a) for a in ("section", "dp", "tensor"))
    section_idx = lax.axis_index("section")
    micro_count, share_rows, width = images.shape
    own_count = micro_count // n_section
    depth = qkv_weight.shape[1]
    part = qkv_weight.shape[3]

    own = section_idx * own_count

    def own_rows(values):
        mine = lax.dynamic_slice_in_dim(values, own, own_count, 0).reshape(-1, SEQ, values.shape[-1])
        return jnp.pad(mine, ((0, 0), (0, ROWS - SEQ), (0, 0))).reshape(-1, values.shape[-1])

    row_place = lax.axis_index("tensor") * share_rows + jnp.arange(share_rows)
    own_counts = lax.dynamic_slice_in_dim(counts, own, own_count, 0)
    live_rows = (row_place // SEQ < own_counts).astype(jnp.float32)
    live_rows = live_rows.reshape(-1, SEQ)
    live_rows = jnp.pad(live_rows, ((0, 0), (0, ROWS - SEQ))).reshape(-1, 1)

    shard = jnp.stack(
        [
            jnp.concatenate([qkv_weight[0].reshape(depth, -1), out_weight[0].T], axis=1),
            up_weight[0],
            down_weight[0].T,
        ]
    )
    gathered = gather_weights(shard, n_section, n_dp, n_tensor)

    small = [ln1_gain, ln1_bias, out_bias, ln2_gain, ln2_bias, down_bias, q_bias, v_bias, up_bias]
    sizes = [piece.size for piece in small]
    all_small = lax.all_gather(jnp.concatenate([s.reshape(-1) for s in small]), AXES, axis=0)
    all_small = all_small.reshape(n_section, n_tensor, n_dp, -1).astype(jnp.float32)

    def params_of(sec):
        pieces, start = [], 0
        for size in sizes:
            pieces.append(all_small[sec, :, :, start : start + size])
            start += size
        vec = jnp.stack([p[0].reshape(-1) for p in pieces[:6]])
        heads = [
            p.reshape(n_tensor, n_dp, -1, DH // n_dp).transpose(0, 2, 1, 3).reshape(n_tensor, 1, -1)
            for p in pieces[6:]
        ]
        qkv_bias = jnp.concatenate([heads[0], jnp.zeros_like(heads[0]), heads[1]], axis=2)
        return vec, qkv_bias, heads[2]

    params = [params_of(sec) for sec in range(n_section)]
    first_rows = own_rows(images)
    first_out, *first_saved = forward_layer(0, gathered, first_rows, live_rows, *params[0])
    second_out, *second_saved = forward_layer(1, gathered, first_out, live_rows, *params[1])
    second_grad, *second_parts = backward_layer(
        1, gathered, own_rows(cotangent), first_out, live_rows, params[1][0], second_saved
    )
    first_grad, *first_parts = backward_layer(
        0, gathered, second_grad, first_rows, live_rows, params[0][0], first_saved
    )

    def placed_rows(first, second):
        is_first = section_idx == 0
        away = jnp.where(is_first, second, first)
        came = lax.ppermute(away, "section", [(0, 1), (1, 0)])
        home = jnp.where(is_first, first, second)
        home, came = (
            v.reshape(-1, ROWS, width)[:, :SEQ].reshape(own_count, share_rows, width)
            for v in (home, came)
        )
        low = jnp.where(is_first, home, came)
        high = jnp.where(is_first, came, home)
        return jnp.concatenate([low, high], axis=0)[None]

    section_out = placed_rows(first_out, second_out)
    input_grad = placed_rows(first_grad, second_grad)

    weight_sum = reduce_weights([*first_parts[:3], *second_parts[:3]], n_dp, n_tensor, 3)

    def small_parts(vector_grads, qkv_sum, up_sum):
        q_sum, _, v_sum = jnp.split(qkv_sum, 3, axis=2)
        vec = vector_grads.reshape(6, n_dp, n_tensor, -1).transpose(2, 1, 0, 3)
        heads = [
            h.reshape(n_tensor, -1, n_dp, DH // n_dp).transpose(0, 2, 1, 3)
            for h in (q_sum, v_sum, up_sum)
        ]
        return jnp.concatenate([p.reshape(n_tensor, n_dp, -1) for p in (vec, *heads)], axis=2)

    small_all = jnp.stack([small_parts(*first_parts[3:]), small_parts(*second_parts[3:])])
    small_sum = lax.psum_scatter(
        small_all.reshape(n_section * n_tensor * n_dp, -1), AXES, scatter_dimension=0
    )
    vec_size = 6 * width // (n_dp * n_tensor)
    head_size = q_bias.size
    vec = small_sum[:vec_size].reshape(1, 6, -1)
    q_sum = small_sum[vec_size : vec_size + head_size].reshape(q_bias.shape)
    v_sum = small_sum[vec_size + head_size : vec_size + 2 * head_size].reshape(v_bias.shape)
    up_sum = small_sum[vec_size + 2 * head_size :].reshape(up_bias.shape)

    return (
        section_out,
        input_grad,
        weight_sum[0, :, : 3 * part].reshape(qkv_weight.shape),
        weight_sum[0, :, 3 * part :].T[None],
        weight_sum[1][None],
        weight_sum[2].T[None],
        q_sum,
        v_sum,
        up_sum,
        vec,
    )


def solution(mesh):
    placed = (
        P(None, ("dp", "tensor"), None),
        P(None, ("dp", "tensor"), None),
        P(None, "dp"),
        P("section", "dp"),
        P("section", "dp"),
        P("section", "tensor", "dp"),
        P("section", "tensor", "dp"),
        P("section", "dp", None, "tensor"),
        P("section", "tensor", "dp"),
        P("section", "dp"),
        P("section", "dp"),
        P("section", "dp"),
        P("section", "dp", "tensor"),
        P("section", "tensor", "dp"),
        P("section", "tensor", "dp"),
        P("section", "dp"),
    )
    return jax.shard_map(
        shards,
        mesh=mesh,
        in_specs=placed,
        out_specs=(
            P("section", None, ("dp", "tensor"), None),
            P("section", None, ("dp", "tensor"), None),
            P("section", "dp", None, "tensor"),
            P("section", "tensor", "dp"),
            P("section", "dp", "tensor"),
            P("section", "tensor", "dp"),
            P("section", "tensor", "dp"),
            P("section", "tensor", "dp"),
            P("section", "tensor", "dp"),
            P("section", None, ("dp", "tensor")),
        ),
        check_vma=False,
    )
```

```python
import functools
import jax
import jax.numpy as jnp
from jax import lax
from jax.experimental import pallas as pl
from jax.experimental.pallas import tpu as pltpu
from jax.sharding import PartitionSpec as P

CHUNK_ROWS = 48
BLOCK_TICKS = 3
PAUSE = 0
SMALL_TICKS = 2
RLAGS = [0, 0, 2, 5, 8, 10, 12, 14]
MESH_ID = pl.DeviceIdType.MESH


def slot_sizes(n_dp, n_tensor):
    bits = [b for b in range(n_dp.bit_length()) if (1 << b) < n_dp]
    mid = n_tensor // 2
    weights = [bin(e).count("1") for e in range(n_dp)]

    def plane(weight):
        total = 0
        for j in range(mid):
            for e in range(n_dp):
                if weights[e] == weight:
                    for b in bits:
                        if not e >> b & 1:
                            chosen = [c for c in bits if (e | 1 << b) >> c & 1]
                            total += chosen[j % len(chosen)] == b
                    total += 2 * (weight >= 2) + 1
        return total

    first = [2 + len(bits)]
    columns = [2 * (2 + len(bits))] * (n_tensor - 1)
    planes = [plane(w) for w in range(1, len(bits) + 1)]
    crossed = [3 * mid * sum(w >= 2 for w in weights)]
    rest = [mid * sum(w == 1 for w in weights)]
    return first + [columns[0], planes[0], columns[1]] + planes[1:] + columns[2:] + crossed + rest


class Place:
    def __init__(self, n_dp, n_tensor):
        self.n_dp, self.n_tensor = n_dp, n_tensor
        self.mid = n_tensor // 2
        self.bits = [b for b in range(n_dp.bit_length()) if (1 << b) < n_dp]
        self.s = lax.axis_index("section")
        self.d = lax.axis_index("dp")
        self.t = lax.axis_index("tensor")
        self.upper = lax.div(self.t, self.mid)
        self.has_next = self.t < n_tensor - 1
        self.has_prev = self.t > 0

    def away(self, e):
        other = self.d
        for b in self.bits:
            if e >> b & 1:
                other = other + (1 << b) * (1 - 2 * lax.rem(lax.div(self.d, 1 << b), 2))
        return other

    def last_bit(self, e, j):
        chosen = [b for b in self.bits if e >> b & 1]
        return chosen[j % len(chosen)]

    def own_side(self, j):
        return self.upper * self.mid + j

    def other_side(self, j):
        return (1 - self.upper) * self.mid + j

    def sibling(self):
        return (1 - self.s, self.d, self.t)

    def along(self, step):
        return (self.s, self.d, self.t + step)

    def hop(self, b):
        return (self.s, self.away(1 << b), self.t)

    def meet(self, whole_line=False):
        barrier = pltpu.get_barrier_semaphore()

        def greet(device):
            pl.semaphore_signal(barrier, inc=1, device_id=device, device_id_type=MESH_ID)

        greet(self.sibling())
        for b in self.bits:
            greet(self.hop(b))
        if whole_line:
            for k in range(1, self.n_tensor):
                greet((self.s, self.d, lax.rem(self.t + k, self.n_tensor)))
            pl.semaphore_wait(barrier, len(self.bits) + self.n_tensor)
            return

        @pl.when(self.has_next)
        def _():
            greet(self.along(1))

        @pl.when(self.has_prev)
        def _():
            greet(self.along(-1))

        ends = jnp.where(self.has_next, 1, 0) + jnp.where(self.has_prev, 1, 0)
        pl.semaphore_wait(barrier, 1 + len(self.bits) + ends)

    def by_weight(self, weight):
        return [e for e in range(self.n_dp) if bin(e).count("1") == weight]


def gather_kernel(n_dp, n_tensor, shard, out, own_sem, sib_sem, recv_sem, send_sem, part_sem):
    at = Place(n_dp, n_tensor)
    n_blk, depth, span = shard.shape
    half = span // 2
    n_all = out.shape[0] * n_blk
    at.meet()

    def rows(e):
        return pl.ds(pl.multiple_of(at.away(e) * depth, 16), depth)

    lanes = pl.ds(pl.multiple_of(at.s * half, 128), half)

    def piece(i, e, tt):
        return out.at[lax.div(i, n_blk), lax.rem(i, n_blk), tt, rows(e), lanes]

    def whole(sec, b):
        return out.at[sec, b, at.t, rows(0), :]

    def share(b):
        return pltpu.make_async_remote_copy(
            src_ref=shard.at[b],
            dst_ref=whole(at.s, b),
            send_sem=own_sem.at[1, b],
            recv_sem=own_sem.at[2, b],
            device_id=at.sibling(),
            device_id_type=MESH_ID,
        )

    def keep(b):
        return pltpu.make_async_copy(shard.at[b], whole(at.s, b), own_sem.at[0, b])

    for b in range(n_blk):
        keep(b).start()
        share(b).start()

    def push(i, e, tt, device, e_there, slot, start):
        copy = pltpu.make_async_remote_copy(
            src_ref=piece(i, e, tt),
            dst_ref=piece(i, e, tt),
            send_sem=send_sem.at[i, slot],
            recv_sem=recv_sem.at[i, e_there * n_tensor + tt],
            device_id=device,
            device_id_type=MESH_ID,
        )
        if start:
            copy.start()
        else:
            copy.wait_send()

    def push_sib(i, e, tt, slot, start):
        copy = pltpu.make_async_remote_copy(
            src_ref=piece(i, e, tt),
            dst_ref=piece(i, e, tt),
            send_sem=send_sem.at[i, slot],
            recv_sem=part_sem.at[i, 0 if e == 0 else 1],
            device_id=at.sibling(),
            device_id_type=MESH_ID,
        )
        if start:
            copy.start()
        else:
            copy.wait_send()

    def await_piece(i, e, tt):
        pltpu.make_async_remote_copy(
            src_ref=piece(i, e, tt),
            dst_ref=piece(i, e, tt),
            send_sem=send_sem.at[i, 0],
            recv_sem=recv_sem.at[i, e * n_tensor + tt],
            device_id=at.sibling(),
            device_id_type=MESH_ID,
        ).wait_recv()

    def steps(i, start):
        slots = iter(range(10_000))

        def maybe(cond, action):
            if cond is None:
                action()
            else:
                pl.when(cond)(action)

        def ready(e, tt, cond=None):
            if start:
                maybe(cond, lambda: await_piece(i, e, tt))

        def go(e, tt, device, e_there, cond=None):
            slot = next(slots)
            maybe(cond, lambda: push(i, e, tt, device, e_there, slot, start))

        def go_sib(e, tt, cond=None):
            slot = next(slots)
            maybe(cond, lambda: push_sib(i, e, tt, slot, start))

        def first():
            sec, b = lax.div(i, n_blk), lax.rem(i, n_blk)
            if start:

                @pl.when(sec == at.s)
                def _():
                    pltpu.make_async_copy(shard.at[b], whole(at.s, b), own_sem.at[0, b]).wait()

                @pl.when(sec != at.s)
                def _():
                    pltpu.make_async_remote_copy(
                        src_ref=shard.at[b],
                        dst_ref=whole(1 - at.s, b),
                        send_sem=own_sem.at[1, b],
                        recv_sem=own_sem.at[2, b],
                        device_id=at.sibling(),
                        device_id_type=MESH_ID,
                    ).wait_recv()

            go(0, at.t, at.along(1), 0, at.has_next)
            go(0, at.t, at.along(-1), 0, at.has_prev)
            for b in at.bits:
                go(0, at.t, at.hop(b), 1 << b)

        def column(k):
            low, high = at.t >= k, at.t + k < n_tensor
            for tt, cond, dev, more in (
                (at.t - k, low, at.along(1), jnp.logical_and(low, at.has_next)),
                (at.t + k, high, at.along(-1), jnp.logical_and(high, at.has_prev)),
            ):
                ready(0, tt, cond)
                go(0, tt, dev, 0, more)
                for b in at.bits:
                    go(0, tt, at.hop(b), 1 << b, cond)
                go_sib(0, tt, cond)

        def plane(weight):
            for j in range(at.mid):
                for e in at.by_weight(weight):
                    tt = at.own_side(j)
                    ready(e, tt)
                    for b in at.bits:
                        if not e >> b & 1 and at.last_bit(e | 1 << b, j) == b:
                            go(e, tt, at.hop(b), e | 1 << b)
                    if weight >= 2:
                        go(e, tt, at.along(1), e, at.t == at.mid - 1)
                        go(e, tt, at.along(-1), e, at.t == at.mid)
                    go_sib(e, tt)

        def crossed():
            for weight in range(2, len(at.bits) + 1):
                for e in at.by_weight(weight):
                    for j in range(at.mid):
                        tt = at.other_side(j)
                        ready(e, tt)
                        up = jnp.logical_and(at.t >= at.mid, at.has_next)
                        down = jnp.logical_and(at.t < at.mid, at.has_prev)
                        go(e, tt, at.along(1), e, up)
                        go(e, tt, at.along(-1), e, down)
                        go_sib(e, tt)

        def rest():
            for e in at.by_weight(1):
                for j in range(at.mid):
                    tt = at.other_side(j)
                    ready(e, tt)
                    go_sib(e, tt)

        groups = [first]
        for k in range(1, n_tensor):
            groups.append(functools.partial(column, k))
        planes = [functools.partial(plane, w) for w in range(1, len(at.bits) + 1)]
        merged = [groups[0]]
        order = [groups[1], planes[0], groups[2]] + planes[1:] + groups[3:] + [crossed, rest]
        return merged + order, slots

    lags = [g - (g >= 3) - (g >= 5) for g in range(len(slot_sizes(n_dp, n_tensor)))]
    tail = max(lags)

    def body(it, carry):
        for g, lag in sorted(enumerate(lags), key=lambda item: item[1]):
            i = it - lag

            @pl.when(jnp.logical_and(i >= 0, i < n_all))
            def _():
                run_group(i, g)

        return carry

    def run_group(i, g):
        groups, slots = steps(i, True)
        sizes = slot_sizes(n_dp, n_tensor)
        for _ in range(sum(sizes[:g])):
            next(slots)
        groups[g]()

    def all_of(i, start):
        groups, _ = steps(i, start)
        for g in groups:
            g()

    lax.fori_loop(0, n_all + tail, body, 0)

    def finish(i, carry):
        all_of(i, False)
        sec, b = lax.div(i, n_blk), lax.rem(i, n_blk)
        for k, ref in (
            (0, out.at[sec, b, pl.ds(0, n_tensor - 1), pl.ds(0, depth), pl.ds(0, half)]),
            (1, out.at[sec, b, :, pl.ds(0, (n_dp - 1) * depth), pl.ds(0, half)]),
        ):
            pltpu.make_async_copy(ref, ref, part_sem.at[i, k]).wait()
        return carry

    lax.fori_loop(0, n_all, finish, 0)
    for b in range(n_blk):
        share(b).wait_send()


def gather_weights(shard, n_section, n_dp, n_tensor):
    n_blk, depth, span = shard.shape
    n_all = n_section * n_blk
    n_bits = n_dp.bit_length() - 1
    n_sends = (2 + n_bits) + (n_tensor - 1) * 2 * (2 + n_bits) + 6 * n_dp * n_tensor
    return pl.pallas_call(
        functools.partial(gather_kernel, n_dp, n_tensor),
        out_shape=jax.ShapeDtypeStruct((n_section, n_blk, n_tensor, n_dp * depth, span), shard.dtype),
        in_specs=[pl.BlockSpec(memory_space=pl.ANY)],
        out_specs=pl.BlockSpec(memory_space=pl.ANY),
        scratch_shapes=[
            pltpu.SemaphoreType.DMA((3, n_blk)),
            pltpu.SemaphoreType.DMA((1,)),
            pltpu.SemaphoreType.DMA((n_all, n_dp * n_tensor)),
            pltpu.SemaphoreType.DMA((n_all, n_sends)),
            pltpu.SemaphoreType.DMA((n_all, 2)),
        ],
        compiler_params=pltpu.CompilerParams(collective_id=0, has_side_effects=True),
    )(shard)


DH = 64
SEQ = 197
EPS = 1e-06
F32 = jnp.float32
BF16 = jnp.bfloat16
ROWS = 208


def dot(left, right):
    return jnp.dot(left, right, preferred_element_type=F32)


def dot_cols(left, right):
    return lax.dot_general(left, right, (((1,), (1,)), ((), ())), preferred_element_type=F32)


def unit_rows(values):
    average = jnp.mean(values, axis=-1, keepdims=True)
    centered = values - average
    scale = lax.rsqrt(jnp.mean(centered * centered, axis=-1, keepdims=True) + EPS)
    return centered * scale, scale


def unit_rows_back(grad_unit, unit, scale):
    along = jnp.mean(grad_unit * unit, axis=-1, keepdims=True)
    return scale * (grad_unit - jnp.mean(grad_unit, axis=-1, keepdims=True) - unit * along)


def gelu_parts(hidden):
    below = 0.5 * (1.0 + lax.erf(hidden * (0.5**0.5)))
    density = jnp.exp(-0.5 * hidden * hidden) * 0.3989422804014327
    return hidden * below, below + hidden * density


def forward_kernel(
    n_tensor, images, rows, live, vec, qkv_bias, up_bias, w_attn, w_up, w_down,
    out, qkv_out, p_out, heads_out, middle_out, active_out, slope_out, normed, acc,
):
    j = pl.program_id(0)
    part = vec.shape[1] // n_tensor
    n_heads = part // DH

    @pl.when(j == 0)
    def _():
        values = rows[...].astype(F32)
        unit, _ = unit_rows(values)
        normed[...] = (unit * vec[0:1] + vec[1:2]).astype(BF16)
        acc[...] = values + vec[2:3]

    @pl.when(j < n_tensor)
    def _():
        mixed = (dot(normed[...], w_attn[:, : 3 * part]) + qkv_bias[...]).astype(BF16)
        qkv_out[...] = mixed
        keep = lax.broadcasted_iota(jnp.int32, (ROWS, ROWS), 0) < SEQ
        per_image = []
        for image in range(images):
            here = mixed[image * ROWS : (image + 1) * ROWS]
            per_head = []
            for head in range(n_heads):
                q, k, v = (
                    here[:, c * part + head * DH : c * part + (head + 1) * DH] for c in range(3)
                )
                scores = jnp.where(keep, dot_cols(k, q) * DH**-0.5, -1e30)
                scores = jnp.exp(scores - jnp.max(scores, axis=0, keepdims=True))
                total = jnp.sum(scores, axis=0, keepdims=True)
                chances = (scores * (1.0 / total)).astype(BF16)
                p_out[image, head] = chances
                per_head.append(dot(v.T, chances).T.astype(BF16))
            per_image.append(jnp.concatenate(per_head, axis=1))
        heads = jnp.concatenate(per_image, axis=0)
        heads_out[...] = heads
        acc[...] += dot_cols(heads, w_attn[:, 3 * part :])

    @pl.when(j == n_tensor)
    def _():
        middle = acc[...]
        middle_out[...] = middle
        unit, _ = unit_rows(middle)
        normed[...] = (unit * vec[3:4] + vec[4:5]).astype(BF16)
        acc[...] = middle + vec[5:6]

    @pl.when(j >= n_tensor)
    def _():
        hidden = dot(normed[...], w_up[...]) + up_bias[...]
        active, slope = gelu_parts(hidden)
        active = active.astype(BF16)
        active_out[...] = active
        slope_out[...] = slope.astype(BF16)
        acc[...] += dot_cols(active, w_down[...])

    @pl.when(j == 2 * n_tensor - 1)
    def _():
        out[...] = (acc[...] * live[...]).astype(BF16)


def whole(*shape):
    return pl.BlockSpec(shape, lambda j: (0,) * len(shape))


def layer_specs(n_tensor, n_rows, width, images, span, section, first):
    part = width // n_tensor

    def attn(j):
        return jnp.clip(j - first * n_tensor, 0, n_tensor - 1)

    def ffn(j):
        return jnp.clip(j - (1 - first) * n_tensor, 0, n_tensor - 1)

    block = (None, None, None, width, span)
    return {
        "w_attn": pl.BlockSpec(block, lambda j: (section, 0, attn(j), 0, 0)),
        "w_up": pl.BlockSpec(block, lambda j: (section, 1, ffn(j), 0, 0)),
        "w_down": pl.BlockSpec(block, lambda j: (section, 2, ffn(j), 0, 0)),
        "qkv": pl.BlockSpec((None, n_rows, 3 * part), lambda j: (attn(j), 0, 0)),
        "p": pl.BlockSpec((None, images, part // DH, ROWS, ROWS), lambda j: (attn(j), 0, 0, 0, 0)),
        "heads": pl.BlockSpec((None, n_rows, part), lambda j: (attn(j), 0, 0)),
        "hidden": pl.BlockSpec((None, n_rows, span), lambda j: (ffn(j), 0, 0)),
        "qkv_bias": pl.BlockSpec((None, 1, 3 * part), lambda j: (attn(j), 0, 0)),
        "up_bias": pl.BlockSpec((None, 1, span), lambda j: (ffn(j), 0, 0)),
        "d_attn": pl.BlockSpec((None, width, span), lambda j: (attn(j), 0, 0)),
        "d_ffn": pl.BlockSpec((None, width, span), lambda j: (ffn(j), 0, 0)),
        "rows": whole(n_rows, width),
        "live": whole(n_rows, 1),
        "vec": whole(6, width),
    }


def forward_layer(section, weights, rows, live, vec, qkv_bias, up_bias):
    _, _, n_tensor, width, span = weights.shape
    n_rows = rows.shape[0]
    images = n_rows // ROWS
    part = width // n_tensor
    spec = layer_specs(n_tensor, n_rows, width, images, span, section, 0)
    shape = jax.ShapeDtypeStruct
    names = ["rows", "live", "vec", "qkv_bias", "up_bias", "w_attn", "w_up", "w_down"]
    out_names = ["rows", "qkv", "p", "heads", "rows", "hidden", "hidden"]
    return pl.pallas_call(
        functools.partial(forward_kernel, n_tensor, images),
        grid=(2 * n_tensor,),
        in_specs=[spec[n] for n in names],
        out_specs=[spec[n] for n in out_names],
        out_shape=[
            shape((n_rows, width), BF16),
            shape((n_tensor, n_rows, 3 * part), BF16),
            shape((n_tensor, images, part // DH, ROWS, ROWS), BF16),
            shape((n_tensor, n_rows, part), BF16),
            shape((n_rows, width), F32),
            shape((n_tensor, n_rows, span), BF16),
            shape((n_tensor, n_rows, span), BF16),
        ],
        scratch_shapes=[pltpu.VMEM((n_rows, width), BF16), pltpu.VMEM((n_rows, width), F32)],
        compiler_params=pltpu.CompilerParams(
            dimension_semantics=("arbitrary",), vmem_limit_bytes=48 * 1024 * 1024
        ),
    )(rows, live, vec, qkv_bias, up_bias, weights, weights, weights)


class Slots:
    def __init__(self, n_dp, n_tensor):
        self.n_tensor = n_tensor
        bits = [b for b in range(n_dp.bit_length()) if (1 << b) < n_dp]
        mid = n_tensor // 2
        count = len(bits) * n_tensor
        self.line = count
        count += n_tensor + 1
        self.hops = {}
        self.cross = {}
        for e in range(1, n_dp):
            if bin(e).count("1") >= 2:
                self.cross[e] = count
                count += n_tensor
            for j in range(mid):
                for b in bits:
                    if not e >> b & 1:
                        chosen = [c for c in bits if (e | 1 << b) >> c & 1]
                        if chosen[j % len(chosen)] == b:
                            self.hops[e, j, b] = count
                            count += 1
        self.count = count


def reduce_lags(n_groups):
    return RLAGS


def backward_kernel(
    n_dp, n_tensor, images, weights, cotangent, live, vec, *refs
):
    saved = {0: refs[:7], 1: refs[7:14]}
    (
        out, grad_out, d_vec, d_qkv_bias, d_up_bias,
        own, came, final, vec_in, qkv_bias_in, up_bias_in, ring, stage, w_buf, hidden_buf, qkv_buf, p_buf, heads_buf, rows_buf, middle_buf,
        grad_low, left_t, right_t, acc, grad_mid,
        load_sem, stage_sem, credit, recv_sem, send_sem, out_sem, small_sem,
    ) = refs[14:]
    at = Place(n_dp, n_tensor)
    slots = Slots(n_dp, n_tensor)
    n_section, n_blk = weights.shape[:2]
    n_all = n_section * n_blk
    depth, half = final.shape[1:]
    part = vec.shape[2] // n_tensor
    n_heads = part // DH
    lanes = pl.ds(pl.multiple_of(at.s * half, 128), half)
    sizes = send_sizes(n_dp, n_tensor)
    at.meet(whole_line=True)

    def place(i):
        return n_section - 1 - lax.div(i, n_blk), n_blk - 1 - lax.rem(i, n_blk)

    def steps(i, start):
        counter = iter(range(10_000))

        def rows(e):
            return pl.multiple_of(at.away(e) * depth, 16)

        def piece(e, tt):
            return own.at[i, tt, pl.ds(rows(e), depth), :]

        def maybe(cond, action):
            if cond is None:
                action()
            else:
                pl.when(cond)(action)

        def remote(e, tt, device, slot):
            k = next(counter)
            return pltpu.make_async_remote_copy(
                src_ref=piece(e, tt),
                dst_ref=came.at[i, slot],
                send_sem=send_sem.at[i, k],
                recv_sem=recv_sem.at[i, slot],
                device_id=device,
                device_id_type=MESH_ID,
            )

        def send(e, tt, device, slot, cond=None):
            copy = remote(e, tt, device, slot)
            maybe(cond, copy.start if start else copy.wait_send)

        def arrive(slot, cond=None):
            if start:
                copy = pltpu.make_async_copy(came.at[i, slot], came.at[i, slot], recv_sem.at[i, slot])
                maybe(cond, copy.wait)

        def total(e, tt, arrived, target=None):
            if not start or (target is None and not arrived):
                return
            base = rows(e)

            def chunk(c, carry):
                here = pl.ds(pl.multiple_of(base + c * CHUNK_ROWS, 16), CHUNK_ROWS)
                local = pl.ds(pl.multiple_of(c * CHUNK_ROWS, 16), CHUNK_ROWS)
                acc = own[i, tt, here, :].astype(jnp.float32)
                for slot in arrived:
                    acc = acc + came[i, slot, local, :].astype(jnp.float32)
                if target is None:
                    own[i, tt, here, :] = acc.astype(own.dtype)
                else:
                    target[i, local, :] = acc
                return carry

            lax.fori_loop(0, depth // CHUNK_ROWS, chunk, 0)

        def more(e, tt, slot, target=None):
            base = rows(e)

            def chunk(c, carry):
                here = pl.ds(pl.multiple_of(base + c * CHUNK_ROWS, 16), CHUNK_ROWS)
                local = pl.ds(pl.multiple_of(c * CHUNK_ROWS, 16), CHUNK_ROWS)
                acc = came[i, slot, local, :].astype(jnp.float32)
                if target is None:
                    own[i, tt, here, :] = (own[i, tt, here, :].astype(jnp.float32) + acc).astype(own.dtype)
                else:
                    target[i, local, :] = target[i, local, :] + acc
                return carry

            lax.fori_loop(0, depth // CHUNK_ROWS, chunk, 0)

        def also(e, tt, slot, cond, target=None):
            if start:

                def add():
                    arrive(slot)
                    more(e, tt, slot, target)

                pl.when(cond)(add)

        def line_slot(tt, from_next):
            return slots.line + tt + (0 if from_next else 1)

        def crossing():
            for e in range(1, n_dp):
                if bin(e).count("1") >= 2:
                    for j in range(at.mid):
                        tt = at.other_side(j)
                        slot = slots.cross[e] + tt
                        total(e, tt, [])
                        is_upper = at.t >= at.mid
                        also(e, tt, slot, jnp.logical_and(is_upper, at.has_next))
                        also(e, tt, slot, jnp.logical_and(jnp.logical_not(is_upper), at.has_prev))
                        send(e, tt, at.along(-1), slot, is_upper)
                        send(e, tt, at.along(1), slot, jnp.logical_not(is_upper))

        def leaves():
            for j in range(at.mid):
                for e in at.by_weight(1):
                    tt = at.other_side(j)
                    b = at.last_bit(e, j)
                    total(e, tt, [])
                    send(e, tt, at.hop(b), b * n_tensor + tt)

        def plane(weight):
            for e in at.by_weight(weight):
                for j in range(at.mid):
                    tt = at.own_side(j)
                    b = at.last_bit(e, j)
                    arrived = [slots.hops[e, j, c] for c in at.bits if (e, j, c) in slots.hops]
                    for slot in arrived:
                        arrive(slot)
                    total(e, tt, arrived)
                    if weight >= 2:
                        slot = slots.cross[e] + tt
                        also(e, tt, slot, at.t == at.mid - 1)
                        also(e, tt, slot, at.t == at.mid)
                    rest = e & ~(1 << b)
                    there = b * n_tensor + tt if rest == 0 else slots.hops[rest, j, b]
                    send(e, tt, at.hop(b), there)

        def column(k):
            low, high = at.t >= k, at.t + k < n_tensor
            for tt, cond, step, chain, from_next in (
                (at.t - k, low, -1, jnp.logical_and(low, at.has_next), True),
                (at.t + k, high, 1, jnp.logical_and(high, at.has_prev), False),
            ):
                arrived = [b * n_tensor + tt for b in at.bits]

                def sums(tt=tt, arrived=arrived):
                    for slot in arrived:
                        arrive(slot)
                    total(0, tt, arrived)

                if start:
                    pl.when(cond)(sums)
                slot = line_slot(tt, from_next)
                also(0, tt, slot, chain)
                send(0, tt, at.along(step), slot, cond)

        def last():
            arrived = [b * n_tensor + at.t for b in at.bits]
            for slot in arrived:
                arrive(slot)
            total(0, at.t, arrived, final)
            also(0, at.t, line_slot(at.t, True), at.has_next, final)
            also(0, at.t, line_slot(at.t, False), at.has_prev, final)
            sec, b = place(i)
            stay = pltpu.make_async_copy(final.at[i], out.at[b, :, lanes], out_sem.at[0, i])
            go = pltpu.make_async_remote_copy(
                src_ref=final.at[i],
                dst_ref=out.at[b, :, lanes],
                send_sem=out_sem.at[1, i],
                recv_sem=out_sem.at[2, i],
                device_id=at.sibling(),
                device_id_type=MESH_ID,
            )

            @pl.when(sec == at.s)
            def _():
                if start:
                    stay.start()
                else:
                    stay.wait()

            @pl.when(sec != at.s)
            def _():
                if start:
                    go.start()
                else:
                    go.wait_send()

        groups = [crossing, leaves]
        groups += [functools.partial(plane, w) for w in range(len(at.bits), 0, -1)]
        groups += [functools.partial(column, k) for k in range(n_tensor - 1, 0, -1)] + [last]
        return groups, counter

    lags = reduce_lags(len(sizes))

    def run_group(i, g):
        groups, counter = steps(i, True)
        for _ in range(sum(sizes[:g])):
            next(counter)
        groups[g]()

    phases = [(kind, sec) for sec in range(n_section - 1, -1, -1) for kind in ("ffn", "attn")]

    def loads(phase, k, par):
        kind, sec = phases[phase]
        rows, qkv, p, heads, middle, active, slope = saved[sec]
        if kind == "ffn":
            pairs = [
                (weights.at[sec, 1, k], w_buf.at[par, 0]),
                (weights.at[sec, 2, k], w_buf.at[par, 1]),
                (active.at[k], hidden_buf.at[par, 0]),
                (slope.at[k], hidden_buf.at[par, 1]),
            ]
            once = (middle, middle_buf)
        else:
            pairs = [
                (weights.at[sec, 0, k], w_buf.at[par, 0]),
                (qkv.at[k], qkv_buf.at[par]),
                (p.at[k], p_buf.at[par]),
                (heads.at[k], heads_buf.at[par]),
            ]
            once = (rows, rows_buf)
        copies = [
            pltpu.make_async_copy(src, dst, load_sem.at[par, n]) for n, (src, dst) in enumerate(pairs)
        ]
        return copies, lambda: pltpu.make_async_copy(*once, load_sem.at[0, 4])

    def start_loads(phase, k, par, is_first):
        copies, once = loads(phase, k, par)
        for copy in copies:
            copy.start()
        if is_first:
            once().start()

    def blocks_of(phase):
        kind, sec = phases[phase]
        base = (n_section - 1 - sec) * n_blk
        return [base, base + 1] if kind == "ffn" else [base + 2]

    def shared(par, q):
        return pltpu.make_async_remote_copy(
            src_ref=stage.at[par, q],
            dst_ref=ring.at[par, q],
            send_sem=stage_sem.at[0, par, q],
            recv_sem=stage_sem.at[1, par, q],
            device_id=at.sibling(),
            device_id_type=MESH_ID,
        )

    def before_emit(phase, k, par):
        if phase == 0:

            @pl.when(k >= 2)
            def _():
                for q in range(2):
                    shared(par, q).wait_send()
                pl.semaphore_wait(credit.at[par], 1)

        else:
            same, back = len(blocks_of(phase)), len(blocks_of(phase - 1))
            for q in range(max(same, back)):
                if q < same and q < back:
                    shared(par, q).wait_send()
                else:

                    @pl.when(k >= 2 if q < same else k < 2)
                    def _():
                        shared(par, q).wait_send()

            pl.semaphore_wait(credit.at[par], 1)

    def emit(phase, q, k, par, low, high):
        first = at.s == 0
        own[blocks_of(phase)[q], k] = jnp.where(first, low, high)
        stage[par, q] = jnp.where(first, high, low)

    def consume(phase, k, par, is_last):
        for q, i in enumerate(blocks_of(phase)):
            shared(par, q).wait_recv()

            def chunk(c, carry):
                here = pl.ds(pl.multiple_of(c * 96, 96), 96)
                total = own[i, k, here].astype(F32) + ring[par, q, here].astype(F32)
                own[i, k, here] = total.astype(own.dtype)
                return carry

            lax.fori_loop(0, own.shape[2] // 96, chunk, 0)
        if not is_last:
            pl.semaphore_signal(
                credit.at[par], inc=1, device_id=at.sibling(), device_id_type=MESH_ID
            )

    def column_sum(values):
        return jnp.sum(values, axis=0, keepdims=True)

    def ffn_step(sec, k, par, emits):
        middle = middle_buf
        gain, shift = vec[sec, 3:4], vec[sec, 4:5]

        @pl.when(k == 0)
        def _():
            source = cotangent if sec == n_section - 1 else grad_out.at[sec + 1]
            low = (source[...].astype(F32) * live[...]).astype(BF16)
            grad_low[...] = low
            left_t[...] = low.T
            unit, _ = unit_rows(middle[...])
            right_t[...] = (unit * gain + shift).astype(BF16).T
            acc[...] = jnp.zeros_like(acc)

        d_down = dot(left_t[...], hidden_buf[par, 0]).astype(BF16)
        emits(0, d_down[:, :half], d_down[:, half:])
        grad_hidden = (dot(grad_low[...], w_buf[par, 1]) * hidden_buf[par, 1].astype(F32)).astype(BF16)
        d_up_bias[sec, k] = column_sum(grad_hidden.astype(F32))
        d_up = dot(right_t[...], grad_hidden).astype(BF16)
        emits(1, d_up[:, :half], d_up[:, half:])
        acc[...] += dot_cols(grad_hidden, w_buf[par, 0])

    def attn_step(sec, k, par, emits):
        w_attn = w_buf.at[par, 0]

        @pl.when(k == 0)
        def _():
            unit, scale = unit_rows(middle_buf[...])
            grad_norm = acc[...]
            low = grad_low[...].astype(F32)
            mid = low + unit_rows_back(grad_norm * vec[sec, 3:4], unit, scale)
            grad_mid[...] = mid
            d_vec[sec, 2:3] = column_sum(mid)
            d_vec[sec, 3:4] = column_sum(grad_norm * unit)
            d_vec[sec, 4:5] = column_sum(grad_norm)
            d_vec[sec, 5:6] = column_sum(low)
            mid = mid.astype(BF16)
            grad_low[...] = mid
            left_t[...] = mid.T
            unit, _ = unit_rows(rows_buf[...].astype(F32))
            right_t[...] = (unit * vec[sec, 0:1] + vec[sec, 1:2]).astype(BF16).T
            acc[...] = jnp.zeros_like(acc)

        d_out = dot(left_t[...], heads_buf[par]).astype(BF16)
        grad_heads = dot(grad_low[...], w_attn[:, 3 * part :]).astype(BF16)
        per_image = []
        for image in range(images):
            span = slice(image * ROWS, (image + 1) * ROWS)
            per_head = [[], [], []]
            for head in range(n_heads):
                q, key, v = (
                    qkv_buf[par, span, c * part + head * DH : c * part + (head + 1) * DH]
                    for c in range(3)
                )
                grad_o = grad_heads[span, head * DH : (head + 1) * DH]
                chosen = p_buf[par, image, head]
                chances = chosen.astype(F32)
                grad_chances = dot_cols(v, grad_o)
                along = jnp.sum(chances * grad_chances, axis=0, keepdims=True)
                grad_scores = (chances * (grad_chances - along)).astype(BF16)
                per_head[0].append((dot(key.T, grad_scores).T * DH**-0.5).astype(BF16))
                per_head[1].append((dot(grad_scores, q) * DH**-0.5).astype(BF16))
                per_head[2].append(dot(chosen, grad_o).astype(BF16))
            per_image.append(jnp.concatenate(per_head[0] + per_head[1] + per_head[2], axis=1))
        grad_mixed = jnp.concatenate(per_image, axis=0)
        d_qkv_bias[sec, k] = column_sum(grad_mixed.astype(F32))
        d_qkv = dot(right_t[...], grad_mixed).astype(BF16)
        emits(0, d_qkv[:, :half], jnp.concatenate([d_qkv[:, half:], d_out], axis=1))
        acc[...] += dot_cols(grad_mixed, w_attn[:, : 3 * part])

        @pl.when(k == n_tensor - 1)
        def _():
            unit, scale = unit_rows(rows_buf[...].astype(F32))
            grad_norm = acc[...]
            d_vec[sec, 0:1] = column_sum(grad_norm * unit)
            d_vec[sec, 1:2] = column_sum(grad_norm)
            total = grad_mid[...] + unit_rows_back(grad_norm * vec[sec, 0:1], unit, scale)
            grad_out[sec] = total.astype(BF16)

    def compute(phase, k):
        kind, sec = phases[phase]
        par = lax.rem(k, 2)
        copies, once = loads(phase, k, par)
        for copy in copies:
            copy.wait()

        @pl.when(k == 0)
        def _():
            once().wait()

        @pl.when(k < n_tensor - 1)
        def _():
            start_loads(phase, k + 1, 1 - par, False)

        if phase + 1 < len(phases):

            @pl.when(k == n_tensor - 1)
            def _():
                start_loads(phase + 1, 0, 0, True)

        before_emit(phase, k, par)

        def emits(q, low, high):
            emit(phase, q, k, par, low, high)

        (ffn_step if kind == "ffn" else attn_step)(sec, k, par, emits)
        for q in range(len(blocks_of(phase))):
            shared(par, q).start()

        @pl.when(k > 0)
        def _():
            consume(phase, k - 1, 1 - par, False)

        if phase:

            @pl.when(k == 0)
            def _():
                consume(phase - 1, n_tensor - 1, 1 - par, False)

    def start_of(i):
        return BLOCK_TICKS * i + PAUSE * (i // n_blk)

    def block_at(tick):
        found, runs = 0, False
        for i in range(n_all):
            here = tick == start_of(i)
            found = jnp.where(here, i, found)
            runs = jnp.logical_or(runs, here)
        return found, runs

    small = [(d_vec, vec_in), (d_qkv_bias, qkv_bias_in), (d_up_bias, up_bias_in)]
    n_hops = len(at.bits)

    def small_copies(stage, device, slot):
        sec = 1 - at.s if stage == 0 else at.s
        return [
            pltpu.make_async_remote_copy(
                src_ref=mine.at[sec],
                dst_ref=came_in.at[slot],
                send_sem=small_sem.at[0, slot, n],
                recv_sem=small_sem.at[1, slot, n],
                device_id=device,
                device_id_type=MESH_ID,
            )
            for n, (mine, came_in) in enumerate(small)
        ]

    def small_send(stage):
        if stage == 0:
            return [small_copies(0, at.sibling(), 0)]
        if stage <= n_hops:
            return [small_copies(stage, at.hop(stage - 1), stage)]
        other = [lax.rem(at.t + k, n_tensor) for k in range(1, n_tensor)]
        return [
            small_copies(stage, (at.s, at.d, tt), n_hops + 1 + k) for k, tt in enumerate(other)
        ]

    def small_take(stage):
        sent = small_send(stage)
        for copies in sent:
            for copy in copies:
                copy.wait()
        first = stage if stage <= n_hops else n_hops + 1
        for mine, came_in in small:
            total = mine[at.s]
            for slot in range(first, first + len(sent)):
                total = total + came_in[slot]
            mine[at.s] = total

    def small_step(tick):
        for stage in range(n_hops + 2):

            @pl.when(tick == SMALL_TICKS * stage)
            def _():
                if stage:
                    small_take(stage - 1)
                for copies in small_send(stage):
                    for copy in copies:
                        copy.start()

        @pl.when(tick == SMALL_TICKS * (n_hops + 2))
        def _():
            small_take(n_hops + 1)

    def prologue(k, carry):
        compute(0, k)
        return carry

    start_loads(0, 0, 0, True)
    lax.fori_loop(0, n_tensor, prologue, 0)

    n_busy = (len(phases) - 1) * n_tensor

    def body(it, carry):
        for phase in range(1, len(phases)):

            @pl.when(lax.div(it, n_tensor) == phase - 1)
            def _():
                compute(phase, lax.rem(it, n_tensor))

        @pl.when(it == n_busy)
        def _():
            consume(len(phases) - 1, n_tensor - 1, (n_tensor - 1) % 2, True)

        for g, lag in sorted(enumerate(lags), key=lambda item: item[1]):
            i, runs = block_at(it - lag)

            @pl.when(runs)
            def _():
                run_group(i, g)

        small_step(it - n_busy)
        return carry

    lax.fori_loop(0, start_of(n_all - 1) + 1 + max(lags), body, 0)

    for par in range(2):
        for q in range(len(blocks_of(len(phases) - 1))):
            shared(par, q).wait_send()
    pl.semaphore_wait(credit.at[0], 1)

    def finish(i, carry):
        groups, _ = steps(i, False)
        for g in groups:
            g()
        sec, b = place(i)

        @pl.when(sec == at.s)
        def _():
            pltpu.make_async_copy(final.at[i], final.at[i], out_sem.at[2, i]).wait()

        return carry

    lax.fori_loop(0, n_all, finish, 0)


def send_sizes(n_dp, n_tensor):
    bits = n_dp.bit_length() - 1
    mid = n_tensor // 2
    weights = [bin(e).count("1") for e in range(n_dp)]
    sizes = [2 * mid * sum(w >= 2 for w in weights), mid * bits]
    sizes += [mid * sum(w == k for w in weights) for k in range(bits, 0, -1)]
    return sizes + [2] * (n_tensor - 1) + [0]


def backward_and_reduce(weights, cotangent, live, vec, first, second, n_dp):
    n_section, n_blk, n_tensor, width, span = weights.shape
    n_rows = cotangent.shape[0]
    images = n_rows // ROWS
    part = width // n_tensor
    n_all = n_section * n_blk
    depth, half = width // n_dp, span // 2
    slots = Slots(n_dp, n_tensor)
    n_sends = sum(send_sizes(n_dp, n_tensor))
    n_small = n_dp.bit_length() + n_tensor - 1
    shape = jax.ShapeDtypeStruct
    hbm = pl.BlockSpec(memory_space=pl.ANY)
    vmem = pl.BlockSpec(memory_space=pltpu.VMEM)
    dma = pltpu.SemaphoreType.DMA
    return pl.pallas_call(
        functools.partial(backward_kernel, n_dp, n_tensor, images),
        out_shape=[
            shape((n_blk, depth, span), F32),
            shape((n_section, n_rows, width), BF16),
            shape((n_section, 6, width), F32),
            shape((n_section, n_tensor, 1, 3 * part), F32),
            shape((n_section, n_tensor, 1, span), F32),
        ],
        in_specs=[hbm] + [vmem] * 3 + [hbm] * 14,
        out_specs=[hbm] + [vmem] * 4,
        scratch_shapes=[
            pltpu.VMEM((n_all, n_tensor, width, half), BF16),
            pltpu.VMEM((n_all, slots.count, depth, half), BF16),
            pltpu.VMEM((n_all, depth, half), F32),
            pltpu.VMEM((n_small, 6, width), F32),
            pltpu.VMEM((n_small, n_tensor, 1, 3 * part), F32),
            pltpu.VMEM((n_small, n_tensor, 1, span), F32),
            pltpu.VMEM((2, 2, width, half), BF16),
            pltpu.VMEM((2, 2, width, half), BF16),
            pltpu.VMEM((2, 2, width, span), BF16),
            pltpu.VMEM((2, 2, n_rows, span), BF16),
            pltpu.VMEM((2, n_rows, 3 * part), BF16),
            pltpu.VMEM((2, images, part // DH, ROWS, ROWS), BF16),
            pltpu.VMEM((2, n_rows, part), BF16),
            pltpu.VMEM((n_rows, width), BF16),
            pltpu.VMEM((n_rows, width), F32),
            pltpu.VMEM((n_rows, width), BF16),
            pltpu.VMEM((width, n_rows), BF16),
            pltpu.VMEM((width, n_rows), BF16),
            pltpu.VMEM((n_rows, width), F32),
            pltpu.VMEM((n_rows, width), F32),
            dma((2, 5)),
            dma((2, 2, 2)),
            pltpu.SemaphoreType.REGULAR((2,)),
            dma((n_all, slots.count)),
            dma((n_all, n_sends)),
            dma((3, n_all)),
            dma((2, n_small, 3)),
        ],
        compiler_params=pltpu.CompilerParams(
            collective_id=1, has_side_effects=True, vmem_limit_bytes=64 * 1024 * 1024 - 256 * 1024
        ),
    )(weights, cotangent, live, vec, *first, *second)


AXES = ("section", "tensor", "dp")


def shards(
    images,
    cotangent,
    counts,
    ln1_gain,
    ln1_bias,
    q_bias,
    v_bias,
    qkv_weight,
    out_weight,
    out_bias,
    ln2_gain,
    ln2_bias,
    up_weight,
    up_bias,
    down_weight,
    down_bias,
):
    n_section, n_dp, n_tensor = (lax.axis_size(a) for a in ("section", "dp", "tensor"))
    section_idx = lax.axis_index("section")
    micro_count, share_rows, width = images.shape
    own_count = micro_count // n_section
    depth = qkv_weight.shape[1]
    part = qkv_weight.shape[3]

    own = section_idx * own_count

    def own_rows(values):
        mine = lax.dynamic_slice_in_dim(values, own, own_count, 0).reshape(-1, SEQ, values.shape[-1])
        return jnp.pad(mine, ((0, 0), (0, ROWS - SEQ), (0, 0))).reshape(-1, values.shape[-1])

    row_place = lax.axis_index("tensor") * share_rows + jnp.arange(share_rows)
    own_counts = lax.dynamic_slice_in_dim(counts, own, own_count, 0)
    live_rows = (row_place // SEQ < own_counts).astype(jnp.float32)
    live_rows = live_rows.reshape(-1, SEQ)
    live_rows = jnp.pad(live_rows, ((0, 0), (0, ROWS - SEQ))).reshape(-1, 1)

    shard = jnp.stack(
        [
            jnp.concatenate([qkv_weight[0].reshape(depth, -1), out_weight[0].T], axis=1),
            up_weight[0],
            down_weight[0].T,
        ]
    )
    gathered = gather_weights(shard, n_section, n_dp, n_tensor)

    small = [ln1_gain, ln1_bias, out_bias, ln2_gain, ln2_bias, down_bias, q_bias, v_bias, up_bias]
    sizes = [piece.size for piece in small]
    all_small = lax.all_gather(jnp.concatenate([s.reshape(-1) for s in small]), AXES, axis=0)
    all_small = all_small.reshape(n_section, n_tensor, n_dp, -1).astype(jnp.float32)

    def params_of(sec):
        pieces, start = [], 0
        for size in sizes:
            pieces.append(all_small[sec, :, :, start : start + size])
            start += size
        vec = jnp.stack([p[0].reshape(-1) for p in pieces[:6]])
        heads = [
            p.reshape(n_tensor, n_dp, -1, DH // n_dp).transpose(0, 2, 1, 3).reshape(n_tensor, 1, -1)
            for p in pieces[6:]
        ]
        qkv_bias = jnp.concatenate([heads[0], jnp.zeros_like(heads[0]), heads[1]], axis=2)
        return vec, qkv_bias, heads[2]

    params = [params_of(sec) for sec in range(n_section)]
    first_rows = own_rows(images)
    first_out, *first_saved = forward_layer(0, gathered, first_rows, live_rows, *params[0])
    second_out, *second_saved = forward_layer(1, gathered, first_out, live_rows, *params[1])
    vec = jnp.stack([p[0] for p in params])
    weight_sum, grad_rows, d_vec, d_qkv_bias, d_up_bias = backward_and_reduce(
        gathered,
        own_rows(cotangent),
        live_rows,
        vec,
        [first_rows, *first_saved],
        [first_out, *second_saved],
        n_dp,
    )

    def placed_rows(first, second):
        is_first = section_idx == 0
        away = jnp.where(is_first, second, first)
        came = lax.ppermute(away, "section", [(0, 1), (1, 0)])
        home = jnp.where(is_first, first, second)
        home, came = (
            v.reshape(-1, ROWS, width)[:, :SEQ].reshape(own_count, share_rows, width)
            for v in (home, came)
        )
        low = jnp.where(is_first, home, came)
        high = jnp.where(is_first, came, home)
        return jnp.concatenate([low, high], axis=0)[None]

    section_out = placed_rows(first_out, second_out)
    input_grad = placed_rows(grad_rows[0], grad_rows[1])

    dp_idx, tensor_idx = lax.axis_index("dp"), lax.axis_index("tensor")

    def own_heads(sums, like):
        _, heads, lanes = like.shape
        sums = sums.reshape(-1, DH)
        return lax.dynamic_slice(sums, (0, dp_idx * lanes), (heads, lanes))[None]

    d_vec, d_qkv_bias, d_up_bias = (
        lax.dynamic_index_in_dim(v, section_idx, 0, keepdims=False)
        for v in (d_vec, d_qkv_bias, d_up_bias)
    )
    q_row, _, v_row = jnp.split(
        lax.dynamic_index_in_dim(d_qkv_bias, tensor_idx, 0, keepdims=False).reshape(-1), 3
    )
    up_row = lax.dynamic_index_in_dim(d_up_bias, tensor_idx, 0, keepdims=False)
    q_sum, v_sum, up_sum = own_heads(q_row, q_bias), own_heads(v_row, v_bias), own_heads(up_row, up_bias)
    block = width // (n_dp * n_tensor)
    vec = lax.dynamic_slice_in_dim(d_vec, (dp_idx * n_tensor + tensor_idx) * block, block, 1)[None]

    return (
        section_out,
        input_grad,
        weight_sum[0, :, : 3 * part].reshape(qkv_weight.shape),
        weight_sum[0, :, 3 * part :].T[None],
        weight_sum[1][None],
        weight_sum[2].T[None],
        q_sum,
        v_sum,
        up_sum,
        vec,
    )


def solution(mesh):
    placed = (
        P(None, ("dp", "tensor"), None),
        P(None, ("dp", "tensor"), None),
        P(None, "dp"),
        P("section", "dp"),
        P("section", "dp"),
        P("section", "tensor", "dp"),
        P("section", "tensor", "dp"),
        P("section", "dp", None, "tensor"),
        P("section", "tensor", "dp"),
        P("section", "dp"),
        P("section", "dp"),
        P("section", "dp"),
        P("section", "dp", "tensor"),
        P("section", "tensor", "dp"),
        P("section", "tensor", "dp"),
        P("section", "dp"),
    )
    return jax.shard_map(
        shards,
        mesh=mesh,
        in_specs=placed,
        out_specs=(
            P("section", None, ("dp", "tensor"), None),
            P("section", None, ("dp", "tensor"), None),
            P("section", "dp", None, "tensor"),
            P("section", "tensor", "dp"),
            P("section", "dp", "tensor"),
            P("section", "tensor", "dp"),
            P("section", "tensor", "dp"),
            P("section", "tensor", "dp"),
            P("section", "tensor", "dp"),
            P("section", None, ("dp", "tensor")),
        ),
        check_vma=False,
    )
```

```python
import functools
import jax
import jax.numpy as jnp
from jax import lax
from jax.experimental import pallas as pl
from jax.experimental.pallas import tpu as pltpu
from jax.sharding import PartitionSpec as P

CHUNK_ROWS = 48
BLOCK_TICKS = 3
PAUSE = 0
SMALL_TICKS = 2
GLAGS = [0, 2, 4, 5, 8, 9, 12, 14]
MESH_ID = pl.DeviceIdType.MESH


def slot_sizes(n_dp, n_tensor):
    bits = [b for b in range(n_dp.bit_length()) if (1 << b) < n_dp]
    mid = n_tensor // 2
    weights = [bin(e).count("1") for e in range(n_dp)]

    def plane(weight):
        total = 0
        for j in range(mid):
            for e in range(n_dp):
                if weights[e] == weight:
                    for b in bits:
                        if not e >> b & 1:
                            chosen = [c for c in bits if (e | 1 << b) >> c & 1]
                            total += chosen[j % len(chosen)] == b
                    total += 2 * (weight >= 2) + 1
        return total

    first = [2 + len(bits)]
    columns = [2 * (2 + len(bits))] * (n_tensor - 1)
    planes = [plane(w) for w in range(1, len(bits) + 1)]
    crossed = [3 * mid * sum(w >= 2 for w in weights)]
    rest = [mid * sum(w == 1 for w in weights)]
    return first + [columns[0], planes[0], columns[1]] + planes[1:] + columns[2:] + crossed + rest


class Place:
    def __init__(self, n_dp, n_tensor):
        self.n_dp, self.n_tensor = n_dp, n_tensor
        self.mid = n_tensor // 2
        self.bits = [b for b in range(n_dp.bit_length()) if (1 << b) < n_dp]
        self.s = lax.axis_index("section")
        self.d = lax.axis_index("dp")
        self.t = lax.axis_index("tensor")
        self.upper = lax.div(self.t, self.mid)
        self.has_next = self.t < n_tensor - 1
        self.has_prev = self.t > 0

    def away(self, e):
        other = self.d
        for b in self.bits:
            if e >> b & 1:
                other = other + (1 << b) * (1 - 2 * lax.rem(lax.div(self.d, 1 << b), 2))
        return other

    def last_bit(self, e, j):
        chosen = [b for b in self.bits if e >> b & 1]
        return chosen[j % len(chosen)]

    def own_side(self, j):
        return self.upper * self.mid + j

    def other_side(self, j):
        return (1 - self.upper) * self.mid + j

    def sibling(self):
        return (1 - self.s, self.d, self.t)

    def along(self, step):
        return (self.s, self.d, self.t + step)

    def hop(self, b):
        return (self.s, self.away(1 << b), self.t)

    def meet(self):
        barrier = pltpu.get_barrier_semaphore()
        line = [(self.s, self.d, lax.rem(self.t + k, self.n_tensor)) for k in range(1, self.n_tensor)]
        others = [self.sibling()] + [self.hop(b) for b in self.bits] + line
        for device in others:
            pl.semaphore_signal(barrier, inc=1, device_id=device, device_id_type=MESH_ID)
        pl.semaphore_wait(barrier, len(others))

    def rows_away(self, source, target, sec, sems):
        return pltpu.make_async_remote_copy(
            src_ref=source.at[sec],
            dst_ref=target.at[self.s],
            send_sem=sems.at[1],
            recv_sem=sems.at[2],
            device_id=self.sibling(),
            device_id_type=MESH_ID,
        )

    def hand_out(self, source, target, sec, sems):
        @pl.when(sec == self.s)
        def _():
            pltpu.make_async_copy(source.at[sec], target.at[self.s], sems.at[0]).start()

        @pl.when(sec != self.s)
        def _():
            self.rows_away(source, target, sec, sems).start()

    def handed_out(self, source, target, sems):
        pltpu.make_async_copy(source.at[0], target.at[self.s], sems.at[0]).wait()
        self.rows_away(source, target, 0, sems).wait()

    def by_weight(self, weight):
        return [e for e in range(self.n_dp) if bin(e).count("1") == weight]


DH = 64
SEQ = 197
EPS = 1e-06
F32 = jnp.float32
BF16 = jnp.bfloat16
ROWS = 208


def dot(left, right):
    return jnp.dot(left, right, preferred_element_type=F32)


def dot_cols(left, right):
    return lax.dot_general(left, right, (((1,), (1,)), ((), ())), preferred_element_type=F32)


def unit_rows(values):
    average = jnp.mean(values, axis=-1, keepdims=True)
    centered = values - average
    scale = lax.rsqrt(jnp.mean(centered * centered, axis=-1, keepdims=True) + EPS)
    return centered * scale, scale


def unit_rows_back(grad_unit, unit, scale):
    along = jnp.mean(grad_unit * unit, axis=-1, keepdims=True)
    return scale * (grad_unit - jnp.mean(grad_unit, axis=-1, keepdims=True) - unit * along)


def gelu_parts(hidden):
    below = 0.5 * (1.0 + lax.erf(hidden * (0.5**0.5)))
    density = jnp.exp(-0.5 * hidden * hidden) * 0.3989422804014327
    return hidden * below, below + hidden * density


def forward_kernel(n_dp, n_tensor, images, *refs):
    (
        shard, rows, live, *given,
        out, sec_rows, row_out, qkv_out, p_out, heads_out, middle_out, active_out, slope_out, vec,
        w_buf, qkv_st, p_st, heads_st, active_st, slope_st, middle_st, normed, acc, row_buf,
        qkv_bias, up_bias, vec_in, qkv_bias_in, up_bias_in,
        own_sem, recv_sem, send_sem, part_sem, load_sem, store_sem, active_sem, once_sem, row_sem, small_sem,
    ) = refs
    at = Place(n_dp, n_tensor)
    n_section = out.shape[0]
    n_blk, depth, span = shard.shape
    half = span // 2
    n_all = n_section * n_blk
    part = vec.shape[2] // n_tensor
    n_heads = part // DH

    def spread(value):
        return jnp.concatenate([jnp.where(at.d == k, value, 0.0) for k in range(n_dp)], axis=1)

    def spread_heads(ref):
        values = ref[0].astype(F32)
        return jnp.concatenate([spread(values[h : h + 1]) for h in range(values.shape[0])], axis=1)

    vec[...] = jnp.zeros_like(vec)
    qkv_bias[...] = jnp.zeros_like(qkv_bias)
    up_bias[...] = jnp.zeros_like(up_bias)
    placed = jnp.concatenate([spread(ref[...].astype(F32)) for ref in given[:6]], axis=0)
    vec[at.s] = jnp.where(at.t == 0, placed, 0.0)
    q_row, v_row = spread_heads(given[6]), spread_heads(given[7])
    qkv_bias[at.s, at.t] = jnp.concatenate([q_row, jnp.zeros_like(q_row), v_row], axis=1)
    up_bias[at.s, at.t] = spread_heads(given[8])
    at.meet()

    def whole(sec, b):
        return out.at[sec, b, at.t, rows_of(0), :]

    def rows_of(e):
        return pl.ds(pl.multiple_of(at.away(e) * depth, 16), depth)

    lanes = pl.ds(pl.multiple_of(at.s * half, 128), half)

    def piece(i, e, tt):
        return out.at[lax.div(i, n_blk), lax.rem(i, n_blk), tt, rows_of(e), lanes]

    def share(b):
        return pltpu.make_async_remote_copy(
            src_ref=shard.at[b],
            dst_ref=whole(at.s, b),
            send_sem=own_sem.at[1, b],
            recv_sem=own_sem.at[2, b],
            device_id=at.sibling(),
            device_id_type=MESH_ID,
        )

    for b in range(n_blk):
        pltpu.make_async_copy(shard.at[b], whole(at.s, b), own_sem.at[0, b]).start()
        share(b).start()

    def push(i, e, tt, device, e_there, slot, start):
        copy = pltpu.make_async_remote_copy(
            src_ref=piece(i, e, tt),
            dst_ref=piece(i, e, tt),
            send_sem=send_sem.at[i, slot],
            recv_sem=recv_sem.at[i, e_there * n_tensor + tt],
            device_id=device,
            device_id_type=MESH_ID,
        )
        if start:
            copy.start()
        else:
            copy.wait_send()

    def push_sib(i, e, tt, slot, start):
        copy = pltpu.make_async_remote_copy(
            src_ref=piece(i, e, tt),
            dst_ref=piece(i, e, tt),
            send_sem=send_sem.at[i, slot],
            recv_sem=part_sem.at[i, 0 if e == 0 else 1],
            device_id=at.sibling(),
            device_id_type=MESH_ID,
        )
        if start:
            copy.start()
        else:
            copy.wait_send()

    def await_piece(i, e, tt):
        pltpu.make_async_remote_copy(
            src_ref=piece(i, e, tt),
            dst_ref=piece(i, e, tt),
            send_sem=send_sem.at[i, 0],
            recv_sem=recv_sem.at[i, e * n_tensor + tt],
            device_id=at.sibling(),
            device_id_type=MESH_ID,
        ).wait_recv()

    def steps(i, start):
        slots = iter(range(10_000))

        def maybe(cond, action):
            if cond is None:
                action()
            else:
                pl.when(cond)(action)

        def ready(e, tt, cond=None):
            if start:
                maybe(cond, lambda: await_piece(i, e, tt))

        def go(e, tt, device, e_there, cond=None):
            slot = next(slots)
            maybe(cond, lambda: push(i, e, tt, device, e_there, slot, start))

        def go_sib(e, tt, cond=None):
            slot = next(slots)
            maybe(cond, lambda: push_sib(i, e, tt, slot, start))

        def first():
            sec, b = lax.div(i, n_blk), lax.rem(i, n_blk)
            if start:

                @pl.when(sec == at.s)
                def _():
                    pltpu.make_async_copy(shard.at[b], whole(at.s, b), own_sem.at[0, b]).wait()

                @pl.when(sec != at.s)
                def _():
                    pltpu.make_async_remote_copy(
                        src_ref=shard.at[b],
                        dst_ref=whole(1 - at.s, b),
                        send_sem=own_sem.at[1, b],
                        recv_sem=own_sem.at[2, b],
                        device_id=at.sibling(),
                        device_id_type=MESH_ID,
                    ).wait_recv()

            go(0, at.t, at.along(1), 0, at.has_next)
            go(0, at.t, at.along(-1), 0, at.has_prev)
            for b in at.bits:
                go(0, at.t, at.hop(b), 1 << b)

        def column(k):
            low, high = at.t >= k, at.t + k < n_tensor
            for tt, cond, dev, more in (
                (at.t - k, low, at.along(1), jnp.logical_and(low, at.has_next)),
                (at.t + k, high, at.along(-1), jnp.logical_and(high, at.has_prev)),
            ):
                ready(0, tt, cond)
                go(0, tt, dev, 0, more)
                for b in at.bits:
                    go(0, tt, at.hop(b), 1 << b, cond)
                go_sib(0, tt, cond)

        def plane(weight):
            for j in range(at.mid):
                for e in at.by_weight(weight):
                    tt = at.own_side(j)
                    ready(e, tt)
                    for b in at.bits:
                        if not e >> b & 1 and at.last_bit(e | 1 << b, j) == b:
                            go(e, tt, at.hop(b), e | 1 << b)
                    if weight >= 2:
                        go(e, tt, at.along(1), e, at.t == at.mid - 1)
                        go(e, tt, at.along(-1), e, at.t == at.mid)
                    go_sib(e, tt)

        def crossed():
            for weight in range(2, len(at.bits) + 1):
                for e in at.by_weight(weight):
                    for j in range(at.mid):
                        tt = at.other_side(j)
                        ready(e, tt)
                        up = jnp.logical_and(at.t >= at.mid, at.has_next)
                        down = jnp.logical_and(at.t < at.mid, at.has_prev)
                        go(e, tt, at.along(1), e, up)
                        go(e, tt, at.along(-1), e, down)
                        go_sib(e, tt)

        def rest():
            for e in at.by_weight(1):
                for j in range(at.mid):
                    tt = at.other_side(j)
                    ready(e, tt)
                    go_sib(e, tt)

        groups = [first]
        for k in range(1, n_tensor):
            groups.append(functools.partial(column, k))
        planes = [functools.partial(plane, w) for w in range(1, len(at.bits) + 1)]
        merged = [groups[0]]
        order = [groups[1], planes[0], groups[2]] + planes[1:] + groups[3:] + [crossed, rest]
        return merged + order, slots


    small = [(vec, vec_in), (qkv_bias, qkv_bias_in), (up_bias, up_bias_in)]
    n_hops = len(at.bits)

    def small_copies(device, slot, to_place):
        return [
            pltpu.make_async_remote_copy(
                src_ref=mine.at[at.s],
                dst_ref=mine.at[at.s] if to_place else came_in.at[slot],
                send_sem=small_sem.at[0, slot, n],
                recv_sem=small_sem.at[1, slot, n],
                device_id=device,
                device_id_type=MESH_ID,
            )
            for n, (mine, came_in) in enumerate(small)
        ]

    def small_send(stage):
        if stage < n_hops:
            return [small_copies(at.hop(stage), stage, False)]
        if stage == n_hops:
            other = [lax.rem(at.t + k, n_tensor) for k in range(1, n_tensor)]
            return [small_copies((at.s, at.d, tt), n_hops + k, False) for k, tt in enumerate(other)]
        return [small_copies(at.sibling(), n_hops + n_tensor - 1, True)]

    def small_take(stage):
        sent = small_send(stage)
        for copies in sent:
            for copy in copies:
                copy.wait()
        if stage <= n_hops:
            for mine, came_in in small:
                total = mine[at.s]
                for slot in range(stage, stage + len(sent)):
                    total = total + came_in[slot]
                mine[at.s] = total

    def small_step(tick):
        for stage in range(n_hops + 3):

            @pl.when(tick == 1 + 2 * stage)
            def _():
                if stage:
                    small_take(stage - 1)
                if stage < n_hops + 2:
                    for copies in small_send(stage):
                        for copy in copies:
                            copy.start()

    def load(i, k, par):
        return pltpu.make_async_copy(out.at[i // n_blk, i % n_blk, k], w_buf.at[par], load_sem.at[par])

    def stores(i, k, par):
        sec, b = i // n_blk, i % n_blk
        if b == 0:
            pairs = [
                (qkv_st.at[par], qkv_out.at[sec, k], store_sem.at[par, 0]),
                (p_st.at[par], p_out.at[sec, k], store_sem.at[par, 1]),
                (heads_st.at[par], heads_out.at[sec, k], store_sem.at[par, 2]),
            ]
        elif b == 1:
            pairs = [(slope_st.at[par], slope_out.at[sec, k], store_sem.at[par, 3])]
        else:
            pairs = []
        return [pltpu.make_async_copy(*pair) for pair in pairs]

    def store_active(sec, k):
        return pltpu.make_async_copy(active_st.at[k], active_out.at[sec, k], active_sem.at[k])

    def store_middle(sec):
        return pltpu.make_async_copy(middle_st, middle_out.at[sec], once_sem.at[0])

    def store_rows(sec):
        return pltpu.make_async_copy(row_buf.at[sec], row_out.at[sec], once_sem.at[1 + sec])

    def attn_step(sec, k, par):
        @pl.when(k == 0)
        def _():
            values = (rows if sec == 0 else row_buf.at[sec - 1])[...].astype(F32)
            unit, _ = unit_rows(values)
            normed[...] = (unit * vec[sec, 0:1] + vec[sec, 1:2]).astype(BF16)
            acc[...] = values + vec[sec, 2:3]

        mixed = (dot(normed[...], w_buf[par, :, : 3 * part]) + qkv_bias[sec, k]).astype(BF16)
        qkv_st[par] = mixed
        keep = lax.broadcasted_iota(jnp.int32, (ROWS, ROWS), 0) < SEQ
        per_image = []
        for image in range(images):
            here = mixed[image * ROWS : (image + 1) * ROWS]
            per_head = []
            for head in range(n_heads):
                q, key, v = (
                    here[:, c * part + head * DH : c * part + (head + 1) * DH] for c in range(3)
                )
                scores = jnp.where(keep, dot_cols(key, q) * DH**-0.5, -1e30)
                scores = jnp.exp(scores - jnp.max(scores, axis=0, keepdims=True))
                total = jnp.sum(scores, axis=0, keepdims=True)
                chances = (scores * (1.0 / total)).astype(BF16)
                p_st[par, image, head] = chances
                per_head.append(dot(v.T, chances).T.astype(BF16))
            per_image.append(jnp.concatenate(per_head, axis=1))
        heads = jnp.concatenate(per_image, axis=0)
        heads_st[par] = heads
        acc[...] += dot_cols(heads, w_buf[par, :, 3 * part :])

    def up_step(sec, k, par):
        @pl.when(k == 0)
        def _():
            if sec:
                store_middle(sec - 1).wait()
            middle = acc[...]
            middle_st[...] = middle
            unit, _ = unit_rows(middle)
            normed[...] = (unit * vec[sec, 3:4] + vec[sec, 4:5]).astype(BF16)
            acc[...] = middle + vec[sec, 5:6]
            store_middle(sec).start()

        if sec:
            store_active(sec - 1, k).wait()
        hidden = dot(normed[...], w_buf[par]) + up_bias[sec, k]
        active, slope = gelu_parts(hidden)
        active_st[k] = active.astype(BF16)
        slope_st[par] = slope.astype(BF16)
        store_active(sec, k).start()

    def down_step(sec, k, par):
        acc[...] += dot_cols(active_st[k], w_buf[par])

        @pl.when(k == n_tensor - 1)
        def _():
            row_buf[sec] = (acc[...] * live[...]).astype(BF16)
            store_rows(sec).start()
            at.hand_out(row_buf, sec_rows, sec, row_sem)

    def compute(i, k):
        sec, b = i // n_blk, i % n_blk
        par = lax.rem(k, 2)

        @pl.when(k == 0)
        def _():
            for group, ref in (
                (0, out.at[sec, b, pl.ds(0, n_tensor - 1), pl.ds(0, depth), pl.ds(0, half)]),
                (1, out.at[sec, b, :, pl.ds(0, (n_dp - 1) * depth), pl.ds(0, half)]),
            ):
                pltpu.make_async_copy(ref, ref, part_sem.at[i, group]).wait()
            load(i, 0, 0).start()
            if sec and b < 2:
                for back in (n_tensor - 2, n_tensor - 1):
                    for copy in stores(i - n_blk, back, back % 2):
                        copy.wait()

        load(i, k, par).wait()

        @pl.when(k < n_tensor - 1)
        def _():
            load(i, k + 1, 1 - par).start()

        if b < 2:

            @pl.when(k >= 2)
            def _():
                for copy in stores(i, k - 2, par):
                    copy.wait()

        (attn_step, up_step, down_step)[b](sec, k, par)
        for copy in stores(i, k, par):
            copy.start()

    lags = gather_lags(len(slot_sizes(n_dp, n_tensor)))
    base = max(lags) + 1

    def body(it, carry):
        for g, lag in sorted(enumerate(lags), key=lambda item: item[1]):
            i = lax.div(it - lag, n_tensor)

            @pl.when(jnp.logical_and(it - lag == i * n_tensor, jnp.logical_and(it >= lag, i < n_all)))
            def _():
                run_group(i, g)

        small_step(it)
        for i in range(n_all):
            first = base + i * n_tensor

            @pl.when(jnp.logical_and(it >= first, it < first + n_tensor))
            def _():
                compute(i, it - first)

        return carry

    def run_group(i, g):
        groups, slots = steps(i, True)
        for _ in range(sum(slot_sizes(n_dp, n_tensor)[:g])):
            next(slots)
        groups[g]()

    lax.fori_loop(0, base + n_all * n_tensor, body, 0)

    def finish(i, carry):
        groups, _ = steps(i, False)
        for g in groups:
            g()
        return carry

    lax.fori_loop(0, n_all, finish, 0)
    for b in range(n_blk):
        share(b).wait_send()
    last = n_section - 1
    for b in range(2):
        for back in (n_tensor - 2, n_tensor - 1):
            for copy in stores(last * n_blk + b, back, back % 2):
                copy.wait()
    for k in range(n_tensor):
        store_active(last, k).wait()
    store_middle(last).wait()
    for sec in range(n_section):
        store_rows(sec).wait()
    at.handed_out(row_buf, sec_rows, row_sem)


def gather_lags(n_groups):
    return GLAGS


def gather_and_forward(shard, rows, live, given, n_section, n_dp, n_tensor):
    n_blk, depth, span = shard.shape
    n_rows, width = rows.shape
    images = n_rows // ROWS
    part = width // n_tensor
    n_heads = part // DH
    n_all = n_section * n_blk
    n_hops = n_dp.bit_length() - 1
    n_sends = sum(slot_sizes(n_dp, n_tensor))
    n_small = n_hops + n_tensor
    shape = jax.ShapeDtypeStruct
    hbm = pl.BlockSpec(memory_space=pl.ANY)
    vmem = pl.BlockSpec(memory_space=pltpu.VMEM)
    dma = pltpu.SemaphoreType.DMA
    return pl.pallas_call(
        functools.partial(forward_kernel, n_dp, n_tensor, images),
        out_shape=[
            shape((n_section, n_blk, n_tensor, width, span), BF16),
            shape((n_section, n_rows, width), BF16),
            shape((n_section, n_rows, width), BF16),
            shape((n_section, n_tensor, n_rows, 3 * part), BF16),
            shape((n_section, n_tensor, images, n_heads, ROWS, ROWS), BF16),
            shape((n_section, n_tensor, n_rows, part), BF16),
            shape((n_section, n_rows, width), F32),
            shape((n_section, n_tensor, n_rows, span), BF16),
            shape((n_section, n_tensor, n_rows, span), BF16),
            shape((n_section, 6, width), F32),
        ],
        in_specs=[hbm] + [vmem] * (2 + len(given)),
        out_specs=[hbm] * 9 + [vmem],
        scratch_shapes=[
            pltpu.VMEM((2, width, span), BF16),
            pltpu.VMEM((2, n_rows, 3 * part), BF16),
            pltpu.VMEM((2, images, n_heads, ROWS, ROWS), BF16),
            pltpu.VMEM((2, n_rows, part), BF16),
            pltpu.VMEM((n_tensor, n_rows, span), BF16),
            pltpu.VMEM((2, n_rows, span), BF16),
            pltpu.VMEM((n_rows, width), F32),
            pltpu.VMEM((n_rows, width), BF16),
            pltpu.VMEM((n_rows, width), F32),
            pltpu.VMEM((n_section, n_rows, width), BF16),
            pltpu.VMEM((n_section, n_tensor, 1, 3 * part), F32),
            pltpu.VMEM((n_section, n_tensor, 1, span), F32),
            pltpu.VMEM((n_small, 6, width), F32),
            pltpu.VMEM((n_small, n_tensor, 1, 3 * part), F32),
            pltpu.VMEM((n_small, n_tensor, 1, span), F32),
            dma((3, n_blk)),
            dma((n_all, n_dp * n_tensor)),
            dma((n_all, n_sends)),
            dma((n_all, 2)),
            dma((2,)),
            dma((2, 4)),
            dma((n_tensor,)),
            dma((1 + n_section,)),
            dma((3,)),
            dma((2, n_small, 3)),
        ],
        compiler_params=pltpu.CompilerParams(
            collective_id=0, has_side_effects=True, vmem_limit_bytes=56 * 1024 * 1024
        ),
    )(shard, rows, live, *given)


class Slots:
    def __init__(self, n_dp, n_tensor):
        self.n_tensor = n_tensor
        bits = [b for b in range(n_dp.bit_length()) if (1 << b) < n_dp]
        mid = n_tensor // 2
        count = len(bits) * n_tensor
        self.line = count
        count += n_tensor + 1
        self.hops = {}
        self.cross = {}
        for e in range(1, n_dp):
            if bin(e).count("1") >= 2:
                self.cross[e] = count
                count += n_tensor
            for j in range(mid):
                for b in bits:
                    if not e >> b & 1:
                        chosen = [c for c in bits if (e | 1 << b) >> c & 1]
                        if chosen[j % len(chosen)] == b:
                            self.hops[e, j, b] = count
                            count += 1
        self.count = count


def reduce_lags(n_groups):
    return [0, 0] + [2 + 3 * min(g, 2) + 2 * max(g - 2, 0) for g in range(n_groups - 2)]


def backward_kernel(
    n_dp, n_tensor, images, weights, cotangent, live, vec, *refs
):
    first_rows, row_out, *saved = refs[:8]
    (
        out, sec_grads, d_vec, d_qkv_bias, d_up_bias,
        own, came, final, vec_in, qkv_bias_in, up_bias_in, ring, stage, w_buf, hidden_buf, qkv_buf, p_buf, heads_buf, rows_buf, middle_buf,
        grad_out, grad_low, left_t, right_t, acc, grad_mid,
        load_sem, stage_sem, credit, recv_sem, send_sem, out_sem, small_sem, row_sem,
    ) = refs[8:]
    at = Place(n_dp, n_tensor)
    slots = Slots(n_dp, n_tensor)
    n_section, n_blk = weights.shape[:2]
    n_all = n_section * n_blk
    depth, half = final.shape[1:]
    part = vec.shape[2] // n_tensor
    n_heads = part // DH
    lanes = pl.ds(pl.multiple_of(at.s * half, 128), half)
    sizes = send_sizes(n_dp, n_tensor)
    at.meet()

    def place(i):
        return n_section - 1 - lax.div(i, n_blk), n_blk - 1 - lax.rem(i, n_blk)

    def steps(i, start):
        counter = iter(range(10_000))

        def rows(e):
            return pl.multiple_of(at.away(e) * depth, 16)

        def piece(e, tt):
            return own.at[i, tt, pl.ds(rows(e), depth), :]

        def maybe(cond, action):
            if cond is None:
                action()
            else:
                pl.when(cond)(action)

        def remote(e, tt, device, slot):
            k = next(counter)
            return pltpu.make_async_remote_copy(
                src_ref=piece(e, tt),
                dst_ref=came.at[i, slot],
                send_sem=send_sem.at[i, k],
                recv_sem=recv_sem.at[i, slot],
                device_id=device,
                device_id_type=MESH_ID,
            )

        def send(e, tt, device, slot, cond=None):
            copy = remote(e, tt, device, slot)
            maybe(cond, copy.start if start else copy.wait_send)

        def arrive(slot, cond=None):
            if start:
                copy = pltpu.make_async_copy(came.at[i, slot], came.at[i, slot], recv_sem.at[i, slot])
                maybe(cond, copy.wait)

        def total(e, tt, arrived, target=None):
            if not start or (target is None and not arrived):
                return
            base = rows(e)

            def chunk(c, carry):
                here = pl.ds(pl.multiple_of(base + c * CHUNK_ROWS, 16), CHUNK_ROWS)
                local = pl.ds(pl.multiple_of(c * CHUNK_ROWS, 16), CHUNK_ROWS)
                acc = own[i, tt, here, :].astype(jnp.float32)
                for slot in arrived:
                    acc = acc + came[i, slot, local, :].astype(jnp.float32)
                if target is None:
                    own[i, tt, here, :] = acc.astype(own.dtype)
                else:
                    target[i, local, :] = acc
                return carry

            lax.fori_loop(0, depth // CHUNK_ROWS, chunk, 0)

        def more(e, tt, slot, target=None):
            base = rows(e)

            def chunk(c, carry):
                here = pl.ds(pl.multiple_of(base + c * CHUNK_ROWS, 16), CHUNK_ROWS)
                local = pl.ds(pl.multiple_of(c * CHUNK_ROWS, 16), CHUNK_ROWS)
                acc = came[i, slot, local, :].astype(jnp.float32)
                if target is None:
                    own[i, tt, here, :] = (own[i, tt, here, :].astype(jnp.float32) + acc).astype(own.dtype)
                else:
                    target[i, local, :] = target[i, local, :] + acc
                return carry

            lax.fori_loop(0, depth // CHUNK_ROWS, chunk, 0)

        def also(e, tt, slot, cond, target=None):
            if start:

                def add():
                    arrive(slot)
                    more(e, tt, slot, target)

                pl.when(cond)(add)

        def line_slot(tt, from_next):
            return slots.line + tt + (0 if from_next else 1)

        def crossing():
            for e in range(1, n_dp):
                if bin(e).count("1") >= 2:
                    for j in range(at.mid):
                        tt = at.other_side(j)
                        slot = slots.cross[e] + tt
                        total(e, tt, [])
                        is_upper = at.t >= at.mid
                        also(e, tt, slot, jnp.logical_and(is_upper, at.has_next))
                        also(e, tt, slot, jnp.logical_and(jnp.logical_not(is_upper), at.has_prev))
                        send(e, tt, at.along(-1), slot, is_upper)
                        send(e, tt, at.along(1), slot, jnp.logical_not(is_upper))

        def leaves():
            for j in range(at.mid):
                for e in at.by_weight(1):
                    tt = at.other_side(j)
                    b = at.last_bit(e, j)
                    total(e, tt, [])
                    send(e, tt, at.hop(b), b * n_tensor + tt)

        def plane(weight):
            for e in at.by_weight(weight):
                for j in range(at.mid):
                    tt = at.own_side(j)
                    b = at.last_bit(e, j)
                    arrived = [slots.hops[e, j, c] for c in at.bits if (e, j, c) in slots.hops]
                    for slot in arrived:
                        arrive(slot)
                    total(e, tt, arrived)
                    if weight >= 2:
                        slot = slots.cross[e] + tt
                        also(e, tt, slot, at.t == at.mid - 1)
                        also(e, tt, slot, at.t == at.mid)
                    rest = e & ~(1 << b)
                    there = b * n_tensor + tt if rest == 0 else slots.hops[rest, j, b]
                    send(e, tt, at.hop(b), there)

        def column(k):
            low, high = at.t >= k, at.t + k < n_tensor
            for tt, cond, step, chain, from_next in (
                (at.t - k, low, -1, jnp.logical_and(low, at.has_next), True),
                (at.t + k, high, 1, jnp.logical_and(high, at.has_prev), False),
            ):
                arrived = [b * n_tensor + tt for b in at.bits]

                def sums(tt=tt, arrived=arrived):
                    for slot in arrived:
                        arrive(slot)
                    total(0, tt, arrived)

                if start:
                    pl.when(cond)(sums)
                slot = line_slot(tt, from_next)
                also(0, tt, slot, chain)
                send(0, tt, at.along(step), slot, cond)

        def last():
            arrived = [b * n_tensor + at.t for b in at.bits]
            for slot in arrived:
                arrive(slot)
            total(0, at.t, arrived, final)
            also(0, at.t, line_slot(at.t, True), at.has_next, final)
            also(0, at.t, line_slot(at.t, False), at.has_prev, final)
            sec, b = place(i)
            stay = pltpu.make_async_copy(final.at[i], out.at[b, :, lanes], out_sem.at[0, i])
            go = pltpu.make_async_remote_copy(
                src_ref=final.at[i],
                dst_ref=out.at[b, :, lanes],
                send_sem=out_sem.at[1, i],
                recv_sem=out_sem.at[2, i],
                device_id=at.sibling(),
                device_id_type=MESH_ID,
            )

            @pl.when(sec == at.s)
            def _():
                if start:
                    stay.start()
                else:
                    stay.wait()

            @pl.when(sec != at.s)
            def _():
                if start:
                    go.start()
                else:
                    go.wait_send()

        groups = [crossing, leaves]
        groups += [functools.partial(plane, w) for w in range(len(at.bits), 0, -1)]
        groups += [functools.partial(column, k) for k in range(n_tensor - 1, 0, -1)] + [last]
        return groups, counter

    lags = reduce_lags(len(sizes))

    def run_group(i, g):
        groups, counter = steps(i, True)
        for _ in range(sum(sizes[:g])):
            next(counter)
        groups[g]()

    phases = [(kind, sec) for sec in range(n_section - 1, -1, -1) for kind in ("ffn", "attn")]

    def loads(phase, k, par):
        kind, sec = phases[phase]
        rows = first_rows if sec == 0 else row_out.at[sec - 1]
        qkv, p, heads, middle, active, slope = (ref.at[sec] for ref in saved)
        if kind == "ffn":
            pairs = [
                (weights.at[sec, 1, k], w_buf.at[par, 0]),
                (weights.at[sec, 2, k], w_buf.at[par, 1]),
                (active.at[k], hidden_buf.at[par, 0]),
                (slope.at[k], hidden_buf.at[par, 1]),
            ]
            once = (middle, middle_buf)
        else:
            pairs = [
                (weights.at[sec, 0, k], w_buf.at[par, 0]),
                (qkv.at[k], qkv_buf.at[par]),
                (p.at[k], p_buf.at[par]),
                (heads.at[k], heads_buf.at[par]),
            ]
            once = (rows, rows_buf)
        copies = [
            pltpu.make_async_copy(src, dst, load_sem.at[par, n]) for n, (src, dst) in enumerate(pairs)
        ]
        return copies, lambda: pltpu.make_async_copy(*once, load_sem.at[0, 4])

    def start_loads(phase, k, par, is_first):
        copies, once = loads(phase, k, par)
        for copy in copies:
            copy.start()
        if is_first:
            once().start()

    def blocks_of(phase):
        kind, sec = phases[phase]
        base = (n_section - 1 - sec) * n_blk
        return [base, base + 1] if kind == "ffn" else [base + 2]

    def shared(par, q):
        return pltpu.make_async_remote_copy(
            src_ref=stage.at[par, q],
            dst_ref=ring.at[par, q],
            send_sem=stage_sem.at[0, par, q],
            recv_sem=stage_sem.at[1, par, q],
            device_id=at.sibling(),
            device_id_type=MESH_ID,
        )

    def before_emit(phase, k, par):
        if phase == 0:

            @pl.when(k >= 2)
            def _():
                for q in range(2):
                    shared(par, q).wait_send()
                pl.semaphore_wait(credit.at[par], 1)

        else:
            same, back = len(blocks_of(phase)), len(blocks_of(phase - 1))
            for q in range(max(same, back)):
                if q < same and q < back:
                    shared(par, q).wait_send()
                else:

                    @pl.when(k >= 2 if q < same else k < 2)
                    def _():
                        shared(par, q).wait_send()

            pl.semaphore_wait(credit.at[par], 1)

    def emit(phase, q, k, par, low, high):
        first = at.s == 0
        own[blocks_of(phase)[q], k] = jnp.where(first, low, high)
        stage[par, q] = jnp.where(first, high, low)

    def consume(phase, k, par, is_last):
        for q, i in enumerate(blocks_of(phase)):
            shared(par, q).wait_recv()

            def chunk(c, carry):
                here = pl.ds(pl.multiple_of(c * 96, 96), 96)
                total = own[i, k, here].astype(F32) + ring[par, q, here].astype(F32)
                own[i, k, here] = total.astype(own.dtype)
                return carry

            lax.fori_loop(0, own.shape[2] // 96, chunk, 0)
        if not is_last:
            pl.semaphore_signal(
                credit.at[par], inc=1, device_id=at.sibling(), device_id_type=MESH_ID
            )

    def column_sum(values):
        return jnp.sum(values, axis=0, keepdims=True)

    def ffn_step(sec, k, par, emits):
        middle = middle_buf
        gain, shift = vec[sec, 3:4], vec[sec, 4:5]

        @pl.when(k == 0)
        def _():
            source = cotangent if sec == n_section - 1 else grad_out.at[sec + 1]
            low = (source[...].astype(F32) * live[...]).astype(BF16)
            grad_low[...] = low
            left_t[...] = low.T
            unit, _ = unit_rows(middle[...])
            right_t[...] = (unit * gain + shift).astype(BF16).T
            acc[...] = jnp.zeros_like(acc)

        d_down = dot(left_t[...], hidden_buf[par, 0]).astype(BF16)
        emits(0, d_down[:, :half], d_down[:, half:])
        grad_hidden = (dot(grad_low[...], w_buf[par, 1]) * hidden_buf[par, 1].astype(F32)).astype(BF16)
        d_up_bias[sec, k] = column_sum(grad_hidden.astype(F32))
        d_up = dot(right_t[...], grad_hidden).astype(BF16)
        emits(1, d_up[:, :half], d_up[:, half:])
        acc[...] += dot_cols(grad_hidden, w_buf[par, 0])

    def attn_step(sec, k, par, emits):
        w_attn = w_buf.at[par, 0]

        @pl.when(k == 0)
        def _():
            unit, scale = unit_rows(middle_buf[...])
            grad_norm = acc[...]
            low = grad_low[...].astype(F32)
            mid = low + unit_rows_back(grad_norm * vec[sec, 3:4], unit, scale)
            grad_mid[...] = mid
            d_vec[sec, 2:3] = column_sum(mid)
            d_vec[sec, 3:4] = column_sum(grad_norm * unit)
            d_vec[sec, 4:5] = column_sum(grad_norm)
            d_vec[sec, 5:6] = column_sum(low)
            mid = mid.astype(BF16)
            grad_low[...] = mid
            left_t[...] = mid.T
            unit, _ = unit_rows(rows_buf[...].astype(F32))
            right_t[...] = (unit * vec[sec, 0:1] + vec[sec, 1:2]).astype(BF16).T
            acc[...] = jnp.zeros_like(acc)

        d_out = dot(left_t[...], heads_buf[par]).astype(BF16)
        grad_heads = dot(grad_low[...], w_attn[:, 3 * part :]).astype(BF16)
        per_image = []
        for image in range(images):
            span = slice(image * ROWS, (image + 1) * ROWS)
            per_head = [[], [], []]
            for head in range(n_heads):
                q, key, v = (
                    qkv_buf[par, span, c * part + head * DH : c * part + (head + 1) * DH]
                    for c in range(3)
                )
                grad_o = grad_heads[span, head * DH : (head + 1) * DH]
                chosen = p_buf[par, image, head]
                chances = chosen.astype(F32)
                grad_chances = dot_cols(v, grad_o)
                along = jnp.sum(chances * grad_chances, axis=0, keepdims=True)
                grad_scores = (chances * (grad_chances - along)).astype(BF16)
                per_head[0].append((dot(key.T, grad_scores).T * DH**-0.5).astype(BF16))
                per_head[1].append((dot(grad_scores, q) * DH**-0.5).astype(BF16))
                per_head[2].append(dot(chosen, grad_o).astype(BF16))
            per_image.append(jnp.concatenate(per_head[0] + per_head[1] + per_head[2], axis=1))
        grad_mixed = jnp.concatenate(per_image, axis=0)
        d_qkv_bias[sec, k] = column_sum(grad_mixed.astype(F32))
        d_qkv = dot(right_t[...], grad_mixed).astype(BF16)
        emits(0, d_qkv[:, :half], jnp.concatenate([d_qkv[:, half:], d_out], axis=1))
        acc[...] += dot_cols(grad_mixed, w_attn[:, : 3 * part])

        @pl.when(k == n_tensor - 1)
        def _():
            unit, scale = unit_rows(rows_buf[...].astype(F32))
            grad_norm = acc[...]
            d_vec[sec, 0:1] = column_sum(grad_norm * unit)
            d_vec[sec, 1:2] = column_sum(grad_norm)
            total = grad_mid[...] + unit_rows_back(grad_norm * vec[sec, 0:1], unit, scale)
            grad_out[sec] = total.astype(BF16)
            at.hand_out(grad_out, sec_grads, sec, row_sem)

    def compute(phase, k):
        kind, sec = phases[phase]
        par = lax.rem(k, 2)
        copies, once = loads(phase, k, par)
        for copy in copies:
            copy.wait()

        @pl.when(k == 0)
        def _():
            once().wait()

        @pl.when(k < n_tensor - 1)
        def _():
            start_loads(phase, k + 1, 1 - par, False)

        if phase + 1 < len(phases):

            @pl.when(k == n_tensor - 1)
            def _():
                start_loads(phase + 1, 0, 0, True)

        before_emit(phase, k, par)

        def emits(q, low, high):
            emit(phase, q, k, par, low, high)

        (ffn_step if kind == "ffn" else attn_step)(sec, k, par, emits)
        for q in range(len(blocks_of(phase))):
            shared(par, q).start()

        @pl.when(k > 0)
        def _():
            consume(phase, k - 1, 1 - par, False)

        if phase:

            @pl.when(k == 0)
            def _():
                consume(phase - 1, n_tensor - 1, 1 - par, False)

    def start_of(i):
        return BLOCK_TICKS * i + PAUSE * (i // n_blk)

    def block_at(tick):
        found, runs = 0, False
        for i in range(n_all):
            here = tick == start_of(i)
            found = jnp.where(here, i, found)
            runs = jnp.logical_or(runs, here)
        return found, runs

    small = [(d_vec, vec_in), (d_qkv_bias, qkv_bias_in), (d_up_bias, up_bias_in)]
    n_hops = len(at.bits)

    def small_copies(stage, device, slot):
        sec = 1 - at.s if stage == 0 else at.s
        return [
            pltpu.make_async_remote_copy(
                src_ref=mine.at[sec],
                dst_ref=came_in.at[slot],
                send_sem=small_sem.at[0, slot, n],
                recv_sem=small_sem.at[1, slot, n],
                device_id=device,
                device_id_type=MESH_ID,
            )
            for n, (mine, came_in) in enumerate(small)
        ]

    def small_send(stage):
        if stage == 0:
            return [small_copies(0, at.sibling(), 0)]
        if stage <= n_hops:
            return [small_copies(stage, at.hop(stage - 1), stage)]
        other = [lax.rem(at.t + k, n_tensor) for k in range(1, n_tensor)]
        return [
            small_copies(stage, (at.s, at.d, tt), n_hops + 1 + k) for k, tt in enumerate(other)
        ]

    def small_take(stage):
        sent = small_send(stage)
        for copies in sent:
            for copy in copies:
                copy.wait()
        first = stage if stage <= n_hops else n_hops + 1
        for mine, came_in in small:
            total = mine[at.s]
            for slot in range(first, first + len(sent)):
                total = total + came_in[slot]
            mine[at.s] = total

    def small_step(tick):
        for stage in range(n_hops + 2):

            @pl.when(tick == SMALL_TICKS * stage)
            def _():
                if stage:
                    small_take(stage - 1)
                for copies in small_send(stage):
                    for copy in copies:
                        copy.start()

        @pl.when(tick == SMALL_TICKS * (n_hops + 2))
        def _():
            small_take(n_hops + 1)

    def prologue(k, carry):
        compute(0, k)
        return carry

    start_loads(0, 0, 0, True)
    lax.fori_loop(0, n_tensor, prologue, 0)

    n_busy = (len(phases) - 1) * n_tensor

    def body(it, carry):
        for phase in range(1, len(phases)):

            @pl.when(lax.div(it, n_tensor) == phase - 1)
            def _():
                compute(phase, lax.rem(it, n_tensor))

        @pl.when(it == n_busy)
        def _():
            consume(len(phases) - 1, n_tensor - 1, (n_tensor - 1) % 2, True)

        for g, lag in sorted(enumerate(lags), key=lambda item: item[1]):
            i, runs = block_at(it - lag)

            @pl.when(runs)
            def _():
                run_group(i, g)

        small_step(it - n_busy)
        return carry

    lax.fori_loop(0, start_of(n_all - 1) + 1 + max(lags), body, 0)

    for par in range(2):
        for q in range(len(blocks_of(len(phases) - 1))):
            shared(par, q).wait_send()
    pl.semaphore_wait(credit.at[0], 1)

    def finish(i, carry):
        groups, _ = steps(i, False)
        for g in groups:
            g()
        sec, b = place(i)

        @pl.when(sec == at.s)
        def _():
            pltpu.make_async_copy(final.at[i], final.at[i], out_sem.at[2, i]).wait()

        return carry

    lax.fori_loop(0, n_all, finish, 0)
    at.handed_out(grad_out, sec_grads, row_sem)


def send_sizes(n_dp, n_tensor):
    bits = n_dp.bit_length() - 1
    mid = n_tensor // 2
    weights = [bin(e).count("1") for e in range(n_dp)]
    sizes = [2 * mid * sum(w >= 2 for w in weights), mid * bits]
    sizes += [mid * sum(w == k for w in weights) for k in range(bits, 0, -1)]
    return sizes + [2] * (n_tensor - 1) + [0]


def backward_and_reduce(weights, cotangent, live, vec, saved, n_dp):
    n_section, n_blk, n_tensor, width, span = weights.shape
    n_rows = cotangent.shape[0]
    images = n_rows // ROWS
    part = width // n_tensor
    n_all = n_section * n_blk
    depth, half = width // n_dp, span // 2
    slots = Slots(n_dp, n_tensor)
    n_sends = sum(send_sizes(n_dp, n_tensor))
    n_small = n_dp.bit_length() + n_tensor - 1
    shape = jax.ShapeDtypeStruct
    hbm = pl.BlockSpec(memory_space=pl.ANY)
    vmem = pl.BlockSpec(memory_space=pltpu.VMEM)
    dma = pltpu.SemaphoreType.DMA
    return pl.pallas_call(
        functools.partial(backward_kernel, n_dp, n_tensor, images),
        out_shape=[
            shape((n_blk, depth, span), F32),
            shape((n_section, n_rows, width), BF16),
            shape((n_section, 6, width), F32),
            shape((n_section, n_tensor, 1, 3 * part), F32),
            shape((n_section, n_tensor, 1, span), F32),
        ],
        in_specs=[hbm] + [vmem] * 3 + [hbm] * len(saved),
        out_specs=[hbm] * 2 + [vmem] * 3,
        scratch_shapes=[
            pltpu.VMEM((n_all, n_tensor, width, half), BF16),
            pltpu.VMEM((n_all, slots.count, depth, half), BF16),
            pltpu.VMEM((n_all, depth, half), F32),
            pltpu.VMEM((n_small, 6, width), F32),
            pltpu.VMEM((n_small, n_tensor, 1, 3 * part), F32),
            pltpu.VMEM((n_small, n_tensor, 1, span), F32),
            pltpu.VMEM((2, 2, width, half), BF16),
            pltpu.VMEM((2, 2, width, half), BF16),
            pltpu.VMEM((2, 2, width, span), BF16),
            pltpu.VMEM((2, 2, n_rows, span), BF16),
            pltpu.VMEM((2, n_rows, 3 * part), BF16),
            pltpu.VMEM((2, images, part // DH, ROWS, ROWS), BF16),
            pltpu.VMEM((2, n_rows, part), BF16),
            pltpu.VMEM((n_rows, width), BF16),
            pltpu.VMEM((n_rows, width), F32),
            pltpu.VMEM((n_section, n_rows, width), BF16),
            pltpu.VMEM((n_rows, width), BF16),
            pltpu.VMEM((width, n_rows), BF16),
            pltpu.VMEM((width, n_rows), BF16),
            pltpu.VMEM((n_rows, width), F32),
            pltpu.VMEM((n_rows, width), F32),
            dma((2, 5)),
            dma((2, 2, 2)),
            pltpu.SemaphoreType.REGULAR((2,)),
            dma((n_all, slots.count)),
            dma((n_all, n_sends)),
            dma((3, n_all)),
            dma((2, n_small, 3)),
            dma((3,)),
        ],
        compiler_params=pltpu.CompilerParams(
            collective_id=1, has_side_effects=True, vmem_limit_bytes=64 * 1024 * 1024 - 256 * 1024
        ),
    )(weights, cotangent, live, vec, *saved)


AXES = ("section", "tensor", "dp")


def shards(
    images,
    cotangent,
    counts,
    ln1_gain,
    ln1_bias,
    q_bias,
    v_bias,
    qkv_weight,
    out_weight,
    out_bias,
    ln2_gain,
    ln2_bias,
    up_weight,
    up_bias,
    down_weight,
    down_bias,
):
    n_section, n_dp, n_tensor = (lax.axis_size(a) for a in ("section", "dp", "tensor"))
    section_idx = lax.axis_index("section")
    micro_count, share_rows, width = images.shape
    own_count = micro_count // n_section
    depth = qkv_weight.shape[1]
    part = qkv_weight.shape[3]

    own = section_idx * own_count

    def own_rows(values):
        mine = lax.dynamic_slice_in_dim(values, own, own_count, 0).reshape(-1, SEQ, values.shape[-1])
        return jnp.pad(mine, ((0, 0), (0, ROWS - SEQ), (0, 0))).reshape(-1, values.shape[-1])

    row_place = lax.axis_index("tensor") * share_rows + jnp.arange(share_rows)
    own_counts = lax.dynamic_slice_in_dim(counts, own, own_count, 0)
    live_rows = (row_place // SEQ < own_counts).astype(jnp.float32)
    live_rows = live_rows.reshape(-1, SEQ)
    live_rows = jnp.pad(live_rows, ((0, 0), (0, ROWS - SEQ))).reshape(-1, 1)

    shard = jnp.stack(
        [
            jnp.concatenate([qkv_weight[0].reshape(depth, -1), out_weight[0].T], axis=1),
            up_weight[0],
            down_weight[0].T,
        ]
    )
    given = [ln1_gain, ln1_bias, out_bias, ln2_gain, ln2_bias, down_bias, q_bias, v_bias, up_bias]
    first_rows = own_rows(images)
    gathered, sec_rows, row_out, *kept, vec = gather_and_forward(
        shard, first_rows, live_rows, given, n_section, n_dp, n_tensor
    )
    weight_sum, sec_grads, d_vec, d_qkv_bias, d_up_bias = backward_and_reduce(
        gathered, own_rows(cotangent), live_rows, vec, [first_rows, row_out, *kept], n_dp
    )

    def placed_rows(values):
        values = values.reshape(-1, ROWS, width)[:, :SEQ]
        return values.reshape(1, micro_count, share_rows, width)

    section_out = placed_rows(sec_rows)
    input_grad = placed_rows(sec_grads)

    dp_idx, tensor_idx = lax.axis_index("dp"), lax.axis_index("tensor")

    def own_heads(sums, like):
        _, heads, lanes = like.shape
        sums = sums.reshape(-1, DH)
        return lax.dynamic_slice(sums, (0, dp_idx * lanes), (heads, lanes))[None]

    d_vec, d_qkv_bias, d_up_bias = (
        lax.dynamic_index_in_dim(v, section_idx, 0, keepdims=False)
        for v in (d_vec, d_qkv_bias, d_up_bias)
    )
    q_row, _, v_row = jnp.split(
        lax.dynamic_index_in_dim(d_qkv_bias, tensor_idx, 0, keepdims=False).reshape(-1), 3
    )
    up_row = lax.dynamic_index_in_dim(d_up_bias, tensor_idx, 0, keepdims=False)
    q_sum, v_sum, up_sum = own_heads(q_row, q_bias), own_heads(v_row, v_bias), own_heads(up_row, up_bias)
    block = width // (n_dp * n_tensor)
    vec = lax.dynamic_slice_in_dim(d_vec, (dp_idx * n_tensor + tensor_idx) * block, block, 1)[None]

    return (
        section_out,
        input_grad,
        weight_sum[0, :, : 3 * part].reshape(qkv_weight.shape),
        weight_sum[0, :, 3 * part :].T[None],
        weight_sum[1][None],
        weight_sum[2].T[None],
        q_sum,
        v_sum,
        up_sum,
        vec,
    )


def solution(mesh):
    placed = (
        P(None, ("dp", "tensor"), None),
        P(None, ("dp", "tensor"), None),
        P(None, "dp"),
        P("section", "dp"),
        P("section", "dp"),
        P("section", "tensor", "dp"),
        P("section", "tensor", "dp"),
        P("section", "dp", None, "tensor"),
        P("section", "tensor", "dp"),
        P("section", "dp"),
        P("section", "dp"),
        P("section", "dp"),
        P("section", "dp", "tensor"),
        P("section", "tensor", "dp"),
        P("section", "tensor", "dp"),
        P("section", "dp"),
    )
    return jax.shard_map(
        shards,
        mesh=mesh,
        in_specs=placed,
        out_specs=(
            P("section", None, ("dp", "tensor"), None),
            P("section", None, ("dp", "tensor"), None),
            P("section", "dp", None, "tensor"),
            P("section", "tensor", "dp"),
            P("section", "dp", "tensor"),
            P("section", "tensor", "dp"),
            P("section", "tensor", "dp"),
            P("section", "tensor", "dp"),
            P("section", "tensor", "dp"),
            P("section", None, ("dp", "tensor")),
        ),
        check_vma=False,
    )
```

```python
import functools
import jax
import jax.numpy as jnp
from jax import lax
from jax.experimental import pallas as pl
from jax.experimental.pallas import tpu as pltpu
from jax.sharding import PartitionSpec as P

CHUNK_ROWS = 48
SMALL_TICKS = 2
MESH_ID = pl.DeviceIdType.MESH


def sub_blocks(depth):
    return 1


def slot_sizes(n_dp, n_tensor):
    bits = [b for b in range(n_dp.bit_length()) if (1 << b) < n_dp]
    mid = n_tensor // 2
    weights = [bin(e).count("1") for e in range(n_dp)]

    def plane(weight):
        total = 0
        for j in range(mid):
            for e in range(n_dp):
                if weights[e] == weight:
                    for b in bits:
                        if not e >> b & 1:
                            chosen = [c for c in bits if (e | 1 << b) >> c & 1]
                            total += chosen[j % len(chosen)] == b
                    total += 2 * (weight >= 2) + 1
        return total

    first = [2 + len(bits)]
    columns = [2 * (2 + len(bits))] * (n_tensor - 1)
    planes = [plane(w) for w in range(1, len(bits) + 1)]
    crossed = [3 * mid * sum(w >= 2 for w in weights)]
    rest = [mid * sum(w == 1 for w in weights)]
    return first + [columns[0], planes[0], columns[1]] + planes[1:] + columns[2:] + crossed + rest


class Place:
    def __init__(self, n_dp, n_tensor):
        self.n_dp, self.n_tensor = n_dp, n_tensor
        self.mid = n_tensor // 2
        self.bits = [b for b in range(n_dp.bit_length()) if (1 << b) < n_dp]
        self.s = lax.axis_index("section")
        self.d = lax.axis_index("dp")
        self.t = lax.axis_index("tensor")
        self.upper = lax.div(self.t, self.mid)
        self.has_next = self.t < n_tensor - 1
        self.has_prev = self.t > 0

    def away(self, e):
        other = self.d
        for b in self.bits:
            if e >> b & 1:
                other = other + (1 << b) * (1 - 2 * lax.rem(lax.div(self.d, 1 << b), 2))
        return other

    def last_bit(self, e, j):
        chosen = [b for b in self.bits if e >> b & 1]
        return chosen[j % len(chosen)]

    def own_side(self, j):
        return self.upper * self.mid + j

    def other_side(self, j):
        return (1 - self.upper) * self.mid + j

    def sibling(self):
        return (1 - self.s, self.d, self.t)

    def along(self, step):
        return (self.s, self.d, self.t + step)

    def hop(self, b):
        return (self.s, self.away(1 << b), self.t)

    def meet(self):
        barrier = pltpu.get_barrier_semaphore()
        line = [(self.s, self.d, lax.rem(self.t + k, self.n_tensor)) for k in range(1, self.n_tensor)]
        others = [self.sibling()] + [self.hop(b) for b in self.bits] + line
        for device in others:
            pl.semaphore_signal(barrier, inc=1, device_id=device, device_id_type=MESH_ID)
        pl.semaphore_wait(barrier, len(others))

    def rows_away(self, source, target, sec, sems):
        return pltpu.make_async_remote_copy(
            src_ref=source.at[sec],
            dst_ref=target.at[self.s],
            send_sem=sems.at[1],
            recv_sem=sems.at[2],
            device_id=self.sibling(),
            device_id_type=MESH_ID,
        )

    def hand_out(self, source, target, sec, sems):
        @pl.when(sec == self.s)
        def _():
            pltpu.make_async_copy(source.at[sec], target.at[self.s], sems.at[0]).start()

        @pl.when(sec != self.s)
        def _():
            self.rows_away(source, target, sec, sems).start()

    def handed_out(self, source, target, sems):
        pltpu.make_async_copy(source.at[0], target.at[self.s], sems.at[0]).wait()
        self.rows_away(source, target, 0, sems).wait()

    def by_weight(self, weight):
        return [e for e in range(self.n_dp) if bin(e).count("1") == weight]


DH = 64
SEQ = 197
EPS = 1e-06
F32 = jnp.float32
BF16 = jnp.bfloat16
ROWS = 208


def dot(left, right):
    return jnp.dot(left, right, preferred_element_type=F32)


def dot_cols(left, right):
    return lax.dot_general(left, right, (((1,), (1,)), ((), ())), preferred_element_type=F32)


def unit_rows(values):
    average = jnp.mean(values, axis=-1, keepdims=True)
    centered = values - average
    scale = lax.rsqrt(jnp.mean(centered * centered, axis=-1, keepdims=True) + EPS)
    return centered * scale, scale


def unit_rows_back(grad_unit, unit, scale):
    along = jnp.mean(grad_unit * unit, axis=-1, keepdims=True)
    return scale * (grad_unit - jnp.mean(grad_unit, axis=-1, keepdims=True) - unit * along)


def gelu_parts(hidden):
    below = 0.5 * (1.0 + lax.erf(hidden * (0.5**0.5)))
    density = jnp.exp(-0.5 * hidden * hidden) * 0.3989422804014327
    return hidden * below, below + hidden * density


def forward_kernel(n_dp, n_tensor, images, *refs):
    (
        shard, rows, live, *given,
        out, row_out, qkv_out, p_out, heads_out, middle_out, active_out, slope_out, vec,
        w_buf, qkv_st, p_st, heads_st, active_st, slope_st, middle_st, normed, acc, row_buf,
        qkv_bias, up_bias, vec_in, qkv_bias_in, up_bias_in,
        own_sem, recv_sem, send_sem, part_sem, load_sem, store_sem, active_sem, once_sem, small_sem,
    ) = refs
    at = Place(n_dp, n_tensor)
    n_section = out.shape[0]
    n_blk, depth, span = shard.shape
    half = span // 2
    n_all = n_section * n_blk
    n_sub = sub_blocks(depth)
    sub = depth // n_sub
    n_pieces = n_all * n_sub
    part = vec.shape[2] // n_tensor
    n_heads = part // DH

    def spread(value):
        return jnp.concatenate([jnp.where(at.d == k, value, 0.0) for k in range(n_dp)], axis=1)

    def spread_heads(ref):
        values = ref[0].astype(F32)
        return jnp.concatenate([spread(values[h : h + 1]) for h in range(values.shape[0])], axis=1)

    vec[...] = jnp.zeros_like(vec)
    qkv_bias[...] = jnp.zeros_like(qkv_bias)
    up_bias[...] = jnp.zeros_like(up_bias)
    placed = jnp.concatenate([spread(ref[...].astype(F32)) for ref in given[:6]], axis=0)
    vec[at.s] = jnp.where(at.t == 0, placed, 0.0)
    q_row, v_row = spread_heads(given[6]), spread_heads(given[7])
    qkv_bias[at.s, at.t] = jnp.concatenate([q_row, jnp.zeros_like(q_row), v_row], axis=1)
    up_bias[at.s, at.t] = spread_heads(given[8])
    at.meet()

    def whole(sec, b):
        return out.at[sec, b, at.t, rows_of(0), :]

    def rows_of(e):
        return pl.ds(pl.multiple_of(at.away(e) * depth, 16), depth)

    lanes = pl.ds(pl.multiple_of(at.s * half, 128), half)

    def piece(i, e, tt):
        block = lax.div(i, n_sub)
        start = at.away(e) * depth + lax.rem(i, n_sub) * sub
        rows_here = pl.ds(pl.multiple_of(start, 16), sub)
        return out.at[lax.div(block, n_blk), lax.rem(block, n_blk), tt, rows_here, lanes]

    def share(b):
        return pltpu.make_async_remote_copy(
            src_ref=shard.at[b],
            dst_ref=whole(at.s, b),
            send_sem=own_sem.at[1, b],
            recv_sem=own_sem.at[2, b],
            device_id=at.sibling(),
            device_id_type=MESH_ID,
        )

    for b in range(n_blk):
        pltpu.make_async_copy(shard.at[b], whole(at.s, b), own_sem.at[0, b]).start()
        share(b).start()

    def push(i, e, tt, device, e_there, slot, start):
        copy = pltpu.make_async_remote_copy(
            src_ref=piece(i, e, tt),
            dst_ref=piece(i, e, tt),
            send_sem=send_sem.at[i, slot],
            recv_sem=recv_sem.at[i, e_there * n_tensor + tt],
            device_id=device,
            device_id_type=MESH_ID,
        )
        if start:
            copy.start()
        else:
            copy.wait_send()

    def push_sib(i, e, tt, slot, start):
        copy = pltpu.make_async_remote_copy(
            src_ref=piece(i, e, tt),
            dst_ref=piece(i, e, tt),
            send_sem=send_sem.at[i, slot],
            recv_sem=part_sem.at[i, 0 if e == 0 else 1],
            device_id=at.sibling(),
            device_id_type=MESH_ID,
        )
        if start:
            copy.start()
        else:
            copy.wait_send()

    def await_piece(i, e, tt):
        pltpu.make_async_remote_copy(
            src_ref=piece(i, e, tt),
            dst_ref=piece(i, e, tt),
            send_sem=send_sem.at[i, 0],
            recv_sem=recv_sem.at[i, e * n_tensor + tt],
            device_id=at.sibling(),
            device_id_type=MESH_ID,
        ).wait_recv()

    def steps(i, start):
        slots = iter(range(10_000))

        def maybe(cond, action):
            if cond is None:
                action()
            else:
                pl.when(cond)(action)

        def ready(e, tt, cond=None):
            if start:
                maybe(cond, lambda: await_piece(i, e, tt))

        def go(e, tt, device, e_there, cond=None):
            slot = next(slots)
            maybe(cond, lambda: push(i, e, tt, device, e_there, slot, start))

        def go_sib(e, tt, cond=None):
            slot = next(slots)
            maybe(cond, lambda: push_sib(i, e, tt, slot, start))

        def first():
            block = lax.div(i, n_sub)
            sec, b = lax.div(block, n_blk), lax.rem(block, n_blk)
            is_first = lax.rem(i, n_sub) == 0
            if start:

                @pl.when(jnp.logical_and(sec == at.s, is_first))
                def _():
                    pltpu.make_async_copy(shard.at[b], whole(at.s, b), own_sem.at[0, b]).wait()

                @pl.when(jnp.logical_and(sec != at.s, is_first))
                def _():
                    pltpu.make_async_remote_copy(
                        src_ref=shard.at[b],
                        dst_ref=whole(1 - at.s, b),
                        send_sem=own_sem.at[1, b],
                        recv_sem=own_sem.at[2, b],
                        device_id=at.sibling(),
                        device_id_type=MESH_ID,
                    ).wait_recv()

            go(0, at.t, at.along(1), 0, at.has_next)
            go(0, at.t, at.along(-1), 0, at.has_prev)
            for b in at.bits:
                go(0, at.t, at.hop(b), 1 << b)

        def column(k):
            low, high = at.t >= k, at.t + k < n_tensor
            for tt, cond, dev, more in (
                (at.t - k, low, at.along(1), jnp.logical_and(low, at.has_next)),
                (at.t + k, high, at.along(-1), jnp.logical_and(high, at.has_prev)),
            ):
                ready(0, tt, cond)
                go(0, tt, dev, 0, more)
                for b in at.bits:
                    go(0, tt, at.hop(b), 1 << b, cond)
                go_sib(0, tt, cond)

        def plane(weight):
            for j in range(at.mid):
                for e in at.by_weight(weight):
                    tt = at.own_side(j)
                    ready(e, tt)
                    for b in at.bits:
                        if not e >> b & 1 and at.last_bit(e | 1 << b, j) == b:
                            go(e, tt, at.hop(b), e | 1 << b)
                    if weight >= 2:
                        go(e, tt, at.along(1), e, at.t == at.mid - 1)
                        go(e, tt, at.along(-1), e, at.t == at.mid)
                    go_sib(e, tt)

        def crossed():
            for weight in range(2, len(at.bits) + 1):
                for e in at.by_weight(weight):
                    for j in range(at.mid):
                        tt = at.other_side(j)
                        ready(e, tt)
                        up = jnp.logical_and(at.t >= at.mid, at.has_next)
                        down = jnp.logical_and(at.t < at.mid, at.has_prev)
                        go(e, tt, at.along(1), e, up)
                        go(e, tt, at.along(-1), e, down)
                        go_sib(e, tt)

        def rest():
            for e in at.by_weight(1):
                for j in range(at.mid):
                    tt = at.other_side(j)
                    ready(e, tt)
                    go_sib(e, tt)

        groups = [first]
        for k in range(1, n_tensor):
            groups.append(functools.partial(column, k))
        planes = [functools.partial(plane, w) for w in range(1, len(at.bits) + 1)]
        merged = [groups[0]]
        order = [groups[1], planes[0], groups[2]] + planes[1:] + groups[3:] + [crossed, rest]
        return merged + order, slots


    small = [(vec, vec_in), (qkv_bias, qkv_bias_in), (up_bias, up_bias_in)]
    n_hops = len(at.bits)

    def small_copies(device, slot, to_place):
        return [
            pltpu.make_async_remote_copy(
                src_ref=mine.at[at.s],
                dst_ref=mine.at[at.s] if to_place else came_in.at[slot],
                send_sem=small_sem.at[0, slot, n],
                recv_sem=small_sem.at[1, slot, n],
                device_id=device,
                device_id_type=MESH_ID,
            )
            for n, (mine, came_in) in enumerate(small)
        ]

    def small_send(stage):
        if stage < n_hops:
            return [small_copies(at.hop(stage), stage, False)]
        if stage == n_hops:
            other = [lax.rem(at.t + k, n_tensor) for k in range(1, n_tensor)]
            return [small_copies((at.s, at.d, tt), n_hops + k, False) for k, tt in enumerate(other)]
        return [small_copies(at.sibling(), n_hops + n_tensor - 1, True)]

    def small_take(stage):
        sent = small_send(stage)
        for copies in sent:
            for copy in copies:
                copy.wait()
        if stage <= n_hops:
            for mine, came_in in small:
                total = mine[at.s]
                for slot in range(stage, stage + len(sent)):
                    total = total + came_in[slot]
                mine[at.s] = total

    def small_step(tick):
        for stage in range(n_hops + 3):

            @pl.when(tick == 1 + 2 * stage)
            def _():
                if stage:
                    small_take(stage - 1)
                if stage < n_hops + 2:
                    for copies in small_send(stage):
                        for copy in copies:
                            copy.start()

    lags = gather_lags(len(slot_sizes(n_dp, n_tensor)))
    pace = n_tensor // n_sub
    base = max(lags) + (n_sub - 1) * pace + 1
    n_phases = n_all - 1
    settle = max(lags) + n_tensor
    n_ticks = base + n_phases * n_tensor

    def finish(i):
        groups, _ = steps(i, False)
        for g in groups:
            g()

    def load(i, k, par):
        return pltpu.make_async_copy(out.at[i // n_blk, i % n_blk, k], w_buf.at[par], load_sem.at[par])

    def stores(i, k, par):
        sec, b = i // n_blk, i % n_blk
        if b == 0:
            pairs = [
                (qkv_st.at[par], qkv_out.at[sec, k], store_sem.at[par, 0]),
                (p_st.at[par], p_out.at[sec, k], store_sem.at[par, 1]),
                (heads_st.at[par], heads_out.at[sec, k], store_sem.at[par, 2]),
            ]
        elif b == 1:
            pairs = [(slope_st.at[par], slope_out.at[sec, k], store_sem.at[par, 3])]
        else:
            pairs = []
        return [pltpu.make_async_copy(*pair) for pair in pairs]

    def store_active(sec, k):
        return pltpu.make_async_copy(active_st.at[k], active_out.at[sec, k], active_sem.at[k])

    def store_middle(sec):
        return pltpu.make_async_copy(middle_st, middle_out.at[sec], once_sem.at[0])

    def store_rows(sec):
        return pltpu.make_async_copy(row_buf.at[sec], row_out.at[sec], once_sem.at[1 + sec])

    def attn_step(sec, k, par):
        @pl.when(k == 0)
        def _():
            values = (rows if sec == 0 else row_buf.at[sec - 1])[...].astype(F32)
            unit, _ = unit_rows(values)
            normed[...] = (unit * vec[sec, 0:1] + vec[sec, 1:2]).astype(BF16)
            acc[...] = values + vec[sec, 2:3]

        mixed = (dot(normed[...], w_buf[par, :, : 3 * part]) + qkv_bias[sec, k]).astype(BF16)
        qkv_st[par] = mixed
        keep = lax.broadcasted_iota(jnp.int32, (ROWS, ROWS), 0) < SEQ
        per_image = []
        for image in range(images):
            here = mixed[image * ROWS : (image + 1) * ROWS]
            per_head = []
            for head in range(n_heads):
                q, key, v = (
                    here[:, c * part + head * DH : c * part + (head + 1) * DH] for c in range(3)
                )
                scores = jnp.where(keep, dot_cols(key, q) * DH**-0.5, -1e30)
                scores = jnp.exp(scores - jnp.max(scores, axis=0, keepdims=True))
                total = jnp.sum(scores, axis=0, keepdims=True)
                chances = (scores * (1.0 / total)).astype(BF16)
                p_st[par, image, head] = chances
                per_head.append(dot(v.T, chances).T.astype(BF16))
            per_image.append(jnp.concatenate(per_head, axis=1))
        heads = jnp.concatenate(per_image, axis=0)
        heads_st[par] = heads
        acc[...] += dot_cols(heads, w_buf[par, :, 3 * part :])

    def up_step(sec, k, par):
        @pl.when(k == 0)
        def _():
            if sec:
                store_middle(sec - 1).wait()
            middle = acc[...]
            middle_st[...] = middle
            unit, _ = unit_rows(middle)
            normed[...] = (unit * vec[sec, 3:4] + vec[sec, 4:5]).astype(BF16)
            acc[...] = middle + vec[sec, 5:6]
            store_middle(sec).start()

        if sec:
            store_active(sec - 1, k).wait()
        hidden = dot(normed[...], w_buf[par]) + up_bias[sec, k]
        active, slope = gelu_parts(hidden)
        active_st[k] = active.astype(BF16)
        slope_st[par] = slope.astype(BF16)
        store_active(sec, k).start()

    def down_step(sec, k, par):
        acc[...] += dot_cols(active_st[k], w_buf[par])

        @pl.when(k == n_tensor - 1)
        def _():
            row_buf[sec] = (acc[...] * live[...]).astype(BF16)
            store_rows(sec).start()

    def await_block(i):
        sec, b = i // n_blk, i % n_blk
        for each in range(i * n_sub, (i + 1) * n_sub):
            for group, ref in (
                (0, out.at[sec, b, pl.ds(0, n_tensor - 1), pl.ds(0, sub), pl.ds(0, half)]),
                (1, out.at[sec, b, :, pl.ds(0, (n_dp - 1) * sub), pl.ds(0, half)]),
            ):
                pltpu.make_async_copy(ref, ref, part_sem.at[each, group]).wait()

    def compute(i, k):
        sec, b = i // n_blk, i % n_blk
        par = lax.rem(k, 2)

        if i == 0:

            @pl.when(k == 0)
            def _():
                await_block(0)
                load(0, 0, 0).start()

        if sec and b < 2:

            @pl.when(k == 0)
            def _():
                for back in (n_tensor - 2, n_tensor - 1):
                    for copy in stores(i - n_blk, back, back % 2):
                        copy.wait()

        load(i, k, par).wait()

        @pl.when(k < n_tensor - 1)
        def _():
            load(i, k + 1, 1 - par).start()

        if b < 2:

            @pl.when(k >= 2)
            def _():
                for copy in stores(i, k - 2, par):
                    copy.wait()

        (attn_step, up_step, down_step)[b](sec, k, par)
        for copy in stores(i, k, par):
            copy.start()

        @pl.when(k == n_tensor - 1)
        def _():
            if i + 1 < n_all:
                await_block(i + 1)
            if i + 1 < n_phases:
                load(i + 1, 0, 0).start()

    def body(it, carry):
        for g, lag in sorted(enumerate(lags), key=lambda item: item[1]):
            i = lax.div(it - lag, pace)

            @pl.when(jnp.logical_and(it - lag == i * pace, jnp.logical_and(it >= lag, i < n_pieces)))
            def _():
                run_group(i, g)

        small_step(it)
        i = lax.div(it - settle, pace)

        @pl.when(jnp.logical_and(it - settle == i * pace, jnp.logical_and(it >= settle, i < n_pieces)))
        def _():
            finish(i)

        for i in range(n_phases):
            first = base + i * n_tensor

            @pl.when(jnp.logical_and(it >= first, it < first + n_tensor))
            def _():
                compute(i, it - first)

        return carry

    def run_group(i, g):
        groups, slots = steps(i, True)
        for _ in range(sum(slot_sizes(n_dp, n_tensor)[:g])):
            next(slots)
        groups[g]()

    lax.fori_loop(0, n_ticks, body, 0)
    for i in range(n_pieces):
        if settle + i * pace >= n_ticks:
            finish(i)
    for b in range(n_blk):
        share(b).wait_send()
    last = n_section - 1
    for b in range(2):
        for back in (n_tensor - 2, n_tensor - 1):
            for copy in stores(last * n_blk + b, back, back % 2):
                copy.wait()
    for k in range(n_tensor):
        store_active(last, k).wait()
    store_middle(last).wait()
    for sec in range(last):
        store_rows(sec).wait()


def gather_lags(n_groups):
    known = [0, 3, 6, 7, 10, 11, 14, 17]
    return [known[g] if g < len(known) else known[-1] + 3 * (g - len(known) + 1) for g in range(n_groups)]


def gather_and_forward(shard, rows, live, given, n_section, n_dp, n_tensor):
    n_blk, depth, span = shard.shape
    n_rows, width = rows.shape
    images = n_rows // ROWS
    part = width // n_tensor
    n_heads = part // DH
    n_pieces = n_section * n_blk * sub_blocks(depth)
    n_hops = n_dp.bit_length() - 1
    n_sends = sum(slot_sizes(n_dp, n_tensor))
    n_small = n_hops + n_tensor
    shape = jax.ShapeDtypeStruct
    hbm = pl.BlockSpec(memory_space=pl.ANY)
    vmem = pl.BlockSpec(memory_space=pltpu.VMEM)
    dma = pltpu.SemaphoreType.DMA
    return pl.pallas_call(
        functools.partial(forward_kernel, n_dp, n_tensor, images),
        out_shape=[
            shape((n_section, n_blk, n_tensor, width, span), BF16),
            shape((n_section - 1, n_rows, width), BF16),
            shape((n_section, n_tensor, n_rows, 3 * part), BF16),
            shape((n_section, n_tensor, images, n_heads, ROWS, ROWS), BF16),
            shape((n_section, n_tensor, n_rows, part), BF16),
            shape((n_section, n_rows, width), F32),
            shape((n_section, n_tensor, n_rows, span), BF16),
            shape((n_section, n_tensor, n_rows, span), BF16),
            shape((n_section, 6, width), F32),
        ],
        in_specs=[hbm] + [vmem] * (2 + len(given)),
        out_specs=[hbm] * 8 + [vmem],
        scratch_shapes=[
            pltpu.VMEM((2, width, span), BF16),
            pltpu.VMEM((2, n_rows, 3 * part), BF16),
            pltpu.VMEM((2, images, n_heads, ROWS, ROWS), BF16),
            pltpu.VMEM((2, n_rows, part), BF16),
            pltpu.VMEM((n_tensor, n_rows, span), BF16),
            pltpu.VMEM((2, n_rows, span), BF16),
            pltpu.VMEM((n_rows, width), F32),
            pltpu.VMEM((n_rows, width), BF16),
            pltpu.VMEM((n_rows, width), F32),
            pltpu.VMEM((n_section - 1, n_rows, width), BF16),
            pltpu.VMEM((n_section, n_tensor, 1, 3 * part), F32),
            pltpu.VMEM((n_section, n_tensor, 1, span), F32),
            pltpu.VMEM((n_small, 6, width), F32),
            pltpu.VMEM((n_small, n_tensor, 1, 3 * part), F32),
            pltpu.VMEM((n_small, n_tensor, 1, span), F32),
            dma((3, n_blk)),
            dma((n_pieces, n_dp * n_tensor)),
            dma((n_pieces, n_sends)),
            dma((n_pieces, 2)),
            dma((2,)),
            dma((2, 4)),
            dma((n_tensor,)),
            dma((1 + n_section,)),
            dma((2, n_small, 3)),
        ],
        compiler_params=pltpu.CompilerParams(
            collective_id=0, has_side_effects=True, vmem_limit_bytes=56 * 1024 * 1024
        ),
    )(shard, rows, live, *given)


class Slots:
    def __init__(self, n_dp, n_tensor):
        self.n_tensor = n_tensor
        bits = [b for b in range(n_dp.bit_length()) if (1 << b) < n_dp]
        mid = n_tensor // 2
        count = len(bits) * n_tensor
        self.line = count
        count += n_tensor + 1
        self.hops = {}
        self.cross = {}
        for e in range(1, n_dp):
            if bin(e).count("1") >= 2:
                self.cross[e] = count
                count += n_tensor
            for j in range(mid):
                for b in bits:
                    if not e >> b & 1:
                        chosen = [c for c in bits if (e | 1 << b) >> c & 1]
                        if chosen[j % len(chosen)] == b:
                            self.hops[e, j, b] = count
                            count += 1
        self.count = count


def reduce_lags(n_groups):
    return [0, 0] + [2 + 3 * min(g, 2) + 2 * max(g - 2, 0) for g in range(n_groups - 2)]


def backward_kernel(
    n_dp, n_tensor, images, weights, cotangent, live, vec, *refs
):
    first_rows, row_out, *saved = refs[:8]
    (
        out, sec_rows, sec_grads, d_vec, d_qkv_bias, d_up_bias,
        own, came, final, vec_in, qkv_bias_in, up_bias_in, ring, stage, w_buf, active_buf, slope_buf, qkv_buf, p_buf, heads_buf, rows_buf, middle_buf,
        grad_out, last_rows, grad_low, left_t, right_t, acc, grad_mid,
        load_sem, stage_sem, credit, recv_sem, send_sem, out_sem, small_sem, row_sem,
    ) = refs[8:]
    at = Place(n_dp, n_tensor)
    slots = Slots(n_dp, n_tensor)
    n_section, n_blk = weights.shape[:2]
    n_all = n_section * n_blk
    sub, half = final.shape[1:]
    n_pieces = final.shape[0]
    n_sub = n_pieces // n_all
    depth = sub * n_sub
    part = vec.shape[2] // n_tensor
    n_heads = part // DH
    lanes = pl.ds(pl.multiple_of(at.s * half, 128), half)
    sizes = send_sizes(n_dp, n_tensor)
    at.meet()

    def place(i):
        block = lax.div(i, n_sub)
        return n_section - 1 - lax.div(block, n_blk), n_blk - 1 - lax.rem(block, n_blk)

    def steps(i, start):
        counter = iter(range(10_000))

        def rows(e):
            return pl.multiple_of(at.away(e) * depth + lax.rem(i, n_sub) * sub, 16)

        def piece(e, tt):
            return own.at[lax.div(i, n_sub), tt, pl.ds(rows(e), sub), :]

        def maybe(cond, action):
            if cond is None:
                action()
            else:
                pl.when(cond)(action)

        def remote(e, tt, device, slot):
            k = next(counter)
            return pltpu.make_async_remote_copy(
                src_ref=piece(e, tt),
                dst_ref=came.at[i, slot],
                send_sem=send_sem.at[i, k],
                recv_sem=recv_sem.at[i, slot],
                device_id=device,
                device_id_type=MESH_ID,
            )

        def send(e, tt, device, slot, cond=None):
            copy = remote(e, tt, device, slot)
            maybe(cond, copy.start if start else copy.wait_send)

        def arrive(slot, cond=None):
            if start:
                copy = pltpu.make_async_copy(came.at[i, slot], came.at[i, slot], recv_sem.at[i, slot])
                maybe(cond, copy.wait)

        def total(e, tt, arrived, target=None):
            if not start or (target is None and not arrived):
                return
            base = rows(e)

            def chunk(c, carry):
                here = pl.ds(pl.multiple_of(base + c * CHUNK_ROWS, 16), CHUNK_ROWS)
                local = pl.ds(pl.multiple_of(c * CHUNK_ROWS, 16), CHUNK_ROWS)
                acc = own[lax.div(i, n_sub), tt, here, :].astype(jnp.float32)
                for slot in arrived:
                    acc = acc + came[i, slot, local, :].astype(jnp.float32)
                if target is None:
                    own[lax.div(i, n_sub), tt, here, :] = acc.astype(own.dtype)
                else:
                    target[i, local, :] = acc
                return carry

            lax.fori_loop(0, sub // CHUNK_ROWS, chunk, 0)

        def more(e, tt, slot, target=None):
            base = rows(e)

            def chunk(c, carry):
                here = pl.ds(pl.multiple_of(base + c * CHUNK_ROWS, 16), CHUNK_ROWS)
                local = pl.ds(pl.multiple_of(c * CHUNK_ROWS, 16), CHUNK_ROWS)
                acc = came[i, slot, local, :].astype(jnp.float32)
                if target is None:
                    own[lax.div(i, n_sub), tt, here, :] = (own[lax.div(i, n_sub), tt, here, :].astype(jnp.float32) + acc).astype(own.dtype)
                else:
                    target[i, local, :] = target[i, local, :] + acc
                return carry

            lax.fori_loop(0, sub // CHUNK_ROWS, chunk, 0)

        def also(e, tt, slot, cond, target=None):
            if start:

                def add():
                    arrive(slot)
                    more(e, tt, slot, target)

                pl.when(cond)(add)

        def line_slot(tt, from_next):
            return slots.line + tt + (0 if from_next else 1)

        def crossing():
            for e in range(1, n_dp):
                if bin(e).count("1") >= 2:
                    for j in range(at.mid):
                        tt = at.other_side(j)
                        slot = slots.cross[e] + tt
                        total(e, tt, [])
                        is_upper = at.t >= at.mid
                        also(e, tt, slot, jnp.logical_and(is_upper, at.has_next))
                        also(e, tt, slot, jnp.logical_and(jnp.logical_not(is_upper), at.has_prev))
                        send(e, tt, at.along(-1), slot, is_upper)
                        send(e, tt, at.along(1), slot, jnp.logical_not(is_upper))

        def leaves():
            for j in range(at.mid):
                for e in at.by_weight(1):
                    tt = at.other_side(j)
                    b = at.last_bit(e, j)
                    total(e, tt, [])
                    send(e, tt, at.hop(b), b * n_tensor + tt)

        def plane(weight):
            for e in at.by_weight(weight):
                for j in range(at.mid):
                    tt = at.own_side(j)
                    b = at.last_bit(e, j)
                    arrived = [slots.hops[e, j, c] for c in at.bits if (e, j, c) in slots.hops]
                    for slot in arrived:
                        arrive(slot)
                    total(e, tt, arrived)
                    if weight >= 2:
                        slot = slots.cross[e] + tt
                        also(e, tt, slot, at.t == at.mid - 1)
                        also(e, tt, slot, at.t == at.mid)
                    rest = e & ~(1 << b)
                    there = b * n_tensor + tt if rest == 0 else slots.hops[rest, j, b]
                    send(e, tt, at.hop(b), there)

        def column(k):
            low, high = at.t >= k, at.t + k < n_tensor
            for tt, cond, step, chain, from_next in (
                (at.t - k, low, -1, jnp.logical_and(low, at.has_next), True),
                (at.t + k, high, 1, jnp.logical_and(high, at.has_prev), False),
            ):
                arrived = [b * n_tensor + tt for b in at.bits]

                def sums(tt=tt, arrived=arrived):
                    for slot in arrived:
                        arrive(slot)
                    total(0, tt, arrived)

                if start:
                    pl.when(cond)(sums)
                slot = line_slot(tt, from_next)
                also(0, tt, slot, chain)
                send(0, tt, at.along(step), slot, cond)

        def last():
            arrived = [b * n_tensor + at.t for b in at.bits]
            for slot in arrived:
                arrive(slot)
            total(0, at.t, arrived, final)
            also(0, at.t, line_slot(at.t, True), at.has_next, final)
            also(0, at.t, line_slot(at.t, False), at.has_prev, final)
            sec, b = place(i)
            there = out.at[b, pl.ds(pl.multiple_of(lax.rem(i, n_sub) * sub, 16), sub), lanes]
            stay = pltpu.make_async_copy(final.at[i], there, out_sem.at[0, i])
            go = pltpu.make_async_remote_copy(
                src_ref=final.at[i],
                dst_ref=there,
                send_sem=out_sem.at[1, i],
                recv_sem=out_sem.at[2, i],
                device_id=at.sibling(),
                device_id_type=MESH_ID,
            )

            @pl.when(sec == at.s)
            def _():
                if start:
                    stay.start()
                else:
                    stay.wait()

            @pl.when(sec != at.s)
            def _():
                if start:
                    go.start()
                else:
                    go.wait_send()

        groups = [crossing, leaves]
        groups += [functools.partial(plane, w) for w in range(len(at.bits), 0, -1)]
        groups += [functools.partial(column, k) for k in range(n_tensor - 1, 0, -1)] + [last]
        return groups, counter

    lags = reduce_lags(len(sizes))

    def run_group(i, g):
        groups, counter = steps(i, True)
        for _ in range(sum(sizes[:g])):
            next(counter)
        groups[g]()

    phases = [(kind, sec) for sec in range(n_section - 1, -1, -1) for kind in ("down", "up", "attn")]
    phases.append(("out", n_section - 1))

    def loads(phase, k, par):
        kind, sec = phases[phase]
        rows = first_rows if sec == 0 else row_out.at[sec - 1]
        qkv, p, heads, middle, active, slope = (ref.at[sec] for ref in saved)
        if kind == "down":
            pairs = [(active.at[k], active_buf.at[par])]
            once = (middle, middle_buf)
        elif kind == "up":
            pairs = [
                (weights.at[sec, 1, k], w_buf.at[par, 0]),
                (weights.at[sec, 2, k], w_buf.at[par, 1]),
                (slope.at[k], slope_buf.at[par]),
            ]
            once = (rows, rows_buf)
        elif kind == "out":
            pairs = [(active.at[k], active_buf.at[par]), (weights.at[sec, 2, k], w_buf.at[par, 0])]
            once = (middle, middle_buf)
        else:
            pairs = [
                (weights.at[sec, 0, k], w_buf.at[par, 0]),
                (qkv.at[k], qkv_buf.at[par]),
                (p.at[k], p_buf.at[par]),
                (heads.at[k], heads_buf.at[par]),
            ]
            once = None
        copies = [
            pltpu.make_async_copy(src, dst, load_sem.at[par, n]) for n, (src, dst) in enumerate(pairs)
        ]
        return copies, lambda: pltpu.make_async_copy(*once, load_sem.at[0, 4])

    def start_loads(phase, k, par, is_first):
        copies, once = loads(phase, k, par)
        for copy in copies:
            copy.start()
        if is_first and phases[phase][0] != "attn":
            once().start()

    def shared(k):
        return pltpu.make_async_remote_copy(
            src_ref=stage.at[k],
            dst_ref=ring.at[k],
            send_sem=stage_sem.at[0, k],
            recv_sem=stage_sem.at[1, k],
            device_id=at.sibling(),
            device_id_type=MESH_ID,
        )

    def before_emit(k):
        shared(k).wait_send()
        pl.semaphore_wait(credit.at[k], 1)

    def emit(phase, k, low, high):
        first = at.s == 0
        own[phase, k] = jnp.where(first, low, high)
        stage[k] = jnp.where(first, high, low)

    def consume(phase, k, is_last):
        shared(k).wait_recv()

        def chunk(c, carry):
            here = pl.ds(pl.multiple_of(c * 96, 96), 96)
            total = own[phase, k, here].astype(F32) + ring[k, here].astype(F32)
            own[phase, k, here] = total.astype(own.dtype)
            return carry

        lax.fori_loop(0, own.shape[2] // 96, chunk, 0)
        if not is_last:
            pl.semaphore_signal(
                credit.at[k], inc=1, device_id=at.sibling(), device_id_type=MESH_ID
            )

    def column_sum(values):
        return jnp.sum(values, axis=0, keepdims=True)

    def down_step(sec, k, par, emits):
        @pl.when(k == 0)
        def _():
            source = cotangent if sec == n_section - 1 else grad_out.at[sec + 1]
            low = (source[...].astype(F32) * live[...]).astype(BF16)
            grad_low[...] = low
            left_t[...] = low.T

        d_down = dot(left_t[...], active_buf[par]).astype(BF16)
        emits(d_down[:, :half], d_down[:, half:])

    def out_step(sec, k, par):
        @pl.when(k == 0)
        def _():
            acc[...] = middle_buf[...] + vec[sec, 5:6]

        acc[...] += dot_cols(active_buf[par], w_buf[par, 0])

        @pl.when(k == n_tensor - 1)
        def _():
            last_rows[sec] = (acc[...] * live[...]).astype(BF16)
            for done in range(n_section - 1):
                pltpu.make_async_copy(row_out.at[done], last_rows.at[done], row_sem.at[2, 0]).wait()
            for each in range(n_section):
                at.hand_out(last_rows, sec_rows, each, row_sem.at[1])

    def up_step(sec, k, par, emits):
        @pl.when(k == 0)
        def _():
            unit, _ = unit_rows(middle_buf[...])
            right_t[...] = (unit * vec[sec, 3:4] + vec[sec, 4:5]).astype(BF16).T
            acc[...] = jnp.zeros_like(acc)

        grad_hidden = (dot(grad_low[...], w_buf[par, 1]) * slope_buf[par].astype(F32)).astype(BF16)
        d_up_bias[sec, k] = column_sum(grad_hidden.astype(F32))
        d_up = dot(right_t[...], grad_hidden).astype(BF16)
        emits(d_up[:, :half], d_up[:, half:])
        acc[...] += dot_cols(grad_hidden, w_buf[par, 0])

    def attn_step(sec, k, par, emits):
        w_attn = w_buf.at[par, 0]

        @pl.when(k == 0)
        def _():
            unit, scale = unit_rows(middle_buf[...])
            grad_norm = acc[...]
            low = grad_low[...].astype(F32)
            mid = low + unit_rows_back(grad_norm * vec[sec, 3:4], unit, scale)
            grad_mid[...] = mid
            d_vec[sec, 2:3] = column_sum(mid)
            d_vec[sec, 3:4] = column_sum(grad_norm * unit)
            d_vec[sec, 4:5] = column_sum(grad_norm)
            d_vec[sec, 5:6] = column_sum(low)
            mid = mid.astype(BF16)
            grad_low[...] = mid
            left_t[...] = mid.T
            unit, _ = unit_rows(rows_buf[...].astype(F32))
            right_t[...] = (unit * vec[sec, 0:1] + vec[sec, 1:2]).astype(BF16).T
            acc[...] = jnp.zeros_like(acc)

        d_out = dot(left_t[...], heads_buf[par]).astype(BF16)
        grad_heads = dot(grad_low[...], w_attn[:, 3 * part :]).astype(BF16)
        per_image = []
        for image in range(images):
            span = slice(image * ROWS, (image + 1) * ROWS)
            per_head = [[], [], []]
            for head in range(n_heads):
                q, key, v = (
                    qkv_buf[par, span, c * part + head * DH : c * part + (head + 1) * DH]
                    for c in range(3)
                )
                grad_o = grad_heads[span, head * DH : (head + 1) * DH]
                chosen = p_buf[par, image, head]
                chances = chosen.astype(F32)
                grad_chances = dot_cols(v, grad_o)
                along = jnp.sum(chances * grad_chances, axis=0, keepdims=True)
                grad_scores = (chances * (grad_chances - along)).astype(BF16)
                per_head[0].append((dot(key.T, grad_scores).T * DH**-0.5).astype(BF16))
                per_head[1].append((dot(grad_scores, q) * DH**-0.5).astype(BF16))
                per_head[2].append(dot(chosen, grad_o).astype(BF16))
            per_image.append(jnp.concatenate(per_head[0] + per_head[1] + per_head[2], axis=1))
        grad_mixed = jnp.concatenate(per_image, axis=0)
        d_qkv_bias[sec, k] = column_sum(grad_mixed.astype(F32))
        d_qkv = dot(right_t[...], grad_mixed).astype(BF16)
        emits(d_qkv[:, :half], jnp.concatenate([d_qkv[:, half:], d_out], axis=1))
        acc[...] += dot_cols(grad_mixed, w_attn[:, : 3 * part])

        @pl.when(k == n_tensor - 1)
        def _():
            unit, scale = unit_rows(rows_buf[...].astype(F32))
            grad_norm = acc[...]
            d_vec[sec, 0:1] = column_sum(grad_norm * unit)
            d_vec[sec, 1:2] = column_sum(grad_norm)
            total = grad_mid[...] + unit_rows_back(grad_norm * vec[sec, 0:1], unit, scale)
            grad_out[sec] = total.astype(BF16)
            at.hand_out(grad_out, sec_grads, sec, row_sem.at[0])

    def compute(phase, k):
        kind, sec = phases[phase]
        par = lax.rem(k, 2)
        copies, once = loads(phase, k, par)
        for copy in copies:
            copy.wait()

        if kind != "attn":

            @pl.when(k == 0)
            def _():
                once().wait()

        @pl.when(k < n_tensor - 1)
        def _():
            start_loads(phase, k + 1, 1 - par, False)

        if phase + 1 < len(phases):

            @pl.when(k == n_tensor - 1)
            def _():
                start_loads(phase + 1, 0, 0, True)

        if kind == "out":
            out_step(sec, k, par)

            @pl.when(k == 0)
            def _():
                for back in (n_tensor - 2, n_tensor - 1):
                    consume(phase - 1, back, True)

            return

        if phase:
            before_emit(k)

        if phase == 0:

            @pl.when(k == 0)
            def _():
                for done in range(n_section - 1):
                    pltpu.make_async_copy(
                        row_out.at[done], last_rows.at[done], row_sem.at[2, 0]
                    ).start()

        def emits(low, high):
            emit(phase, k, low, high)

        {"down": down_step, "up": up_step, "attn": attn_step}[kind](sec, k, par, emits)
        shared(k).start()

        @pl.when(k >= 2)
        def _():
            consume(phase, k - 2, phase == n_all - 1)

        if phase:

            @pl.when(k == 0)
            def _():
                for back in (n_tensor - 2, n_tensor - 1):
                    consume(phase - 1, back, False)

    n_busy = n_all * n_tensor
    settle = max(lags) + 2
    short = n_tensor // 2
    per_section = short + 2 * n_tensor

    def tick_of(it):
        sec, step = lax.div(it, n_blk * n_tensor), lax.rem(it, n_blk * n_tensor)
        is_short = step < n_tensor
        tick = sec * per_section + jnp.where(is_short, lax.div(step, 2), step - n_tensor + short)
        over = it >= len(phases) * n_tensor
        tick = jnp.where(over, n_section * per_section + short + it - len(phases) * n_tensor, tick)
        return tick, jnp.logical_or(over, jnp.logical_or(jnp.logical_not(is_short), lax.rem(step, 2) == 1))

    def start_of(i):
        block, within = i // n_sub, i % n_sub
        sec, b = block // n_blk, block % n_blk
        first = sec * per_section + (short, short + n_tensor, per_section)[b]
        return first + within * (2 if b == 0 else 2 if b == 1 else 1)

    def piece_at(tick):
        found, starts = 0, False
        for i in range(n_pieces):
            here = tick == start_of(i)
            found = jnp.where(here, i, found)
            starts = jnp.logical_or(starts, here)
        return found, starts


    small = [(d_vec, vec_in), (d_qkv_bias, qkv_bias_in), (d_up_bias, up_bias_in)]
    n_hops = len(at.bits)

    def small_copies(stage, device, slot):
        sec = 1 - at.s if stage == 0 else at.s
        return [
            pltpu.make_async_remote_copy(
                src_ref=mine.at[sec],
                dst_ref=came_in.at[slot],
                send_sem=small_sem.at[0, slot, n],
                recv_sem=small_sem.at[1, slot, n],
                device_id=device,
                device_id_type=MESH_ID,
            )
            for n, (mine, came_in) in enumerate(small)
        ]

    def small_send(stage):
        if stage == 0:
            return [small_copies(0, at.sibling(), 0)]
        if stage <= n_hops:
            return [small_copies(stage, at.hop(stage - 1), stage)]
        other = [lax.rem(at.t + k, n_tensor) for k in range(1, n_tensor)]
        return [
            small_copies(stage, (at.s, at.d, tt), n_hops + 1 + k) for k, tt in enumerate(other)
        ]

    def small_take(stage):
        sent = small_send(stage)
        for copies in sent:
            for copy in copies:
                copy.wait()
        first = stage if stage <= n_hops else n_hops + 1
        for mine, came_in in small:
            total = mine[at.s]
            for slot in range(first, first + len(sent)):
                total = total + came_in[slot]
            mine[at.s] = total

    def small_step(tick):
        for stage in range(n_hops + 2):

            @pl.when(tick == SMALL_TICKS * stage)
            def _():
                if stage:
                    small_take(stage - 1)
                for copies in small_send(stage):
                    for copy in copies:
                        copy.start()

        @pl.when(tick == SMALL_TICKS * (n_hops + 2))
        def _():
            small_take(n_hops + 1)

    def finish(i):
        groups, _ = steps(i, False)
        for g in groups:
            g()
        sec, b = place(i)

        @pl.when(sec == at.s)
        def _():
            pltpu.make_async_copy(final.at[i], final.at[i], out_sem.at[2, i]).wait()

    def body(it, carry):
        for phase in range(len(phases)):

            @pl.when(lax.div(it, n_tensor) == phase)
            def _():
                compute(phase, lax.rem(it, n_tensor))

        tick, ticks = tick_of(it)
        for g, lag in sorted(enumerate(lags), key=lambda item: item[1]):
            i, starts = piece_at(tick - lag)

            @pl.when(jnp.logical_and(ticks, starts))
            def _():
                run_group(i, g)

        small_step(it - n_busy)
        i, starts = piece_at(tick - settle)

        @pl.when(jnp.logical_and(ticks, starts))
        def _():
            finish(i)

        return carry

    start_loads(0, 0, 0, True)
    last_tick = start_of(n_pieces - 1) + max(lags)
    tail = max(last_tick + 1, n_section * per_section + short + SMALL_TICKS * (n_hops + 2)) - n_section * per_section - short
    n_ticks = len(phases) * n_tensor + tail
    last_tick = n_section * per_section + short + tail - 1
    lax.fori_loop(0, n_ticks, body, 0)
    for i in range(n_pieces):
        if start_of(i) + settle > last_tick:
            finish(i)
    for k in range(n_tensor):
        shared(k).wait_send()
    at.handed_out(grad_out, sec_grads, row_sem.at[0])
    at.handed_out(last_rows, sec_rows, row_sem.at[1])


def send_sizes(n_dp, n_tensor):
    bits = n_dp.bit_length() - 1
    mid = n_tensor // 2
    weights = [bin(e).count("1") for e in range(n_dp)]
    sizes = [2 * mid * sum(w >= 2 for w in weights), mid * bits]
    sizes += [mid * sum(w == k for w in weights) for k in range(bits, 0, -1)]
    return sizes + [2] * (n_tensor - 1) + [0]


def backward_and_reduce(weights, cotangent, live, vec, saved, n_dp):
    n_section, n_blk, n_tensor, width, span = weights.shape
    n_rows = cotangent.shape[0]
    images = n_rows // ROWS
    part = width // n_tensor
    n_all = n_section * n_blk
    depth, half = width // n_dp, span // 2
    n_pieces = n_all * sub_blocks(depth)
    sub = depth // sub_blocks(depth)
    slots = Slots(n_dp, n_tensor)
    n_sends = sum(send_sizes(n_dp, n_tensor))
    n_small = n_dp.bit_length() + n_tensor - 1
    shape = jax.ShapeDtypeStruct
    hbm = pl.BlockSpec(memory_space=pl.ANY)
    vmem = pl.BlockSpec(memory_space=pltpu.VMEM)
    dma = pltpu.SemaphoreType.DMA
    return pl.pallas_call(
        functools.partial(backward_kernel, n_dp, n_tensor, images),
        out_shape=[
            shape((n_blk, depth, span), F32),
            shape((n_section, n_rows, width), BF16),
            shape((n_section, n_rows, width), BF16),
            shape((n_section, 6, width), F32),
            shape((n_section, n_tensor, 1, 3 * part), F32),
            shape((n_section, n_tensor, 1, span), F32),
        ],
        in_specs=[hbm] + [vmem] * 3 + [hbm] * len(saved),
        out_specs=[hbm] * 3 + [vmem] * 3,
        scratch_shapes=[
            pltpu.VMEM((n_all, n_tensor, width, half), BF16),
            pltpu.VMEM((n_pieces, slots.count, sub, half), BF16),
            pltpu.VMEM((n_pieces, sub, half), F32),
            pltpu.VMEM((n_small, 6, width), F32),
            pltpu.VMEM((n_small, n_tensor, 1, 3 * part), F32),
            pltpu.VMEM((n_small, n_tensor, 1, span), F32),
            pltpu.VMEM((n_tensor, width, half), BF16),
            pltpu.VMEM((n_tensor, width, half), BF16),
            pltpu.VMEM((2, 2, width, span), BF16),
            pltpu.VMEM((2, n_rows, span), BF16),
            pltpu.VMEM((2, n_rows, span), BF16),
            pltpu.VMEM((2, n_rows, 3 * part), BF16),
            pltpu.VMEM((2, images, part // DH, ROWS, ROWS), BF16),
            pltpu.VMEM((2, n_rows, part), BF16),
            pltpu.VMEM((n_rows, width), BF16),
            pltpu.VMEM((n_rows, width), F32),
            pltpu.VMEM((n_section, n_rows, width), BF16),
            pltpu.VMEM((n_section, n_rows, width), BF16),
            pltpu.VMEM((n_rows, width), BF16),
            pltpu.VMEM((width, n_rows), BF16),
            pltpu.VMEM((width, n_rows), BF16),
            pltpu.VMEM((n_rows, width), F32),
            pltpu.VMEM((n_rows, width), F32),
            dma((2, 5)),
            dma((2, n_tensor)),
            pltpu.SemaphoreType.REGULAR((n_tensor,)),
            dma((n_pieces, slots.count)),
            dma((n_pieces, n_sends)),
            dma((3, n_pieces)),
            dma((2, n_small, 3)),
            dma((3, 3)),
        ],
        compiler_params=pltpu.CompilerParams(
            collective_id=1, has_side_effects=True, vmem_limit_bytes=64 * 1024 * 1024 - 256 * 1024
        ),
    )(weights, cotangent, live, vec, *saved)


AXES = ("section", "tensor", "dp")


def shards(
    images,
    cotangent,
    counts,
    ln1_gain,
    ln1_bias,
    q_bias,
    v_bias,
    qkv_weight,
    out_weight,
    out_bias,
    ln2_gain,
    ln2_bias,
    up_weight,
    up_bias,
    down_weight,
    down_bias,
):
    n_section, n_dp, n_tensor = (lax.axis_size(a) for a in ("section", "dp", "tensor"))
    section_idx = lax.axis_index("section")
    micro_count, share_rows, width = images.shape
    own_count = micro_count // n_section
    depth = qkv_weight.shape[1]
    part = qkv_weight.shape[3]

    own = section_idx * own_count

    def own_rows(values):
        mine = lax.dynamic_slice_in_dim(values, own, own_count, 0).reshape(-1, SEQ, values.shape[-1])
        return jnp.pad(mine, ((0, 0), (0, ROWS - SEQ), (0, 0))).reshape(-1, values.shape[-1])

    row_place = lax.axis_index("tensor") * share_rows + jnp.arange(share_rows)
    own_counts = lax.dynamic_slice_in_dim(counts, own, own_count, 0)
    live_rows = (row_place // SEQ < own_counts).astype(jnp.float32)
    live_rows = live_rows.reshape(-1, SEQ)
    live_rows = jnp.pad(live_rows, ((0, 0), (0, ROWS - SEQ))).reshape(-1, 1)

    shard = jnp.stack(
        [
            jnp.concatenate([qkv_weight[0].reshape(depth, -1), out_weight[0].T], axis=1),
            up_weight[0],
            down_weight[0].T,
        ]
    )
    given = [ln1_gain, ln1_bias, out_bias, ln2_gain, ln2_bias, down_bias, q_bias, v_bias, up_bias]
    first_rows = own_rows(images)
    gathered, row_out, *kept, vec = gather_and_forward(
        shard, first_rows, live_rows, given, n_section, n_dp, n_tensor
    )
    weight_sum, sec_rows, sec_grads, d_vec, d_qkv_bias, d_up_bias = backward_and_reduce(
        gathered, own_rows(cotangent), live_rows, vec, [first_rows, row_out, *kept], n_dp
    )

    def placed_rows(values):
        values = values.reshape(-1, ROWS, width)[:, :SEQ]
        return values.reshape(1, micro_count, share_rows, width)

    section_out = placed_rows(sec_rows)
    input_grad = placed_rows(sec_grads)

    dp_idx, tensor_idx = lax.axis_index("dp"), lax.axis_index("tensor")

    def own_heads(sums, like):
        _, heads, lanes = like.shape
        sums = sums.reshape(-1, DH)
        return lax.dynamic_slice(sums, (0, dp_idx * lanes), (heads, lanes))[None]

    d_vec, d_qkv_bias, d_up_bias = (
        lax.dynamic_index_in_dim(v, section_idx, 0, keepdims=False)
        for v in (d_vec, d_qkv_bias, d_up_bias)
    )
    q_row, _, v_row = jnp.split(
        lax.dynamic_index_in_dim(d_qkv_bias, tensor_idx, 0, keepdims=False).reshape(-1), 3
    )
    up_row = lax.dynamic_index_in_dim(d_up_bias, tensor_idx, 0, keepdims=False)
    q_sum, v_sum, up_sum = own_heads(q_row, q_bias), own_heads(v_row, v_bias), own_heads(up_row, up_bias)
    block = width // (n_dp * n_tensor)
    vec = lax.dynamic_slice_in_dim(d_vec, (dp_idx * n_tensor + tensor_idx) * block, block, 1)[None]

    return (
        section_out,
        input_grad,
        weight_sum[0, :, : 3 * part].reshape(qkv_weight.shape),
        weight_sum[0, :, 3 * part :].T[None],
        weight_sum[1][None],
        weight_sum[2].T[None],
        q_sum,
        v_sum,
        up_sum,
        vec,
    )


def solution(mesh):
    placed = (
        P(None, ("dp", "tensor"), None),
        P(None, ("dp", "tensor"), None),
        P(None, "dp"),
        P("section", "dp"),
        P("section", "dp"),
        P("section", "tensor", "dp"),
        P("section", "tensor", "dp"),
        P("section", "dp", None, "tensor"),
        P("section", "tensor", "dp"),
        P("section", "dp"),
        P("section", "dp"),
        P("section", "dp"),
        P("section", "dp", "tensor"),
        P("section", "tensor", "dp"),
        P("section", "tensor", "dp"),
        P("section", "dp"),
    )
    return jax.shard_map(
        shards,
        mesh=mesh,
        in_specs=placed,
        out_specs=(
            P("section", None, ("dp", "tensor"), None),
            P("section", None, ("dp", "tensor"), None),
            P("section", "dp", None, "tensor"),
            P("section", "tensor", "dp"),
            P("section", "dp", "tensor"),
            P("section", "tensor", "dp"),
            P("section", "tensor", "dp"),
            P("section", "tensor", "dp"),
            P("section", "tensor", "dp"),
            P("section", None, ("dp", "tensor")),
        ),
        check_vma=False,
    )
```

```python
import functools
import jax
import jax.numpy as jnp
from jax import lax
from jax.experimental import pallas as pl
from jax.experimental.pallas import tpu as pltpu
from jax.sharding import PartitionSpec as P

CHUNK_ROWS = 48
SMALL_TICKS = 2
MESH_ID = pl.DeviceIdType.MESH


def sub_blocks(depth):
    return 1


def slot_sizes(n_dp, n_tensor):
    bits = [b for b in range(n_dp.bit_length()) if (1 << b) < n_dp]
    mid = n_tensor // 2
    weights = [bin(e).count("1") for e in range(n_dp)]

    def plane(weight):
        total = 0
        for j in range(mid):
            for e in range(n_dp):
                if weights[e] == weight:
                    for b in bits:
                        if not e >> b & 1:
                            chosen = [c for c in bits if (e | 1 << b) >> c & 1]
                            total += chosen[j % len(chosen)] == b
                    total += 2 * (weight >= 2) + 1
        return total

    first = [2 + len(bits)]
    columns = [2 * (2 + len(bits))] * (n_tensor - 1)
    planes = [plane(w) for w in range(1, len(bits) + 1)]
    over = mid * sum(w >= 2 for w in weights)
    crossed = [3 * over] * (mid - 1) + [over]
    rest = [mid * sum(w == 1 for w in weights)]
    return first + [columns[0], planes[0], columns[1]] + planes[1:] + columns[2:] + crossed + rest


class Place:
    def __init__(self, n_dp, n_tensor):
        self.n_dp, self.n_tensor = n_dp, n_tensor
        self.mid = n_tensor // 2
        self.bits = [b for b in range(n_dp.bit_length()) if (1 << b) < n_dp]
        self.s = lax.axis_index("section")
        self.d = lax.axis_index("dp")
        self.t = lax.axis_index("tensor")
        self.upper = lax.div(self.t, self.mid)
        self.has_next = self.t < n_tensor - 1
        self.has_prev = self.t > 0

    def away(self, e):
        other = self.d
        for b in self.bits:
            if e >> b & 1:
                other = other + (1 << b) * (1 - 2 * lax.rem(lax.div(self.d, 1 << b), 2))
        return other

    def last_bit(self, e, j):
        chosen = [b for b in self.bits if e >> b & 1]
        return chosen[j % len(chosen)]

    def own_side(self, j):
        return self.upper * self.mid + j

    def other_side(self, j):
        return (1 - self.upper) * self.mid + j

    def sibling(self):
        return (1 - self.s, self.d, self.t)

    def along(self, step):
        return (self.s, self.d, self.t + step)

    def hop(self, b):
        return (self.s, self.away(1 << b), self.t)

    def meet(self):
        barrier = pltpu.get_barrier_semaphore()
        line = [(self.s, self.d, lax.rem(self.t + k, self.n_tensor)) for k in range(1, self.n_tensor)]
        others = [self.sibling()] + [self.hop(b) for b in self.bits] + line
        for device in others:
            pl.semaphore_signal(barrier, inc=1, device_id=device, device_id_type=MESH_ID)
        pl.semaphore_wait(barrier, len(others))

    def rows_away(self, source, target, sec, sems):
        return pltpu.make_async_remote_copy(
            src_ref=source.at[sec],
            dst_ref=target.at[self.s],
            send_sem=sems.at[1],
            recv_sem=sems.at[2],
            device_id=self.sibling(),
            device_id_type=MESH_ID,
        )

    def hand_out(self, source, target, sec, sems):
        @pl.when(sec == self.s)
        def _():
            pltpu.make_async_copy(source.at[sec], target.at[self.s], sems.at[0]).start()

        @pl.when(sec != self.s)
        def _():
            self.rows_away(source, target, sec, sems).start()

    def handed_out(self, source, target, sems):
        pltpu.make_async_copy(source.at[0], target.at[self.s], sems.at[0]).wait()
        self.rows_away(source, target, 0, sems).wait()

    def by_weight(self, weight):
        return [e for e in range(self.n_dp) if bin(e).count("1") == weight]


DH = 64
SEQ = 197
EPS = 1e-06
F32 = jnp.float32
BF16 = jnp.bfloat16
ROWS = 208


def dot(left, right):
    return jnp.dot(left, right, preferred_element_type=F32)


def dot_cols(left, right):
    return lax.dot_general(left, right, (((1,), (1,)), ((), ())), preferred_element_type=F32)


def unit_rows(values):
    average = jnp.mean(values, axis=-1, keepdims=True)
    centered = values - average
    scale = lax.rsqrt(jnp.mean(centered * centered, axis=-1, keepdims=True) + EPS)
    return centered * scale, scale


def unit_rows_back(grad_unit, unit, scale):
    along = jnp.mean(grad_unit * unit, axis=-1, keepdims=True)
    return scale * (grad_unit - jnp.mean(grad_unit, axis=-1, keepdims=True) - unit * along)


def gelu_parts(hidden):
    below = 0.5 * (1.0 + lax.erf(hidden * (0.5**0.5)))
    density = jnp.exp(-0.5 * hidden * hidden) * 0.3989422804014327
    return hidden * below, below + hidden * density


def forward_kernel(n_dp, n_tensor, images, *refs):
    (
        shard, rows, live, *given,
        out, row_out, qkv_out, p_out, heads_out, middle_out, active_out, slope_out, vec,
        w_buf, qkv_st, p_st, heads_st, active_st, slope_st, middle_st, normed, acc, row_buf,
        qkv_bias, up_bias, vec_in, qkv_bias_in, up_bias_in,
        own_sem, recv_sem, send_sem, part_sem, load_sem, store_sem, active_sem, once_sem, small_sem,
    ) = refs
    at = Place(n_dp, n_tensor)
    n_section = out.shape[0]
    n_blk, depth, span = shard.shape
    half = span // 2
    n_all = n_section * n_blk
    n_sub = sub_blocks(depth)
    sub = depth // n_sub
    n_pieces = n_all * n_sub
    part = vec.shape[2] // n_tensor
    n_heads = part // DH

    def spread(value):
        return jnp.concatenate([jnp.where(at.d == k, value, 0.0) for k in range(n_dp)], axis=1)

    def spread_heads(ref):
        values = ref[0].astype(F32)
        return jnp.concatenate([spread(values[h : h + 1]) for h in range(values.shape[0])], axis=1)

    vec[...] = jnp.zeros_like(vec)
    qkv_bias[...] = jnp.zeros_like(qkv_bias)
    up_bias[...] = jnp.zeros_like(up_bias)
    placed = jnp.concatenate([spread(ref[...].astype(F32)) for ref in given[:6]], axis=0)
    vec[at.s] = jnp.where(at.t == 0, placed, 0.0)
    q_row, v_row = spread_heads(given[6]), spread_heads(given[7])
    qkv_bias[at.s, at.t] = jnp.concatenate([q_row, jnp.zeros_like(q_row), v_row], axis=1)
    up_bias[at.s, at.t] = spread_heads(given[8])
    at.meet()

    def whole(sec, b):
        return out.at[sec, b, at.t, rows_of(0), :]

    def rows_of(e):
        return pl.ds(pl.multiple_of(at.away(e) * depth, 16), depth)

    lanes = pl.ds(pl.multiple_of(at.s * half, 128), half)

    def piece(i, e, tt):
        block = lax.div(i, n_sub)
        start = at.away(e) * depth + lax.rem(i, n_sub) * sub
        rows_here = pl.ds(pl.multiple_of(start, 16), sub)
        return out.at[lax.div(block, n_blk), lax.rem(block, n_blk), tt, rows_here, lanes]

    def share(b):
        return pltpu.make_async_remote_copy(
            src_ref=shard.at[b],
            dst_ref=whole(at.s, b),
            send_sem=own_sem.at[1, b],
            recv_sem=own_sem.at[2, b],
            device_id=at.sibling(),
            device_id_type=MESH_ID,
        )

    for b in range(n_blk):
        pltpu.make_async_copy(shard.at[b], whole(at.s, b), own_sem.at[0, b]).start()
        share(b).start()

    def push(i, e, tt, device, e_there, slot, start):
        copy = pltpu.make_async_remote_copy(
            src_ref=piece(i, e, tt),
            dst_ref=piece(i, e, tt),
            send_sem=send_sem.at[i, slot],
            recv_sem=recv_sem.at[i, e_there * n_tensor + tt],
            device_id=device,
            device_id_type=MESH_ID,
        )
        if start:
            copy.start()
        else:
            copy.wait_send()

    def push_sib(i, e, tt, slot, start):
        copy = pltpu.make_async_remote_copy(
            src_ref=piece(i, e, tt),
            dst_ref=piece(i, e, tt),
            send_sem=send_sem.at[i, slot],
            recv_sem=part_sem.at[i, 0 if e == 0 else 1],
            device_id=at.sibling(),
            device_id_type=MESH_ID,
        )
        if start:
            copy.start()
        else:
            copy.wait_send()

    def await_piece(i, e, tt):
        pltpu.make_async_remote_copy(
            src_ref=piece(i, e, tt),
            dst_ref=piece(i, e, tt),
            send_sem=send_sem.at[i, 0],
            recv_sem=recv_sem.at[i, e * n_tensor + tt],
            device_id=at.sibling(),
            device_id_type=MESH_ID,
        ).wait_recv()

    def steps(i, start):
        slots = iter(range(10_000))

        def maybe(cond, action):
            if cond is None:
                action()
            else:
                pl.when(cond)(action)

        def ready(e, tt, cond=None):
            if start:
                maybe(cond, lambda: await_piece(i, e, tt))

        def go(e, tt, device, e_there, cond=None):
            slot = next(slots)
            maybe(cond, lambda: push(i, e, tt, device, e_there, slot, start))

        def go_sib(e, tt, cond=None):
            slot = next(slots)
            maybe(cond, lambda: push_sib(i, e, tt, slot, start))

        def first():
            block = lax.div(i, n_sub)
            sec, b = lax.div(block, n_blk), lax.rem(block, n_blk)
            is_first = lax.rem(i, n_sub) == 0
            if start:

                @pl.when(jnp.logical_and(sec == at.s, is_first))
                def _():
                    pltpu.make_async_copy(shard.at[b], whole(at.s, b), own_sem.at[0, b]).wait()

                @pl.when(jnp.logical_and(sec != at.s, is_first))
                def _():
                    pltpu.make_async_remote_copy(
                        src_ref=shard.at[b],
                        dst_ref=whole(1 - at.s, b),
                        send_sem=own_sem.at[1, b],
                        recv_sem=own_sem.at[2, b],
                        device_id=at.sibling(),
                        device_id_type=MESH_ID,
                    ).wait_recv()

            go(0, at.t, at.along(1), 0, at.has_next)
            go(0, at.t, at.along(-1), 0, at.has_prev)
            for b in at.bits:
                go(0, at.t, at.hop(b), 1 << b)

        def column(k):
            low, high = at.t >= k, at.t + k < n_tensor
            for tt, cond, dev, more in (
                (at.t - k, low, at.along(1), jnp.logical_and(low, at.has_next)),
                (at.t + k, high, at.along(-1), jnp.logical_and(high, at.has_prev)),
            ):
                ready(0, tt, cond)
                go(0, tt, dev, 0, more)
                for b in at.bits:
                    go(0, tt, at.hop(b), 1 << b, cond)
                go_sib(0, tt, cond)

        def plane(weight):
            for j in range(at.mid):
                for e in at.by_weight(weight):
                    tt = at.own_side(j)
                    ready(e, tt)
                    for b in at.bits:
                        if not e >> b & 1 and at.last_bit(e | 1 << b, j) == b:
                            go(e, tt, at.hop(b), e | 1 << b)
                    if weight >= 2:
                        go(e, tt, at.along(1), e, at.t == at.mid - 1)
                        go(e, tt, at.along(-1), e, at.t == at.mid)
                    go_sib(e, tt)

        def crossed(k):
            down, up = at.t == at.mid - 1 - k, at.t == at.mid + k
            here = jnp.logical_or(down, up)
            for weight in range(2, len(at.bits) + 1):
                for e in at.by_weight(weight):
                    for j in range(at.mid):
                        tt = at.other_side(j)
                        ready(e, tt, here)
                        if k < at.mid - 1:
                            go(e, tt, at.along(1), e, up)
                            go(e, tt, at.along(-1), e, down)
                        go_sib(e, tt, here)

        def rest():
            for e in at.by_weight(1):
                for j in range(at.mid):
                    tt = at.other_side(j)
                    ready(e, tt)
                    go_sib(e, tt)

        groups = [first]
        for k in range(1, n_tensor):
            groups.append(functools.partial(column, k))
        planes = [functools.partial(plane, w) for w in range(1, len(at.bits) + 1)]
        merged = [groups[0]]
        far = [functools.partial(crossed, k) for k in range(at.mid)]
        order = [groups[1], planes[0], groups[2]] + planes[1:] + groups[3:] + far + [rest]
        return merged + order, slots


    small = [(vec, vec_in), (qkv_bias, qkv_bias_in), (up_bias, up_bias_in)]
    n_hops = len(at.bits)

    def small_copies(device, slot, to_place):
        return [
            pltpu.make_async_remote_copy(
                src_ref=mine.at[at.s],
                dst_ref=mine.at[at.s] if to_place else came_in.at[slot],
                send_sem=small_sem.at[0, slot, n],
                recv_sem=small_sem.at[1, slot, n],
                device_id=device,
                device_id_type=MESH_ID,
            )
            for n, (mine, came_in) in enumerate(small)
        ]

    def small_send(stage):
        if stage < n_hops:
            return [small_copies(at.hop(stage), stage, False)]
        if stage == n_hops:
            other = [lax.rem(at.t + k, n_tensor) for k in range(1, n_tensor)]
            return [small_copies((at.s, at.d, tt), n_hops + k, False) for k, tt in enumerate(other)]
        return [small_copies(at.sibling(), n_hops + n_tensor - 1, True)]

    def small_take(stage):
        sent = small_send(stage)
        for copies in sent:
            for copy in copies:
                copy.wait()
        if stage <= n_hops:
            for mine, came_in in small:
                total = mine[at.s]
                for slot in range(stage, stage + len(sent)):
                    total = total + came_in[slot]
                mine[at.s] = total

    def small_step(tick):
        for stage in range(n_hops + 3):

            @pl.when(tick == 1 + 2 * stage)
            def _():
                if stage:
                    small_take(stage - 1)
                if stage < n_hops + 2:
                    for copies in small_send(stage):
                        for copy in copies:
                            copy.start()

    lags = gather_lags(len(slot_sizes(n_dp, n_tensor)))
    pace = n_tensor // n_sub
    base = max(lags) + (n_sub - 1) * pace + 1
    n_phases = n_all - 1
    settle = max(lags) + n_tensor
    n_ticks = base + n_phases * n_tensor

    def finish(i):
        groups, _ = steps(i, False)
        for g in groups:
            g()

    def load(i, k, par):
        return pltpu.make_async_copy(out.at[i // n_blk, i % n_blk, k], w_buf.at[par], load_sem.at[par])

    def stores(i, k, par):
        sec, b = i // n_blk, i % n_blk
        if b == 0:
            pairs = [
                (qkv_st.at[par], qkv_out.at[sec, k], store_sem.at[par, 0]),
                (p_st.at[par], p_out.at[sec, k], store_sem.at[par, 1]),
                (heads_st.at[par], heads_out.at[sec, k], store_sem.at[par, 2]),
            ]
        elif b == 1:
            pairs = [(slope_st.at[par], slope_out.at[sec, k], store_sem.at[par, 3])]
        else:
            pairs = []
        return [pltpu.make_async_copy(*pair) for pair in pairs]

    def store_active(sec, k):
        return pltpu.make_async_copy(active_st.at[k], active_out.at[sec, k], active_sem.at[k])

    def store_middle(sec):
        return pltpu.make_async_copy(middle_st, middle_out.at[sec], once_sem.at[0])

    def store_rows(sec):
        return pltpu.make_async_copy(row_buf.at[sec], row_out.at[sec], once_sem.at[1 + sec])

    def attn_step(sec, k, par):
        @pl.when(k == 0)
        def _():
            values = (rows if sec == 0 else row_buf.at[sec - 1])[...].astype(F32)
            unit, _ = unit_rows(values)
            normed[...] = (unit * vec[sec, 0:1] + vec[sec, 1:2]).astype(BF16)
            acc[...] = values + vec[sec, 2:3]

        mixed = (dot(normed[...], w_buf[par, :, : 3 * part]) + qkv_bias[sec, k]).astype(BF16)
        qkv_st[par] = mixed
        keep = lax.broadcasted_iota(jnp.int32, (ROWS, ROWS), 0) < SEQ
        per_image = []
        for image in range(images):
            here = mixed[image * ROWS : (image + 1) * ROWS]
            per_head = []
            for head in range(n_heads):
                q, key, v = (
                    here[:, c * part + head * DH : c * part + (head + 1) * DH] for c in range(3)
                )
                scores = jnp.where(keep, dot_cols(key, q) * DH**-0.5, -1e30)
                scores = jnp.exp(scores - jnp.max(scores, axis=0, keepdims=True))
                total = jnp.sum(scores, axis=0, keepdims=True)
                chances = (scores * (1.0 / total)).astype(BF16)
                p_st[par, image, head] = chances
                per_head.append(dot(v.T, chances).T.astype(BF16))
            per_image.append(jnp.concatenate(per_head, axis=1))
        heads = jnp.concatenate(per_image, axis=0)
        heads_st[par] = heads
        acc[...] += dot_cols(heads, w_buf[par, :, 3 * part :])

    def up_step(sec, k, par):
        @pl.when(k == 0)
        def _():
            if sec:
                store_middle(sec - 1).wait()
            middle = acc[...]
            middle_st[...] = middle
            unit, _ = unit_rows(middle)
            normed[...] = (unit * vec[sec, 3:4] + vec[sec, 4:5]).astype(BF16)
            acc[...] = middle + vec[sec, 5:6]
            store_middle(sec).start()

        if sec:
            store_active(sec - 1, k).wait()
        hidden = dot(normed[...], w_buf[par]) + up_bias[sec, k]
        active, slope = gelu_parts(hidden)
        active_st[k] = active.astype(BF16)
        slope_st[par] = slope.astype(BF16)
        store_active(sec, k).start()

    def down_step(sec, k, par):
        acc[...] += dot_cols(active_st[k], w_buf[par])

        @pl.when(k == n_tensor - 1)
        def _():
            row_buf[sec] = (acc[...] * live[...]).astype(BF16)
            store_rows(sec).start()

    def await_block(i):
        sec, b = i // n_blk, i % n_blk
        for each in range(i * n_sub, (i + 1) * n_sub):
            for group, ref in (
                (0, out.at[sec, b, pl.ds(0, n_tensor - 1), pl.ds(0, sub), pl.ds(0, half)]),
                (1, out.at[sec, b, :, pl.ds(0, (n_dp - 1) * sub), pl.ds(0, half)]),
            ):
                pltpu.make_async_copy(ref, ref, part_sem.at[each, group]).wait()

    def compute(i, k):
        sec, b = i // n_blk, i % n_blk
        par = lax.rem(k, 2)

        if i == 0:

            @pl.when(k == 0)
            def _():
                await_block(0)
                load(0, 0, 0).start()

        if sec and b < 2:

            @pl.when(k == 0)
            def _():
                for back in (n_tensor - 2, n_tensor - 1):
                    for copy in stores(i - n_blk, back, back % 2):
                        copy.wait()

        load(i, k, par).wait()

        @pl.when(k < n_tensor - 1)
        def _():
            load(i, k + 1, 1 - par).start()

        if b < 2:

            @pl.when(k >= 2)
            def _():
                for copy in stores(i, k - 2, par):
                    copy.wait()

        (attn_step, up_step, down_step)[b](sec, k, par)
        for copy in stores(i, k, par):
            copy.start()

        @pl.when(k == n_tensor - 1)
        def _():
            if i + 1 < n_all:
                await_block(i + 1)
            if i + 1 < n_phases:
                load(i + 1, 0, 0).start()

    def body(it, carry):
        for g, lag in sorted(enumerate(lags), key=lambda item: item[1]):
            i = lax.div(it - lag, pace)

            @pl.when(jnp.logical_and(it - lag == i * pace, jnp.logical_and(it >= lag, i < n_pieces)))
            def _():
                run_group(i, g)

        small_step(it)
        i = lax.div(it - settle, pace)

        @pl.when(jnp.logical_and(it - settle == i * pace, jnp.logical_and(it >= settle, i < n_pieces)))
        def _():
            finish(i)

        for i in range(n_phases):
            first = base + i * n_tensor

            @pl.when(jnp.logical_and(it >= first, it < first + n_tensor))
            def _():
                compute(i, it - first)

        return carry

    def run_group(i, g):
        groups, slots = steps(i, True)
        for _ in range(sum(slot_sizes(n_dp, n_tensor)[:g])):
            next(slots)
        groups[g]()

    lax.fori_loop(0, n_ticks, body, 0)
    for i in range(n_pieces):
        if settle + i * pace >= n_ticks:
            finish(i)
    for b in range(n_blk):
        share(b).wait_send()
    last = n_section - 1
    for b in range(2):
        for back in (n_tensor - 2, n_tensor - 1):
            for copy in stores(last * n_blk + b, back, back % 2):
                copy.wait()
    for k in range(n_tensor):
        store_active(last, k).wait()
    store_middle(last).wait()
    for sec in range(last):
        store_rows(sec).wait()


def gather_lags(n_groups):
    known = [0, 3, 6, 7, 10, 11, 13, 16, 17]
    return [known[g] if g < len(known) else known[-1] + 3 * (g - len(known) + 1) for g in range(n_groups)]


def gather_and_forward(shard, rows, live, given, n_section, n_dp, n_tensor):
    n_blk, depth, span = shard.shape
    n_rows, width = rows.shape
    images = n_rows // ROWS
    part = width // n_tensor
    n_heads = part // DH
    n_pieces = n_section * n_blk * sub_blocks(depth)
    n_hops = n_dp.bit_length() - 1
    n_sends = sum(slot_sizes(n_dp, n_tensor))
    n_small = n_hops + n_tensor
    shape = jax.ShapeDtypeStruct
    hbm = pl.BlockSpec(memory_space=pl.ANY)
    vmem = pl.BlockSpec(memory_space=pltpu.VMEM)
    dma = pltpu.SemaphoreType.DMA
    return pl.pallas_call(
        functools.partial(forward_kernel, n_dp, n_tensor, images),
        out_shape=[
            shape((n_section, n_blk, n_tensor, width, span), BF16),
            shape((n_section - 1, n_rows, width), BF16),
            shape((n_section, n_tensor, n_rows, 3 * part), BF16),
            shape((n_section, n_tensor, images, n_heads, ROWS, ROWS), BF16),
            shape((n_section, n_tensor, n_rows, part), BF16),
            shape((n_section, n_rows, width), F32),
            shape((n_section, n_tensor, n_rows, span), BF16),
            shape((n_section, n_tensor, n_rows, span), BF16),
            shape((n_section, 6, width), F32),
        ],
        in_specs=[hbm] + [vmem] * (2 + len(given)),
        out_specs=[hbm] * 8 + [vmem],
        scratch_shapes=[
            pltpu.VMEM((2, width, span), BF16),
            pltpu.VMEM((2, n_rows, 3 * part), BF16),
            pltpu.VMEM((2, images, n_heads, ROWS, ROWS), BF16),
            pltpu.VMEM((2, n_rows, part), BF16),
            pltpu.VMEM((n_tensor, n_rows, span), BF16),
            pltpu.VMEM((2, n_rows, span), BF16),
            pltpu.VMEM((n_rows, width), F32),
            pltpu.VMEM((n_rows, width), BF16),
            pltpu.VMEM((n_rows, width), F32),
            pltpu.VMEM((n_section - 1, n_rows, width), BF16),
            pltpu.VMEM((n_section, n_tensor, 1, 3 * part), F32),
            pltpu.VMEM((n_section, n_tensor, 1, span), F32),
            pltpu.VMEM((n_small, 6, width), F32),
            pltpu.VMEM((n_small, n_tensor, 1, 3 * part), F32),
            pltpu.VMEM((n_small, n_tensor, 1, span), F32),
            dma((3, n_blk)),
            dma((n_pieces, n_dp * n_tensor)),
            dma((n_pieces, n_sends)),
            dma((n_pieces, 2)),
            dma((2,)),
            dma((2, 4)),
            dma((n_tensor,)),
            dma((1 + n_section,)),
            dma((2, n_small, 3)),
        ],
        compiler_params=pltpu.CompilerParams(
            collective_id=0, has_side_effects=True, vmem_limit_bytes=56 * 1024 * 1024
        ),
    )(shard, rows, live, *given)


class Slots:
    def __init__(self, n_dp, n_tensor):
        self.n_tensor = n_tensor
        bits = [b for b in range(n_dp.bit_length()) if (1 << b) < n_dp]
        mid = n_tensor // 2
        count = len(bits) * n_tensor
        self.line = count
        count += n_tensor + 1
        self.hops = {}
        self.cross = {}
        for e in range(1, n_dp):
            if bin(e).count("1") >= 2:
                self.cross[e] = count
                count += n_tensor
            for j in range(mid):
                for b in bits:
                    if not e >> b & 1:
                        chosen = [c for c in bits if (e | 1 << b) >> c & 1]
                        if chosen[j % len(chosen)] == b:
                            self.hops[e, j, b] = count
                            count += 1
        self.count = count


def reduce_lags(n_groups):
    known = [0, 0, 2, 5, 5, 6, 12, 19]
    return [known[g] if g < len(known) else known[-1] + 3 * (g - len(known) + 1) for g in range(n_groups)]


def backward_kernel(
    n_dp, n_tensor, images, weights, cotangent, live, vec, *refs
):
    first_rows, row_out, *saved = refs[:8]
    (
        out, sec_rows, sec_grads, d_vec, d_qkv_bias, d_up_bias,
        own, came, final, vec_in, qkv_bias_in, up_bias_in, ring, stage, w_buf, active_buf, slope_buf, qkv_buf, p_buf, heads_buf, rows_buf, middle_buf,
        grad_out, last_rows, grad_low, left_t, right_t, acc, grad_mid,
        load_sem, stage_sem, credit, recv_sem, send_sem, out_sem, small_sem, row_sem,
    ) = refs[8:]
    at = Place(n_dp, n_tensor)
    slots = Slots(n_dp, n_tensor)
    n_section, n_blk = weights.shape[:2]
    n_all = n_section * n_blk
    sub, half = final.shape[1:]
    n_pieces = final.shape[0]
    n_sub = n_pieces // n_all
    depth = sub * n_sub
    part = vec.shape[2] // n_tensor
    n_heads = part // DH
    lanes = pl.ds(pl.multiple_of(at.s * half, 128), half)
    sizes = send_sizes(n_dp, n_tensor)
    at.meet()

    def place(i):
        block = lax.div(i, n_sub)
        return n_section - 1 - lax.div(block, n_blk), n_blk - 1 - lax.rem(block, n_blk)

    def steps(i, start):
        counter = iter(range(10_000))

        def rows(e):
            return pl.multiple_of(at.away(e) * depth + lax.rem(i, n_sub) * sub, 16)

        def piece(e, tt):
            return own.at[lax.div(i, n_sub), tt, pl.ds(rows(e), sub), :]

        def maybe(cond, action):
            if cond is None:
                action()
            else:
                pl.when(cond)(action)

        def remote(e, tt, device, slot):
            k = next(counter)
            return pltpu.make_async_remote_copy(
                src_ref=piece(e, tt),
                dst_ref=came.at[i, slot],
                send_sem=send_sem.at[i, k],
                recv_sem=recv_sem.at[i, slot],
                device_id=device,
                device_id_type=MESH_ID,
            )

        def send(e, tt, device, slot, cond=None):
            copy = remote(e, tt, device, slot)
            maybe(cond, copy.start if start else copy.wait_send)

        def arrive(slot, cond=None):
            if start:
                copy = pltpu.make_async_copy(came.at[i, slot], came.at[i, slot], recv_sem.at[i, slot])
                maybe(cond, copy.wait)

        def total(e, tt, arrived, target=None):
            if not start or (target is None and not arrived):
                return
            base = rows(e)

            def chunk(c, carry):
                here = pl.ds(pl.multiple_of(base + c * CHUNK_ROWS, 16), CHUNK_ROWS)
                local = pl.ds(pl.multiple_of(c * CHUNK_ROWS, 16), CHUNK_ROWS)
                acc = own[lax.div(i, n_sub), tt, here, :].astype(jnp.float32)
                for slot in arrived:
                    acc = acc + came[i, slot, local, :].astype(jnp.float32)
                if target is None:
                    own[lax.div(i, n_sub), tt, here, :] = acc.astype(own.dtype)
                else:
                    target[i, local, :] = acc
                return carry

            lax.fori_loop(0, sub // CHUNK_ROWS, chunk, 0)

        def more(e, tt, slot, target=None):
            base = rows(e)

            def chunk(c, carry):
                here = pl.ds(pl.multiple_of(base + c * CHUNK_ROWS, 16), CHUNK_ROWS)
                local = pl.ds(pl.multiple_of(c * CHUNK_ROWS, 16), CHUNK_ROWS)
                acc = came[i, slot, local, :].astype(jnp.float32)
                if target is None:
                    own[lax.div(i, n_sub), tt, here, :] = (own[lax.div(i, n_sub), tt, here, :].astype(jnp.float32) + acc).astype(own.dtype)
                else:
                    target[i, local, :] = target[i, local, :] + acc
                return carry

            lax.fori_loop(0, sub // CHUNK_ROWS, chunk, 0)

        def also(e, tt, slot, cond, target=None):
            if start:

                def add():
                    arrive(slot)
                    more(e, tt, slot, target)

                pl.when(cond)(add)

        def line_slot(tt, from_next):
            return slots.line + tt + (0 if from_next else 1)

        def crossing():
            for e in range(1, n_dp):
                if bin(e).count("1") >= 2:
                    for j in range(at.mid):
                        tt = at.other_side(j)
                        slot = slots.cross[e] + tt
                        total(e, tt, [])
                        is_upper = at.t >= at.mid
                        also(e, tt, slot, jnp.logical_and(is_upper, at.has_next))
                        also(e, tt, slot, jnp.logical_and(jnp.logical_not(is_upper), at.has_prev))
                        send(e, tt, at.along(-1), slot, is_upper)
                        send(e, tt, at.along(1), slot, jnp.logical_not(is_upper))

        def leaves():
            for j in range(at.mid):
                for e in at.by_weight(1):
                    tt = at.other_side(j)
                    b = at.last_bit(e, j)
                    total(e, tt, [])
                    send(e, tt, at.hop(b), b * n_tensor + tt)

        def plane(weight):
            for e in at.by_weight(weight):
                for j in range(at.mid):
                    tt = at.own_side(j)
                    b = at.last_bit(e, j)
                    arrived = [slots.hops[e, j, c] for c in at.bits if (e, j, c) in slots.hops]
                    for slot in arrived:
                        arrive(slot)
                    total(e, tt, arrived)
                    if weight >= 2:
                        slot = slots.cross[e] + tt
                        also(e, tt, slot, at.t == at.mid - 1)
                        also(e, tt, slot, at.t == at.mid)
                    rest = e & ~(1 << b)
                    there = b * n_tensor + tt if rest == 0 else slots.hops[rest, j, b]
                    send(e, tt, at.hop(b), there)

        def column(k):
            low, high = at.t >= k, at.t + k < n_tensor
            for tt, cond, step, chain, from_next in (
                (at.t - k, low, -1, jnp.logical_and(low, at.has_next), True),
                (at.t + k, high, 1, jnp.logical_and(high, at.has_prev), False),
            ):
                arrived = [b * n_tensor + tt for b in at.bits]

                def sums(tt=tt, arrived=arrived):
                    for slot in arrived:
                        arrive(slot)
                    total(0, tt, arrived)

                if start:
                    pl.when(cond)(sums)
                slot = line_slot(tt, from_next)
                also(0, tt, slot, chain)
                send(0, tt, at.along(step), slot, cond)

        def last():
            arrived = [b * n_tensor + at.t for b in at.bits]
            for slot in arrived:
                arrive(slot)
            total(0, at.t, arrived, final)
            also(0, at.t, line_slot(at.t, True), at.has_next, final)
            also(0, at.t, line_slot(at.t, False), at.has_prev, final)
            sec, b = place(i)
            there = out.at[b, pl.ds(pl.multiple_of(lax.rem(i, n_sub) * sub, 16), sub), lanes]
            stay = pltpu.make_async_copy(final.at[i], there, out_sem.at[0, i])
            go = pltpu.make_async_remote_copy(
                src_ref=final.at[i],
                dst_ref=there,
                send_sem=out_sem.at[1, i],
                recv_sem=out_sem.at[2, i],
                device_id=at.sibling(),
                device_id_type=MESH_ID,
            )

            @pl.when(sec == at.s)
            def _():
                if start:
                    stay.start()
                else:
                    stay.wait()

            @pl.when(sec != at.s)
            def _():
                if start:
                    go.start()
                else:
                    go.wait_send()

        groups = [crossing, leaves]
        groups += [functools.partial(plane, w) for w in range(len(at.bits), 0, -1)]
        groups += [functools.partial(column, k) for k in range(n_tensor - 1, 0, -1)] + [last]
        return groups, counter

    lags = reduce_lags(len(sizes))

    def run_group(i, g):
        groups, counter = steps(i, True)
        for _ in range(sum(sizes[:g])):
            next(counter)
        groups[g]()

    phases = [(kind, sec) for sec in range(n_section - 1, -1, -1) for kind in ("down", "up", "attn")]
    phases.append(("out", n_section - 1))

    def loads(phase, k, par):
        kind, sec = phases[phase]
        rows = first_rows if sec == 0 else row_out.at[sec - 1]
        qkv, p, heads, middle, active, slope = (ref.at[sec] for ref in saved)
        if kind == "down":
            pairs = [(active.at[k], active_buf.at[par])]
            once = (middle, middle_buf)
        elif kind == "up":
            pairs = [
                (weights.at[sec, 1, k], w_buf.at[par, 0]),
                (weights.at[sec, 2, k], w_buf.at[par, 1]),
                (slope.at[k], slope_buf.at[par]),
            ]
            once = (rows, rows_buf)
        elif kind == "out":
            pairs = [(active.at[k], active_buf.at[par]), (weights.at[sec, 2, k], w_buf.at[par, 0])]
            once = (middle, middle_buf)
        else:
            pairs = [
                (weights.at[sec, 0, k], w_buf.at[par, 0]),
                (qkv.at[k], qkv_buf.at[par]),
                (p.at[k], p_buf.at[par]),
                (heads.at[k], heads_buf.at[par]),
            ]
            once = None
        copies = [
            pltpu.make_async_copy(src, dst, load_sem.at[par, n]) for n, (src, dst) in enumerate(pairs)
        ]
        return copies, lambda: pltpu.make_async_copy(*once, load_sem.at[0, 4])

    def start_loads(phase, k, par, is_first):
        copies, once = loads(phase, k, par)
        for copy in copies:
            copy.start()
        if is_first and phases[phase][0] != "attn":
            once().start()

    def shared(k):
        return pltpu.make_async_remote_copy(
            src_ref=stage.at[k],
            dst_ref=ring.at[k],
            send_sem=stage_sem.at[0, k],
            recv_sem=stage_sem.at[1, k],
            device_id=at.sibling(),
            device_id_type=MESH_ID,
        )

    def before_emit(k):
        shared(k).wait_send()
        pl.semaphore_wait(credit.at[k], 1)

    def emit(phase, k, low, high):
        first = at.s == 0
        own[phase, k] = jnp.where(first, low, high)
        stage[k] = jnp.where(first, high, low)

    def consume(phase, k, is_last):
        shared(k).wait_recv()

        def chunk(c, carry):
            here = pl.ds(pl.multiple_of(c * 96, 96), 96)
            total = own[phase, k, here].astype(F32) + ring[k, here].astype(F32)
            own[phase, k, here] = total.astype(own.dtype)
            return carry

        lax.fori_loop(0, own.shape[2] // 96, chunk, 0)
        if not is_last:
            pl.semaphore_signal(
                credit.at[k], inc=1, device_id=at.sibling(), device_id_type=MESH_ID
            )

    def column_sum(values):
        return jnp.sum(values, axis=0, keepdims=True)

    def down_step(sec, k, par, emits):
        @pl.when(k == 0)
        def _():
            source = cotangent if sec == n_section - 1 else grad_out.at[sec + 1]
            low = (source[...].astype(F32) * live[...]).astype(BF16)
            grad_low[...] = low
            left_t[...] = low.T

        d_down = dot(left_t[...], active_buf[par]).astype(BF16)
        emits(d_down[:, :half], d_down[:, half:])

    def out_step(sec, k, par):
        @pl.when(k == 0)
        def _():
            acc[...] = middle_buf[...] + vec[sec, 5:6]

        acc[...] += dot_cols(active_buf[par], w_buf[par, 0])

        @pl.when(k == n_tensor - 1)
        def _():
            last_rows[sec] = (acc[...] * live[...]).astype(BF16)
            for done in range(n_section - 1):
                pltpu.make_async_copy(row_out.at[done], last_rows.at[done], row_sem.at[2, 0]).wait()
            for each in range(n_section):
                at.hand_out(last_rows, sec_rows, each, row_sem.at[1])

    def up_step(sec, k, par, emits):
        @pl.when(k == 0)
        def _():
            unit, _ = unit_rows(middle_buf[...])
            right_t[...] = (unit * vec[sec, 3:4] + vec[sec, 4:5]).astype(BF16).T
            acc[...] = jnp.zeros_like(acc)

        grad_hidden = (dot(grad_low[...], w_buf[par, 1]) * slope_buf[par].astype(F32)).astype(BF16)
        d_up_bias[sec, k] = column_sum(grad_hidden.astype(F32))
        d_up = dot(right_t[...], grad_hidden).astype(BF16)
        emits(d_up[:, :half], d_up[:, half:])
        acc[...] += dot_cols(grad_hidden, w_buf[par, 0])

    def attn_step(sec, k, par, emits):
        w_attn = w_buf.at[par, 0]

        @pl.when(k == 0)
        def _():
            unit, scale = unit_rows(middle_buf[...])
            grad_norm = acc[...]
            low = grad_low[...].astype(F32)
            mid = low + unit_rows_back(grad_norm * vec[sec, 3:4], unit, scale)
            grad_mid[...] = mid
            d_vec[sec, 2:3] = column_sum(mid)
            d_vec[sec, 3:4] = column_sum(grad_norm * unit)
            d_vec[sec, 4:5] = column_sum(grad_norm)
            d_vec[sec, 5:6] = column_sum(low)
            mid = mid.astype(BF16)
            grad_low[...] = mid
            left_t[...] = mid.T
            unit, _ = unit_rows(rows_buf[...].astype(F32))
            right_t[...] = (unit * vec[sec, 0:1] + vec[sec, 1:2]).astype(BF16).T
            acc[...] = jnp.zeros_like(acc)

        d_out = dot(left_t[...], heads_buf[par]).astype(BF16)
        grad_heads = dot(grad_low[...], w_attn[:, 3 * part :]).astype(BF16)
        per_image = []
        for image in range(images):
            span = slice(image * ROWS, (image + 1) * ROWS)
            per_head = [[], [], []]
            for head in range(n_heads):
                q, key, v = (
                    qkv_buf[par, span, c * part + head * DH : c * part + (head + 1) * DH]
                    for c in range(3)
                )
                grad_o = grad_heads[span, head * DH : (head + 1) * DH]
                chosen = p_buf[par, image, head]
                chances = chosen.astype(F32)
                grad_chances = dot_cols(v, grad_o)
                along = jnp.sum(chances * grad_chances, axis=0, keepdims=True)
                grad_scores = (chances * (grad_chances - along)).astype(BF16)
                per_head[0].append((dot(key.T, grad_scores).T * DH**-0.5).astype(BF16))
                per_head[1].append((dot(grad_scores, q) * DH**-0.5).astype(BF16))
                per_head[2].append(dot(chosen, grad_o).astype(BF16))
            per_image.append(jnp.concatenate(per_head[0] + per_head[1] + per_head[2], axis=1))
        grad_mixed = jnp.concatenate(per_image, axis=0)
        d_qkv_bias[sec, k] = column_sum(grad_mixed.astype(F32))
        d_qkv = dot(right_t[...], grad_mixed).astype(BF16)
        emits(d_qkv[:, :half], jnp.concatenate([d_qkv[:, half:], d_out], axis=1))
        acc[...] += dot_cols(grad_mixed, w_attn[:, : 3 * part])

        @pl.when(k == n_tensor - 1)
        def _():
            unit, scale = unit_rows(rows_buf[...].astype(F32))
            grad_norm = acc[...]
            d_vec[sec, 0:1] = column_sum(grad_norm * unit)
            d_vec[sec, 1:2] = column_sum(grad_norm)
            total = grad_mid[...] + unit_rows_back(grad_norm * vec[sec, 0:1], unit, scale)
            grad_out[sec] = total.astype(BF16)
            at.hand_out(grad_out, sec_grads, sec, row_sem.at[0])

    def compute(phase, k):
        kind, sec = phases[phase]
        par = lax.rem(k, 2)
        copies, once = loads(phase, k, par)
        for copy in copies:
            copy.wait()

        if kind != "attn":

            @pl.when(k == 0)
            def _():
                once().wait()

        @pl.when(k < n_tensor - 1)
        def _():
            start_loads(phase, k + 1, 1 - par, False)

        if phase + 1 < len(phases):

            @pl.when(k == n_tensor - 1)
            def _():
                start_loads(phase + 1, 0, 0, True)

        if kind == "out":
            out_step(sec, k, par)

            @pl.when(k == 0)
            def _():
                for back in (n_tensor - 2, n_tensor - 1):
                    consume(phase - 1, back, True)

            return

        if phase:
            before_emit(k)

        if phase == 0:

            @pl.when(k == 0)
            def _():
                for done in range(n_section - 1):
                    pltpu.make_async_copy(
                        row_out.at[done], last_rows.at[done], row_sem.at[2, 0]
                    ).start()

        def emits(low, high):
            emit(phase, k, low, high)

        {"down": down_step, "up": up_step, "attn": attn_step}[kind](sec, k, par, emits)
        shared(k).start()

        @pl.when(k >= 2)
        def _():
            consume(phase, k - 2, phase == n_all - 1)

        if phase:

            @pl.when(k == 0)
            def _():
                for back in (n_tensor - 2, n_tensor - 1):
                    consume(phase - 1, back, False)

    n_busy = n_all * n_tensor
    settle = max(lags) + 2
    short = n_tensor // 2
    per_section = short + 2 * n_tensor

    def tick_of(it):
        sec, step = lax.div(it, n_blk * n_tensor), lax.rem(it, n_blk * n_tensor)
        is_short = step < n_tensor
        tick = sec * per_section + jnp.where(is_short, lax.div(step, 2), step - n_tensor + short)
        over = it >= len(phases) * n_tensor
        tick = jnp.where(over, n_section * per_section + short + it - len(phases) * n_tensor, tick)
        return tick, jnp.logical_or(over, jnp.logical_or(jnp.logical_not(is_short), lax.rem(step, 2) == 1))

    def start_of(i):
        block, within = i // n_sub, i % n_sub
        sec, b = block // n_blk, block % n_blk
        first = sec * per_section + (short, short + n_tensor, per_section)[b]
        return first + (2 if i == 1 else 0) + within

    def piece_at(tick):
        found, starts = 0, False
        for i in range(n_pieces):
            here = tick == start_of(i)
            found = jnp.where(here, i, found)
            starts = jnp.logical_or(starts, here)
        return found, starts


    small = [(d_vec, vec_in), (d_qkv_bias, qkv_bias_in), (d_up_bias, up_bias_in)]
    n_hops = len(at.bits)

    def small_copies(stage, device, slot):
        sec = 1 - at.s if stage == 0 else at.s
        return [
            pltpu.make_async_remote_copy(
                src_ref=mine.at[sec],
                dst_ref=came_in.at[slot],
                send_sem=small_sem.at[0, slot, n],
                recv_sem=small_sem.at[1, slot, n],
                device_id=device,
                device_id_type=MESH_ID,
            )
            for n, (mine, came_in) in enumerate(small)
        ]

    def small_send(stage):
        if stage == 0:
            return [small_copies(0, at.sibling(), 0)]
        if stage <= n_hops:
            return [small_copies(stage, at.hop(stage - 1), stage)]
        other = [lax.rem(at.t + k, n_tensor) for k in range(1, n_tensor)]
        return [
            small_copies(stage, (at.s, at.d, tt), n_hops + 1 + k) for k, tt in enumerate(other)
        ]

    def small_take(stage):
        sent = small_send(stage)
        for copies in sent:
            for copy in copies:
                copy.wait()
        first = stage if stage <= n_hops else n_hops + 1
        for mine, came_in in small:
            total = mine[at.s]
            for slot in range(first, first + len(sent)):
                total = total + came_in[slot]
            mine[at.s] = total

    def small_step(tick):
        for stage in range(n_hops + 2):

            @pl.when(tick == SMALL_TICKS * stage)
            def _():
                if stage:
                    small_take(stage - 1)
                for copies in small_send(stage):
                    for copy in copies:
                        copy.start()

        @pl.when(tick == SMALL_TICKS * (n_hops + 2))
        def _():
            small_take(n_hops + 1)

    def finish(i):
        groups, _ = steps(i, False)
        for g in groups:
            g()
        sec, b = place(i)

        @pl.when(sec == at.s)
        def _():
            pltpu.make_async_copy(final.at[i], final.at[i], out_sem.at[2, i]).wait()

    def body(it, carry):
        for phase in range(len(phases)):

            @pl.when(lax.div(it, n_tensor) == phase)
            def _():
                compute(phase, lax.rem(it, n_tensor))

        tick, ticks = tick_of(it)
        for g, lag in sorted(enumerate(lags), key=lambda item: item[1]):
            i, starts = piece_at(tick - lag)

            @pl.when(jnp.logical_and(ticks, starts))
            def _():
                run_group(i, g)

        small_step(it - n_busy)
        i, starts = piece_at(tick - settle)

        @pl.when(jnp.logical_and(ticks, starts))
        def _():
            finish(i)

        return carry

    start_loads(0, 0, 0, True)
    last_tick = start_of(n_pieces - 1) + max(lags)
    tail = max(last_tick + 1, n_section * per_section + short + SMALL_TICKS * (n_hops + 2)) - n_section * per_section - short
    n_ticks = len(phases) * n_tensor + tail
    last_tick = n_section * per_section + short + tail - 1
    lax.fori_loop(0, n_ticks, body, 0)
    for i in range(n_pieces):
        if start_of(i) + settle > last_tick:
            finish(i)
    for k in range(n_tensor):
        shared(k).wait_send()
    at.handed_out(grad_out, sec_grads, row_sem.at[0])
    at.handed_out(last_rows, sec_rows, row_sem.at[1])


def send_sizes(n_dp, n_tensor):
    bits = n_dp.bit_length() - 1
    mid = n_tensor // 2
    weights = [bin(e).count("1") for e in range(n_dp)]
    sizes = [2 * mid * sum(w >= 2 for w in weights), mid * bits]
    sizes += [mid * sum(w == k for w in weights) for k in range(bits, 0, -1)]
    return sizes + [2] * (n_tensor - 1) + [0]


def backward_and_reduce(weights, cotangent, live, vec, saved, n_dp):
    n_section, n_blk, n_tensor, width, span = weights.shape
    n_rows = cotangent.shape[0]
    images = n_rows // ROWS
    part = width // n_tensor
    n_all = n_section * n_blk
    depth, half = width // n_dp, span // 2
    n_pieces = n_all * sub_blocks(depth)
    sub = depth // sub_blocks(depth)
    slots = Slots(n_dp, n_tensor)
    n_sends = sum(send_sizes(n_dp, n_tensor))
    n_small = n_dp.bit_length() + n_tensor - 1
    shape = jax.ShapeDtypeStruct
    hbm = pl.BlockSpec(memory_space=pl.ANY)
    vmem = pl.BlockSpec(memory_space=pltpu.VMEM)
    dma = pltpu.SemaphoreType.DMA
    return pl.pallas_call(
        functools.partial(backward_kernel, n_dp, n_tensor, images),
        out_shape=[
            shape((n_blk, depth, span), F32),
            shape((n_section, n_rows, width), BF16),
            shape((n_section, n_rows, width), BF16),
            shape((n_section, 6, width), F32),
            shape((n_section, n_tensor, 1, 3 * part), F32),
            shape((n_section, n_tensor, 1, span), F32),
        ],
        in_specs=[hbm] + [vmem] * 3 + [hbm] * len(saved),
        out_specs=[hbm] * 3 + [vmem] * 3,
        scratch_shapes=[
            pltpu.VMEM((n_all, n_tensor, width, half), BF16),
            pltpu.VMEM((n_pieces, slots.count, sub, half), BF16),
            pltpu.VMEM((n_pieces, sub, half), F32),
            pltpu.VMEM((n_small, 6, width), F32),
            pltpu.VMEM((n_small, n_tensor, 1, 3 * part), F32),
            pltpu.VMEM((n_small, n_tensor, 1, span), F32),
            pltpu.VMEM((n_tensor, width, half), BF16),
            pltpu.VMEM((n_tensor, width, half), BF16),
            pltpu.VMEM((2, 2, width, span), BF16),
            pltpu.VMEM((2, n_rows, span), BF16),
            pltpu.VMEM((2, n_rows, span), BF16),
            pltpu.VMEM((2, n_rows, 3 * part), BF16),
            pltpu.VMEM((2, images, part // DH, ROWS, ROWS), BF16),
            pltpu.VMEM((2, n_rows, part), BF16),
            pltpu.VMEM((n_rows, width), BF16),
            pltpu.VMEM((n_rows, width), F32),
            pltpu.VMEM((n_section, n_rows, width), BF16),
            pltpu.VMEM((n_section, n_rows, width), BF16),
            pltpu.VMEM((n_rows, width), BF16),
            pltpu.VMEM((width, n_rows), BF16),
            pltpu.VMEM((width, n_rows), BF16),
            pltpu.VMEM((n_rows, width), F32),
            pltpu.VMEM((n_rows, width), F32),
            dma((2, 5)),
            dma((2, n_tensor)),
            pltpu.SemaphoreType.REGULAR((n_tensor,)),
            dma((n_pieces, slots.count)),
            dma((n_pieces, n_sends)),
            dma((3, n_pieces)),
            dma((2, n_small, 3)),
            dma((3, 3)),
        ],
        compiler_params=pltpu.CompilerParams(
            collective_id=1, has_side_effects=True, vmem_limit_bytes=64 * 1024 * 1024 - 256 * 1024
        ),
    )(weights, cotangent, live, vec, *saved)


AXES = ("section", "tensor", "dp")


def shards(
    images,
    cotangent,
    counts,
    ln1_gain,
    ln1_bias,
    q_bias,
    v_bias,
    qkv_weight,
    out_weight,
    out_bias,
    ln2_gain,
    ln2_bias,
    up_weight,
    up_bias,
    down_weight,
    down_bias,
):
    n_section, n_dp, n_tensor = (lax.axis_size(a) for a in ("section", "dp", "tensor"))
    section_idx = lax.axis_index("section")
    micro_count, share_rows, width = images.shape
    own_count = micro_count // n_section
    depth = qkv_weight.shape[1]
    part = qkv_weight.shape[3]

    own = section_idx * own_count

    def own_rows(values):
        mine = lax.dynamic_slice_in_dim(values, own, own_count, 0).reshape(-1, SEQ, values.shape[-1])
        return jnp.pad(mine, ((0, 0), (0, ROWS - SEQ), (0, 0))).reshape(-1, values.shape[-1])

    row_place = lax.axis_index("tensor") * share_rows + jnp.arange(share_rows)
    own_counts = lax.dynamic_slice_in_dim(counts, own, own_count, 0)
    live_rows = (row_place // SEQ < own_counts).astype(jnp.float32)
    live_rows = live_rows.reshape(-1, SEQ)
    live_rows = jnp.pad(live_rows, ((0, 0), (0, ROWS - SEQ))).reshape(-1, 1)

    shard = jnp.stack(
        [
            jnp.concatenate([qkv_weight[0].reshape(depth, -1), out_weight[0].T], axis=1),
            up_weight[0],
            down_weight[0].T,
        ]
    )
    given = [ln1_gain, ln1_bias, out_bias, ln2_gain, ln2_bias, down_bias, q_bias, v_bias, up_bias]
    first_rows = own_rows(images)
    gathered, row_out, *kept, vec = gather_and_forward(
        shard, first_rows, live_rows, given, n_section, n_dp, n_tensor
    )
    weight_sum, sec_rows, sec_grads, d_vec, d_qkv_bias, d_up_bias = backward_and_reduce(
        gathered, own_rows(cotangent), live_rows, vec, [first_rows, row_out, *kept], n_dp
    )

    def placed_rows(values):
        values = values.reshape(-1, ROWS, width)[:, :SEQ]
        return values.reshape(1, micro_count, share_rows, width)

    section_out = placed_rows(sec_rows)
    input_grad = placed_rows(sec_grads)

    dp_idx, tensor_idx = lax.axis_index("dp"), lax.axis_index("tensor")

    def own_heads(sums, like):
        _, heads, lanes = like.shape
        sums = sums.reshape(-1, DH)
        return lax.dynamic_slice(sums, (0, dp_idx * lanes), (heads, lanes))[None]

    d_vec, d_qkv_bias, d_up_bias = (
        lax.dynamic_index_in_dim(v, section_idx, 0, keepdims=False)
        for v in (d_vec, d_qkv_bias, d_up_bias)
    )
    q_row, _, v_row = jnp.split(
        lax.dynamic_index_in_dim(d_qkv_bias, tensor_idx, 0, keepdims=False).reshape(-1), 3
    )
    up_row = lax.dynamic_index_in_dim(d_up_bias, tensor_idx, 0, keepdims=False)
    q_sum, v_sum, up_sum = own_heads(q_row, q_bias), own_heads(v_row, v_bias), own_heads(up_row, up_bias)
    block = width // (n_dp * n_tensor)
    vec = lax.dynamic_slice_in_dim(d_vec, (dp_idx * n_tensor + tensor_idx) * block, block, 1)[None]

    return (
        section_out,
        input_grad,
        weight_sum[0, :, : 3 * part].reshape(qkv_weight.shape),
        weight_sum[0, :, 3 * part :].T[None],
        weight_sum[1][None],
        weight_sum[2].T[None],
        q_sum,
        v_sum,
        up_sum,
        vec,
    )


def solution(mesh):
    placed = (
        P(None, ("dp", "tensor"), None),
        P(None, ("dp", "tensor"), None),
        P(None, "dp"),
        P("section", "dp"),
        P("section", "dp"),
        P("section", "tensor", "dp"),
        P("section", "tensor", "dp"),
        P("section", "dp", None, "tensor"),
        P("section", "tensor", "dp"),
        P("section", "dp"),
        P("section", "dp"),
        P("section", "dp"),
        P("section", "dp", "tensor"),
        P("section", "tensor", "dp"),
        P("section", "tensor", "dp"),
        P("section", "dp"),
    )
    return jax.shard_map(
        shards,
        mesh=mesh,
        in_specs=placed,
        out_specs=(
            P("section", None, ("dp", "tensor"), None),
            P("section", None, ("dp", "tensor"), None),
            P("section", "dp", None, "tensor"),
            P("section", "tensor", "dp"),
            P("section", "dp", "tensor"),
            P("section", "tensor", "dp"),
            P("section", "tensor", "dp"),
            P("section", "tensor", "dp"),
            P("section", "tensor", "dp"),
            P("section", None, ("dp", "tensor")),
        ),
        check_vma=False,
    )
```

```python
import functools
import jax
import jax.numpy as jnp
from jax import lax
from jax.experimental import pallas as pl
from jax.experimental.pallas import tpu as pltpu
from jax.sharding import PartitionSpec as P

CHUNK_ROWS = 48
SMALL_TICKS = 2
MESH_ID = pl.DeviceIdType.MESH


def sub_blocks(depth):
    return 1


def slot_sizes(n_dp, n_tensor):
    bits = [b for b in range(n_dp.bit_length()) if (1 << b) < n_dp]
    mid = n_tensor // 2
    weights = [bin(e).count("1") for e in range(n_dp)]

    def plane(weight):
        total = 0
        for j in range(mid):
            for e in range(n_dp):
                if weights[e] == weight:
                    for b in bits:
                        if not e >> b & 1:
                            chosen = [c for c in bits if (e | 1 << b) >> c & 1]
                            total += chosen[j % len(chosen)] == b
                    total += 2 * (weight >= 2) + 1
        return total

    first = [2 + len(bits)]
    columns = [2 * (2 + len(bits))] * (n_tensor - 1)
    planes = [plane(w) for w in range(1, len(bits) + 1)]
    over = mid * sum(w >= 2 for w in weights)
    crossed = [3 * over] * (mid - 1) + [over]
    rest = [mid * sum(w == 1 for w in weights)]
    return first + [columns[0], planes[0], columns[1]] + planes[1:] + columns[2:] + crossed + rest


class Place:
    def __init__(self, n_dp, n_tensor):
        self.n_dp, self.n_tensor = n_dp, n_tensor
        self.mid = n_tensor // 2
        self.bits = [b for b in range(n_dp.bit_length()) if (1 << b) < n_dp]
        self.s = lax.axis_index("section")
        self.d = lax.axis_index("dp")
        self.t = lax.axis_index("tensor")
        self.upper = lax.div(self.t, self.mid)
        self.has_next = self.t < n_tensor - 1
        self.has_prev = self.t > 0

    def away(self, e):
        other = self.d
        for b in self.bits:
            if e >> b & 1:
                other = other + (1 << b) * (1 - 2 * lax.rem(lax.div(self.d, 1 << b), 2))
        return other

    def last_bit(self, e, j):
        chosen = [b for b in self.bits if e >> b & 1]
        return chosen[j % len(chosen)]

    def own_side(self, j):
        return self.upper * self.mid + j

    def other_side(self, j):
        return (1 - self.upper) * self.mid + j

    def sibling(self):
        return (1 - self.s, self.d, self.t)

    def along(self, step):
        return (self.s, self.d, self.t + step)

    def hop(self, b):
        return (self.s, self.away(1 << b), self.t)

    def meet(self):
        barrier = pltpu.get_barrier_semaphore()
        line = [(self.s, self.d, lax.rem(self.t + k, self.n_tensor)) for k in range(1, self.n_tensor)]
        others = [self.sibling()] + [self.hop(b) for b in self.bits] + line
        for device in others:
            pl.semaphore_signal(barrier, inc=1, device_id=device, device_id_type=MESH_ID)
        pl.semaphore_wait(barrier, len(others))

    def rows_away(self, source, target, sec, sems):
        return pltpu.make_async_remote_copy(
            src_ref=source.at[sec],
            dst_ref=target.at[self.s],
            send_sem=sems.at[1],
            recv_sem=sems.at[2],
            device_id=self.sibling(),
            device_id_type=MESH_ID,
        )

    def hand_out(self, source, target, sec, sems):
        @pl.when(sec == self.s)
        def _():
            pltpu.make_async_copy(source.at[sec], target.at[self.s], sems.at[0]).start()

        @pl.when(sec != self.s)
        def _():
            self.rows_away(source, target, sec, sems).start()

    def handed_out(self, source, target, sems):
        pltpu.make_async_copy(source.at[0], target.at[self.s], sems.at[0]).wait()
        self.rows_away(source, target, 0, sems).wait()

    def by_weight(self, weight):
        return [e for e in range(self.n_dp) if bin(e).count("1") == weight]


DH = 64
SEQ = 197
EPS = 1e-06
F32 = jnp.float32
BF16 = jnp.bfloat16
ROWS = 208


def dot(left, right):
    return jnp.dot(left, right, preferred_element_type=F32)


def dot_cols(left, right):
    return lax.dot_general(left, right, (((1,), (1,)), ((), ())), preferred_element_type=F32)


def unit_rows(values):
    average = jnp.mean(values, axis=-1, keepdims=True)
    centered = values - average
    scale = lax.rsqrt(jnp.mean(centered * centered, axis=-1, keepdims=True) + EPS)
    return centered * scale, scale


def unit_rows_back(grad_unit, unit, scale):
    along = jnp.mean(grad_unit * unit, axis=-1, keepdims=True)
    return scale * (grad_unit - jnp.mean(grad_unit, axis=-1, keepdims=True) - unit * along)


def gelu_parts(hidden):
    below = 0.5 * (1.0 + lax.erf(hidden * (0.5**0.5)))
    density = jnp.exp(-0.5 * hidden * hidden) * 0.3989422804014327
    return hidden * below, below + hidden * density


def forward_kernel(n_dp, n_tensor, images, *refs):
    (
        shard, rows, live, *given,
        out, row_out, qkv_out, p_out, heads_out, middle_out, active_out, slope_out, vec,
        w_buf, qkv_st, p_st, heads_st, active_st, slope_st, middle_st, normed, acc, row_buf,
        qkv_bias, up_bias, vec_in, qkv_bias_in, up_bias_in,
        own_sem, recv_sem, send_sem, part_sem, load_sem, store_sem, active_sem, once_sem, small_sem,
    ) = refs
    at = Place(n_dp, n_tensor)
    n_section = out.shape[0]
    n_blk, depth, span = shard.shape
    half = span // 2
    n_all = n_section * n_blk
    n_sub = sub_blocks(depth)
    sub = depth // n_sub
    n_pieces = n_all * n_sub
    part = vec.shape[2] // n_tensor
    n_heads = part // DH

    def spread(value):
        return jnp.concatenate([jnp.where(at.d == k, value, 0.0) for k in range(n_dp)], axis=1)

    def spread_heads(ref):
        values = ref[0].astype(F32)
        return jnp.concatenate([spread(values[h : h + 1]) for h in range(values.shape[0])], axis=1)

    vec[...] = jnp.zeros_like(vec)
    qkv_bias[...] = jnp.zeros_like(qkv_bias)
    up_bias[...] = jnp.zeros_like(up_bias)
    placed = jnp.concatenate([spread(ref[...].astype(F32)) for ref in given[:6]], axis=0)
    vec[at.s] = jnp.where(at.t == 0, placed, 0.0)
    q_row, v_row = spread_heads(given[6]), spread_heads(given[7])
    qkv_bias[at.s, at.t] = jnp.concatenate([q_row, jnp.zeros_like(q_row), v_row], axis=1)
    up_bias[at.s, at.t] = spread_heads(given[8])
    at.meet()

    def whole(sec, b):
        return out.at[sec, b, at.t, rows_of(0), :]

    def rows_of(e):
        return pl.ds(pl.multiple_of(at.away(e) * depth, 16), depth)

    lanes = pl.ds(pl.multiple_of(at.s * half, 128), half)

    def piece(i, e, tt):
        block = lax.div(i, n_sub)
        start = at.away(e) * depth + lax.rem(i, n_sub) * sub
        rows_here = pl.ds(pl.multiple_of(start, 16), sub)
        return out.at[lax.div(block, n_blk), lax.rem(block, n_blk), tt, rows_here, lanes]

    def share(b):
        return pltpu.make_async_remote_copy(
            src_ref=shard.at[b],
            dst_ref=whole(at.s, b),
            send_sem=own_sem.at[1, b],
            recv_sem=own_sem.at[2, b],
            device_id=at.sibling(),
            device_id_type=MESH_ID,
        )

    for b in range(n_blk):
        pltpu.make_async_copy(shard.at[b], whole(at.s, b), own_sem.at[0, b]).start()
        share(b).start()

    def push(i, e, tt, device, e_there, slot, start):
        copy = pltpu.make_async_remote_copy(
            src_ref=piece(i, e, tt),
            dst_ref=piece(i, e, tt),
            send_sem=send_sem.at[i, slot],
            recv_sem=recv_sem.at[i, e_there * n_tensor + tt],
            device_id=device,
            device_id_type=MESH_ID,
        )
        if start:
            copy.start()
        else:
            copy.wait_send()

    def push_sib(i, e, tt, slot, start):
        copy = pltpu.make_async_remote_copy(
            src_ref=piece(i, e, tt),
            dst_ref=piece(i, e, tt),
            send_sem=send_sem.at[i, slot],
            recv_sem=part_sem.at[i, 0 if e == 0 else 1],
            device_id=at.sibling(),
            device_id_type=MESH_ID,
        )
        if start:
            copy.start()
        else:
            copy.wait_send()

    def await_piece(i, e, tt):
        pltpu.make_async_remote_copy(
            src_ref=piece(i, e, tt),
            dst_ref=piece(i, e, tt),
            send_sem=send_sem.at[i, 0],
            recv_sem=recv_sem.at[i, e * n_tensor + tt],
            device_id=at.sibling(),
            device_id_type=MESH_ID,
        ).wait_recv()

    def steps(i, start):
        slots = iter(range(10_000))

        def maybe(cond, action):
            if cond is None:
                action()
            else:
                pl.when(cond)(action)

        def ready(e, tt, cond=None):
            if start:
                maybe(cond, lambda: await_piece(i, e, tt))

        def go(e, tt, device, e_there, cond=None):
            slot = next(slots)
            maybe(cond, lambda: push(i, e, tt, device, e_there, slot, start))

        def go_sib(e, tt, cond=None):
            slot = next(slots)
            maybe(cond, lambda: push_sib(i, e, tt, slot, start))

        def first():
            block = lax.div(i, n_sub)
            sec, b = lax.div(block, n_blk), lax.rem(block, n_blk)
            is_first = lax.rem(i, n_sub) == 0
            if start:

                @pl.when(jnp.logical_and(sec == at.s, is_first))
                def _():
                    pltpu.make_async_copy(shard.at[b], whole(at.s, b), own_sem.at[0, b]).wait()

                @pl.when(jnp.logical_and(sec != at.s, is_first))
                def _():
                    pltpu.make_async_remote_copy(
                        src_ref=shard.at[b],
                        dst_ref=whole(1 - at.s, b),
                        send_sem=own_sem.at[1, b],
                        recv_sem=own_sem.at[2, b],
                        device_id=at.sibling(),
                        device_id_type=MESH_ID,
                    ).wait_recv()

            go(0, at.t, at.along(1), 0, at.has_next)
            go(0, at.t, at.along(-1), 0, at.has_prev)
            for b in at.bits:
                go(0, at.t, at.hop(b), 1 << b)

        def column(k):
            low, high = at.t >= k, at.t + k < n_tensor
            for tt, cond, dev, more in (
                (at.t - k, low, at.along(1), jnp.logical_and(low, at.has_next)),
                (at.t + k, high, at.along(-1), jnp.logical_and(high, at.has_prev)),
            ):
                ready(0, tt, cond)
                go(0, tt, dev, 0, more)
                for b in at.bits:
                    go(0, tt, at.hop(b), 1 << b, cond)
                go_sib(0, tt, cond)

        def plane(weight):
            for j in range(at.mid):
                for e in at.by_weight(weight):
                    tt = at.own_side(j)
                    ready(e, tt)
                    for b in at.bits:
                        if not e >> b & 1 and at.last_bit(e | 1 << b, j) == b:
                            go(e, tt, at.hop(b), e | 1 << b)
                    if weight >= 2:
                        go(e, tt, at.along(1), e, at.t == at.mid - 1)
                        go(e, tt, at.along(-1), e, at.t == at.mid)
                    go_sib(e, tt)

        def crossed(k):
            down, up = at.t == at.mid - 1 - k, at.t == at.mid + k
            here = jnp.logical_or(down, up)
            for weight in range(2, len(at.bits) + 1):
                for e in at.by_weight(weight):
                    for j in range(at.mid):
                        tt = at.other_side(j)
                        ready(e, tt, here)
                        if k < at.mid - 1:
                            go(e, tt, at.along(1), e, up)
                            go(e, tt, at.along(-1), e, down)
                        go_sib(e, tt, here)

        def rest():
            for e in at.by_weight(1):
                for j in range(at.mid):
                    tt = at.other_side(j)
                    ready(e, tt)
                    go_sib(e, tt)

        groups = [first]
        for k in range(1, n_tensor):
            groups.append(functools.partial(column, k))
        planes = [functools.partial(plane, w) for w in range(1, len(at.bits) + 1)]
        merged = [groups[0]]
        far = [functools.partial(crossed, k) for k in range(at.mid)]
        order = [groups[1], planes[0], groups[2]] + planes[1:] + groups[3:] + far + [rest]
        return merged + order, slots


    small = [(vec, vec_in), (qkv_bias, qkv_bias_in), (up_bias, up_bias_in)]
    n_hops = len(at.bits)

    def small_copies(device, slot, to_place):
        return [
            pltpu.make_async_remote_copy(
                src_ref=mine.at[at.s],
                dst_ref=mine.at[at.s] if to_place else came_in.at[slot],
                send_sem=small_sem.at[0, slot, n],
                recv_sem=small_sem.at[1, slot, n],
                device_id=device,
                device_id_type=MESH_ID,
            )
            for n, (mine, came_in) in enumerate(small)
        ]

    def small_send(stage):
        if stage < n_hops:
            return [small_copies(at.hop(stage), stage, False)]
        if stage == n_hops:
            other = [lax.rem(at.t + k, n_tensor) for k in range(1, n_tensor)]
            return [small_copies((at.s, at.d, tt), n_hops + k, False) for k, tt in enumerate(other)]
        return [small_copies(at.sibling(), n_hops + n_tensor - 1, True)]

    def small_take(stage):
        sent = small_send(stage)
        for copies in sent:
            for copy in copies:
                copy.wait()
        if stage <= n_hops:
            for mine, came_in in small:
                total = mine[at.s]
                for slot in range(stage, stage + len(sent)):
                    total = total + came_in[slot]
                mine[at.s] = total

    def small_step(tick):
        for stage in range(n_hops + 3):

            @pl.when(tick == 1 + 2 * stage)
            def _():
                if stage:
                    small_take(stage - 1)
                if stage < n_hops + 2:
                    for copies in small_send(stage):
                        for copy in copies:
                            copy.start()

    lags = gather_lags(len(slot_sizes(n_dp, n_tensor)))
    pace = n_tensor // n_sub
    base = max(lags) + (n_sub - 1) * pace + 1
    n_phases = n_all - 1
    settle = max(lags) + n_tensor
    n_ticks = base + n_phases * n_tensor

    def finish(i):
        groups, _ = steps(i, False)
        for g in groups:
            g()

    def load(i, k, par):
        return pltpu.make_async_copy(out.at[i // n_blk, i % n_blk, k], w_buf.at[par], load_sem.at[par])

    def stores(i, k, par):
        sec, b = i // n_blk, i % n_blk
        if b == 0:
            pairs = [
                (qkv_st.at[par], qkv_out.at[sec, k], store_sem.at[par, 0]),
                (p_st.at[par], p_out.at[sec, k], store_sem.at[par, 1]),
                (heads_st.at[par], heads_out.at[sec, k], store_sem.at[par, 2]),
            ]
        elif b == 1:
            pairs = [(slope_st.at[par], slope_out.at[sec, k], store_sem.at[par, 3])]
        else:
            pairs = []
        return [pltpu.make_async_copy(*pair) for pair in pairs]

    def store_active(sec, k):
        return pltpu.make_async_copy(active_st.at[k], active_out.at[sec, k], active_sem.at[k])

    def store_middle(sec):
        return pltpu.make_async_copy(middle_st, middle_out.at[sec], once_sem.at[0])

    def store_rows(sec):
        return pltpu.make_async_copy(row_buf.at[sec], row_out.at[sec], once_sem.at[1 + sec])

    def attn_step(sec, k, par):
        @pl.when(k == 0)
        def _():
            values = (rows if sec == 0 else row_buf.at[sec - 1])[...].astype(F32)
            unit, _ = unit_rows(values)
            normed[...] = (unit * vec[sec, 0:1] + vec[sec, 1:2]).astype(BF16)
            acc[...] = values + vec[sec, 2:3]

        mixed = (dot(normed[...], w_buf[par, :, : 3 * part]) + qkv_bias[sec, k]).astype(BF16)
        qkv_st[par] = mixed
        keep = lax.broadcasted_iota(jnp.int32, (ROWS, ROWS), 0) < SEQ
        per_image = []
        for image in range(images):
            here = mixed[image * ROWS : (image + 1) * ROWS]
            per_head = []
            for head in range(n_heads):
                q, key, v = (
                    here[:, c * part + head * DH : c * part + (head + 1) * DH] for c in range(3)
                )
                scores = jnp.where(keep, dot_cols(key, q) * DH**-0.5, -1e30)
                scores = jnp.exp(scores - jnp.max(scores, axis=0, keepdims=True))
                total = jnp.sum(scores, axis=0, keepdims=True)
                chances = (scores * (1.0 / total)).astype(BF16)
                p_st[par, image, head] = chances
                per_head.append(dot(v.T, chances).T.astype(BF16))
            per_image.append(jnp.concatenate(per_head, axis=1))
        heads = jnp.concatenate(per_image, axis=0)
        heads_st[par] = heads
        acc[...] += dot_cols(heads, w_buf[par, :, 3 * part :])

    def up_step(sec, k, par):
        @pl.when(k == 0)
        def _():
            if sec:
                store_middle(sec - 1).wait()
            middle = acc[...]
            middle_st[...] = middle
            unit, _ = unit_rows(middle)
            normed[...] = (unit * vec[sec, 3:4] + vec[sec, 4:5]).astype(BF16)
            acc[...] = middle + vec[sec, 5:6]
            store_middle(sec).start()

        if sec:
            store_active(sec - 1, k).wait()
        hidden = dot(normed[...], w_buf[par]) + up_bias[sec, k]
        active, slope = gelu_parts(hidden)
        active_st[k] = active.astype(BF16)
        slope_st[par] = slope.astype(BF16)
        store_active(sec, k).start()

    def down_step(sec, k, par):
        acc[...] += dot_cols(active_st[k], w_buf[par])

        @pl.when(k == n_tensor - 1)
        def _():
            row_buf[sec] = (acc[...] * live[...]).astype(BF16)
            store_rows(sec).start()

    def await_block(i):
        sec, b = i // n_blk, i % n_blk
        for each in range(i * n_sub, (i + 1) * n_sub):
            for group, ref in (
                (0, out.at[sec, b, pl.ds(0, n_tensor - 1), pl.ds(0, sub), pl.ds(0, half)]),
                (1, out.at[sec, b, :, pl.ds(0, (n_dp - 1) * sub), pl.ds(0, half)]),
            ):
                pltpu.make_async_copy(ref, ref, part_sem.at[each, group]).wait()

    def compute(i, k):
        sec, b = i // n_blk, i % n_blk
        par = lax.rem(k, 2)

        if i == 0:

            @pl.when(k == 0)
            def _():
                await_block(0)
                load(0, 0, 0).start()

        if sec and b < 2:

            @pl.when(k == 0)
            def _():
                for back in (n_tensor - 2, n_tensor - 1):
                    for copy in stores(i - n_blk, back, back % 2):
                        copy.wait()

        load(i, k, par).wait()

        @pl.when(k < n_tensor - 1)
        def _():
            load(i, k + 1, 1 - par).start()

        if b < 2:

            @pl.when(k >= 2)
            def _():
                for copy in stores(i, k - 2, par):
                    copy.wait()

        (attn_step, up_step, down_step)[b](sec, k, par)
        for copy in stores(i, k, par):
            copy.start()

        @pl.when(k == n_tensor - 1)
        def _():
            if i + 1 < n_all:
                await_block(i + 1)
            if i + 1 < n_phases:
                load(i + 1, 0, 0).start()

    def body(it, carry):
        for g, lag in sorted(enumerate(lags), key=lambda item: item[1]):
            i = lax.div(it - lag, pace)

            @pl.when(jnp.logical_and(it - lag == i * pace, jnp.logical_and(it >= lag, i < n_pieces)))
            def _():
                run_group(i, g)

        small_step(it)
        i = lax.div(it - settle, pace)

        @pl.when(jnp.logical_and(it - settle == i * pace, jnp.logical_and(it >= settle, i < n_pieces)))
        def _():
            finish(i)

        for i in range(n_phases):
            first = base + i * n_tensor

            @pl.when(jnp.logical_and(it >= first, it < first + n_tensor))
            def _():
                compute(i, it - first)

        return carry

    def run_group(i, g):
        groups, slots = steps(i, True)
        for _ in range(sum(slot_sizes(n_dp, n_tensor)[:g])):
            next(slots)
        groups[g]()

    lax.fori_loop(0, n_ticks, body, 0)
    for i in range(n_pieces):
        if settle + i * pace >= n_ticks:
            finish(i)
    for b in range(n_blk):
        share(b).wait_send()
    last = n_section - 1
    for b in range(2):
        for back in (n_tensor - 2, n_tensor - 1):
            for copy in stores(last * n_blk + b, back, back % 2):
                copy.wait()
    for k in range(n_tensor):
        store_active(last, k).wait()
    store_middle(last).wait()
    for sec in range(last):
        store_rows(sec).wait()


def gather_lags(n_groups):
    known = [0, 3, 6, 7, 10, 11, 13, 16, 17]
    return [known[g] if g < len(known) else known[-1] + 3 * (g - len(known) + 1) for g in range(n_groups)]


def gather_and_forward(shard, rows, live, given, n_section, n_dp, n_tensor):
    n_blk, depth, span = shard.shape
    n_rows, width = rows.shape
    images = n_rows // ROWS
    part = width // n_tensor
    n_heads = part // DH
    n_pieces = n_section * n_blk * sub_blocks(depth)
    n_hops = n_dp.bit_length() - 1
    n_sends = sum(slot_sizes(n_dp, n_tensor))
    n_small = n_hops + n_tensor
    shape = jax.ShapeDtypeStruct
    hbm = pl.BlockSpec(memory_space=pl.ANY)
    vmem = pl.BlockSpec(memory_space=pltpu.VMEM)
    dma = pltpu.SemaphoreType.DMA
    return pl.pallas_call(
        functools.partial(forward_kernel, n_dp, n_tensor, images),
        out_shape=[
            shape((n_section, n_blk, n_tensor, width, span), BF16),
            shape((n_section - 1, n_rows, width), BF16),
            shape((n_section, n_tensor, n_rows, 3 * part), BF16),
            shape((n_section, n_tensor, images, n_heads, ROWS, ROWS), BF16),
            shape((n_section, n_tensor, n_rows, part), BF16),
            shape((n_section, n_rows, width), F32),
            shape((n_section, n_tensor, n_rows, span), BF16),
            shape((n_section, n_tensor, n_rows, span), BF16),
            shape((n_section, 6, width), F32),
        ],
        in_specs=[hbm] + [vmem] * (2 + len(given)),
        out_specs=[hbm] * 8 + [vmem],
        scratch_shapes=[
            pltpu.VMEM((2, width, span), BF16),
            pltpu.VMEM((2, n_rows, 3 * part), BF16),
            pltpu.VMEM((2, images, n_heads, ROWS, ROWS), BF16),
            pltpu.VMEM((2, n_rows, part), BF16),
            pltpu.VMEM((n_tensor, n_rows, span), BF16),
            pltpu.VMEM((2, n_rows, span), BF16),
            pltpu.VMEM((n_rows, width), F32),
            pltpu.VMEM((n_rows, width), BF16),
            pltpu.VMEM((n_rows, width), F32),
            pltpu.VMEM((n_section - 1, n_rows, width), BF16),
            pltpu.VMEM((n_section, n_tensor, 1, 3 * part), F32),
            pltpu.VMEM((n_section, n_tensor, 1, span), F32),
            pltpu.VMEM((n_small, 6, width), F32),
            pltpu.VMEM((n_small, n_tensor, 1, 3 * part), F32),
            pltpu.VMEM((n_small, n_tensor, 1, span), F32),
            dma((3, n_blk)),
            dma((n_pieces, n_dp * n_tensor)),
            dma((n_pieces, n_sends)),
            dma((n_pieces, 2)),
            dma((2,)),
            dma((2, 4)),
            dma((n_tensor,)),
            dma((1 + n_section,)),
            dma((2, n_small, 3)),
        ],
        compiler_params=pltpu.CompilerParams(
            collective_id=0, has_side_effects=True, vmem_limit_bytes=56 * 1024 * 1024
        ),
    )(shard, rows, live, *given)


class Slots:
    def __init__(self, n_dp, n_tensor):
        self.n_tensor = n_tensor
        bits = [b for b in range(n_dp.bit_length()) if (1 << b) < n_dp]
        mid = n_tensor // 2
        count = len(bits) * n_tensor
        self.line = count
        count += n_tensor + 1
        self.hops = {}
        self.cross = {}
        for e in range(1, n_dp):
            if bin(e).count("1") >= 2:
                self.cross[e] = count
                count += n_tensor
            for j in range(mid):
                for b in bits:
                    if not e >> b & 1:
                        chosen = [c for c in bits if (e | 1 << b) >> c & 1]
                        if chosen[j % len(chosen)] == b:
                            self.hops[e, j, b] = count
                            count += 1
        self.count = count


def reduce_lags(n_groups):
    known = [0, 0, 2, 5, 5, 6, 12, 19]
    return [known[g] if g < len(known) else known[-1] + 3 * (g - len(known) + 1) for g in range(n_groups)]


def backward_kernel(
    n_dp, n_tensor, images, weights, cotangent, live, vec, *refs
):
    first_rows, row_out, *saved = refs[:8]
    (
        out, sec_rows, sec_grads, d_vec, d_qkv_bias, d_up_bias, own_vec, own_q, own_v, own_up,
        own, came, final, vec_in, qkv_bias_in, up_bias_in, ring, stage, w_buf, active_buf, slope_buf, qkv_buf, p_buf, heads_buf, rows_buf, middle_buf,
        grad_out, last_rows, grad_low, left_t, right_t, acc, grad_mid,
        load_sem, stage_sem, credit, recv_sem, send_sem, out_sem, small_sem, row_sem,
    ) = refs[8:]
    at = Place(n_dp, n_tensor)
    slots = Slots(n_dp, n_tensor)
    n_section, n_blk = weights.shape[:2]
    n_all = n_section * n_blk
    sub, half = final.shape[1:]
    n_pieces = final.shape[0]
    n_sub = n_pieces // n_all
    depth = sub * n_sub
    part = vec.shape[2] // n_tensor
    n_heads = part // DH
    lanes = pl.ds(pl.multiple_of(at.s * half, 128), half)
    sizes = send_sizes(n_dp, n_tensor)
    at.meet()

    def place(i):
        block = lax.div(i, n_sub)
        return n_section - 1 - lax.div(block, n_blk), n_blk - 1 - lax.rem(block, n_blk)

    def steps(i, start):
        counter = iter(range(10_000))

        def rows(e):
            return pl.multiple_of(at.away(e) * depth + lax.rem(i, n_sub) * sub, 16)

        def piece(e, tt):
            return own.at[lax.div(i, n_sub), tt, pl.ds(rows(e), sub), :]

        def maybe(cond, action):
            if cond is None:
                action()
            else:
                pl.when(cond)(action)

        def remote(e, tt, device, slot):
            k = next(counter)
            return pltpu.make_async_remote_copy(
                src_ref=piece(e, tt),
                dst_ref=came.at[i, slot],
                send_sem=send_sem.at[i, k],
                recv_sem=recv_sem.at[i, slot],
                device_id=device,
                device_id_type=MESH_ID,
            )

        def send(e, tt, device, slot, cond=None):
            copy = remote(e, tt, device, slot)
            maybe(cond, copy.start if start else copy.wait_send)

        def arrive(slot, cond=None):
            if start:
                copy = pltpu.make_async_copy(came.at[i, slot], came.at[i, slot], recv_sem.at[i, slot])
                maybe(cond, copy.wait)

        def total(e, tt, arrived, target=None):
            if not start or (target is None and not arrived):
                return
            base = rows(e)

            def chunk(c, carry):
                here = pl.ds(pl.multiple_of(base + c * CHUNK_ROWS, 16), CHUNK_ROWS)
                local = pl.ds(pl.multiple_of(c * CHUNK_ROWS, 16), CHUNK_ROWS)
                acc = own[lax.div(i, n_sub), tt, here, :].astype(jnp.float32)
                for slot in arrived:
                    acc = acc + came[i, slot, local, :].astype(jnp.float32)
                if target is None:
                    own[lax.div(i, n_sub), tt, here, :] = acc.astype(own.dtype)
                else:
                    target[i, local, :] = acc
                return carry

            lax.fori_loop(0, sub // CHUNK_ROWS, chunk, 0)

        def more(e, tt, slot, target=None):
            base = rows(e)

            def chunk(c, carry):
                here = pl.ds(pl.multiple_of(base + c * CHUNK_ROWS, 16), CHUNK_ROWS)
                local = pl.ds(pl.multiple_of(c * CHUNK_ROWS, 16), CHUNK_ROWS)
                acc = came[i, slot, local, :].astype(jnp.float32)
                if target is None:
                    own[lax.div(i, n_sub), tt, here, :] = (own[lax.div(i, n_sub), tt, here, :].astype(jnp.float32) + acc).astype(own.dtype)
                else:
                    target[i, local, :] = target[i, local, :] + acc
                return carry

            lax.fori_loop(0, sub // CHUNK_ROWS, chunk, 0)

        def also(e, tt, slot, cond, target=None):
            if start:

                def add():
                    arrive(slot)
                    more(e, tt, slot, target)

                pl.when(cond)(add)

        def line_slot(tt, from_next):
            return slots.line + tt + (0 if from_next else 1)

        def crossing():
            for e in range(1, n_dp):
                if bin(e).count("1") >= 2:
                    for j in range(at.mid):
                        tt = at.other_side(j)
                        slot = slots.cross[e] + tt
                        total(e, tt, [])
                        is_upper = at.t >= at.mid
                        also(e, tt, slot, jnp.logical_and(is_upper, at.has_next))
                        also(e, tt, slot, jnp.logical_and(jnp.logical_not(is_upper), at.has_prev))
                        send(e, tt, at.along(-1), slot, is_upper)
                        send(e, tt, at.along(1), slot, jnp.logical_not(is_upper))

        def leaves():
            for j in range(at.mid):
                for e in at.by_weight(1):
                    tt = at.other_side(j)
                    b = at.last_bit(e, j)
                    total(e, tt, [])
                    send(e, tt, at.hop(b), b * n_tensor + tt)

        def plane(weight):
            for e in at.by_weight(weight):
                for j in range(at.mid):
                    tt = at.own_side(j)
                    b = at.last_bit(e, j)
                    arrived = [slots.hops[e, j, c] for c in at.bits if (e, j, c) in slots.hops]
                    for slot in arrived:
                        arrive(slot)
                    total(e, tt, arrived)
                    if weight >= 2:
                        slot = slots.cross[e] + tt
                        also(e, tt, slot, at.t == at.mid - 1)
                        also(e, tt, slot, at.t == at.mid)
                    rest = e & ~(1 << b)
                    there = b * n_tensor + tt if rest == 0 else slots.hops[rest, j, b]
                    send(e, tt, at.hop(b), there)

        def column(k):
            low, high = at.t >= k, at.t + k < n_tensor
            for tt, cond, step, chain, from_next in (
                (at.t - k, low, -1, jnp.logical_and(low, at.has_next), True),
                (at.t + k, high, 1, jnp.logical_and(high, at.has_prev), False),
            ):
                arrived = [b * n_tensor + tt for b in at.bits]

                def sums(tt=tt, arrived=arrived):
                    for slot in arrived:
                        arrive(slot)
                    total(0, tt, arrived)

                if start:
                    pl.when(cond)(sums)
                slot = line_slot(tt, from_next)
                also(0, tt, slot, chain)
                send(0, tt, at.along(step), slot, cond)

        def last():
            arrived = [b * n_tensor + at.t for b in at.bits]
            for slot in arrived:
                arrive(slot)
            total(0, at.t, arrived, final)
            also(0, at.t, line_slot(at.t, True), at.has_next, final)
            also(0, at.t, line_slot(at.t, False), at.has_prev, final)
            sec, b = place(i)
            there = out.at[b, pl.ds(pl.multiple_of(lax.rem(i, n_sub) * sub, 16), sub), lanes]
            stay = pltpu.make_async_copy(final.at[i], there, out_sem.at[0, i])
            go = pltpu.make_async_remote_copy(
                src_ref=final.at[i],
                dst_ref=there,
                send_sem=out_sem.at[1, i],
                recv_sem=out_sem.at[2, i],
                device_id=at.sibling(),
                device_id_type=MESH_ID,
            )

            @pl.when(sec == at.s)
            def _():
                if start:
                    stay.start()
                else:
                    stay.wait()

            @pl.when(sec != at.s)
            def _():
                if start:
                    go.start()
                else:
                    go.wait_send()

        groups = [crossing, leaves]
        groups += [functools.partial(plane, w) for w in range(len(at.bits), 0, -1)]
        groups += [functools.partial(column, k) for k in range(n_tensor - 1, 0, -1)] + [last]
        return groups, counter

    lags = reduce_lags(len(sizes))

    def run_group(i, g):
        groups, counter = steps(i, True)
        for _ in range(sum(sizes[:g])):
            next(counter)
        groups[g]()

    phases = [(kind, sec) for sec in range(n_section - 1, -1, -1) for kind in ("down", "up", "attn")]
    phases.append(("out", n_section - 1))

    def loads(phase, k, par):
        kind, sec = phases[phase]
        rows = first_rows if sec == 0 else row_out.at[sec - 1]
        qkv, p, heads, middle, active, slope = (ref.at[sec] for ref in saved)
        if kind == "down":
            pairs = [(active.at[k], active_buf.at[par])]
            once = (middle, middle_buf)
        elif kind == "up":
            pairs = [
                (weights.at[sec, 1, k], w_buf.at[par, 0]),
                (weights.at[sec, 2, k], w_buf.at[par, 1]),
                (slope.at[k], slope_buf.at[par]),
            ]
            once = (rows, rows_buf)
        elif kind == "out":
            pairs = [(active.at[k], active_buf.at[par]), (weights.at[sec, 2, k], w_buf.at[par, 0])]
            once = (middle, middle_buf)
        else:
            pairs = [
                (weights.at[sec, 0, k], w_buf.at[par, 0]),
                (qkv.at[k], qkv_buf.at[par]),
                (p.at[k], p_buf.at[par]),
                (heads.at[k], heads_buf.at[par]),
            ]
            once = None
        copies = [
            pltpu.make_async_copy(src, dst, load_sem.at[par, n]) for n, (src, dst) in enumerate(pairs)
        ]
        return copies, lambda: pltpu.make_async_copy(*once, load_sem.at[0, 4])

    def start_loads(phase, k, par, is_first):
        copies, once = loads(phase, k, par)
        for copy in copies:
            copy.start()
        if is_first and phases[phase][0] != "attn":
            once().start()

    def shared(k):
        return pltpu.make_async_remote_copy(
            src_ref=stage.at[k],
            dst_ref=ring.at[k],
            send_sem=stage_sem.at[0, k],
            recv_sem=stage_sem.at[1, k],
            device_id=at.sibling(),
            device_id_type=MESH_ID,
        )

    def before_emit(k):
        shared(k).wait_send()
        pl.semaphore_wait(credit.at[k], 1)

    def emit(phase, k, low, high):
        first = at.s == 0
        own[phase, k] = jnp.where(first, low, high)
        stage[k] = jnp.where(first, high, low)

    def consume(phase, k, is_last):
        shared(k).wait_recv()

        def chunk(c, carry):
            here = pl.ds(pl.multiple_of(c * 96, 96), 96)
            total = own[phase, k, here].astype(F32) + ring[k, here].astype(F32)
            own[phase, k, here] = total.astype(own.dtype)
            return carry

        lax.fori_loop(0, own.shape[2] // 96, chunk, 0)
        if not is_last:
            pl.semaphore_signal(
                credit.at[k], inc=1, device_id=at.sibling(), device_id_type=MESH_ID
            )

    def column_sum(values):
        return jnp.sum(values, axis=0, keepdims=True)

    def down_step(sec, k, par, emits):
        @pl.when(k == 0)
        def _():
            source = cotangent if sec == n_section - 1 else grad_out.at[sec + 1]
            low = (source[...].astype(F32) * live[...]).astype(BF16)
            grad_low[...] = low
            left_t[...] = low.T

        d_down = dot(left_t[...], active_buf[par]).astype(BF16)
        emits(d_down[:, :half], d_down[:, half:])

    def out_step(sec, k, par):
        @pl.when(k == 0)
        def _():
            acc[...] = middle_buf[...] + vec[sec, 5:6]

        acc[...] += dot_cols(active_buf[par], w_buf[par, 0])

        @pl.when(k == n_tensor - 1)
        def _():
            last_rows[sec] = (acc[...] * live[...]).astype(BF16)
            for done in range(n_section - 1):
                pltpu.make_async_copy(row_out.at[done], last_rows.at[done], row_sem.at[2, 0]).wait()
            for each in range(n_section):
                at.hand_out(last_rows, sec_rows, each, row_sem.at[1])

    def up_step(sec, k, par, emits):
        @pl.when(k == 0)
        def _():
            unit, _ = unit_rows(middle_buf[...])
            right_t[...] = (unit * vec[sec, 3:4] + vec[sec, 4:5]).astype(BF16).T
            acc[...] = jnp.zeros_like(acc)

        grad_hidden = (dot(grad_low[...], w_buf[par, 1]) * slope_buf[par].astype(F32)).astype(BF16)
        d_up_bias[sec, k] = column_sum(grad_hidden.astype(F32))
        d_up = dot(right_t[...], grad_hidden).astype(BF16)
        emits(d_up[:, :half], d_up[:, half:])
        acc[...] += dot_cols(grad_hidden, w_buf[par, 0])

    def attn_step(sec, k, par, emits):
        w_attn = w_buf.at[par, 0]

        @pl.when(k == 0)
        def _():
            unit, scale = unit_rows(middle_buf[...])
            grad_norm = acc[...]
            low = grad_low[...].astype(F32)
            mid = low + unit_rows_back(grad_norm * vec[sec, 3:4], unit, scale)
            grad_mid[...] = mid
            d_vec[sec, 2:3] = column_sum(mid)
            d_vec[sec, 3:4] = column_sum(grad_norm * unit)
            d_vec[sec, 4:5] = column_sum(grad_norm)
            d_vec[sec, 5:6] = column_sum(low)
            mid = mid.astype(BF16)
            grad_low[...] = mid
            left_t[...] = mid.T
            unit, _ = unit_rows(rows_buf[...].astype(F32))
            right_t[...] = (unit * vec[sec, 0:1] + vec[sec, 1:2]).astype(BF16).T
            acc[...] = jnp.zeros_like(acc)

        d_out = dot(left_t[...], heads_buf[par]).astype(BF16)
        grad_heads = dot(grad_low[...], w_attn[:, 3 * part :]).astype(BF16)
        per_image = []
        for image in range(images):
            span = slice(image * ROWS, (image + 1) * ROWS)
            per_head = [[], [], []]
            for head in range(n_heads):
                q, key, v = (
                    qkv_buf[par, span, c * part + head * DH : c * part + (head + 1) * DH]
                    for c in range(3)
                )
                grad_o = grad_heads[span, head * DH : (head + 1) * DH]
                chosen = p_buf[par, image, head]
                chances = chosen.astype(F32)
                grad_chances = dot_cols(v, grad_o)
                along = jnp.sum(chances * grad_chances, axis=0, keepdims=True)
                grad_scores = (chances * (grad_chances - along)).astype(BF16)
                per_head[0].append((dot(key.T, grad_scores).T * DH**-0.5).astype(BF16))
                per_head[1].append((dot(grad_scores, q) * DH**-0.5).astype(BF16))
                per_head[2].append(dot(chosen, grad_o).astype(BF16))
            per_image.append(jnp.concatenate(per_head[0] + per_head[1] + per_head[2], axis=1))
        grad_mixed = jnp.concatenate(per_image, axis=0)
        d_qkv_bias[sec, k] = column_sum(grad_mixed.astype(F32))
        d_qkv = dot(right_t[...], grad_mixed).astype(BF16)
        emits(d_qkv[:, :half], jnp.concatenate([d_qkv[:, half:], d_out], axis=1))
        acc[...] += dot_cols(grad_mixed, w_attn[:, : 3 * part])

        @pl.when(k == n_tensor - 1)
        def _():
            unit, scale = unit_rows(rows_buf[...].astype(F32))
            grad_norm = acc[...]
            d_vec[sec, 0:1] = column_sum(grad_norm * unit)
            d_vec[sec, 1:2] = column_sum(grad_norm)
            total = grad_mid[...] + unit_rows_back(grad_norm * vec[sec, 0:1], unit, scale)
            grad_out[sec] = total.astype(BF16)
            at.hand_out(grad_out, sec_grads, sec, row_sem.at[0])

    def compute(phase, k):
        kind, sec = phases[phase]
        par = lax.rem(k, 2)
        copies, once = loads(phase, k, par)
        for copy in copies:
            copy.wait()

        if kind != "attn":

            @pl.when(k == 0)
            def _():
                once().wait()

        @pl.when(k < n_tensor - 1)
        def _():
            start_loads(phase, k + 1, 1 - par, False)

        if phase + 1 < len(phases):

            @pl.when(k == n_tensor - 1)
            def _():
                start_loads(phase + 1, 0, 0, True)

        if kind == "out":
            out_step(sec, k, par)

            @pl.when(k == 0)
            def _():
                for back in (n_tensor - 2, n_tensor - 1):
                    consume(phase - 1, back, True)

            return

        if phase:
            before_emit(k)

        if phase == 0:

            @pl.when(k == 0)
            def _():
                for done in range(n_section - 1):
                    pltpu.make_async_copy(
                        row_out.at[done], last_rows.at[done], row_sem.at[2, 0]
                    ).start()

        def emits(low, high):
            emit(phase, k, low, high)

        {"down": down_step, "up": up_step, "attn": attn_step}[kind](sec, k, par, emits)
        shared(k).start()

        @pl.when(k >= 2)
        def _():
            consume(phase, k - 2, phase == n_all - 1)

        if phase:

            @pl.when(k == 0)
            def _():
                for back in (n_tensor - 2, n_tensor - 1):
                    consume(phase - 1, back, False)

    n_busy = n_all * n_tensor
    settle = max(lags) + 2
    short = n_tensor // 2
    per_section = short + 2 * n_tensor

    def tick_of(it):
        sec, step = lax.div(it, n_blk * n_tensor), lax.rem(it, n_blk * n_tensor)
        is_short = step < n_tensor
        tick = sec * per_section + jnp.where(is_short, lax.div(step, 2), step - n_tensor + short)
        over = it >= len(phases) * n_tensor
        tick = jnp.where(over, n_section * per_section + short + it - len(phases) * n_tensor, tick)
        return tick, jnp.logical_or(over, jnp.logical_or(jnp.logical_not(is_short), lax.rem(step, 2) == 1))

    def start_of(i):
        block, within = i // n_sub, i % n_sub
        sec, b = block // n_blk, block % n_blk
        first = sec * per_section + (short, short + n_tensor, per_section)[b]
        return first + (2 if i == 1 else 0) + within

    def piece_at(tick):
        found, starts = 0, False
        for i in range(n_pieces):
            here = tick == start_of(i)
            found = jnp.where(here, i, found)
            starts = jnp.logical_or(starts, here)
        return found, starts


    small = [(d_vec, vec_in), (d_qkv_bias, qkv_bias_in), (d_up_bias, up_bias_in)]
    n_hops = len(at.bits)

    def small_copies(stage, device, slot):
        sec = 1 - at.s if stage == 0 else at.s
        return [
            pltpu.make_async_remote_copy(
                src_ref=mine.at[sec],
                dst_ref=came_in.at[slot],
                send_sem=small_sem.at[0, slot, n],
                recv_sem=small_sem.at[1, slot, n],
                device_id=device,
                device_id_type=MESH_ID,
            )
            for n, (mine, came_in) in enumerate(small)
        ]

    def small_send(stage):
        if stage == 0:
            return [small_copies(0, at.sibling(), 0)]
        if stage <= n_hops:
            return [small_copies(stage, at.hop(stage - 1), stage)]
        other = [lax.rem(at.t + k, n_tensor) for k in range(1, n_tensor)]
        return [
            small_copies(stage, (at.s, at.d, tt), n_hops + 1 + k) for k, tt in enumerate(other)
        ]

    def small_take(stage):
        sent = small_send(stage)
        for copies in sent:
            for copy in copies:
                copy.wait()
        first = stage if stage <= n_hops else n_hops + 1
        for mine, came_in in small:
            total = mine[at.s]
            for slot in range(first, first + len(sent)):
                total = total + came_in[slot]
            mine[at.s] = total

    def small_step(tick):
        for stage in range(n_hops + 2):

            @pl.when(tick == SMALL_TICKS * stage)
            def _():
                if stage:
                    small_take(stage - 1)
                for copies in small_send(stage):
                    for copy in copies:
                        copy.start()

        @pl.when(tick == SMALL_TICKS * (n_hops + 2))
        def _():
            small_take(n_hops + 1)
            own_small()

    def own_small():
        def pick(values, index, count, width):
            parts = [jnp.where(index == c, values[:, c * width : (c + 1) * width], 0.0) for c in range(count)]
            return functools.reduce(jnp.add, parts)

        n_places = n_dp * n_tensor
        own_vec[0] = pick(d_vec[at.s], at.d * n_tensor + at.t, n_places, own_vec.shape[2])
        qkv_row, up_row = d_qkv_bias[at.s, at.t], d_up_bias[at.s, at.t]
        for target, row in (
            (own_q, qkv_row[:, :part]),
            (own_v, qkv_row[:, 2 * part :]),
            (own_up, up_row),
        ):
            for head in range(target.shape[1]):
                lanes_of = row[:, head * DH : (head + 1) * DH]
                target[0, head : head + 1] = pick(lanes_of, at.d, n_dp, DH // n_dp)

    def finish(i):
        groups, _ = steps(i, False)
        for g in groups:
            g()
        sec, b = place(i)

        @pl.when(sec == at.s)
        def _():
            pltpu.make_async_copy(final.at[i], final.at[i], out_sem.at[2, i]).wait()

    def body(it, carry):
        for phase in range(len(phases)):

            @pl.when(lax.div(it, n_tensor) == phase)
            def _():
                compute(phase, lax.rem(it, n_tensor))

        tick, ticks = tick_of(it)
        for g, lag in sorted(enumerate(lags), key=lambda item: item[1]):
            i, starts = piece_at(tick - lag)

            @pl.when(jnp.logical_and(ticks, starts))
            def _():
                run_group(i, g)

        small_step(it - n_busy)
        i, starts = piece_at(tick - settle)

        @pl.when(jnp.logical_and(ticks, starts))
        def _():
            finish(i)

        return carry

    start_loads(0, 0, 0, True)
    last_tick = start_of(n_pieces - 1) + max(lags)
    tail = max(last_tick + 1, n_section * per_section + short + SMALL_TICKS * (n_hops + 2)) - n_section * per_section - short
    n_ticks = len(phases) * n_tensor + tail
    last_tick = n_section * per_section + short + tail - 1
    lax.fori_loop(0, n_ticks, body, 0)
    for i in range(n_pieces):
        if start_of(i) + settle > last_tick:
            finish(i)
    for k in range(n_tensor):
        shared(k).wait_send()
    at.handed_out(grad_out, sec_grads, row_sem.at[0])
    at.handed_out(last_rows, sec_rows, row_sem.at[1])


def send_sizes(n_dp, n_tensor):
    bits = n_dp.bit_length() - 1
    mid = n_tensor // 2
    weights = [bin(e).count("1") for e in range(n_dp)]
    sizes = [2 * mid * sum(w >= 2 for w in weights), mid * bits]
    sizes += [mid * sum(w == k for w in weights) for k in range(bits, 0, -1)]
    return sizes + [2] * (n_tensor - 1) + [0]


def backward_and_reduce(weights, cotangent, live, vec, saved, n_dp):
    n_section, n_blk, n_tensor, width, span = weights.shape
    n_rows = cotangent.shape[0]
    images = n_rows // ROWS
    part = width // n_tensor
    n_all = n_section * n_blk
    depth, half = width // n_dp, span // 2
    n_pieces = n_all * sub_blocks(depth)
    sub = depth // sub_blocks(depth)
    slots = Slots(n_dp, n_tensor)
    n_sends = sum(send_sizes(n_dp, n_tensor))
    n_small = n_dp.bit_length() + n_tensor - 1
    shape = jax.ShapeDtypeStruct
    hbm = pl.BlockSpec(memory_space=pl.ANY)
    vmem = pl.BlockSpec(memory_space=pltpu.VMEM)
    dma = pltpu.SemaphoreType.DMA
    return pl.pallas_call(
        functools.partial(backward_kernel, n_dp, n_tensor, images),
        out_shape=[
            shape((n_blk, depth, span), F32),
            shape((n_section, n_rows, width), BF16),
            shape((n_section, n_rows, width), BF16),
            shape((n_section, 6, width), F32),
            shape((n_section, n_tensor, 1, 3 * part), F32),
            shape((n_section, n_tensor, 1, span), F32),
            shape((1, 6, width // (n_dp * n_tensor)), F32),
            shape((1, part // DH, DH // n_dp), F32),
            shape((1, part // DH, DH // n_dp), F32),
            shape((1, span // DH, DH // n_dp), F32),
        ],
        in_specs=[hbm] + [vmem] * 3 + [hbm] * len(saved),
        out_specs=[hbm] * 3 + [vmem] * 7,
        scratch_shapes=[
            pltpu.VMEM((n_all, n_tensor, width, half), BF16),
            pltpu.VMEM((n_pieces, slots.count, sub, half), BF16),
            pltpu.VMEM((n_pieces, sub, half), F32),
            pltpu.VMEM((n_small, 6, width), F32),
            pltpu.VMEM((n_small, n_tensor, 1, 3 * part), F32),
            pltpu.VMEM((n_small, n_tensor, 1, span), F32),
            pltpu.VMEM((n_tensor, width, half), BF16),
            pltpu.VMEM((n_tensor, width, half), BF16),
            pltpu.VMEM((2, 2, width, span), BF16),
            pltpu.VMEM((2, n_rows, span), BF16),
            pltpu.VMEM((2, n_rows, span), BF16),
            pltpu.VMEM((2, n_rows, 3 * part), BF16),
            pltpu.VMEM((2, images, part // DH, ROWS, ROWS), BF16),
            pltpu.VMEM((2, n_rows, part), BF16),
            pltpu.VMEM((n_rows, width), BF16),
            pltpu.VMEM((n_rows, width), F32),
            pltpu.VMEM((n_section, n_rows, width), BF16),
            pltpu.VMEM((n_section, n_rows, width), BF16),
            pltpu.VMEM((n_rows, width), BF16),
            pltpu.VMEM((width, n_rows), BF16),
            pltpu.VMEM((width, n_rows), BF16),
            pltpu.VMEM((n_rows, width), F32),
            pltpu.VMEM((n_rows, width), F32),
            dma((2, 5)),
            dma((2, n_tensor)),
            pltpu.SemaphoreType.REGULAR((n_tensor,)),
            dma((n_pieces, slots.count)),
            dma((n_pieces, n_sends)),
            dma((3, n_pieces)),
            dma((2, n_small, 3)),
            dma((3, 3)),
        ],
        compiler_params=pltpu.CompilerParams(
            collective_id=1, has_side_effects=True, vmem_limit_bytes=64 * 1024 * 1024 - 256 * 1024
        ),
    )(weights, cotangent, live, vec, *saved)


AXES = ("section", "tensor", "dp")


def shards(
    images,
    cotangent,
    counts,
    ln1_gain,
    ln1_bias,
    q_bias,
    v_bias,
    qkv_weight,
    out_weight,
    out_bias,
    ln2_gain,
    ln2_bias,
    up_weight,
    up_bias,
    down_weight,
    down_bias,
):
    n_section, n_dp, n_tensor = (lax.axis_size(a) for a in ("section", "dp", "tensor"))
    section_idx = lax.axis_index("section")
    micro_count, share_rows, width = images.shape
    own_count = micro_count // n_section
    depth = qkv_weight.shape[1]
    part = qkv_weight.shape[3]

    own = section_idx * own_count

    def own_rows(values):
        mine = lax.dynamic_slice_in_dim(values, own, own_count, 0).reshape(-1, SEQ, values.shape[-1])
        return jnp.pad(mine, ((0, 0), (0, ROWS - SEQ), (0, 0))).reshape(-1, values.shape[-1])

    row_place = lax.axis_index("tensor") * share_rows + jnp.arange(share_rows)
    own_counts = lax.dynamic_slice_in_dim(counts, own, own_count, 0)
    live_rows = (row_place // SEQ < own_counts).astype(jnp.float32)
    live_rows = live_rows.reshape(-1, SEQ)
    live_rows = jnp.pad(live_rows, ((0, 0), (0, ROWS - SEQ))).reshape(-1, 1)

    shard = jnp.stack(
        [
            jnp.concatenate([qkv_weight[0].reshape(depth, -1), out_weight[0].T], axis=1),
            up_weight[0],
            down_weight[0].T,
        ]
    )
    given = [ln1_gain, ln1_bias, out_bias, ln2_gain, ln2_bias, down_bias, q_bias, v_bias, up_bias]
    first_rows = own_rows(images)
    gathered, row_out, *kept, vec = gather_and_forward(
        shard, first_rows, live_rows, given, n_section, n_dp, n_tensor
    )
    weight_sum, sec_rows, sec_grads, _, _, _, vec, q_sum, v_sum, up_sum = backward_and_reduce(
        gathered, own_rows(cotangent), live_rows, vec, [first_rows, row_out, *kept], n_dp
    )

    def placed_rows(values):
        values = values.reshape(-1, ROWS, width)[:, :SEQ]
        return values.reshape(1, micro_count, share_rows, width)

    section_out = placed_rows(sec_rows)
    input_grad = placed_rows(sec_grads)

    return (
        section_out,
        input_grad,
        weight_sum[0, :, : 3 * part].reshape(qkv_weight.shape),
        weight_sum[0, :, 3 * part :].T[None],
        weight_sum[1][None],
        weight_sum[2].T[None],
        q_sum,
        v_sum,
        up_sum,
        vec,
    )


def solution(mesh):
    placed = (
        P(None, ("dp", "tensor"), None),
        P(None, ("dp", "tensor"), None),
        P(None, "dp"),
        P("section", "dp"),
        P("section", "dp"),
        P("section", "tensor", "dp"),
        P("section", "tensor", "dp"),
        P("section", "dp", None, "tensor"),
        P("section", "tensor", "dp"),
        P("section", "dp"),
        P("section", "dp"),
        P("section", "dp"),
        P("section", "dp", "tensor"),
        P("section", "tensor", "dp"),
        P("section", "tensor", "dp"),
        P("section", "dp"),
    )
    return jax.shard_map(
        shards,
        mesh=mesh,
        in_specs=placed,
        out_specs=(
            P("section", None, ("dp", "tensor"), None),
            P("section", None, ("dp", "tensor"), None),
            P("section", "dp", None, "tensor"),
            P("section", "tensor", "dp"),
            P("section", "dp", "tensor"),
            P("section", "tensor", "dp"),
            P("section", "tensor", "dp"),
            P("section", "tensor", "dp"),
            P("section", "tensor", "dp"),
            P("section", None, ("dp", "tensor")),
        ),
        check_vma=False,
    )
```

```python
import functools
import jax
import jax.numpy as jnp
from jax import lax
from jax.experimental import pallas as pl
from jax.experimental.pallas import tpu as pltpu
from jax.sharding import PartitionSpec as P

CHUNK_ROWS = 48
SMALL_TICKS = 2
MESH_ID = pl.DeviceIdType.MESH


def sub_blocks(depth):
    return 1


def slot_sizes(n_dp, n_tensor):
    bits = [b for b in range(n_dp.bit_length()) if (1 << b) < n_dp]
    mid = n_tensor // 2
    weights = [bin(e).count("1") for e in range(n_dp)]

    def plane(weight):
        total = 0
        for j in range(mid):
            for e in range(n_dp):
                if weights[e] == weight:
                    for b in bits:
                        if not e >> b & 1:
                            chosen = [c for c in bits if (e | 1 << b) >> c & 1]
                            total += chosen[j % len(chosen)] == b
                    total += 2 * (weight >= 2) + 1
        return total

    first = [2 + len(bits)]
    columns = [2 * (2 + len(bits))] * (n_tensor - 1)
    planes = [plane(w) for w in range(1, len(bits) + 1)]
    over = mid * sum(w >= 2 for w in weights)
    crossed = [3 * over] * (mid - 1) + [over]
    rest = [mid * sum(w == 1 for w in weights)]
    return first + [columns[0], planes[0], columns[1]] + planes[1:] + columns[2:] + crossed + rest


class Place:
    def __init__(self, n_dp, n_tensor):
        self.n_dp, self.n_tensor = n_dp, n_tensor
        self.mid = n_tensor // 2
        self.bits = [b for b in range(n_dp.bit_length()) if (1 << b) < n_dp]
        self.s = lax.axis_index("section")
        self.d = lax.axis_index("dp")
        self.t = lax.axis_index("tensor")
        self.upper = lax.div(self.t, self.mid)
        self.has_next = self.t < n_tensor - 1
        self.has_prev = self.t > 0

    def away(self, e):
        other = self.d
        for b in self.bits:
            if e >> b & 1:
                other = other + (1 << b) * (1 - 2 * lax.rem(lax.div(self.d, 1 << b), 2))
        return other

    def last_bit(self, e, j):
        chosen = [b for b in self.bits if e >> b & 1]
        return chosen[j % len(chosen)]

    def own_side(self, j):
        return self.upper * self.mid + j

    def other_side(self, j):
        return (1 - self.upper) * self.mid + j

    def sibling(self):
        return (1 - self.s, self.d, self.t)

    def along(self, step):
        return (self.s, self.d, self.t + step)

    def hop(self, b):
        return (self.s, self.away(1 << b), self.t)

    def meet(self):
        barrier = pltpu.get_barrier_semaphore()
        line = [(self.s, self.d, lax.rem(self.t + k, self.n_tensor)) for k in range(1, self.n_tensor)]
        others = [self.sibling()] + [self.hop(b) for b in self.bits] + line
        for device in others:
            pl.semaphore_signal(barrier, inc=1, device_id=device, device_id_type=MESH_ID)
        pl.semaphore_wait(barrier, len(others))

    def rows_away(self, source, target, sec, sems):
        return pltpu.make_async_remote_copy(
            src_ref=source.at[sec],
            dst_ref=target.at[self.s],
            send_sem=sems.at[1],
            recv_sem=sems.at[2],
            device_id=self.sibling(),
            device_id_type=MESH_ID,
        )

    def hand_out(self, source, target, sec, sems):
        @pl.when(sec == self.s)
        def _():
            pltpu.make_async_copy(source.at[sec], target.at[self.s], sems.at[0]).start()

        @pl.when(sec != self.s)
        def _():
            self.rows_away(source, target, sec, sems).start()

    def handed_out(self, source, target, sems):
        pltpu.make_async_copy(source.at[0], target.at[self.s], sems.at[0]).wait()
        self.rows_away(source, target, 0, sems).wait()

    def by_weight(self, weight):
        return [e for e in range(self.n_dp) if bin(e).count("1") == weight]


DH = 64
SEQ = 197
EPS = 1e-06
F32 = jnp.float32
BF16 = jnp.bfloat16
ROWS = 208


def dot(left, right):
    return jnp.dot(left, right, preferred_element_type=F32)


def dot_cols(left, right):
    return lax.dot_general(left, right, (((1,), (1,)), ((), ())), preferred_element_type=F32)


def unit_rows(values):
    average = jnp.mean(values, axis=-1, keepdims=True)
    centered = values - average
    scale = lax.rsqrt(jnp.mean(centered * centered, axis=-1, keepdims=True) + EPS)
    return centered * scale, scale


def unit_rows_back(grad_unit, unit, scale):
    along = jnp.mean(grad_unit * unit, axis=-1, keepdims=True)
    return scale * (grad_unit - jnp.mean(grad_unit, axis=-1, keepdims=True) - unit * along)


def gelu_parts(hidden):
    below = 0.5 * (1.0 + lax.erf(hidden * (0.5**0.5)))
    density = jnp.exp(-0.5 * hidden * hidden) * 0.3989422804014327
    return hidden * below, below + hidden * density


def forward_kernel(n_dp, n_tensor, images, *refs):
    (
        attn_shard, up_shard, down_shard, rows, live, *given,
        out, row_out, qkv_out, p_out, heads_out, middle_out, active_out, slope_out, vec,
        w_buf, qkv_st, p_st, heads_st, active_st, slope_st, middle_st, normed, acc, row_buf,
        qkv_bias, up_bias, vec_in, qkv_bias_in, up_bias_in,
        own_sem, recv_sem, send_sem, part_sem, load_sem, store_sem, active_sem, once_sem, small_sem,
    ) = refs
    at = Place(n_dp, n_tensor)
    n_section = out.shape[0]
    shards = (attn_shard, up_shard, down_shard)
    n_blk = len(shards)
    depth, span = up_shard.shape
    half = span // 2
    n_all = n_section * n_blk
    n_sub = sub_blocks(depth)
    sub = depth // n_sub
    n_pieces = n_all * n_sub
    part = vec.shape[2] // n_tensor
    n_heads = part // DH

    def spread(value):
        return jnp.concatenate([jnp.where(at.d == k, value, 0.0) for k in range(n_dp)], axis=1)

    def spread_heads(ref):
        values = ref[0].astype(F32)
        return jnp.concatenate([spread(values[h : h + 1]) for h in range(values.shape[0])], axis=1)

    vec[...] = jnp.zeros_like(vec)
    qkv_bias[...] = jnp.zeros_like(qkv_bias)
    up_bias[...] = jnp.zeros_like(up_bias)
    placed = jnp.concatenate([spread(ref[...].astype(F32)) for ref in given[:6]], axis=0)
    vec[at.s] = jnp.where(at.t == 0, placed, 0.0)
    q_row, v_row = spread_heads(given[6]), spread_heads(given[7])
    qkv_bias[at.s, at.t] = jnp.concatenate([q_row, jnp.zeros_like(q_row), v_row], axis=1)
    up_bias[at.s, at.t] = spread_heads(given[8])
    at.meet()

    def whole(sec, b):
        return out.at[sec, b, at.t, rows_of(0), :]

    def rows_of(e):
        return pl.ds(pl.multiple_of(at.away(e) * depth, 16), depth)

    lanes = pl.ds(pl.multiple_of(at.s * half, 128), half)

    def piece(i, e, tt):
        block = lax.div(i, n_sub)
        start = at.away(e) * depth + lax.rem(i, n_sub) * sub
        rows_here = pl.ds(pl.multiple_of(start, 16), sub)
        return out.at[lax.div(block, n_blk), lax.rem(block, n_blk), tt, rows_here, lanes]

    def share(b):
        return pltpu.make_async_remote_copy(
            src_ref=shards[b],
            dst_ref=whole(at.s, b),
            send_sem=own_sem.at[1, b],
            recv_sem=own_sem.at[2, b],
            device_id=at.sibling(),
            device_id_type=MESH_ID,
        )

    for b in range(n_blk):
        pltpu.make_async_copy(shards[b], whole(at.s, b), own_sem.at[0, b]).start()
        share(b).start()

    def push(i, e, tt, device, e_there, slot, start):
        copy = pltpu.make_async_remote_copy(
            src_ref=piece(i, e, tt),
            dst_ref=piece(i, e, tt),
            send_sem=send_sem.at[i, slot],
            recv_sem=recv_sem.at[i, e_there * n_tensor + tt],
            device_id=device,
            device_id_type=MESH_ID,
        )
        if start:
            copy.start()
        else:
            copy.wait_send()

    def push_sib(i, e, tt, slot, start):
        copy = pltpu.make_async_remote_copy(
            src_ref=piece(i, e, tt),
            dst_ref=piece(i, e, tt),
            send_sem=send_sem.at[i, slot],
            recv_sem=part_sem.at[i, 0 if e == 0 else 1],
            device_id=at.sibling(),
            device_id_type=MESH_ID,
        )
        if start:
            copy.start()
        else:
            copy.wait_send()

    def await_piece(i, e, tt):
        pltpu.make_async_remote_copy(
            src_ref=piece(i, e, tt),
            dst_ref=piece(i, e, tt),
            send_sem=send_sem.at[i, 0],
            recv_sem=recv_sem.at[i, e * n_tensor + tt],
            device_id=at.sibling(),
            device_id_type=MESH_ID,
        ).wait_recv()

    def steps(i, start):
        slots = iter(range(10_000))

        def maybe(cond, action):
            if cond is None:
                action()
            else:
                pl.when(cond)(action)

        def ready(e, tt, cond=None):
            if start:
                maybe(cond, lambda: await_piece(i, e, tt))

        def go(e, tt, device, e_there, cond=None):
            slot = next(slots)
            maybe(cond, lambda: push(i, e, tt, device, e_there, slot, start))

        def go_sib(e, tt, cond=None):
            slot = next(slots)
            maybe(cond, lambda: push_sib(i, e, tt, slot, start))

        def first():
            block = lax.div(i, n_sub)
            sec, b = lax.div(block, n_blk), lax.rem(block, n_blk)
            is_first = lax.rem(i, n_sub) == 0
            if start:

                @pl.when(jnp.logical_and(sec == at.s, is_first))
                def _():
                    pltpu.make_async_copy(whole(at.s, b), whole(at.s, b), own_sem.at[0, b]).wait()

                @pl.when(jnp.logical_and(sec != at.s, is_first))
                def _():
                    pltpu.make_async_remote_copy(
                        src_ref=whole(1 - at.s, b),
                        dst_ref=whole(1 - at.s, b),
                        send_sem=own_sem.at[1, b],
                        recv_sem=own_sem.at[2, b],
                        device_id=at.sibling(),
                        device_id_type=MESH_ID,
                    ).wait_recv()

            go(0, at.t, at.along(1), 0, at.has_next)
            go(0, at.t, at.along(-1), 0, at.has_prev)
            for b in at.bits:
                go(0, at.t, at.hop(b), 1 << b)

        def column(k):
            low, high = at.t >= k, at.t + k < n_tensor
            for tt, cond, dev, more in (
                (at.t - k, low, at.along(1), jnp.logical_and(low, at.has_next)),
                (at.t + k, high, at.along(-1), jnp.logical_and(high, at.has_prev)),
            ):
                ready(0, tt, cond)
                go(0, tt, dev, 0, more)
                for b in at.bits:
                    go(0, tt, at.hop(b), 1 << b, cond)
                go_sib(0, tt, cond)

        def plane(weight):
            for j in range(at.mid):
                for e in at.by_weight(weight):
                    tt = at.own_side(j)
                    ready(e, tt)
                    for b in at.bits:
                        if not e >> b & 1 and at.last_bit(e | 1 << b, j) == b:
                            go(e, tt, at.hop(b), e | 1 << b)
                    if weight >= 2:
                        go(e, tt, at.along(1), e, at.t == at.mid - 1)
                        go(e, tt, at.along(-1), e, at.t == at.mid)
                    go_sib(e, tt)

        def crossed(k):
            down, up = at.t == at.mid - 1 - k, at.t == at.mid + k
            here = jnp.logical_or(down, up)
            for weight in range(2, len(at.bits) + 1):
                for e in at.by_weight(weight):
                    for j in range(at.mid):
                        tt = at.other_side(j)
                        ready(e, tt, here)
                        if k < at.mid - 1:
                            go(e, tt, at.along(1), e, up)
                            go(e, tt, at.along(-1), e, down)
                        go_sib(e, tt, here)

        def rest():
            for e in at.by_weight(1):
                for j in range(at.mid):
                    tt = at.other_side(j)
                    ready(e, tt)
                    go_sib(e, tt)

        groups = [first]
        for k in range(1, n_tensor):
            groups.append(functools.partial(column, k))
        planes = [functools.partial(plane, w) for w in range(1, len(at.bits) + 1)]
        merged = [groups[0]]
        far = [functools.partial(crossed, k) for k in range(at.mid)]
        order = [groups[1], planes[0], groups[2]] + planes[1:] + groups[3:] + far + [rest]
        return merged + order, slots


    small = [(vec, vec_in), (qkv_bias, qkv_bias_in), (up_bias, up_bias_in)]
    n_hops = len(at.bits)

    def small_copies(device, slot, to_place):
        return [
            pltpu.make_async_remote_copy(
                src_ref=mine.at[at.s],
                dst_ref=mine.at[at.s] if to_place else came_in.at[slot],
                send_sem=small_sem.at[0, slot, n],
                recv_sem=small_sem.at[1, slot, n],
                device_id=device,
                device_id_type=MESH_ID,
            )
            for n, (mine, came_in) in enumerate(small)
        ]

    def small_send(stage):
        if stage < n_hops:
            return [small_copies(at.hop(stage), stage, False)]
        if stage == n_hops:
            other = [lax.rem(at.t + k, n_tensor) for k in range(1, n_tensor)]
            return [small_copies((at.s, at.d, tt), n_hops + k, False) for k, tt in enumerate(other)]
        return [small_copies(at.sibling(), n_hops + n_tensor - 1, True)]

    def small_take(stage):
        sent = small_send(stage)
        for copies in sent:
            for copy in copies:
                copy.wait()
        if stage <= n_hops:
            for mine, came_in in small:
                total = mine[at.s]
                for slot in range(stage, stage + len(sent)):
                    total = total + came_in[slot]
                mine[at.s] = total

    def small_step(tick):
        for stage in range(n_hops + 3):

            @pl.when(tick == 1 + 2 * stage)
            def _():
                if stage:
                    small_take(stage - 1)
                if stage < n_hops + 2:
                    for copies in small_send(stage):
                        for copy in copies:
                            copy.start()

    lags = gather_lags(len(slot_sizes(n_dp, n_tensor)))
    pace = n_tensor // n_sub
    base = max(lags) + (n_sub - 1) * pace + 1
    n_phases = n_all - 1
    settle = max(lags) + n_tensor
    n_ticks = base + n_phases * n_tensor

    def finish(i):
        groups, _ = steps(i, False)
        for g in groups:
            g()

    def load(i, k, par):
        return pltpu.make_async_copy(out.at[i // n_blk, i % n_blk, k], w_buf.at[par], load_sem.at[par])

    def stores(i, k, par):
        sec, b = i // n_blk, i % n_blk
        if b == 0:
            pairs = [
                (qkv_st.at[par], qkv_out.at[sec, k], store_sem.at[par, 0]),
                (p_st.at[par], p_out.at[sec, k], store_sem.at[par, 1]),
                (heads_st.at[par], heads_out.at[sec, k], store_sem.at[par, 2]),
            ]
        elif b == 1:
            pairs = [(slope_st.at[par], slope_out.at[sec, k], store_sem.at[par, 3])]
        else:
            pairs = []
        return [pltpu.make_async_copy(*pair) for pair in pairs]

    def store_active(sec, k):
        return pltpu.make_async_copy(active_st.at[k], active_out.at[sec, k], active_sem.at[k])

    def store_middle(sec):
        return pltpu.make_async_copy(middle_st, middle_out.at[sec], once_sem.at[0])

    def store_rows(sec):
        return pltpu.make_async_copy(row_buf.at[sec], row_out.at[sec], once_sem.at[1 + sec])

    def attn_step(sec, k, par):
        @pl.when(k == 0)
        def _():
            values = (rows if sec == 0 else row_buf.at[sec - 1])[...].astype(F32)
            unit, _ = unit_rows(values)
            normed[...] = (unit * vec[sec, 0:1] + vec[sec, 1:2]).astype(BF16)
            acc[...] = values + vec[sec, 2:3]

        mixed = (dot(normed[...], w_buf[par, :, : 3 * part]) + qkv_bias[sec, k]).astype(BF16)
        qkv_st[par] = mixed
        keep = lax.broadcasted_iota(jnp.int32, (ROWS, ROWS), 0) < SEQ
        per_image = []
        for image in range(images):
            here = mixed[image * ROWS : (image + 1) * ROWS]
            per_head = []
            for head in range(n_heads):
                q, key, v = (
                    here[:, c * part + head * DH : c * part + (head + 1) * DH] for c in range(3)
                )
                scores = jnp.where(keep, dot_cols(key, q) * DH**-0.5, -1e30)
                scores = jnp.exp(scores - jnp.max(scores, axis=0, keepdims=True))
                total = jnp.sum(scores, axis=0, keepdims=True)
                chances = (scores * (1.0 / total)).astype(BF16)
                p_st[par, image, head] = chances
                per_head.append(dot(v.T, chances).T.astype(BF16))
            per_image.append(jnp.concatenate(per_head, axis=1))
        heads = jnp.concatenate(per_image, axis=0)
        heads_st[par] = heads
        acc[...] += dot_cols(heads, w_buf[par, :, 3 * part :])

    def up_step(sec, k, par):
        @pl.when(k == 0)
        def _():
            if sec:
                store_middle(sec - 1).wait()
            middle = acc[...]
            middle_st[...] = middle
            unit, _ = unit_rows(middle)
            normed[...] = (unit * vec[sec, 3:4] + vec[sec, 4:5]).astype(BF16)
            acc[...] = middle + vec[sec, 5:6]
            store_middle(sec).start()

        if sec:
            store_active(sec - 1, k).wait()
        hidden = dot(normed[...], w_buf[par]) + up_bias[sec, k]
        active, slope = gelu_parts(hidden)
        active_st[k] = active.astype(BF16)
        slope_st[par] = slope.astype(BF16)
        store_active(sec, k).start()

    def down_step(sec, k, par):
        acc[...] += dot_cols(active_st[k], w_buf[par])

        @pl.when(k == n_tensor - 1)
        def _():
            row_buf[sec] = (acc[...] * live[...]).astype(BF16)
            store_rows(sec).start()

    def await_block(i):
        sec, b = i // n_blk, i % n_blk
        for each in range(i * n_sub, (i + 1) * n_sub):
            for group, ref in (
                (0, out.at[sec, b, pl.ds(0, n_tensor - 1), pl.ds(0, sub), pl.ds(0, half)]),
                (1, out.at[sec, b, :, pl.ds(0, (n_dp - 1) * sub), pl.ds(0, half)]),
            ):
                pltpu.make_async_copy(ref, ref, part_sem.at[each, group]).wait()

    def compute(i, k):
        sec, b = i // n_blk, i % n_blk
        par = lax.rem(k, 2)

        if i == 0:

            @pl.when(k == 0)
            def _():
                await_block(0)
                load(0, 0, 0).start()

        if sec and b < 2:

            @pl.when(k == 0)
            def _():
                for back in (n_tensor - 2, n_tensor - 1):
                    for copy in stores(i - n_blk, back, back % 2):
                        copy.wait()

        load(i, k, par).wait()

        @pl.when(k < n_tensor - 1)
        def _():
            load(i, k + 1, 1 - par).start()

        if b < 2:

            @pl.when(k >= 2)
            def _():
                for copy in stores(i, k - 2, par):
                    copy.wait()

        (attn_step, up_step, down_step)[b](sec, k, par)
        for copy in stores(i, k, par):
            copy.start()

        @pl.when(k == n_tensor - 1)
        def _():
            if i + 1 < n_all:
                await_block(i + 1)
            if i + 1 < n_phases:
                load(i + 1, 0, 0).start()

    def body(it, carry):
        for g, lag in sorted(enumerate(lags), key=lambda item: item[1]):
            i = lax.div(it - lag, pace)

            @pl.when(jnp.logical_and(it - lag == i * pace, jnp.logical_and(it >= lag, i < n_pieces)))
            def _():
                run_group(i, g)

        small_step(it)
        i = lax.div(it - settle, pace)

        @pl.when(jnp.logical_and(it - settle == i * pace, jnp.logical_and(it >= settle, i < n_pieces)))
        def _():
            finish(i)

        for i in range(n_phases):
            first = base + i * n_tensor

            @pl.when(jnp.logical_and(it >= first, it < first + n_tensor))
            def _():
                compute(i, it - first)

        return carry

    def run_group(i, g):
        groups, slots = steps(i, True)
        for _ in range(sum(slot_sizes(n_dp, n_tensor)[:g])):
            next(slots)
        groups[g]()

    lax.fori_loop(0, n_ticks, body, 0)
    for i in range(n_pieces):
        if settle + i * pace >= n_ticks:
            finish(i)
    for b in range(n_blk):
        share(b).wait_send()
    last = n_section - 1
    for b in range(2):
        for back in (n_tensor - 2, n_tensor - 1):
            for copy in stores(last * n_blk + b, back, back % 2):
                copy.wait()
    for k in range(n_tensor):
        store_active(last, k).wait()
    store_middle(last).wait()
    for sec in range(last):
        store_rows(sec).wait()


def gather_lags(n_groups):
    known = [0, 3, 6, 7, 10, 11, 13, 16, 17]
    return [known[g] if g < len(known) else known[-1] + 3 * (g - len(known) + 1) for g in range(n_groups)]


def gather_and_forward(shards, rows, live, given, n_section, n_dp, n_tensor):
    n_blk = len(shards)
    depth, span = shards[1].shape
    n_rows, width = rows.shape
    images = n_rows // ROWS
    part = width // n_tensor
    n_heads = part // DH
    n_pieces = n_section * n_blk * sub_blocks(depth)
    n_hops = n_dp.bit_length() - 1
    n_sends = sum(slot_sizes(n_dp, n_tensor))
    n_small = n_hops + n_tensor
    shape = jax.ShapeDtypeStruct
    hbm = pl.BlockSpec(memory_space=pl.ANY)
    vmem = pl.BlockSpec(memory_space=pltpu.VMEM)
    dma = pltpu.SemaphoreType.DMA
    return pl.pallas_call(
        functools.partial(forward_kernel, n_dp, n_tensor, images),
        out_shape=[
            shape((n_section, n_blk, n_tensor, width, span), BF16),
            shape((n_section - 1, n_rows, width), BF16),
            shape((n_section, n_tensor, n_rows, 3 * part), BF16),
            shape((n_section, n_tensor, images, n_heads, ROWS, ROWS), BF16),
            shape((n_section, n_tensor, n_rows, part), BF16),
            shape((n_section, n_rows, width), F32),
            shape((n_section, n_tensor, n_rows, span), BF16),
            shape((n_section, n_tensor, n_rows, span), BF16),
            shape((n_section, 6, width), F32),
        ],
        in_specs=[hbm] * n_blk + [vmem] * (2 + len(given)),
        out_specs=[hbm] * 8 + [vmem],
        scratch_shapes=[
            pltpu.VMEM((2, width, span), BF16),
            pltpu.VMEM((2, n_rows, 3 * part), BF16),
            pltpu.VMEM((2, images, n_heads, ROWS, ROWS), BF16),
            pltpu.VMEM((2, n_rows, part), BF16),
            pltpu.VMEM((n_tensor, n_rows, span), BF16),
            pltpu.VMEM((2, n_rows, span), BF16),
            pltpu.VMEM((n_rows, width), F32),
            pltpu.VMEM((n_rows, width), BF16),
            pltpu.VMEM((n_rows, width), F32),
            pltpu.VMEM((n_section - 1, n_rows, width), BF16),
            pltpu.VMEM((n_section, n_tensor, 1, 3 * part), F32),
            pltpu.VMEM((n_section, n_tensor, 1, span), F32),
            pltpu.VMEM((n_small, 6, width), F32),
            pltpu.VMEM((n_small, n_tensor, 1, 3 * part), F32),
            pltpu.VMEM((n_small, n_tensor, 1, span), F32),
            dma((3, n_blk)),
            dma((n_pieces, n_dp * n_tensor)),
            dma((n_pieces, n_sends)),
            dma((n_pieces, 2)),
            dma((2,)),
            dma((2, 4)),
            dma((n_tensor,)),
            dma((1 + n_section,)),
            dma((2, n_small, 3)),
        ],
        compiler_params=pltpu.CompilerParams(
            collective_id=0, has_side_effects=True, vmem_limit_bytes=56 * 1024 * 1024
        ),
    )(*shards, rows, live, *given)


class Slots:
    def __init__(self, n_dp, n_tensor):
        self.n_tensor = n_tensor
        bits = [b for b in range(n_dp.bit_length()) if (1 << b) < n_dp]
        mid = n_tensor // 2
        count = len(bits) * n_tensor
        self.line = count
        count += n_tensor + 1
        self.hops = {}
        self.cross = {}
        for e in range(1, n_dp):
            if bin(e).count("1") >= 2:
                self.cross[e] = count
                count += n_tensor
            for j in range(mid):
                for b in bits:
                    if not e >> b & 1:
                        chosen = [c for c in bits if (e | 1 << b) >> c & 1]
                        if chosen[j % len(chosen)] == b:
                            self.hops[e, j, b] = count
                            count += 1
        self.count = count


def reduce_lags(n_groups):
    known = [0, 0, 2, 5, 5, 6, 12, 19]
    return [known[g] if g < len(known) else known[-1] + 3 * (g - len(known) + 1) for g in range(n_groups)]


def backward_kernel(
    n_dp, n_tensor, images, weights, cotangent, live, vec, *refs
):
    first_rows, row_out, *saved = refs[:8]
    (
        out, sec_rows, sec_grads, d_vec, d_qkv_bias, d_up_bias, own_vec, own_q, own_v, own_up,
        own, came, final, vec_in, qkv_bias_in, up_bias_in, ring, stage, w_buf, active_buf, slope_buf, qkv_buf, p_buf, heads_buf, rows_buf, middle_buf,
        grad_out, last_rows, grad_low, left_t, right_t, acc, grad_mid,
        load_sem, stage_sem, credit, recv_sem, send_sem, out_sem, small_sem, row_sem,
    ) = refs[8:]
    at = Place(n_dp, n_tensor)
    slots = Slots(n_dp, n_tensor)
    n_section, n_blk = weights.shape[:2]
    n_all = n_section * n_blk
    sub, half = final.shape[1:]
    n_pieces = final.shape[0]
    n_sub = n_pieces // n_all
    depth = sub * n_sub
    part = vec.shape[2] // n_tensor
    n_heads = part // DH
    lanes = pl.ds(pl.multiple_of(at.s * half, 128), half)
    sizes = send_sizes(n_dp, n_tensor)
    at.meet()

    def place(i):
        block = lax.div(i, n_sub)
        return n_section - 1 - lax.div(block, n_blk), n_blk - 1 - lax.rem(block, n_blk)

    def steps(i, start):
        counter = iter(range(10_000))

        def rows(e):
            return pl.multiple_of(at.away(e) * depth + lax.rem(i, n_sub) * sub, 16)

        def piece(e, tt):
            return own.at[lax.div(i, n_sub), tt, pl.ds(rows(e), sub), :]

        def maybe(cond, action):
            if cond is None:
                action()
            else:
                pl.when(cond)(action)

        def remote(e, tt, device, slot):
            k = next(counter)
            return pltpu.make_async_remote_copy(
                src_ref=piece(e, tt),
                dst_ref=came.at[i, slot],
                send_sem=send_sem.at[i, k],
                recv_sem=recv_sem.at[i, slot],
                device_id=device,
                device_id_type=MESH_ID,
            )

        def send(e, tt, device, slot, cond=None):
            copy = remote(e, tt, device, slot)
            maybe(cond, copy.start if start else copy.wait_send)

        def arrive(slot, cond=None):
            if start:
                copy = pltpu.make_async_copy(came.at[i, slot], came.at[i, slot], recv_sem.at[i, slot])
                maybe(cond, copy.wait)

        def total(e, tt, arrived, target=None):
            if not start or (target is None and not arrived):
                return
            base = rows(e)

            def chunk(c, carry):
                here = pl.ds(pl.multiple_of(base + c * CHUNK_ROWS, 16), CHUNK_ROWS)
                local = pl.ds(pl.multiple_of(c * CHUNK_ROWS, 16), CHUNK_ROWS)
                acc = own[lax.div(i, n_sub), tt, here, :].astype(jnp.float32)
                for slot in arrived:
                    acc = acc + came[i, slot, local, :].astype(jnp.float32)
                if target is None:
                    own[lax.div(i, n_sub), tt, here, :] = acc.astype(own.dtype)
                else:
                    target[i, local, :] = acc
                return carry

            lax.fori_loop(0, sub // CHUNK_ROWS, chunk, 0)

        def more(e, tt, slot, target=None):
            base = rows(e)

            def chunk(c, carry):
                here = pl.ds(pl.multiple_of(base + c * CHUNK_ROWS, 16), CHUNK_ROWS)
                local = pl.ds(pl.multiple_of(c * CHUNK_ROWS, 16), CHUNK_ROWS)
                acc = came[i, slot, local, :].astype(jnp.float32)
                if target is None:
                    own[lax.div(i, n_sub), tt, here, :] = (own[lax.div(i, n_sub), tt, here, :].astype(jnp.float32) + acc).astype(own.dtype)
                else:
                    target[i, local, :] = target[i, local, :] + acc
                return carry

            lax.fori_loop(0, sub // CHUNK_ROWS, chunk, 0)

        def also(e, tt, slot, cond, target=None):
            if start:

                def add():
                    arrive(slot)
                    more(e, tt, slot, target)

                pl.when(cond)(add)

        def line_slot(tt, from_next):
            return slots.line + tt + (0 if from_next else 1)

        def crossing():
            for e in range(1, n_dp):
                if bin(e).count("1") >= 2:
                    for j in range(at.mid):
                        tt = at.other_side(j)
                        slot = slots.cross[e] + tt
                        total(e, tt, [])
                        is_upper = at.t >= at.mid
                        also(e, tt, slot, jnp.logical_and(is_upper, at.has_next))
                        also(e, tt, slot, jnp.logical_and(jnp.logical_not(is_upper), at.has_prev))
                        send(e, tt, at.along(-1), slot, is_upper)
                        send(e, tt, at.along(1), slot, jnp.logical_not(is_upper))

        def leaves():
            for j in range(at.mid):
                for e in at.by_weight(1):
                    tt = at.other_side(j)
                    b = at.last_bit(e, j)
                    total(e, tt, [])
                    send(e, tt, at.hop(b), b * n_tensor + tt)

        def plane(weight):
            for e in at.by_weight(weight):
                for j in range(at.mid):
                    tt = at.own_side(j)
                    b = at.last_bit(e, j)
                    arrived = [slots.hops[e, j, c] for c in at.bits if (e, j, c) in slots.hops]
                    for slot in arrived:
                        arrive(slot)
                    total(e, tt, arrived)
                    if weight >= 2:
                        slot = slots.cross[e] + tt
                        also(e, tt, slot, at.t == at.mid - 1)
                        also(e, tt, slot, at.t == at.mid)
                    rest = e & ~(1 << b)
                    there = b * n_tensor + tt if rest == 0 else slots.hops[rest, j, b]
                    send(e, tt, at.hop(b), there)

        def column(k):
            low, high = at.t >= k, at.t + k < n_tensor
            for tt, cond, step, chain, from_next in (
                (at.t - k, low, -1, jnp.logical_and(low, at.has_next), True),
                (at.t + k, high, 1, jnp.logical_and(high, at.has_prev), False),
            ):
                arrived = [b * n_tensor + tt for b in at.bits]

                def sums(tt=tt, arrived=arrived):
                    for slot in arrived:
                        arrive(slot)
                    total(0, tt, arrived)

                if start:
                    pl.when(cond)(sums)
                slot = line_slot(tt, from_next)
                also(0, tt, slot, chain)
                send(0, tt, at.along(step), slot, cond)

        def last():
            arrived = [b * n_tensor + at.t for b in at.bits]
            for slot in arrived:
                arrive(slot)
            total(0, at.t, arrived, final)
            also(0, at.t, line_slot(at.t, True), at.has_next, final)
            also(0, at.t, line_slot(at.t, False), at.has_prev, final)
            sec, b = place(i)
            there = out.at[b, pl.ds(pl.multiple_of(lax.rem(i, n_sub) * sub, 16), sub), lanes]
            stay = pltpu.make_async_copy(final.at[i], there, out_sem.at[0, i])
            go = pltpu.make_async_remote_copy(
                src_ref=final.at[i],
                dst_ref=there,
                send_sem=out_sem.at[1, i],
                recv_sem=out_sem.at[2, i],
                device_id=at.sibling(),
                device_id_type=MESH_ID,
            )

            @pl.when(sec == at.s)
            def _():
                if start:
                    stay.start()
                else:
                    stay.wait()

            @pl.when(sec != at.s)
            def _():
                if start:
                    go.start()
                else:
                    go.wait_send()

        groups = [crossing, leaves]
        groups += [functools.partial(plane, w) for w in range(len(at.bits), 0, -1)]
        groups += [functools.partial(column, k) for k in range(n_tensor - 1, 0, -1)] + [last]
        return groups, counter

    lags = reduce_lags(len(sizes))

    def run_group(i, g):
        groups, counter = steps(i, True)
        for _ in range(sum(sizes[:g])):
            next(counter)
        groups[g]()

    phases = [(kind, sec) for sec in range(n_section - 1, -1, -1) for kind in ("down", "up", "attn")]
    phases.append(("out", n_section - 1))

    def loads(phase, k, par):
        kind, sec = phases[phase]
        rows = first_rows if sec == 0 else row_out.at[sec - 1]
        qkv, p, heads, middle, active, slope = (ref.at[sec] for ref in saved)
        if kind == "down":
            pairs = [(active.at[k], active_buf.at[par])]
            once = (middle, middle_buf)
        elif kind == "up":
            pairs = [
                (weights.at[sec, 1, k], w_buf.at[par, 0]),
                (weights.at[sec, 2, k], w_buf.at[par, 1]),
                (slope.at[k], slope_buf.at[par]),
            ]
            once = (rows, rows_buf)
        elif kind == "out":
            pairs = [(active.at[k], active_buf.at[par]), (weights.at[sec, 2, k], w_buf.at[par, 0])]
            once = (middle, middle_buf)
        else:
            pairs = [
                (weights.at[sec, 0, k], w_buf.at[par, 0]),
                (qkv.at[k], qkv_buf.at[par]),
                (p.at[k], p_buf.at[par]),
                (heads.at[k], heads_buf.at[par]),
            ]
            once = None
        copies = [
            pltpu.make_async_copy(src, dst, load_sem.at[par, n]) for n, (src, dst) in enumerate(pairs)
        ]
        return copies, lambda: pltpu.make_async_copy(*once, load_sem.at[0, 4])

    def start_loads(phase, k, par, is_first):
        copies, once = loads(phase, k, par)
        for copy in copies:
            copy.start()
        if is_first and phases[phase][0] != "attn":
            once().start()

    def shared(k):
        return pltpu.make_async_remote_copy(
            src_ref=stage.at[k],
            dst_ref=ring.at[k],
            send_sem=stage_sem.at[0, k],
            recv_sem=stage_sem.at[1, k],
            device_id=at.sibling(),
            device_id_type=MESH_ID,
        )

    def before_emit(k):
        shared(k).wait_send()
        pl.semaphore_wait(credit.at[k], 1)

    def emit(phase, k, low, high):
        first = at.s == 0
        own[phase, k] = jnp.where(first, low, high)
        stage[k] = jnp.where(first, high, low)

    def consume(phase, k, is_last):
        shared(k).wait_recv()

        def chunk(c, carry):
            here = pl.ds(pl.multiple_of(c * 96, 96), 96)
            total = own[phase, k, here].astype(F32) + ring[k, here].astype(F32)
            own[phase, k, here] = total.astype(own.dtype)
            return carry

        lax.fori_loop(0, own.shape[2] // 96, chunk, 0)
        if not is_last:
            pl.semaphore_signal(
                credit.at[k], inc=1, device_id=at.sibling(), device_id_type=MESH_ID
            )

    def column_sum(values):
        return jnp.sum(values, axis=0, keepdims=True)

    def down_step(sec, k, par, emits):
        @pl.when(k == 0)
        def _():
            source = cotangent if sec == n_section - 1 else grad_out.at[sec + 1]
            low = (source[...].astype(F32) * live[...]).astype(BF16)
            grad_low[...] = low
            left_t[...] = low.T

        d_down = dot(left_t[...], active_buf[par]).astype(BF16)
        emits(d_down[:, :half], d_down[:, half:])

    def out_step(sec, k, par):
        @pl.when(k == 0)
        def _():
            acc[...] = middle_buf[...] + vec[sec, 5:6]

        acc[...] += dot_cols(active_buf[par], w_buf[par, 0])

        @pl.when(k == n_tensor - 1)
        def _():
            last_rows[sec] = (acc[...] * live[...]).astype(BF16)
            for done in range(n_section - 1):
                pltpu.make_async_copy(row_out.at[done], last_rows.at[done], row_sem.at[2, 0]).wait()
            for each in range(n_section):
                at.hand_out(last_rows, sec_rows, each, row_sem.at[1])

    def up_step(sec, k, par, emits):
        @pl.when(k == 0)
        def _():
            unit, _ = unit_rows(middle_buf[...])
            right_t[...] = (unit * vec[sec, 3:4] + vec[sec, 4:5]).astype(BF16).T
            acc[...] = jnp.zeros_like(acc)

        grad_hidden = (dot(grad_low[...], w_buf[par, 1]) * slope_buf[par].astype(F32)).astype(BF16)
        d_up_bias[sec, k] = column_sum(grad_hidden.astype(F32))
        d_up = dot(right_t[...], grad_hidden).astype(BF16)
        emits(d_up[:, :half], d_up[:, half:])
        acc[...] += dot_cols(grad_hidden, w_buf[par, 0])

    def attn_step(sec, k, par, emits):
        w_attn = w_buf.at[par, 0]

        @pl.when(k == 0)
        def _():
            unit, scale = unit_rows(middle_buf[...])
            grad_norm = acc[...]
            low = grad_low[...].astype(F32)
            mid = low + unit_rows_back(grad_norm * vec[sec, 3:4], unit, scale)
            grad_mid[...] = mid
            d_vec[sec, 2:3] = column_sum(mid)
            d_vec[sec, 3:4] = column_sum(grad_norm * unit)
            d_vec[sec, 4:5] = column_sum(grad_norm)
            d_vec[sec, 5:6] = column_sum(low)
            mid = mid.astype(BF16)
            grad_low[...] = mid
            left_t[...] = mid.T
            unit, _ = unit_rows(rows_buf[...].astype(F32))
            right_t[...] = (unit * vec[sec, 0:1] + vec[sec, 1:2]).astype(BF16).T
            acc[...] = jnp.zeros_like(acc)

        d_out = dot(left_t[...], heads_buf[par]).astype(BF16)
        grad_heads = dot(grad_low[...], w_attn[:, 3 * part :]).astype(BF16)
        per_image = []
        for image in range(images):
            span = slice(image * ROWS, (image + 1) * ROWS)
            per_head = [[], [], []]
            for head in range(n_heads):
                q, key, v = (
                    qkv_buf[par, span, c * part + head * DH : c * part + (head + 1) * DH]
                    for c in range(3)
                )
                grad_o = grad_heads[span, head * DH : (head + 1) * DH]
                chosen = p_buf[par, image, head]
                chances = chosen.astype(F32)
                grad_chances = dot_cols(v, grad_o)
                along = jnp.sum(chances * grad_chances, axis=0, keepdims=True)
                grad_scores = (chances * (grad_chances - along)).astype(BF16)
                per_head[0].append((dot(key.T, grad_scores).T * DH**-0.5).astype(BF16))
                per_head[1].append((dot(grad_scores, q) * DH**-0.5).astype(BF16))
                per_head[2].append(dot(chosen, grad_o).astype(BF16))
            per_image.append(jnp.concatenate(per_head[0] + per_head[1] + per_head[2], axis=1))
        grad_mixed = jnp.concatenate(per_image, axis=0)
        d_qkv_bias[sec, k] = column_sum(grad_mixed.astype(F32))
        d_qkv = dot(right_t[...], grad_mixed).astype(BF16)
        emits(d_qkv[:, :half], jnp.concatenate([d_qkv[:, half:], d_out], axis=1))
        acc[...] += dot_cols(grad_mixed, w_attn[:, : 3 * part])

        @pl.when(k == n_tensor - 1)
        def _():
            unit, scale = unit_rows(rows_buf[...].astype(F32))
            grad_norm = acc[...]
            d_vec[sec, 0:1] = column_sum(grad_norm * unit)
            d_vec[sec, 1:2] = column_sum(grad_norm)
            total = grad_mid[...] + unit_rows_back(grad_norm * vec[sec, 0:1], unit, scale)
            grad_out[sec] = total.astype(BF16)
            at.hand_out(grad_out, sec_grads, sec, row_sem.at[0])

    def compute(phase, k):
        kind, sec = phases[phase]
        par = lax.rem(k, 2)
        copies, once = loads(phase, k, par)
        for copy in copies:
            copy.wait()

        if kind != "attn":

            @pl.when(k == 0)
            def _():
                once().wait()

        @pl.when(k < n_tensor - 1)
        def _():
            start_loads(phase, k + 1, 1 - par, False)

        if phase + 1 < len(phases):

            @pl.when(k == n_tensor - 1)
            def _():
                start_loads(phase + 1, 0, 0, True)

        if kind == "out":
            out_step(sec, k, par)

            @pl.when(k == 0)
            def _():
                for back in (n_tensor - 2, n_tensor - 1):
                    consume(phase - 1, back, True)

            return

        if phase:
            before_emit(k)

        if phase == 0:

            @pl.when(k == 0)
            def _():
                for done in range(n_section - 1):
                    pltpu.make_async_copy(
                        row_out.at[done], last_rows.at[done], row_sem.at[2, 0]
                    ).start()

        def emits(low, high):
            emit(phase, k, low, high)

        {"down": down_step, "up": up_step, "attn": attn_step}[kind](sec, k, par, emits)
        shared(k).start()

        @pl.when(k >= 2)
        def _():
            consume(phase, k - 2, phase == n_all - 1)

        if phase:

            @pl.when(k == 0)
            def _():
                for back in (n_tensor - 2, n_tensor - 1):
                    consume(phase - 1, back, False)

    n_busy = n_all * n_tensor
    settle = max(lags) + 2
    short = n_tensor // 2
    per_section = short + 2 * n_tensor

    def tick_of(it):
        sec, step = lax.div(it, n_blk * n_tensor), lax.rem(it, n_blk * n_tensor)
        is_short = step < n_tensor
        tick = sec * per_section + jnp.where(is_short, lax.div(step, 2), step - n_tensor + short)
        over = it >= len(phases) * n_tensor
        tick = jnp.where(over, n_section * per_section + short + it - len(phases) * n_tensor, tick)
        return tick, jnp.logical_or(over, jnp.logical_or(jnp.logical_not(is_short), lax.rem(step, 2) == 1))

    def start_of(i):
        block, within = i // n_sub, i % n_sub
        sec, b = block // n_blk, block % n_blk
        first = sec * per_section + (short, short + n_tensor, per_section)[b]
        return first + (2 if i == 1 else 0) + within

    def piece_at(tick):
        found, starts = 0, False
        for i in range(n_pieces):
            here = tick == start_of(i)
            found = jnp.where(here, i, found)
            starts = jnp.logical_or(starts, here)
        return found, starts


    small = [(d_vec, vec_in), (d_qkv_bias, qkv_bias_in), (d_up_bias, up_bias_in)]
    n_hops = len(at.bits)

    def small_copies(stage, device, slot):
        sec = 1 - at.s if stage == 0 else at.s
        return [
            pltpu.make_async_remote_copy(
                src_ref=mine.at[sec],
                dst_ref=came_in.at[slot],
                send_sem=small_sem.at[0, slot, n],
                recv_sem=small_sem.at[1, slot, n],
                device_id=device,
                device_id_type=MESH_ID,
            )
            for n, (mine, came_in) in enumerate(small)
        ]

    def small_send(stage):
        if stage == 0:
            return [small_copies(0, at.sibling(), 0)]
        if stage <= n_hops:
            return [small_copies(stage, at.hop(stage - 1), stage)]
        other = [lax.rem(at.t + k, n_tensor) for k in range(1, n_tensor)]
        return [
            small_copies(stage, (at.s, at.d, tt), n_hops + 1 + k) for k, tt in enumerate(other)
        ]

    def small_take(stage):
        sent = small_send(stage)
        for copies in sent:
            for copy in copies:
                copy.wait()
        first = stage if stage <= n_hops else n_hops + 1
        for mine, came_in in small:
            total = mine[at.s]
            for slot in range(first, first + len(sent)):
                total = total + came_in[slot]
            mine[at.s] = total

    def small_step(tick):
        for stage in range(n_hops + 2):

            @pl.when(tick == SMALL_TICKS * stage)
            def _():
                if stage:
                    small_take(stage - 1)
                for copies in small_send(stage):
                    for copy in copies:
                        copy.start()

        @pl.when(tick == SMALL_TICKS * (n_hops + 2))
        def _():
            small_take(n_hops + 1)
            own_small()

    def own_small():
        def pick(values, index, count, width):
            parts = [jnp.where(index == c, values[:, c * width : (c + 1) * width], 0.0) for c in range(count)]
            return functools.reduce(jnp.add, parts)

        n_places = n_dp * n_tensor
        own_vec[0] = pick(d_vec[at.s], at.d * n_tensor + at.t, n_places, own_vec.shape[2])
        qkv_row, up_row = d_qkv_bias[at.s, at.t], d_up_bias[at.s, at.t]
        for target, row in (
            (own_q, qkv_row[:, :part]),
            (own_v, qkv_row[:, 2 * part :]),
            (own_up, up_row),
        ):
            for head in range(target.shape[1]):
                lanes_of = row[:, head * DH : (head + 1) * DH]
                target[0, head : head + 1] = pick(lanes_of, at.d, n_dp, DH // n_dp)

    def finish(i):
        groups, _ = steps(i, False)
        for g in groups:
            g()
        sec, b = place(i)

        @pl.when(sec == at.s)
        def _():
            pltpu.make_async_copy(final.at[i], final.at[i], out_sem.at[2, i]).wait()

    def body(it, carry):
        for phase in range(len(phases)):

            @pl.when(lax.div(it, n_tensor) == phase)
            def _():
                compute(phase, lax.rem(it, n_tensor))

        tick, ticks = tick_of(it)
        for g, lag in sorted(enumerate(lags), key=lambda item: item[1]):
            i, starts = piece_at(tick - lag)

            @pl.when(jnp.logical_and(ticks, starts))
            def _():
                run_group(i, g)

        small_step(it - n_busy)
        i, starts = piece_at(tick - settle)

        @pl.when(jnp.logical_and(ticks, starts))
        def _():
            finish(i)

        return carry

    start_loads(0, 0, 0, True)
    last_tick = start_of(n_pieces - 1) + max(lags)
    tail = max(last_tick + 1, n_section * per_section + short + SMALL_TICKS * (n_hops + 2)) - n_section * per_section - short
    n_ticks = len(phases) * n_tensor + tail
    last_tick = n_section * per_section + short + tail - 1
    lax.fori_loop(0, n_ticks, body, 0)
    for i in range(n_pieces):
        if start_of(i) + settle > last_tick:
            finish(i)
    for k in range(n_tensor):
        shared(k).wait_send()
    at.handed_out(grad_out, sec_grads, row_sem.at[0])
    at.handed_out(last_rows, sec_rows, row_sem.at[1])


def send_sizes(n_dp, n_tensor):
    bits = n_dp.bit_length() - 1
    mid = n_tensor // 2
    weights = [bin(e).count("1") for e in range(n_dp)]
    sizes = [2 * mid * sum(w >= 2 for w in weights), mid * bits]
    sizes += [mid * sum(w == k for w in weights) for k in range(bits, 0, -1)]
    return sizes + [2] * (n_tensor - 1) + [0]


def backward_and_reduce(weights, cotangent, live, vec, saved, n_dp):
    n_section, n_blk, n_tensor, width, span = weights.shape
    n_rows = cotangent.shape[0]
    images = n_rows // ROWS
    part = width // n_tensor
    n_all = n_section * n_blk
    depth, half = width // n_dp, span // 2
    n_pieces = n_all * sub_blocks(depth)
    sub = depth // sub_blocks(depth)
    slots = Slots(n_dp, n_tensor)
    n_sends = sum(send_sizes(n_dp, n_tensor))
    n_small = n_dp.bit_length() + n_tensor - 1
    shape = jax.ShapeDtypeStruct
    hbm = pl.BlockSpec(memory_space=pl.ANY)
    vmem = pl.BlockSpec(memory_space=pltpu.VMEM)
    dma = pltpu.SemaphoreType.DMA
    return pl.pallas_call(
        functools.partial(backward_kernel, n_dp, n_tensor, images),
        out_shape=[
            shape((n_blk, depth, span), F32),
            shape((n_section, n_rows, width), BF16),
            shape((n_section, n_rows, width), BF16),
            shape((n_section, 6, width), F32),
            shape((n_section, n_tensor, 1, 3 * part), F32),
            shape((n_section, n_tensor, 1, span), F32),
            shape((1, 6, width // (n_dp * n_tensor)), F32),
            shape((1, part // DH, DH // n_dp), F32),
            shape((1, part // DH, DH // n_dp), F32),
            shape((1, span // DH, DH // n_dp), F32),
        ],
        in_specs=[hbm] + [vmem] * 3 + [hbm] * len(saved),
        out_specs=[hbm] * 3 + [vmem] * 7,
        scratch_shapes=[
            pltpu.VMEM((n_all, n_tensor, width, half), BF16),
            pltpu.VMEM((n_pieces, slots.count, sub, half), BF16),
            pltpu.VMEM((n_pieces, sub, half), F32),
            pltpu.VMEM((n_small, 6, width), F32),
            pltpu.VMEM((n_small, n_tensor, 1, 3 * part), F32),
            pltpu.VMEM((n_small, n_tensor, 1, span), F32),
            pltpu.VMEM((n_tensor, width, half), BF16),
            pltpu.VMEM((n_tensor, width, half), BF16),
            pltpu.VMEM((2, 2, width, span), BF16),
            pltpu.VMEM((2, n_rows, span), BF16),
            pltpu.VMEM((2, n_rows, span), BF16),
            pltpu.VMEM((2, n_rows, 3 * part), BF16),
            pltpu.VMEM((2, images, part // DH, ROWS, ROWS), BF16),
            pltpu.VMEM((2, n_rows, part), BF16),
            pltpu.VMEM((n_rows, width), BF16),
            pltpu.VMEM((n_rows, width), F32),
            pltpu.VMEM((n_section, n_rows, width), BF16),
            pltpu.VMEM((n_section, n_rows, width), BF16),
            pltpu.VMEM((n_rows, width), BF16),
            pltpu.VMEM((width, n_rows), BF16),
            pltpu.VMEM((width, n_rows), BF16),
            pltpu.VMEM((n_rows, width), F32),
            pltpu.VMEM((n_rows, width), F32),
            dma((2, 5)),
            dma((2, n_tensor)),
            pltpu.SemaphoreType.REGULAR((n_tensor,)),
            dma((n_pieces, slots.count)),
            dma((n_pieces, n_sends)),
            dma((3, n_pieces)),
            dma((2, n_small, 3)),
            dma((3, 3)),
        ],
        compiler_params=pltpu.CompilerParams(
            collective_id=1, has_side_effects=True, vmem_limit_bytes=64 * 1024 * 1024 - 256 * 1024
        ),
    )(weights, cotangent, live, vec, *saved)


AXES = ("section", "tensor", "dp")


def shards(
    images,
    cotangent,
    counts,
    ln1_gain,
    ln1_bias,
    q_bias,
    v_bias,
    qkv_weight,
    out_weight,
    out_bias,
    ln2_gain,
    ln2_bias,
    up_weight,
    up_bias,
    down_weight,
    down_bias,
):
    n_section, n_dp, n_tensor = (lax.axis_size(a) for a in ("section", "dp", "tensor"))
    section_idx = lax.axis_index("section")
    micro_count, share_rows, width = images.shape
    own_count = micro_count // n_section
    depth = qkv_weight.shape[1]
    part = qkv_weight.shape[3]

    own = section_idx * own_count

    def own_rows(values):
        mine = lax.dynamic_slice_in_dim(values, own, own_count, 0).reshape(-1, SEQ, values.shape[-1])
        return jnp.pad(mine, ((0, 0), (0, ROWS - SEQ), (0, 0))).reshape(-1, values.shape[-1])

    row_place = lax.axis_index("tensor") * share_rows + jnp.arange(share_rows)
    own_counts = lax.dynamic_slice_in_dim(counts, own, own_count, 0)
    live_rows = (row_place // SEQ < own_counts).astype(jnp.float32)
    live_rows = live_rows.reshape(-1, SEQ)
    live_rows = jnp.pad(live_rows, ((0, 0), (0, ROWS - SEQ))).reshape(-1, 1)

    weight_shards = (
        jnp.concatenate([qkv_weight[0].reshape(depth, -1), out_weight[0].T], axis=1),
        up_weight[0],
        down_weight[0].T,
    )
    given = [ln1_gain, ln1_bias, out_bias, ln2_gain, ln2_bias, down_bias, q_bias, v_bias, up_bias]
    first_rows = own_rows(images)
    gathered, row_out, *kept, vec = gather_and_forward(
        weight_shards, first_rows, live_rows, given, n_section, n_dp, n_tensor
    )
    weight_sum, sec_rows, sec_grads, _, _, _, vec, q_sum, v_sum, up_sum = backward_and_reduce(
        gathered, own_rows(cotangent), live_rows, vec, [first_rows, row_out, *kept], n_dp
    )

    def placed_rows(values):
        values = values.reshape(-1, ROWS, width)[:, :SEQ]
        return values.reshape(1, micro_count, share_rows, width)

    section_out = placed_rows(sec_rows)
    input_grad = placed_rows(sec_grads)

    return (
        section_out,
        input_grad,
        weight_sum[0, :, : 3 * part].reshape(qkv_weight.shape),
        weight_sum[0, :, 3 * part :].T[None],
        weight_sum[1][None],
        weight_sum[2].T[None],
        q_sum,
        v_sum,
        up_sum,
        vec,
    )


def solution(mesh):
    placed = (
        P(None, ("dp", "tensor"), None),
        P(None, ("dp", "tensor"), None),
        P(None, "dp"),
        P("section", "dp"),
        P("section", "dp"),
        P("section", "tensor", "dp"),
        P("section", "tensor", "dp"),
        P("section", "dp", None, "tensor"),
        P("section", "tensor", "dp"),
        P("section", "dp"),
        P("section", "dp"),
        P("section", "dp"),
        P("section", "dp", "tensor"),
        P("section", "tensor", "dp"),
        P("section", "tensor", "dp"),
        P("section", "dp"),
    )
    return jax.shard_map(
        shards,
        mesh=mesh,
        in_specs=placed,
        out_specs=(
            P("section", None, ("dp", "tensor"), None),
            P("section", None, ("dp", "tensor"), None),
            P("section", "dp", None, "tensor"),
            P("section", "tensor", "dp"),
            P("section", "dp", "tensor"),
            P("section", "tensor", "dp"),
            P("section", "tensor", "dp"),
            P("section", "tensor", "dp"),
            P("section", "tensor", "dp"),
            P("section", None, ("dp", "tensor")),
        ),
        check_vma=False,
    )
```
